32 devices in a mesh: dp: 8 (over z, y), chan: 4 (over x, core).
Axes of the slice: x: 2, y: 2, z: 4, core: 2. Of those that a mesh axis runs over, the one named last changes fastest.
Arguments:
- clips: bfloat16 [16, 14, 14, 6656], P('dp', None, None, 'chan'), may hold values from -6 to 6
- clip_len: int32 [16], P('dp'), may hold values from 4 to 8, as said below
- w_plain: bfloat16 [2, 212992], P(None, 'chan'), may hold values from -0.21875 to 0.21875
- w_mid: bfloat16 [2, 133120], P(None, 'chan'), may hold values from -0.21875 to 0.21875
- k_mid: bfloat16 [2, 460800], P(None, 'chan'), may hold values from -0.15625 to 0.15625
- w_small: bfloat16 [2, 26624], P(None, 'chan'), may hold values from -0.21875 to 0.21875
- k_small: bfloat16 [2, 36864], P(None, 'chan'), may hold values from -0.375 to 0.375
- w_pool: bfloat16 [2, 106496], P(None, 'chan'), may hold values from -0.21875 to 0.21875
- gains: bfloat16 [2, 1024], P(None, 'chan'), may hold values from 0.5 to 1.5
- shifts: bfloat16 [2, 1024], P(None, 'chan'), may hold values from -3 to 3
- grad_out: bfloat16 [8, 7, 7, 6656], P('dp', None, None, 'chan'), may hold values from -6 to 6
Outputs:
- mixed_out: bfloat16 [8, 7, 7, 6656], P('dp', None, None, 'chan')
- clips_grad: float32 [16, 14, 14, 6656], P('dp', None, None, 'chan')
- w_plain_grad: float32 [2, 212992], P(None, 'chan')
- w_mid_grad: float32 [2, 133120], P(None, 'chan')
- k_mid_grad: float32 [2, 460800], P(None, 'chan')
- w_small_grad: float32 [2, 26624], P(None, 'chan')
- k_small_grad: float32 [2, 36864], P(None, 'chan')
- w_pool_grad: float32 [2, 106496], P(None, 'chan')
- gains_grad: float32 [2, 1024], P(None, 'chan')
- shifts_grad: float32 [2, 1024], P(None, 'chan')
The draws below stay inside these ranges and needn't reach their ends.
Inputs may be any that keep to these rules, and one draw needn't show every extreme that they name: `clip_len`: clip lengths are even; the 2 clips of each group fit its 16 slots, and each group has one clip of exactly 8 frames.
All inputs are finite; a program needn't handle non-finite values.
Results may differ from the reference program's by a relative error of at most 0.0095.
Values may be sent and summed in bfloat16 or wider, within the bound.
No kernel may reach another device: no remote copies, remote signals or barrier semaphores. Data moves between devices by JAX's collectives and lax.ppermute only.
A program may use at most 256 MiB of HBM per device.

```python
import jax
import jax.numpy as jnp
from jax import lax

C0 = 256
C1A = 160
C1B = 320
C2A = 32
C2B = 128
C3 = 128
HW = 14
MOST = 8
FR_DEV = 16
CLIPS = 2
FRAMES = 128
CLIP_COUNT = 16
CIN = 832
GN = 1024
N_CHAN = 4


def draw_clip_len(key, part):
    key = jax.random.fold_in(key, 7)
    first_key, second_key = jax.random.split(key)
    halves = jax.random.randint(first_key, (CLIP_COUNT,), 2, MOST // 2 + 1)
    groups = CLIP_COUNT // CLIPS
    chosen = jax.random.randint(second_key, (groups,), 0, CLIPS)
    order = jnp.arange(CLIP_COUNT, dtype=jnp.int32)
    longest = order % CLIPS == chosen[order // CLIPS]
    return jnp.where(longest, MOST, 2 * halves).astype(jnp.int32)


def levels(key, shape, shards, least, largest):
    def one(position, parts):
        draws = jax.random.uniform(jax.random.fold_in(jax.random.fold_in(key, 6), position), (parts,), jnp.float32, least / len(shards), largest / len(shards))
        return jnp.repeat(jnp.exp(draws), shape[position] // parts).reshape((-1,) + (1,) * (len(shape) - position - 1))

    level = one(*shards[0])
    for cut in shards[1:]:
        level = level * one(*cut)
    return level


def normal_values(rng, extent, scale, reach, cuts=(), kind=jnp.bfloat16):
    level = levels(rng, extent, cuts, -0.22, 0.18) if cuts else 1.0
    entries = jax.random.normal(rng, extent, jnp.float32) * scale * level
    return jnp.minimum(jnp.maximum(entries, -reach), reach).astype(kind)


def setup_inputs(seed: int = 0) -> dict:
    arg_keys = jax.random.split(jax.random.key(seed), 12)
    clips = normal_values(arg_keys[0], (FRAMES // 8, HW, HW, 8 * CIN), 1.0, 6.0, ((0, 8), (3, 4)))
    clip_len = draw_clip_len(jax.random.fold_in(arg_keys[11], 71), 0)
    w_plain = normal_values(arg_keys[2], (2, C0 * CIN), CIN ** -0.5, 0.21875, ((1, 4),))
    w_mid = normal_values(arg_keys[3], (2, C1A * CIN), CIN ** -0.5, 0.21875, ((1, 4),))
    k_mid = normal_values(arg_keys[4], (2, C1B * 9 * C1A), (9 * C1A) ** -0.5, 0.15625, ((1, 4),))
    w_small = normal_values(arg_keys[5], (2, C2A * CIN), CIN ** -0.5, 0.21875, ((1, 4),))
    k_small = normal_values(arg_keys[6], (2, C2B * 9 * C2A), (9 * C2A) ** -0.5, 0.375, ((1, 4),))
    w_pool = normal_values(arg_keys[7], (2, C3 * CIN), CIN ** -0.5, 0.21875, ((1, 4),))
    gains = jnp.clip(1.0 + 0.1 * jax.random.normal(arg_keys[8], (2, GN), jnp.float32), 0.5, 1.5).astype(jnp.bfloat16)
    shifts = normal_values(arg_keys[9], (2, GN), 0.5, 3.0, ((1, 4),))
    grad_out = normal_values(arg_keys[10], (FRAMES // 16, HW // 2, HW // 2, 8 * CIN), 1.0, 6.0, ((0, 8), (3, 4)))
    return {"clips": clips, "clip_len": clip_len, "w_plain": w_plain, "w_mid": w_mid, "k_mid": k_mid, "w_small": w_small, "k_small": k_small, "w_pool": w_pool, "gains": gains, "shifts": shifts, "grad_out": grad_out}


@jax.custom_vjp
def low(v):
    return lax.optimization_barrier(v.astype(jnp.bfloat16)).astype(jnp.float32)

@jax.custom_vjp
def low_back(v):
    return v

def low_keep(v):
    return (low(v), None)

def low_pass(kept, grad):
    return (grad,)

def back_keep(v):
    return (v, None)

def back_low(kept, grad):
    return (low(grad),)
low.defvjp(low_keep, low_pass)
low_back.defvjp(back_keep, back_low)
epsilon = 1e-05

def frame_info(clip_len, frames):
    lengths = clip_len.reshape(-1, CLIPS)
    ends = jnp.cumsum(lengths, axis=1).astype(jnp.int32)
    local = jnp.arange(frames, dtype=jnp.int32)
    passed = lax.optimization_barrier(jnp.sum((local[None, :, None] >= ends[:, None, :]).astype(jnp.int32), axis=2)).astype(jnp.int32)
    groups = lengths.shape[0]
    ident = passed + jnp.arange(groups, dtype=jnp.int32)[:, None] * (CLIPS + 1)
    valid = (local[None, :] < ends[:, CLIPS - 1:]).astype(jnp.float32)
    return (ident.reshape(-1).astype(jnp.int32), valid.reshape(-1))

def unpack_field(field):
    blocks, side, width = (field.shape[0], field.shape[1], field.shape[3])
    quarter = width // (8 * N_CHAN)
    moved = field.reshape(blocks, side, side, N_CHAN, 8, quarter).transpose(0, 4, 1, 2, 3, 5)
    return moved.reshape(blocks * 8, side, side, N_CHAN * quarter)

def pack_field(field):
    frames, side, width = (field.shape[0], field.shape[1], field.shape[3])
    quarter = width // N_CHAN
    moved = field.reshape(frames // 8, 8, side, side, N_CHAN, quarter).transpose(0, 2, 3, 4, 1, 5)
    return moved.reshape(frames // 8, side, side, 8 * width)

def open_matrix(flat, outputs):
    return flat.reshape(2, outputs, -1).transpose(0, 2, 1)

def open_kernel(flat, outputs, inputs):
    return flat.reshape(2, outputs, 3, 3, inputs).transpose(0, 2, 3, 4, 1)

def time_shift(field, ident, step):
    blank = jnp.zeros_like(field[:1])
    outside = jnp.full((1,), -1, jnp.int32)
    if step > 0:
        moved = jnp.concatenate([field[1:], blank], 0)
        other = jnp.concatenate([ident[1:], outside], 0)
    else:
        moved = jnp.concatenate([blank, field[:-1]], 0)
        other = jnp.concatenate([outside, ident[:-1]], 0)
    keep = (other == ident).astype(field.dtype)
    return moved * keep[:, None, None, None]

def time_box(field, ident):
    return time_shift(field, ident, -1) + field + time_shift(field, ident, 1)

def box_pool(field, ident):
    total = time_box(field, ident)
    side = field.shape[1]
    padded = jnp.pad(total, ((0, 0), (1, 1), (1, 1), (0, 0)))
    result = jnp.zeros_like(field)
    for row in range(3):
        for column in range(3):
            result = result + padded[:, row:row + side, column:column + side]
    return result / 27.0

def conv_plane(field, kernel):
    return lax.conv_general_dilated(field, kernel, (1, 1), 'SAME', dimension_numbers=('NHWC', 'HWIO', 'NHWC'), precision=lax.Precision.HIGHEST, preferred_element_type=jnp.float32)

def matmul(left, right):
    return jnp.dot(left, right, precision=lax.Precision.HIGHEST, preferred_element_type=jnp.float32)

def conv_parts(vector, widths):
    table = vector.reshape(N_CHAN, -1)
    pieces = []
    start = 0
    for width in widths:
        pieces.append(table[:, start:start + width].reshape(-1))
        start += width
    return pieces

def quarters(branches):
    cells = branches[0].shape[0]
    return jnp.concatenate([branch.reshape(cells, N_CHAN, -1) for branch in branches], 2).reshape(cells, -1)

def norm_act(values, mask, gain, shift):
    total = lax.optimization_barrier(jnp.sum(values * mask, 0))
    squares = lax.optimization_barrier(jnp.sum(values * values * mask, 0))
    count = jnp.sum(mask)
    mean = total / count
    variance = squares / count - mean * mean
    inverse = lax.rsqrt(variance + epsilon)
    normed = (values - mean) * inverse
    return jax.nn.silu(gain * normed + shift) * mask

def layer(field, weights, ident, valid):
    w_plain, w_mid, k_mid, w_small, k_small, w_pool, gain, shift = weights
    frames, side = (field.shape[0], field.shape[1])
    cells = frames * side * side
    mask = jnp.repeat(valid, side * side)[:, None]
    flat = field.reshape(cells, -1)
    pooled = low(box_pool(field, ident)).reshape(cells, -1)
    widths = (C0 // N_CHAN, C1A // N_CHAN, C1B // N_CHAN, C2A // N_CHAN, C2B // N_CHAN, C3 // N_CHAN)
    gain_parts = conv_parts(gain, widths)
    shift_parts = conv_parts(shift, widths)
    z_plain = low_back(matmul(flat, w_plain))
    z_mid = low_back(matmul(flat, w_mid))
    z_small = low_back(matmul(flat, w_small))
    z_pool = low_back(matmul(pooled, w_pool))
    a_plain = norm_act(z_plain, mask, gain_parts[0], shift_parts[0])
    a_mid = low(norm_act(z_mid, mask, gain_parts[1], shift_parts[1]))
    a_small = low(norm_act(z_small, mask, gain_parts[3], shift_parts[3]))
    a_pool = norm_act(z_pool, mask, gain_parts[5], shift_parts[5])
    z_wide = low_back((conv_plane(time_box(a_mid.reshape(frames, side, side, -1), ident), k_mid) / 3.0).reshape(cells, -1))
    z_narrow = low_back((conv_plane(time_box(a_small.reshape(frames, side, side, -1), ident), k_small) / 3.0).reshape(cells, -1))
    a_wide = norm_act(z_wide, mask, gain_parts[2], shift_parts[2])
    a_narrow = norm_act(z_narrow, mask, gain_parts[4], shift_parts[4])
    return quarters([a_plain, a_wide, a_narrow, a_pool]).reshape(frames, side, side, -1)

def pool_pairs(field):
    frames, side, width = (field.shape[0], field.shape[1], field.shape[3])
    return field.reshape(frames // 2, 2, side // 2, 2, side // 2, 2, width).mean(axis=(1, 3, 5))

def reference(clips, clip_len, w_plain, w_mid, k_mid, w_small, k_small, w_pool, gains, shifts, grad_out):
    ident, valid = frame_info(clip_len, FR_DEV)
    ident_half = ident.reshape(-1, 2)[:, 0]
    valid_half = valid.reshape(-1, 2)[:, 0]
    params = tuple((item.astype(jnp.float32) for item in (clips, w_plain, w_mid, k_mid, w_small, k_small, w_pool, gains, shifts)))

    def forward(packed, plain_flat, mid_flat, kmid_flat, small_flat, ksmall_flat, pool_flat, gain_all, shift_all):
        field = unpack_field(packed)
        weights = (open_matrix(plain_flat, C0), open_matrix(mid_flat, C1A), open_kernel(kmid_flat, C1B, C1A), open_matrix(small_flat, C2A), open_kernel(ksmall_flat, C2B, C2A), open_matrix(pool_flat, C3), gain_all, shift_all)
        first = layer(field, tuple((item[0] for item in weights)), ident, valid)
        halved = low(pool_pairs(first))
        second = layer(halved, tuple((item[1] for item in weights)), ident_half, valid_half)
        return pack_field(second)
    output, pullback = jax.vjp(forward, *params)
    grads = pullback(grad_out.astype(jnp.float32))
    return (output.astype(jnp.bfloat16), grads[0], grads[1], grads[2], grads[3], grads[4], grads[5], grads[6], grads[7], grads[8])
```

```python
import functools

import jax
import jax.numpy as jnp
from jax import lax
from jax.experimental import pallas as pl
from jax.experimental.pallas import tpu as pltpu
from jax.sharding import PartitionSpec as P

CIN = 832
QUARTER = 208
WIDE, NARROW = 80, 32
MID, SMALL, PLAIN, POOL = 40, 8, 64, 32
REDUCED = MID + SMALL
DENSE = REDUCED + PLAIN
ROWS = DENSE + POOL
CLIPS = 2
EPSILON = 1e-05
F32 = jnp.float32
BF16 = jnp.bfloat16
LANES = 128


class Size:
    def __init__(self, side, frames):
        self.side = side
        self.frames = frames
        self.cells = side * side
        self.rows = self.cells * frames
        self.padded = -(-self.rows // LANES) * LANES
        self.band = 2 if side % 2 == 0 else side
        self.chunks = side // self.band
        self.step = self.band * side
        self.group = LANES // frames
        self.full = self.cells // self.group
        self.rest = self.cells - self.full * self.group
        self.kept = BF16 if frames % 16 == 0 else F32


def call(body, outs, scratch, scalars, args, flops=0):
    specs = [pl.BlockSpec(memory_space=pltpu.SMEM)] * len(scalars)
    specs += [pl.BlockSpec(memory_space=pltpu.VMEM)] * len(args)
    moved = sum(a.size * a.dtype.itemsize for a in args)
    moved += sum(o.size * o.dtype.itemsize for o in outs)
    return pl.pallas_call(
        body,
        out_shape=outs,
        in_specs=specs,
        out_specs=[pl.BlockSpec(memory_space=pltpu.VMEM)] * len(outs),
        scratch_shapes=scratch,
        compiler_params=pltpu.CompilerParams(vmem_limit_bytes=40 * 1024 * 1024),
        cost_estimate=pl.CostEstimate(flops=flops, bytes_accessed=moved, transcendentals=0),
    )(*scalars, *args)


def shaped(shape, dtype=F32):
    return jax.ShapeDtypeStruct(shape, dtype)


def sigmoid(value):
    return 0.5 * jnp.tanh(0.5 * value) + 0.5


def row_table(rows):
    index = lax.broadcasted_iota(jnp.int32, (8, LANES), 0)
    table = jnp.zeros((8, LANES), F32)
    for position, row in enumerate(rows):
        table = jnp.where(index == position, row, table)
    return table


def time_box(value, mask_ref):
    cells, frames, width = value.shape
    flat = value.reshape(cells * frames, width)
    before = pltpu.roll(flat, 1, 0).reshape(value.shape)
    after = pltpu.roll(flat, cells * frames - 1, 0).reshape(value.shape)
    return value + before * mask_ref[1] + after * mask_ref[2]


def norm_rows(all_ref, table_ref, tile):
    total = jnp.sum(all_ref[...], 0)
    count = total[4:5]
    mean = total[2 * tile : 2 * tile + 1] / count
    variance = total[2 * tile + 1 : 2 * tile + 2] / count - mean * mean
    inverse = lax.rsqrt(variance + EPSILON)
    gain = table_ref[2 * tile : 2 * tile + 1]
    shift = table_ref[2 * tile + 1 : 2 * tile + 2]
    return mean, inverse, gain, shift, count


def activate(value, rows, mask_ref):
    mean, inverse, gain, shift, _ = rows
    shifted = gain * ((value - mean) * inverse) + shift
    return shifted * sigmoid(shifted) * mask_ref[0]


def inner_grad(grad, value, rows, mask_ref):
    mean, inverse, gain, shift, _ = rows
    normed = (value - mean) * inverse
    shifted = gain * normed + shift
    sigma = sigmoid(shifted)
    return grad * mask_ref[0] * sigma * (1.0 + shifted * (1.0 - sigma)), normed


def norm_delta(inner, value, rows, back_ref, tile, mask_ref):
    mean, inverse, gain, _, count = rows
    total = jnp.sum(back_ref[...], 0)
    shift_grad = total[2 * tile : 2 * tile + 1] / count
    gain_grad = total[2 * tile + 1 : 2 * tile + 2] / count
    normed = (value - mean) * inverse
    return (gain * inverse) * (inner - mask_ref[0] * (shift_grad + normed * gain_grad))


def publish(stat_ref, rows):
    stat_ref[...] = jnp.broadcast_to(row_table(rows)[None], stat_ref.shape)


def collapse(value):
    return jnp.sum(value, 0, keepdims=True)


def windows():
    result = []
    for frame in range(8):
        start = frame * QUARTER
        first, offset = start // LANES, start % LANES
        result.append((first, -(-(offset + QUARTER) // LANES), offset))
    return result


def unpack_rows(line, frame):
    first, tiles, offset = windows()[frame]
    value = line[:, first * LANES : (first + tiles) * LANES]
    if offset:
        value = pltpu.roll(value, tiles * LANES - offset, 1)
    return value[:, : 2 * LANES]


def pack_rows(parts):
    tiles = [None] * 13
    for frame, value in enumerate(parts):
        first, count, offset = windows()[frame]
        if count == 3:
            value = jnp.concatenate([value, jnp.zeros((value.shape[0], LANES), value.dtype)], 1)
        if offset:
            value = pltpu.roll(value, offset, 1)
        for index in range(count):
            piece = value[:, index * LANES : (index + 1) * LANES]
            place = first + index
            tiles[place] = piece if tiles[place] is None else tiles[place] + piece
    return tiles


def assemble(first, second, third):
    blank = jnp.zeros_like(first)
    lane = lax.broadcasted_iota(jnp.int32, (first.shape[0], 2 * LANES), 1)
    plain = pltpu.roll(jnp.concatenate([first, blank], 1), 2 * LANES - REDUCED, 1)
    middle = pltpu.roll(jnp.concatenate([second, blank], 1), PLAIN, 1)
    pool = pltpu.roll(jnp.concatenate([third, blank], 1), PLAIN + WIDE + NARROW, 1)
    return jnp.where(lane < PLAIN, plain, 0.0) + middle + pool


def separate(value):
    lane = lax.broadcasted_iota(jnp.int32, (value.shape[0], LANES), 1)
    plain = pltpu.roll(value, REDUCED, 1)[:, :LANES]
    middle = pltpu.roll(value, 2 * LANES - PLAIN, 1)[:, :LANES]
    pool = pltpu.roll(value, 2 * LANES - PLAIN - WIDE - NARROW, 1)[:, :LANES]
    first = jnp.where((lane >= REDUCED) & (lane < DENSE), plain, 0.0)
    second = jnp.where(lane < WIDE + NARROW, middle, 0.0)
    third = jnp.where(lane < POOL, pool, 0.0)
    return first, second, third


def unpack_kernel(size, raw, out, scratch):
    side, frames = size.side, size.frames

    def line(row, carry):
        for block in range(frames // 8):
            value = raw[block, row].astype(F32)
            for frame in range(8):
                place = pl.ds(row * side * frames + 8 * block + frame, side, stride=frames)
                part = unpack_rows(value, frame)
                scratch[0, place, :] = part[:, :LANES]
                scratch[1, place, :] = part[:, LANES:]
        return carry

    lax.fori_loop(0, side, line, 0)

    def narrow(index, carry):
        place = pl.ds(index * size.step * frames, size.step * frames)
        out[place, :LANES] = scratch[0, place, :].astype(BF16)
        out[place, LANES:] = scratch[1, place, : QUARTER - LANES].astype(BF16)
        return carry

    lax.fori_loop(0, size.chunks, narrow, 0)


def grad_kernel(size, raw, first, second, third, scratch):
    side, frames = size.side, size.frames

    def line(row, carry):
        value = raw[0, row].astype(F32)
        for frame in range(8):
            place = pl.ds(row * side * frames + frame, side, stride=frames)
            part = unpack_rows(value, frame)
            scratch[0, place, :] = part[:, :LANES]
            scratch[1, place, :] = part[:, LANES:]
        return carry

    lax.fori_loop(0, side, line, 0)
    parts = separate(jnp.concatenate([scratch[0], scratch[1]], 1))
    for ref, part in zip((first, second, third), parts):
        ref[...] = part.reshape(ref.shape)


def dot(left, right, dims=((1,), (0,))):
    return lax.dot_general(left, right, (dims, ((), ())), preferred_element_type=F32)


def project_kernel(size, me, x0, x1, x2, x3, w_ref, mask, z0, z1, stat, weights, field):
    side, frames, step = size.side, size.frames, size.step
    weights[...] = jnp.zeros_like(weights)
    for position in range(4):
        owner = me[0] ^ position
        weights[position, 0:DENSE] = w_ref[owner, 0:DENSE]
        weights[position, LANES : LANES + POOL] = w_ref[owner, DENSE:ROWS]
    field[...] = jnp.zeros_like(field)
    blank = jnp.zeros((frames, LANES), F32)

    def chunk(index, carry):
        total, squares = carry
        rows = pl.ds(index * step * frames, step * frames)
        value = dot(x0[rows, :], weights[0], ((1,), (1,)))
        value += dot(x1[rows, :], weights[1], ((1,), (1,)))
        value += dot(x2[rows, :], weights[2], ((1,), (1,)))
        value += dot(x3[rows, :], weights[3], ((1,), (1,)))
        dense = value[:, :LANES].reshape(step, frames, LANES)
        pool = value[:, LANES:].reshape(size.band, side, frames, LANES)
        z0[pl.ds(index * step, step)] = dense
        field[pl.ds(1 + index * size.band, size.band), 1 : side + 1] = pool
        return total + jnp.sum(dense, 0), squares + jnp.sum(dense * dense, 0)

    total, squares = lax.fori_loop(0, size.chunks, chunk, (blank, blank))

    def line(row, carry):
        pool_total, pool_squares = carry
        pool = pool_line(size, field, row, mask)
        z1[pl.ds(row * side, side)] = pool
        return pool_total + jnp.sum(pool, 0), pool_squares + jnp.sum(pool * pool, 0)

    pool_total, pool_squares = lax.fori_loop(0, side, line, (blank, blank))
    valid = mask[0]
    rows = [collapse(item * valid) for item in (total, squares, pool_total, pool_squares, blank + size.cells)]
    publish(stat, rows)


def pool_line(size, field, row, mask):
    side = size.side
    lines = field[pl.ds(row, 3)]
    column = lines[0] + lines[1] + lines[2]
    value = column[0:side] + column[1 : side + 1] + column[2 : side + 2]
    return time_box(value, mask) * (1.0 / 27.0)


def blocks(size, one):
    def step(index, carry):
        one(index, size.group)
        return carry

    lax.fori_loop(0, size.full, step, 0)
    if size.rest:
        one(size.full, size.rest)


def turn(size, value, cells):
    flat = value.reshape(cells * size.frames, value.shape[-1])
    if cells < size.group:
        blank = jnp.zeros((LANES - cells * size.frames, value.shape[-1]), value.dtype)
        flat = jnp.concatenate([flat, blank], 0)
    return flat.T


def lanes_of(block):
    if isinstance(block, int):
        return pl.ds(block * LANES, LANES)
    return pl.ds(pl.multiple_of(block * LANES, LANES), LANES)


def reduced_kernel(size, z0, totals, table, mask, out):
    rows = norm_rows(totals, table, 0)

    def one(block, cells):
        value = activate(z0[pl.ds(block * size.group, cells)], rows, mask)
        out[:, lanes_of(block)] = turn(size, value, cells)[:REDUCED].astype(BF16)

    blocks(size, one)


def conv_kernel(size, me, p0, p1, p2, p3, kernel, mask, field, z2, stat, joined):
    side, frames, step = size.side, size.frames, size.step
    for position, piece in enumerate((p0, p1, p2, p3)):
        place = pl.multiple_of((me[0] ^ position) * REDUCED, 16)
        joined[pl.ds(place, REDUCED), :] = piece[...]
    field[...] = jnp.zeros_like(field)

    def one(block, cells):
        value = joined[:, lanes_of(block)].astype(F32).T
        value = value.reshape(size.group, frames, 4 * REDUCED).astype(size.kept)
        for index in range(cells):
            cell = block * size.group + index
            row = cell // side if isinstance(cell, int) else lax.div(cell, side)
            field[row + 1, cell - row * side + 1] = value[index]

    blocks(size, one)
    blank = jnp.zeros((frames, LANES), F32)

    def chunk(index, carry):
        total, squares = carry
        value = jnp.zeros((step * frames, LANES), F32)
        for row in range(3):
            for column in range(3):
                part = field[pl.ds(index * size.band + row, size.band), column : column + side]
                part = part.reshape(step * frames, 4 * REDUCED).astype(BF16)
                value += dot(part, kernel[3 * row + column])
        value = time_box(value.reshape(step, frames, LANES), mask) * (1.0 / 3.0)
        z2[pl.ds(index * step, step)] = value
        return total + jnp.sum(value, 0), squares + jnp.sum(value * value, 0)

    total, squares = lax.fori_loop(0, size.chunks, chunk, (blank, blank))
    valid = mask[0]
    one_row = jnp.zeros((1, LANES), F32)
    rows = [collapse(total * valid), collapse(squares * valid), one_row, one_row, collapse(valid) * size.cells]
    publish(stat, rows)


def halve_into(size, value, scratch, index):
    half = size.side // 2
    value = value.reshape(2, half, 2, size.frames, LANES)
    value = value[0] + value[1]
    value = value[:, 0] + value[:, 1]
    rows = half * size.frames
    scratch[pl.ds(index * rows, rows), :] = value.reshape(rows, LANES)


def halved_rows(scratch):
    count = scratch.shape[0] // 2
    return (scratch[pl.ds(0, count, stride=2), :] + scratch[pl.ds(1, count, stride=2), :]) * 0.125


def first_half_kernel(size, z0, z1, totals, table, mask, h0, h1, s0, s1):
    for tile, (z, out, scratch) in enumerate(((z0, h0, s0), (z1, h1, s1))):
        rows = norm_rows(totals, table, tile)

        def chunk(index, carry, z=z, scratch=scratch, rows=rows):
            value = activate(z[pl.ds(index * size.step, size.step)], rows, mask)
            halve_into(size, value, scratch, index)
            return carry

        lax.fori_loop(0, size.chunks, chunk, 0)
        out[...] = halved_rows(scratch).reshape(out.shape)


def second_half_kernel(size, z2, totals, table, mask, h0, h1, out, scratch):
    rows = norm_rows(totals, table, 0)

    def chunk(index, carry):
        value = activate(z2[pl.ds(index * size.step, size.step)], rows, mask)
        halve_into(size, value, scratch, index)
        return carry

    lax.fori_loop(0, size.chunks, chunk, 0)
    count = out.shape[0]
    value = assemble(h0[...].reshape(count, LANES), halved_rows(scratch), h1[...].reshape(count, LANES))
    out[...] = value[:, :QUARTER].astype(BF16)


def strided(scratch, start, count, stride):
    place = pl.ds(start, count, stride=stride)
    return jnp.concatenate([scratch[0, place, :], scratch[1, place, :]], 1)


def output_kernel(size, z0, z1, z2, totals, totals2, table, table2, mask, out, scratch):
    side, frames = size.side, size.frames
    parts = [
        activate(z[...], norm_rows(total, tab, tile), mask).reshape(size.rows, LANES)
        for z, total, tab, tile in ((z0, totals, table, 0), (z2, totals2, table2, 0), (z1, totals, table, 1))
    ]
    value = assemble(*parts)
    scratch[0] = value[:, :LANES]
    scratch[1] = value[:, LANES:]

    def line(row, carry):
        start = row * side * frames
        lines = [strided(scratch, start + frame, side, frames) for frame in range(8)]
        for place, tile in enumerate(pack_rows(lines)):
            out[0, row, :, place * LANES : (place + 1) * LANES] = tile.astype(BF16)
        return carry

    lax.fori_loop(0, side, line, 0)


def spread(size, grad, scratch):
    value = grad[...].reshape(-1, LANES)
    count = value.shape[0]
    scratch[pl.ds(0, count, stride=2), :] = value
    scratch[pl.ds(1, count, stride=2), :] = value


def grad_chunk(size, grad, scratch, index):
    if scratch is None:
        return grad[pl.ds(index * size.step, size.step)]
    half = size.side // 2
    rows = half * size.frames
    value = scratch[pl.ds(index * rows, rows), :].reshape(half, 1, size.frames, LANES)
    value = jnp.broadcast_to(value, (half, 2, size.frames, LANES)).reshape(1, size.side, size.frames, LANES)
    value = jnp.broadcast_to(value, (2, size.side, size.frames, LANES))
    return value.reshape(size.step, size.frames, LANES)


def second_sums_kernel(size, grad, z2, totals, table, mask, stat, *scratch):
    scratch = scratch[0] if scratch else None
    if scratch is not None:
        spread(size, grad, scratch)
    rows = norm_rows(totals, table, 0)
    blank = jnp.zeros((size.frames, LANES), F32)

    def chunk(index, carry):
        shift_grad, gain_grad = carry
        value = z2[pl.ds(index * size.step, size.step)]
        inner, normed = inner_grad(grad_chunk(size, grad, scratch, index), value, rows, mask)
        return shift_grad + jnp.sum(inner, 0), gain_grad + jnp.sum(inner * normed, 0)

    shift_grad, gain_grad = lax.fori_loop(0, size.chunks, chunk, (blank, blank))
    publish(stat, [collapse(shift_grad), collapse(gain_grad)])


def conv_back_kernel(size, me, grad, z2, totals, back, table, mask, kernel, delta, o0, o1, o2, o3, field, result, turned, *scratch):
    side, frames, step = size.side, size.frames, size.step
    scratch = scratch[0] if scratch else None
    if scratch is not None:
        spread(size, grad, scratch)
    rows = norm_rows(totals, table, 0)
    field[...] = jnp.zeros_like(field)

    def first(index, carry):
        value = z2[pl.ds(index * step, step)]
        inner, _ = inner_grad(grad_chunk(size, grad, scratch, index), value, rows, mask)
        value = norm_delta(inner, value, rows, back, 0, mask).astype(BF16).astype(size.kept)
        delta[pl.ds(index * step, step)] = value
        field[pl.ds(1 + index * size.band, size.band), 1 : side + 1] = value.reshape(size.band, side, frames, LANES)
        return carry

    lax.fori_loop(0, size.chunks, first, 0)

    def chunk(index, carry):
        value = jnp.zeros((step * frames, 4 * REDUCED), F32)
        for row in range(3):
            for column in range(3):
                part = field[pl.ds(index * size.band + 2 - row, size.band), 2 - column : 2 - column + side]
                part = part.reshape(step * frames, LANES).astype(BF16)
                value += dot(part, kernel[3 * row + column], ((1,), (1,)))
        result[pl.ds(index * step, step)] = value.reshape(step, frames, 4 * REDUCED)
        return carry

    lax.fori_loop(0, size.chunks, chunk, 0)

    def one(block, cells):
        value = turn(size, result[pl.ds(block * size.group, cells)], cells)
        turned[:, lanes_of(block)] = value.astype(BF16)

    blocks(size, one)
    for position, out in enumerate((o0, o1, o2, o3)):
        place = pl.multiple_of((me[0] ^ position) * REDUCED, 16)
        out[...] = turned[pl.ds(place, REDUCED), :]


def kernel_grad_kernel(size, field, delta, mask, out, total):
    side, frames, step = size.side, size.frames, size.step
    total[...] = jnp.zeros_like(total)

    def chunk(index, carry):
        value = delta[pl.ds(index * step, step)].astype(F32)
        value = time_box(value, mask).reshape(step * frames, LANES)
        upper = value.astype(BF16).astype(F32)
        both = jnp.concatenate([upper, value - upper], 1).T.astype(BF16)
        for row in range(3):
            for column in range(3):
                part = field[pl.ds(index * size.band + row, size.band), column : column + side]
                part = part.reshape(step * frames, 4 * REDUCED).astype(BF16)
                total[3 * row + column] += dot(both, part)
        return carry

    lax.fori_loop(0, size.chunks, chunk, 0)
    for tap in range(9):
        out[tap] = (total[tap, :LANES] + total[tap, LANES:]) * (1.0 / 3.0)


def first_sums_kernel(size, p0, p1, p2, p3, g0, g1, z0, z1, totals, table, mask, i0, i1, stat, field, *scratch):
    step, frames = size.step, size.frames
    s0, s1 = scratch if scratch else (None, None)
    if scratch:
        spread(size, g0, s0)
        spread(size, g1, s1)

    def one(block, cells):
        place = lanes_of(block)
        value = p0[:, place].astype(F32) + p1[:, place].astype(F32)
        value += p2[:, place].astype(F32) + p3[:, place].astype(F32)
        value = jnp.concatenate([value, jnp.zeros((LANES - REDUCED, LANES), F32)], 0).T
        value = value.reshape(size.group, frames, LANES)
        field[pl.ds(block * size.group, cells)] = value[:cells]

    blocks(size, one)
    rows0 = norm_rows(totals, table, 0)
    rows1 = norm_rows(totals, table, 1)
    blank = jnp.zeros((frames, LANES), F32)

    def chunk(index, carry):
        place = pl.ds(index * step, step)
        grad = time_box(field[place], mask) * (1.0 / 3.0) + grad_chunk(size, g0, s0, index)
        inner0, normed0 = inner_grad(grad, z0[place], rows0, mask)
        inner1, normed1 = inner_grad(grad_chunk(size, g1, s1, index), z1[place], rows1, mask)
        i0[place] = inner0
        i1[place] = inner1
        sums = (inner0, inner0 * normed0, inner1, inner1 * normed1)
        return tuple(old + jnp.sum(new, 0) for old, new in zip(carry, sums))

    sums = lax.fori_loop(0, size.chunks, chunk, (blank,) * 4)
    publish(stat, [collapse(item) for item in sums])


def first_delta_kernel(size, z0, z1, i0, i1, totals, back, table, mask, out, field, pooled):
    side, step, frames = size.side, size.step, size.frames
    rows0 = norm_rows(totals, table, 0)
    rows1 = norm_rows(totals, table, 1)
    field[...] = jnp.zeros_like(field)

    def chunk(index, carry):
        place = pl.ds(index * step, step)
        value = norm_delta(i1[place], z1[place], rows1, back, 1, mask).astype(BF16).astype(F32)
        field[pl.ds(1 + index * size.band, size.band), 1 : side + 1] = value.reshape(size.band, side, frames, LANES)
        return carry

    lax.fori_loop(0, size.chunks, chunk, 0)

    def line(row, carry):
        pooled[pl.ds(row * side, side)] = pool_line(size, field, row, mask)
        return carry

    lax.fori_loop(0, side, line, 0)

    def one(block, cells):
        place = pl.ds(block * size.group, cells)
        value = norm_delta(i0[place], z0[place], rows0, back, 0, mask)
        out[0:DENSE, lanes_of(block)] = turn(size, value, cells)[:DENSE].astype(BF16)
        out[DENSE:ROWS, lanes_of(block)] = turn(size, pooled[place], cells)[:POOL].astype(BF16)

    blocks(size, one)


def weight_grad_kernel(size, me, delta, x0, x1, x2, x3, out):
    for position, x in enumerate((x0, x1, x2, x3)):
        out[me[0] ^ position] = dot(delta[:, : size.rows], x[...])


def input_rows(size, d0, d1, d2, d3, weights, turned, scratch):
    for position in range(4):
        value = jnp.concatenate([weights[position].astype(F32), jnp.zeros((ROWS, 2 * LANES - QUARTER), F32)], 1)
        turned[position] = value.T.astype(BF16)
    width = 640 if size.padded % 640 == 0 else size.padded

    def one(block, carry):
        place = pl.ds(pl.multiple_of(block * width, LANES), width)
        value = dot(turned[0], d0[:, place])
        for position, piece in enumerate((d1, d2, d3)):
            value += dot(turned[position + 1], piece[:, place])
        value = value.T
        rows = pl.ds(pl.multiple_of(block * width, LANES), width)
        scratch[0, rows, :] = value[:, :LANES]
        scratch[1, rows, :] = value[:, LANES:]
        return carry

    lax.fori_loop(0, size.padded // width, one, 0)


def input_half_kernel(size, d0, d1, d2, d3, weights, first, second, third, turned, scratch):
    input_rows(size, d0, d1, d2, d3, weights, turned, scratch)
    value = jnp.concatenate([scratch[0, : size.rows, :], scratch[1, : size.rows, :]], 1)
    parts = separate(value * 0.125)
    for ref, part in zip((first, second, third), parts):
        ref[...] = part.reshape(ref.shape)


def input_kernel(size, d0, d1, d2, d3, weights, out, turned, scratch):
    side, frames = size.side, size.frames
    input_rows(size, d0, d1, d2, d3, weights, turned, scratch)

    def line(row, carry):
        for block in range(frames // 8):
            start = row * side * frames + 8 * block
            lines = [strided(scratch, start + frame, side, frames) for frame in range(8)]
            for place, tile in enumerate(pack_rows(lines)):
                out[block, row, :, place * LANES : (place + 1) * LANES] = tile
        return carry

    lax.fori_loop(0, side, line, 0)


def pairs(axis_size, shift):
    return [(index, index ^ shift) for index in range(axis_size)]


def gather_four(piece):
    other = lax.ppermute(piece, "chan", pairs(4, 2))
    core = lax.ppermute(piece, "chan", pairs(4, 1))
    both = lax.ppermute(other, "chan", pairs(4, 1))
    return piece, core, other, both


def exchange_four(pieces):
    result = [pieces[0]]
    for shift in (1, 2, 3):
        result.append(lax.ppermute(pieces[shift], "chan", pairs(4, shift)))
    return result


def share(stat):
    return lax.all_to_all(stat, "dp", 0, 0, tiled=True)


def reduce_flat(parts, count):
    lengths = [part.shape[0] for part in parts]
    whole = jnp.concatenate(parts, 0)
    unit = count * 16 * LANES
    total = -(-whole.shape[0] // unit) * unit
    whole = jnp.pad(whole, (0, total - whole.shape[0])).astype(BF16).reshape(count, -1, LANES)
    mine = jnp.sum(lax.all_to_all(whole, "dp", 0, 0, tiled=True).astype(F32), 0).astype(BF16)
    spread_out = jnp.broadcast_to(mine[None], (count,) + mine.shape)
    whole = lax.all_to_all(spread_out, "dp", 0, 0, tiled=True).astype(F32).reshape(-1)
    result = []
    start = 0
    for length in lengths:
        result.append(whole[start : start + length])
        start += length
    return result


def frame_masks(clip_len, frames):
    ends = jnp.cumsum(clip_len)
    local = jnp.arange(frames, dtype=jnp.int32)
    ident = jnp.sum((local[:, None] >= ends[None, :]).astype(jnp.int32), 1)
    valid = (local < ends[CLIPS - 1]).astype(F32)
    return ident, valid


def mask_table(ident, valid):
    outside = jnp.full((1,), -1, jnp.int32)
    before = (jnp.concatenate([outside, ident[:-1]]) == ident).astype(F32)
    after = (jnp.concatenate([ident[1:], outside]) == ident).astype(F32)
    table = jnp.stack([valid, before, after])
    return jnp.broadcast_to(table[:, :, None], table.shape + (LANES,))


def norm_tables(gain, shift):
    names = {"plain": (0, 64), "mid": (64, 104), "wide": (104, 184), "small": (184, 192), "narrow": (192, 224), "pool": (224, 256)}

    def tile(values, *parts):
        row = jnp.concatenate([values[names[part][0] : names[part][1]] for part in parts])
        return jnp.pad(row, (0, LANES - row.shape[0]))

    gain, shift = gain.astype(F32), shift.astype(F32)
    blank = jnp.zeros((LANES,), F32)
    first = [tile(values, "mid", "small", "plain") for values in (gain, shift)]
    first += [tile(values, "pool") for values in (gain, shift)]
    second = [tile(values, "wide", "narrow") for values in (gain, shift)]
    return jnp.stack(first + [blank] * 4), jnp.stack(second + [blank] * 6)


def norm_grads(first_all, second_all):
    first = jnp.sum(first_all, 0)
    second = jnp.sum(second_all, 0)

    def joined(row):
        return jnp.concatenate(
            [
                first[row, REDUCED:DENSE],
                first[row, 0:MID],
                second[row, 0:WIDE],
                first[row, MID:REDUCED],
                second[row, WIDE : WIDE + NARROW],
                first[row + 2, 0:POOL],
            ]
        )

    return joined(1), joined(0)


def open_weights(w_plain, w_mid, k_mid, w_small, k_small, w_pool):
    rows = [item.reshape(-1, 4, QUARTER) for item in (w_mid, w_small, w_plain, w_pool)]
    dense = jnp.concatenate(rows, 0).transpose(1, 0, 2)
    wide = k_mid.reshape(WIDE, 9, 4, MID).transpose(1, 2, 3, 0)
    narrow = k_small.reshape(NARROW, 9, 4, SMALL).transpose(1, 2, 3, 0)
    wide = jnp.pad(wide, ((0, 0), (0, 0), (0, 0), (0, LANES - WIDE)))
    narrow = jnp.pad(narrow, ((0, 0), (0, 0), (0, 0), (WIDE, LANES - WIDE - NARROW)))
    kernel = jnp.concatenate([wide, narrow], 2).reshape(9, 4 * REDUCED, LANES)
    return dense, kernel


def forward_first(size, me, pieces, dense, mask, table, count):
    cells = size.cells
    tile = shaped((cells, size.frames, LANES))
    z0, z1, stat = call(
        functools.partial(project_kernel, size),
        [tile, tile, shaped((count, 8, LANES))],
        [pltpu.VMEM((4, 2 * LANES, QUARTER), BF16), pltpu.VMEM((size.side + 2, size.side + 2, size.frames, LANES), F32)],
        [me],
        [*pieces, dense, mask],
        flops=2 * size.rows * CIN * 256,
    )
    totals = share(stat)
    (reduced,) = call(
        functools.partial(reduced_kernel, size),
        [shaped((REDUCED, size.padded), BF16)],
        [],
        [],
        [z0, totals, table, mask],
        flops=size.rows * LANES * 20,
    )
    return z0, z1, totals, reduced


def forward_second(size, me, pieces, kernel, mask, count):
    side, frames = size.side, size.frames
    field, z2, stat = call(
        functools.partial(conv_kernel, size),
        [
            shaped((side + 2, side + 2, frames, 4 * REDUCED), size.kept),
            shaped((size.cells, frames, LANES)),
            shaped((count, 8, LANES)),
        ],
        [pltpu.VMEM((4 * REDUCED, size.padded), BF16)],
        [me],
        [*pieces, kernel, mask],
        flops=2 * size.rows * 9 * 256 * 256,
    )
    return field, z2, share(stat)


def backward(size, me, grads, saved, weights_at, count, spreads):
    z0, z1, totals, field, z2, totals2, table, table2, mask, kernel, pieces = saved
    g0, g2, g1 = grads
    side, frames = size.side, size.frames
    spread_rows = [pltpu.VMEM((size.rows // 4, LANES), F32)]
    (stat,) = call(
        functools.partial(second_sums_kernel, size),
        [shaped((count, 8, LANES))],
        spread_rows if spreads else [],
        [],
        [g2, z2, totals2, table2, mask],
        flops=size.rows * LANES * 30,
    )
    back2 = share(stat)
    wire = shaped((REDUCED, size.padded), BF16)
    delta2, o0, o1, o2, o3 = call(
        functools.partial(conv_back_kernel, size),
        [shaped((size.cells, frames, LANES), size.kept), wire, wire, wire, wire],
        [
            pltpu.VMEM((side + 2, side + 2, frames, LANES), size.kept),
            pltpu.VMEM((size.cells, frames, 4 * REDUCED), F32),
            pltpu.VMEM((4 * REDUCED, size.padded), BF16),
        ]
        + (spread_rows if spreads else []),
        [me],
        [g2, z2, totals2, back2, table2, mask, kernel],
        flops=2 * size.rows * 9 * 256 * 256,
    )
    partial = exchange_four([o0, o1, o2, o3])
    (kernel_grad,) = call(
        functools.partial(kernel_grad_kernel, size),
        [shaped((9, LANES, 4 * REDUCED))],
        [pltpu.VMEM((9, 2 * LANES, 4 * REDUCED), F32)],
        [],
        [field, delta2, mask],
        flops=2 * size.rows * 9 * 256 * 256,
    )
    tile = shaped((size.cells, frames, LANES))
    i0, i1, stat = call(
        functools.partial(first_sums_kernel, size),
        [tile, tile, shaped((count, 8, LANES))],
        [pltpu.VMEM((size.cells, frames, LANES), F32)] + (spread_rows * 2 if spreads else []),
        [],
        [*partial, g0, g1, z0, z1, totals, table, mask],
        flops=size.rows * LANES * 60,
    )
    back1 = share(stat)
    (delta1,) = call(
        functools.partial(first_delta_kernel, size),
        [shaped((ROWS, size.padded), BF16)],
        [
            pltpu.VMEM((side + 2, side + 2, frames, LANES), F32),
            pltpu.VMEM((size.cells, frames, LANES), F32),
        ],
        [],
        [z0, z1, i0, i1, totals, back1, table, mask],
        flops=size.rows * LANES * 60,
    )
    deltas = gather_four(delta1)
    (dense_grad,) = call(
        functools.partial(weight_grad_kernel, size),
        [shaped((4, ROWS, QUARTER))],
        [],
        [me],
        [delta1, *pieces],
        flops=2 * size.rows * CIN * 256,
    )
    scratch = [pltpu.VMEM((4, 2 * LANES, ROWS), BF16), pltpu.VMEM((2, size.padded, LANES), F32)]
    if spreads:
        result = call(
            functools.partial(input_kernel, size),
            [shaped((frames // 8, side, side, 8 * QUARTER))],
            scratch,
            [],
            [*deltas, weights_at],
            flops=2 * size.rows * 4 * ROWS * 256,
        )
    else:
        result = call(
            functools.partial(input_half_kernel, size),
            [tile, tile, tile],
            scratch,
            [],
            [*deltas, weights_at],
            flops=2 * size.rows * 4 * ROWS * 256,
        )
    return result, kernel_grad, dense_grad, norm_grads(back1, back2)


def flat_kernel_grads(grad):
    mid = grad[:, :WIDE].reshape(9, WIDE, 4, REDUCED)[..., :MID].transpose(1, 0, 2, 3).reshape(-1)
    small = grad[:, WIDE : WIDE + NARROW].reshape(9, NARROW, 4, REDUCED)[..., MID:]
    return [mid, small.transpose(1, 0, 2, 3).reshape(-1)]


def flat_dense_grads(grad):
    grad = grad.transpose(1, 0, 2)
    bounds = (0, MID, REDUCED, DENSE, ROWS)
    return [grad[start:stop].reshape(-1) for start, stop in zip(bounds[:-1], bounds[1:])]


def on_device(count, clips, clip_len, w_plain, w_mid, k_mid, w_small, k_small, w_pool, gains, shifts, grad_out):
    big = Size(clips.shape[1], 8 * clips.shape[0])
    low = Size(grad_out.shape[1], 8 * grad_out.shape[0])
    place = lax.axis_index("chan").astype(jnp.int32)
    me = place.reshape(1)
    (own,) = call(
        functools.partial(unpack_kernel, big),
        [shaped((big.rows, QUARTER), BF16)],
        [pltpu.VMEM((2, big.rows, LANES), F32)],
        [],
        [clips],
    )
    pieces = gather_four(own)
    ident, valid = frame_masks(clip_len, big.frames)
    mask = mask_table(ident, valid)
    mask_low = mask_table(ident[::2], valid[::2])
    dense0, kernel0 = open_weights(w_plain[0], w_mid[0], k_mid[0], w_small[0], k_small[0], w_pool[0])
    dense1, kernel1 = open_weights(w_plain[1], w_mid[1], k_mid[1], w_small[1], k_small[1], w_pool[1])
    table0, second0 = norm_tables(gains[0], shifts[0])
    table1, second1 = norm_tables(gains[1], shifts[1])
    low_tile = shaped((low.cells, low.frames, LANES))
    grads = call(
        functools.partial(grad_kernel, low),
        [low_tile, low_tile, low_tile],
        [pltpu.VMEM((2, low.rows, LANES), F32)],
        [],
        [grad_out],
    )
    both = jnp.stack([dense0, dense1], 1)
    sent = [lax.dynamic_index_in_dim(both, place ^ shift, 0, keepdims=False) for shift in range(4)]
    received = exchange_four(sent)
    at_first = jnp.stack([item[0] for item in received])
    at_second = jnp.stack([item[1] for item in received])

    z0, z1, totals, reduced = forward_first(big, me, pieces, dense0, mask, table0, count)
    mids = gather_four(reduced)
    half = [pltpu.VMEM((big.rows // 4, LANES), F32)]
    h0, h1 = call(
        functools.partial(first_half_kernel, big),
        [low_tile, low_tile],
        half * 2,
        [],
        [z0, z1, totals, table0, mask],
        flops=big.rows * 2 * LANES * 20,
    )
    field, z2, totals2 = forward_second(big, me, mids, kernel0, mask, count)
    (own1,) = call(
        functools.partial(second_half_kernel, big),
        [shaped((low.rows, QUARTER), BF16)],
        half,
        [],
        [z2, totals2, second0, mask, h0, h1],
        flops=big.rows * LANES * 20,
    )
    saved0 = (z0, z1, totals, field, z2, totals2, table0, second0, mask, kernel0, pieces)

    pieces1 = gather_four(own1)
    z0, z1, totals, reduced = forward_first(low, me, pieces1, dense1, mask_low, table1, count)
    mids = gather_four(reduced)
    field, z2, totals2 = forward_second(low, me, mids, kernel1, mask_low, count)
    (mixed,) = call(
        functools.partial(output_kernel, low),
        [shaped(grad_out.shape, BF16)],
        [pltpu.VMEM((2, low.rows, LANES), F32)],
        [],
        [z0, z1, z2, totals, totals2, table1, second1, mask_low],
        flops=low.rows * 3 * LANES * 20,
    )
    saved1 = (z0, z1, totals, field, z2, totals2, table1, second1, mask_low, kernel1, pieces1)
    first, second, third = grads
    grads, kernel_grad1, dense_grad1, norms1 = backward(low, me, (first, second, third), saved1, at_second, count, False)
    flats1 = flat_kernel_grads(kernel_grad1) + flat_dense_grads(dense_grad1)
    flats1 = lax.psum(tuple(flats1), "dp")
    (clips_grad,), kernel_grad0, dense_grad0, norms0 = backward(big, me, grads, saved0, at_first, count, True)
    flats0 = reduce_flat(flat_kernel_grads(kernel_grad0), count) + reduce_flat(flat_dense_grads(dense_grad0), count)
    k_mid_grad, k_small_grad, w_mid_grad, w_small_grad, w_plain_grad, w_pool_grad = (
        jnp.stack(pair) for pair in zip(flats0, flats1)
    )
    return (
        mixed,
        clips_grad,
        w_plain_grad,
        w_mid_grad,
        k_mid_grad,
        w_small_grad,
        k_small_grad,
        w_pool_grad,
        jnp.stack([norms0[0], norms1[0]]),
        jnp.stack([norms0[1], norms1[1]]),
    )


def solution(mesh):
    frames = P("dp", None, None, "chan")
    flat = P(None, "chan")
    return jax.shard_map(
        functools.partial(on_device, mesh.shape["dp"]),
        mesh=mesh,
        in_specs=(frames, P("dp")) + (flat,) * 8 + (frames,),
        out_specs=(frames, frames) + (flat,) * 8,
        check_vma=False,
    )
```

```python
import functools

import jax
import jax.numpy as jnp
from jax import lax
from jax.experimental import pallas as pl
from jax.experimental.pallas import tpu as pltpu
from jax.sharding import PartitionSpec as P

CIN = 832
QUARTER = 208
WIDE, NARROW = 80, 32
MID, SMALL, PLAIN, POOL = 40, 8, 64, 32
REDUCED = MID + SMALL
DENSE = REDUCED + PLAIN
ROWS = DENSE + POOL
CLIPS = 2
EPSILON = 1e-05
F32 = jnp.float32
BF16 = jnp.bfloat16
LANES = 128
LIMIT = 62
MID_TILES = 4 * 9 * 160 // LANES
MID_ROWS = WIDE // 4 * MID_TILES
SMALL_TILES = 4 * 9 * 32 // LANES
SMALL_ROWS = NARROW // 4 * SMALL_TILES
KERNEL_ROWS = 976
PAIR_TILES = 2 * CIN // LANES
DENSE_ROWS = 944


class Size:
    def __init__(self, side, frames):
        self.side = side
        self.frames = frames
        self.cells = side * side
        self.rows = self.cells * frames
        self.padded = -(-self.rows // LANES) * LANES
        self.band = 2 if side % 2 == 0 else side
        self.chunks = side // self.band
        self.step = self.band * side
        self.group = LANES // frames
        self.full = self.cells // self.group
        self.rest = self.cells - self.full * self.group
        self.kept = BF16 if frames % 16 == 0 else F32


def call(body, outs, scratch, scalars, args, flops=0):
    specs = [pl.BlockSpec(memory_space=pltpu.SMEM)] * len(scalars)
    specs += [pl.BlockSpec(memory_space=pltpu.VMEM)] * len(args)
    moved = sum(a.size * a.dtype.itemsize for a in args)
    moved += sum(o.size * o.dtype.itemsize for o in outs)
    return pl.pallas_call(
        body,
        out_shape=outs,
        in_specs=specs,
        out_specs=[pl.BlockSpec(memory_space=pltpu.VMEM)] * len(outs),
        scratch_shapes=scratch,
        compiler_params=pltpu.CompilerParams(vmem_limit_bytes=LIMIT * 1024 * 1024),
        cost_estimate=pl.CostEstimate(flops=flops, bytes_accessed=moved, transcendentals=0),
    )(*scalars, *args)


def shaped(shape, dtype=F32):
    return jax.ShapeDtypeStruct(shape, dtype)


def sigmoid(value):
    return 0.5 * jnp.tanh(0.5 * value) + 0.5


def row_table(rows):
    index = lax.broadcasted_iota(jnp.int32, (8, LANES), 0)
    table = jnp.zeros((8, LANES), F32)
    for position, row in enumerate(rows):
        table = jnp.where(index == position, row, table)
    return table


def time_box(value, mask_ref):
    cells, frames, width = value.shape
    flat = value.reshape(cells * frames, width)
    before = pltpu.roll(flat, 1, 0).reshape(value.shape)
    after = pltpu.roll(flat, cells * frames - 1, 0).reshape(value.shape)
    return value + before * mask_ref[1] + after * mask_ref[2]


def norm_rows(all_ref, table_ref, tile):
    total = jnp.sum(all_ref[...], 0)
    count = total[4:5]
    mean = total[2 * tile : 2 * tile + 1] / count
    variance = total[2 * tile + 1 : 2 * tile + 2] / count - mean * mean
    inverse = lax.rsqrt(variance + EPSILON)
    gain = table_ref[2 * tile : 2 * tile + 1]
    shift = table_ref[2 * tile + 1 : 2 * tile + 2]
    return mean, inverse, gain, shift, count


def activate(value, rows, mask_ref):
    mean, inverse, gain, shift, _ = rows
    shifted = gain * ((value - mean) * inverse) + shift
    return shifted * sigmoid(shifted) * mask_ref[0]


def inner_grad(grad, value, rows, mask_ref):
    mean, inverse, gain, shift, _ = rows
    normed = (value - mean) * inverse
    shifted = gain * normed + shift
    sigma = sigmoid(shifted)
    return grad * mask_ref[0] * sigma * (1.0 + shifted * (1.0 - sigma)), normed


def norm_delta(inner, value, rows, back_ref, tile, mask_ref):
    mean, inverse, gain, _, count = rows
    total = jnp.sum(back_ref[...], 0)
    shift_grad = total[2 * tile : 2 * tile + 1] / count
    gain_grad = total[2 * tile + 1 : 2 * tile + 2] / count
    normed = (value - mean) * inverse
    return (gain * inverse) * (inner - mask_ref[0] * (shift_grad + normed * gain_grad))


def publish(stat_ref, rows):
    stat_ref[...] = jnp.broadcast_to(row_table(rows)[None], stat_ref.shape)


def collapse(value):
    return jnp.sum(value, 0, keepdims=True)


def windows():
    result = []
    for frame in range(8):
        start = frame * QUARTER
        first, offset = start // LANES, start % LANES
        result.append((first, -(-(offset + QUARTER) // LANES), offset))
    return result


def unpack_rows(line, frame):
    first, tiles, offset = windows()[frame]
    value = line[:, first * LANES : (first + tiles) * LANES]
    if offset:
        value = pltpu.roll(value, tiles * LANES - offset, 1)
    return value[:, : 2 * LANES]


def pack_rows(parts):
    tiles = [None] * 13
    for frame, value in enumerate(parts):
        first, count, offset = windows()[frame]
        if count == 3:
            value = jnp.concatenate([value, jnp.zeros((value.shape[0], LANES), value.dtype)], 1)
        if offset:
            value = pltpu.roll(value, offset, 1)
        for index in range(count):
            piece = value[:, index * LANES : (index + 1) * LANES]
            place = first + index
            tiles[place] = piece if tiles[place] is None else tiles[place] + piece
    return tiles


def assemble(first, second, third):
    blank = jnp.zeros_like(first)
    lane = lax.broadcasted_iota(jnp.int32, (first.shape[0], 2 * LANES), 1)
    plain = pltpu.roll(jnp.concatenate([first, blank], 1), 2 * LANES - REDUCED, 1)
    middle = pltpu.roll(jnp.concatenate([second, blank], 1), PLAIN, 1)
    pool = pltpu.roll(jnp.concatenate([third, blank], 1), PLAIN + WIDE + NARROW, 1)
    return jnp.where(lane < PLAIN, plain, 0.0) + middle + pool


def separate(value):
    lane = lax.broadcasted_iota(jnp.int32, (value.shape[0], LANES), 1)
    plain = pltpu.roll(value, REDUCED, 1)[:, :LANES]
    middle = pltpu.roll(value, 2 * LANES - PLAIN, 1)[:, :LANES]
    pool = pltpu.roll(value, 2 * LANES - PLAIN - WIDE - NARROW, 1)[:, :LANES]
    first = jnp.where((lane >= REDUCED) & (lane < DENSE), plain, 0.0)
    second = jnp.where(lane < WIDE + NARROW, middle, 0.0)
    third = jnp.where(lane < POOL, pool, 0.0)
    return first, second, third


def unpack_kernel(size, raw, out, scratch):
    side, frames = size.side, size.frames
    blocks_of = frames // 8

    def line(row, carry):
        value = raw[pl.ds(row * side, side)].astype(F32).reshape(blocks_of * side, 8 * QUARTER)
        for frame in range(8):
            place = pl.ds(row * side * frames + frame, blocks_of * side, stride=8)
            part = unpack_rows(value, frame)
            scratch[0, place, :] = part[:, :LANES]
            scratch[1, place, :] = part[:, LANES:]
        return carry

    lax.fori_loop(0, side, line, 0)

    def one(block, cells):
        start = block * LANES if isinstance(block, int) else pl.multiple_of(block * LANES, LANES)
        rows = pl.ds(start, cells * frames)
        for tile, (low, high) in enumerate(((0, LANES), (LANES, QUARTER))):
            value = scratch[tile, rows, :].reshape(cells, frames, LANES)
            out[low:high, lanes_of(block)] = turn(size, value, cells)[: high - low].astype(BF16)

    blocks(size, one)


def grad_kernel(size, raw, first, second, third, scratch):
    side, frames = size.side, size.frames

    def line(row, carry):
        value = raw[0, row].astype(F32)
        for frame in range(8):
            place = pl.ds(row * side * frames + frame, side, stride=frames)
            part = unpack_rows(value, frame)
            scratch[0, place, :] = part[:, :LANES]
            scratch[1, place, :] = part[:, LANES:]
        return carry

    lax.fori_loop(0, side, line, 0)
    parts = separate(jnp.concatenate([scratch[0], scratch[1]], 1))
    for ref, part in zip((first, second, third), parts):
        ref[...] = part.reshape(ref.shape)


def dot(left, right, dims=((1,), (0,))):
    return lax.dot_general(left, right, (dims, ((), ())), preferred_element_type=F32)


def columns(size):
    width = 640 if size.padded % 640 == 0 else size.padded
    result = []
    for start in range(0, size.padded, width):
        result.append((start, width, min(width, size.rows - start) // size.frames))
    return result


def into_padded(size, flat, field):
    side = size.side
    field[...] = jnp.zeros_like(field)

    def line(row, carry):
        field[row + 1, 1 : side + 1] = flat[pl.ds(row * side, side)]
        return carry

    lax.fori_loop(0, side, line, 0)


def project_kernel(size, me, x0, x1, x2, x3, w_ref, mask, z0, z1, stat, field, flat):
    side, frames = size.side, size.frames
    blank = jnp.zeros((frames, LANES), F32)
    total, squares = blank, blank
    for start, width, cells in columns(size):
        value = jnp.zeros((2 * LANES, width), F32)
        for position, x in enumerate((x0, x1, x2, x3)):
            value += dot(w_ref[me[0] ^ position], x[:, start : start + width])
        value = value.T.reshape(width // frames, frames, 2 * LANES)[:cells]
        first = start // frames
        dense = value[:, :, :LANES]
        z0[first : first + cells] = dense
        flat[first : first + cells] = value[:, :, LANES:]
        total += jnp.sum(dense, 0)
        squares += jnp.sum(dense * dense, 0)
    into_padded(size, flat, field)

    def line(row, carry):
        pool_total, pool_squares = carry
        pool = pool_line(size, field, row, mask)
        z1[pl.ds(row * side, side)] = pool
        return pool_total + jnp.sum(pool, 0), pool_squares + jnp.sum(pool * pool, 0)

    pool_total, pool_squares = lax.fori_loop(0, side, line, (blank, blank))
    valid = mask[0]
    rows = [collapse(item * valid) for item in (total, squares, pool_total, pool_squares, blank + size.cells)]
    publish(stat, rows)


def pool_line(size, field, row, mask):
    side = size.side
    lines = field[pl.ds(row, 3)]
    column = lines[0] + lines[1] + lines[2]
    value = column[0:side] + column[1 : side + 1] + column[2 : side + 2]
    return time_box(value, mask) * (1.0 / 27.0)


def blocks(size, one):
    def step(index, carry):
        one(index, size.group)
        return carry

    lax.fori_loop(0, size.full, step, 0)
    if size.rest:
        one(size.full, size.rest)


def turn(size, value, cells):
    flat = value.reshape(cells * size.frames, value.shape[-1])
    if cells < size.group:
        blank = jnp.zeros((LANES - cells * size.frames, value.shape[-1]), value.dtype)
        flat = jnp.concatenate([flat, blank], 0)
    return flat.T


def lanes_of(block):
    if isinstance(block, int):
        return pl.ds(block * LANES, LANES)
    return pl.ds(pl.multiple_of(block * LANES, LANES), LANES)


def reduced_kernel(size, z0, totals, table, mask, out):
    rows = norm_rows(totals, table, 0)

    def one(block, cells):
        value = activate(z0[pl.ds(block * size.group, cells)], rows, mask)
        out[:, lanes_of(block)] = turn(size, value, cells)[:REDUCED].astype(BF16)

    blocks(size, one)


def conv_kernel(size, me, p0, p1, p2, p3, kernel, mask, field, z2, stat, joined):
    side, frames, step = size.side, size.frames, size.step
    for position, piece in enumerate((p0, p1, p2, p3)):
        owner = me[0] ^ position
        value = piece[...].astype(F32)
        joined[pl.ds(pl.multiple_of(owner * MID, 8), MID), :] = value[:MID]
        joined[pl.ds(pl.multiple_of(4 * MID + owner * SMALL, 8), SMALL), :] = value[MID:]
    field[...] = jnp.zeros_like(field)

    def one(block, cells):
        value = joined[:, lanes_of(block)].T
        value = value.reshape(size.group, frames, 4 * REDUCED).astype(size.kept)
        for index in range(cells):
            cell = block * size.group + index
            row = cell // side if isinstance(cell, int) else lax.div(cell, side)
            field[row + 1, cell - row * side + 1] = value[index]

    blocks(size, one)
    blank = jnp.zeros((frames, LANES), F32)

    def chunk(index, carry):
        total, squares = carry
        value = jnp.zeros((step * frames, LANES), F32)
        for row in range(3):
            for column in range(3):
                part = field[pl.ds(index * size.band + row, size.band), column : column + side]
                part = part.reshape(step * frames, 4 * REDUCED).astype(BF16)
                value += dot(part, kernel[3 * row + column])
        value = time_box(value.reshape(step, frames, LANES), mask) * (1.0 / 3.0)
        z2[pl.ds(index * step, step)] = value
        return total + jnp.sum(value, 0), squares + jnp.sum(value * value, 0)

    total, squares = lax.fori_loop(0, size.chunks, chunk, (blank, blank))
    valid = mask[0]
    one_row = jnp.zeros((1, LANES), F32)
    rows = [collapse(total * valid), collapse(squares * valid), one_row, one_row, collapse(valid) * size.cells]
    publish(stat, rows)


def halve_into(size, value, scratch, index):
    half = size.side // 2
    value = value.reshape(2, half, 2, size.frames, LANES)
    value = value[0] + value[1]
    value = value[:, 0] + value[:, 1]
    rows = half * size.frames
    scratch[pl.ds(index * rows, rows), :] = value.reshape(rows, LANES)


def halved_rows(scratch):
    count = scratch.shape[0] // 2
    return (scratch[pl.ds(0, count, stride=2), :] + scratch[pl.ds(1, count, stride=2), :]) * 0.125


def first_half_kernel(size, z0, z1, totals, table, mask, h0, h1, s0, s1):
    for tile, (z, out, scratch) in enumerate(((z0, h0, s0), (z1, h1, s1))):
        rows = norm_rows(totals, table, tile)

        def chunk(index, carry, z=z, scratch=scratch, rows=rows):
            value = activate(z[pl.ds(index * size.step, size.step)], rows, mask)
            halve_into(size, value, scratch, index)
            return carry

        lax.fori_loop(0, size.chunks, chunk, 0)
        out[...] = halved_rows(scratch).reshape(out.shape)


def second_half_kernel(size, z2, totals, table, mask, h0, h1, out, scratch):
    rows = norm_rows(totals, table, 0)

    def chunk(index, carry):
        value = activate(z2[pl.ds(index * size.step, size.step)], rows, mask)
        halve_into(size, value, scratch, index)
        return carry

    lax.fori_loop(0, size.chunks, chunk, 0)
    value = halved_rows(scratch)
    count = value.shape[0]
    value = assemble(h0[...].reshape(count, LANES), value, h1[...].reshape(count, LANES))
    value = jnp.concatenate([value, jnp.zeros((out.shape[1] - count, 2 * LANES), F32)], 0)
    out[...] = value.T[:QUARTER].astype(BF16)


def strided(scratch, start, count, stride):
    place = pl.ds(start, count, stride=stride)
    return jnp.concatenate([scratch[0, place, :], scratch[1, place, :]], 1)


def output_kernel(size, z0, z1, z2, totals, totals2, table, table2, mask, out, scratch):
    side, frames = size.side, size.frames
    parts = [
        activate(z[...], norm_rows(total, tab, tile), mask).reshape(size.rows, LANES)
        for z, total, tab, tile in ((z0, totals, table, 0), (z2, totals2, table2, 0), (z1, totals, table, 1))
    ]
    value = assemble(*parts)
    scratch[0] = value[:, :LANES]
    scratch[1] = value[:, LANES:]

    def line(row, carry):
        start = row * side * frames
        lines = [strided(scratch, start + frame, side, frames) for frame in range(8)]
        for place, tile in enumerate(pack_rows(lines)):
            out[0, row, :, place * LANES : (place + 1) * LANES] = tile.astype(BF16)
        return carry

    lax.fori_loop(0, side, line, 0)


def spread(size, grad, scratch):
    value = grad[...].reshape(-1, LANES)
    count = value.shape[0]
    scratch[pl.ds(0, count, stride=2), :] = value
    scratch[pl.ds(1, count, stride=2), :] = value


def grad_chunk(size, grad, scratch, index):
    if scratch is None:
        return grad[pl.ds(index * size.step, size.step)]
    half = size.side // 2
    rows = half * size.frames
    value = scratch[pl.ds(index * rows, rows), :].reshape(half, 1, size.frames, LANES)
    value = jnp.broadcast_to(value, (half, 2, size.frames, LANES)).reshape(1, size.side, size.frames, LANES)
    value = jnp.broadcast_to(value, (2, size.side, size.frames, LANES))
    return value.reshape(size.step, size.frames, LANES)


def second_sums_kernel(size, grad, z2, totals, table, mask, stat, *scratch):
    scratch = scratch[0] if scratch else None
    if scratch is not None:
        spread(size, grad, scratch)
    rows = norm_rows(totals, table, 0)
    blank = jnp.zeros((size.frames, LANES), F32)

    def chunk(index, carry):
        shift_grad, gain_grad = carry
        value = z2[pl.ds(index * size.step, size.step)]
        inner, normed = inner_grad(grad_chunk(size, grad, scratch, index), value, rows, mask)
        return shift_grad + jnp.sum(inner, 0), gain_grad + jnp.sum(inner * normed, 0)

    shift_grad, gain_grad = lax.fori_loop(0, size.chunks, chunk, (blank, blank))
    publish(stat, [collapse(shift_grad), collapse(gain_grad)])


def conv_back_kernel(size, me, grad, z2, totals, back, table, mask, kernel, delta, o0, o1, o2, o3, field, result, turned, *scratch):
    side, frames, step = size.side, size.frames, size.step
    scratch = scratch[0] if scratch else None
    if scratch is not None:
        spread(size, grad, scratch)
    rows = norm_rows(totals, table, 0)
    field[...] = jnp.zeros_like(field)

    def first(index, carry):
        value = z2[pl.ds(index * step, step)]
        inner, _ = inner_grad(grad_chunk(size, grad, scratch, index), value, rows, mask)
        value = norm_delta(inner, value, rows, back, 0, mask).astype(BF16).astype(size.kept)
        delta[pl.ds(index * step, step)] = value
        field[pl.ds(1 + index * size.band, size.band), 1 : side + 1] = value.reshape(size.band, side, frames, LANES)
        return carry

    lax.fori_loop(0, size.chunks, first, 0)

    def chunk(index, carry):
        value = jnp.zeros((step * frames, 4 * REDUCED), F32)
        for row in range(3):
            for column in range(3):
                part = field[pl.ds(index * size.band + 2 - row, size.band), 2 - column : 2 - column + side]
                part = part.reshape(step * frames, LANES).astype(BF16)
                value += dot(part, kernel[3 * row + column])
        result[pl.ds(index * step, step)] = value.reshape(step, frames, 4 * REDUCED)
        return carry

    lax.fori_loop(0, size.chunks, chunk, 0)

    def one(block, cells):
        value = turn(size, result[pl.ds(block * size.group, cells)], cells)
        turned[:, lanes_of(block)] = value

    blocks(size, one)
    for position, out in enumerate((o0, o1, o2, o3)):
        owner = me[0] ^ position
        mid = turned[pl.ds(pl.multiple_of(owner * MID, 8), MID), :]
        small = turned[pl.ds(pl.multiple_of(4 * MID + owner * SMALL, 8), SMALL), :]
        out[...] = jnp.concatenate([mid, small], 0).astype(BF16)


def kernel_grad_kernel(size, field, delta, mask, out, total, taps, flat):
    side, frames, step = size.side, size.frames, size.step
    total[...] = jnp.zeros_like(total)

    def chunk(index, carry):
        value = delta[pl.ds(index * step, step)].astype(F32)
        value = time_box(value, mask).reshape(step * frames, LANES)
        upper = value.astype(BF16).astype(F32)
        both = jnp.concatenate([upper, value - upper], 1).T.astype(BF16)
        for row in range(3):
            for column in range(3):
                part = field[pl.ds(index * size.band + row, size.band), column : column + side]
                part = part.reshape(step * frames, 4 * REDUCED).astype(BF16)
                total[3 * row + column] += dot(both, part)
        return carry

    lax.fori_loop(0, size.chunks, chunk, 0)
    for tap in range(9):
        value = (total[tap, :LANES] + total[tap, LANES:]) * (1.0 / 3.0)
        taps[tap, 0] = value[:, :LANES]
        taps[tap, 1, :, : 4 * REDUCED - LANES] = value[:, LANES:]
    lane = lax.broadcasted_iota(jnp.int32, (WIDE // 4, LANES), 1)
    tiles = [None] * MID_TILES

    def add(place, value):
        tiles[place] = value if tiles[place] is None else tiles[place] + value

    for extra in range(4):
        for tap in range(9):
            rows = pl.ds(extra, WIDE // 4, stride=4)
            rest = jnp.where(lane < 4 * MID - LANES, taps[tap, 1, rows, :], 0.0)
            offset = (extra * 9 + tap) * 4 * MID
            value = jnp.concatenate([taps[tap, 0, rows, :], rest, jnp.zeros_like(rest)], 1)
            value = pltpu.roll(value, offset % LANES, 1)
            for index in range(-(-(offset % LANES + 4 * MID) // LANES)):
                add(offset // LANES + index, value[:, index * LANES : (index + 1) * LANES])
    for place, tile in enumerate(tiles):
        flat[pl.ds(place, WIDE // 4, stride=MID_TILES), :] = tile
    lane = lax.broadcasted_iota(jnp.int32, (NARROW // 4, LANES), 1)
    tiles = [None] * SMALL_TILES
    start = 4 * MID - LANES
    for extra in range(4):
        for tap in range(9):
            value = taps[tap, 1, pl.ds(WIDE + extra, NARROW // 4, stride=4), :]
            value = jnp.where((lane >= start) & (lane < start + 4 * SMALL), value, 0.0)
            offset = (extra * 9 + tap) * 4 * SMALL
            value = pltpu.roll(value, (offset - start) % LANES, 1)
            add(offset // LANES, value)
    for place, tile in enumerate(tiles):
        flat[pl.ds(MID_ROWS + place, NARROW // 4, stride=SMALL_TILES), :] = tile
    flat[MID_ROWS + SMALL_ROWS :, :] = jnp.zeros((KERNEL_ROWS - MID_ROWS - SMALL_ROWS, LANES), F32)
    out[...] = flat[...].astype(BF16)


def first_sums_kernel(size, p0, p1, p2, p3, g0, g1, z0, z1, totals, table, mask, i0, i1, stat, field, *scratch):
    step, frames = size.step, size.frames
    s0, s1 = scratch if scratch else (None, None)
    if scratch:
        spread(size, g0, s0)
        spread(size, g1, s1)

    def one(block, cells):
        place = lanes_of(block)
        value = p0[:, place].astype(F32) + p1[:, place].astype(F32)
        value += p2[:, place].astype(F32) + p3[:, place].astype(F32)
        value = jnp.concatenate([value, jnp.zeros((LANES - REDUCED, LANES), F32)], 0).T
        value = value.reshape(size.group, frames, LANES)
        field[pl.ds(block * size.group, cells)] = value[:cells]

    blocks(size, one)
    rows0 = norm_rows(totals, table, 0)
    rows1 = norm_rows(totals, table, 1)
    blank = jnp.zeros((frames, LANES), F32)

    def chunk(index, carry):
        place = pl.ds(index * step, step)
        grad = time_box(field[place], mask) * (1.0 / 3.0) + grad_chunk(size, g0, s0, index)
        inner0, normed0 = inner_grad(grad, z0[place], rows0, mask)
        inner1, normed1 = inner_grad(grad_chunk(size, g1, s1, index), z1[place], rows1, mask)
        i0[place] = inner0
        i1[place] = inner1
        sums = (inner0, inner0 * normed0, inner1, inner1 * normed1)
        return tuple(old + jnp.sum(new, 0) for old, new in zip(carry, sums))

    sums = lax.fori_loop(0, size.chunks, chunk, (blank,) * 4)
    publish(stat, [collapse(item) for item in sums])


def first_delta_kernel(size, z0, z1, i0, i1, totals, back, table, mask, out, field, pooled):
    side, step, frames = size.side, size.step, size.frames
    rows0 = norm_rows(totals, table, 0)
    rows1 = norm_rows(totals, table, 1)
    field[...] = jnp.zeros_like(field)

    def chunk(index, carry):
        place = pl.ds(index * step, step)
        value = norm_delta(i1[place], z1[place], rows1, back, 1, mask).astype(BF16).astype(F32)
        field[pl.ds(1 + index * size.band, size.band), 1 : side + 1] = value.reshape(size.band, side, frames, LANES)
        return carry

    lax.fori_loop(0, size.chunks, chunk, 0)

    def line(row, carry):
        pooled[pl.ds(row * side, side)] = pool_line(size, field, row, mask)
        return carry

    lax.fori_loop(0, side, line, 0)

    def one(block, cells):
        place = pl.ds(block * size.group, cells)
        value = norm_delta(i0[place], z0[place], rows0, back, 0, mask)
        out[0:DENSE, lanes_of(block)] = turn(size, value, cells)[:DENSE].astype(BF16)
        out[DENSE:ROWS, lanes_of(block)] = turn(size, pooled[place], cells)[:POOL].astype(BF16)

    blocks(size, one)


def weight_grad_kernel(size, me, delta, x0, x1, x2, x3, out, grads, flat):
    for position, x in enumerate((x0, x1, x2, x3)):
        owner = me[0] ^ position
        value = dot(delta[...], x[...], ((1,), (1,)))
        grads[owner, 0] = value[:, :LANES]
        rest = value[:, LANES:]
        grads[owner, 1] = jnp.concatenate([rest, jnp.zeros((ROWS, 2 * LANES - QUARTER), F32)], 1)
    parts = []
    for extra in range(2):
        rows = pl.ds(extra, ROWS // 2, stride=2)
        for owner in range(4):
            parts.append(jnp.concatenate([grads[owner, 0, rows, :], grads[owner, 1, rows, :]], 1))
    for place, tile in enumerate(pack_rows(parts)):
        flat[pl.ds(place, ROWS // 2, stride=PAIR_TILES), :] = tile
    used = ROWS // 2 * PAIR_TILES
    flat[used:, :] = jnp.zeros((DENSE_ROWS - used, LANES), F32)
    out[...] = flat[...].astype(BF16)


def input_rows(size, pieces, weights, block, scratch):
    for start, width, _ in columns(size):
        value = jnp.zeros((QUARTER, width), F32)
        for weight, piece in zip(weights, pieces):
            value += dot(weight[block], piece[:, start : start + width])
        value = jnp.concatenate([value, jnp.zeros((2 * LANES - QUARTER, width), F32)], 0).T
        scratch[0, start : start + width, :] = value[:, :LANES]
        scratch[1, start : start + width, :] = value[:, LANES:]


def input_half_kernel(size, d0, d1, d2, d3, w0, w1, w2, w3, first, second, third, scratch):
    input_rows(size, (d0, d1, d2, d3), (w0, w1, w2, w3), 1, scratch)
    value = jnp.concatenate([scratch[0, : size.rows, :], scratch[1, : size.rows, :]], 1)
    parts = separate(value * 0.125)
    for ref, part in zip((first, second, third), parts):
        ref[...] = part.reshape(ref.shape)


def input_kernel(size, d0, d1, d2, d3, w0, w1, w2, w3, out, scratch):
    side, frames = size.side, size.frames
    lines_of = frames // 8
    input_rows(size, (d0, d1, d2, d3), (w0, w1, w2, w3), 0, scratch)

    def line(row, carry):
        start = row * side * frames
        lines = [strided(scratch, start + frame, lines_of * side, 8) for frame in range(8)]
        for place, tile in enumerate(pack_rows(lines)):
            tile = tile.reshape(side, lines_of, LANES)
            out[pl.ds(row * side, side), :, place * LANES : (place + 1) * LANES] = tile
        return carry

    lax.fori_loop(0, side, line, 0)


def pairs(axis_size, shift):
    return [(index, index ^ shift) for index in range(axis_size)]


def gather_four(piece):
    other = lax.ppermute(piece, "chan", pairs(4, 2))
    core = lax.ppermute(piece, "chan", pairs(4, 1))
    both = lax.ppermute(other, "chan", pairs(4, 1))
    return piece, core, other, both


def exchange_four(pieces):
    result = [pieces[0]]
    for shift in (1, 2, 3):
        result.append(lax.ppermute(pieces[shift], "chan", pairs(4, shift)))
    return result


def share(stat):
    return lax.all_to_all(stat, "dp", 0, 0, tiled=True)


def reduce_rows(parts, count):
    rows = sum(part.shape[0] for part in parts)
    unit = count * 16
    total = -(-rows // unit) * unit
    if total > rows:
        parts = [*parts, jnp.zeros((total - rows, LANES), BF16)]
    whole = jnp.concatenate(parts, 0).reshape(count, total // count, LANES)
    mine = jnp.sum(lax.all_to_all(whole, "dp", 0, 0, tiled=True).astype(F32), 0).astype(BF16)
    whole = lax.all_to_all(jnp.broadcast_to(mine[None], whole.shape), "dp", 0, 0, tiled=True)
    return whole.reshape(total, LANES)


def as_rows(flat):
    return flat.reshape(2, -1, LANES).transpose(1, 0, 2).reshape(-1, LANES)


def as_flat(rows):
    return rows.reshape(-1, 2, LANES).transpose(1, 0, 2).reshape(2, -1)


NORM_LANES = (
    (0, REDUCED, PLAIN, 0),
    (0, 0, MID, 64),
    (2, 0, WIDE, 104),
    (0, MID, SMALL, 184),
    (2, WIDE, NARROW, 192),
    (1, 0, POOL, 224),
)


def shifted_lanes(value, source, width, target):
    lane = lax.broadcasted_iota(jnp.int32, value.shape, 1)
    value = jnp.where((lane >= source) & (lane < source + width), value, 0.0)
    return pltpu.roll(value, (target - source) % value.shape[1], 1)


def mask_rows(length0, length1, frames, stride):
    frame = lax.broadcasted_iota(jnp.int32, (frames, LANES), 0)
    ends = (length0, length0 + length1)

    def ident(step):
        place = (frame + step) * stride
        return jnp.where(place >= ends[0], 1, 0) + jnp.where(place >= ends[1], 1, 0)

    here = ident(0)
    valid = jnp.where(frame * stride < ends[1], 1.0, 0.0)
    before = jnp.where((frame > 0) & (ident(-1) == here), 1.0, 0.0)
    after = jnp.where((frame < frames - 1) & (ident(1) == here), 1.0, 0.0)
    return valid, before, after


def prepare_kernel(me, lengths, plain, mid, small, pool, wide, narrow, gains, shifts, *refs):
    outs, (rows, dense, taps) = refs[:-3], refs[-3:]
    mask0, mask1, tables, sent, weights, kernels = outs[0], outs[1], outs[2:6], outs[6:10], outs[10:12], outs[12:14]
    turned = outs[14:16]
    for mask, stride in ((mask0, 1), (mask1, 2)):
        for index, value in enumerate(mask_rows(lengths[0], lengths[1], mask.shape[1], stride)):
            mask[index] = value
    for block in range(2):
        lines = []
        for source in (gains, shifts):
            value = source[...].astype(F32)
            line = jnp.concatenate([value[block : block + 1], value[block + 2 : block + 3]], 1)
            lines.append(jnp.broadcast_to(line, (8, 2 * LANES)))
        found = [[jnp.zeros((8, LANES), F32)] * 2 for _ in range(3)]
        for tile, lane, width, channel in NORM_LANES:
            for index, line in enumerate(lines):
                part = shifted_lanes(line, channel, width, lane)[:, :LANES]
                found[tile][index] = found[tile][index] + part
        tables[2 * block][...] = row_table([found[0][0], found[0][1], found[1][0], found[1][1]])
        tables[2 * block + 1][...] = row_table([found[2][0], found[2][1]])
    for ref, base, outputs in ((mid, 0, MID), (small, MID, SMALL), (plain, REDUCED, PLAIN), (pool, DENSE, POOL)):
        count = ref.shape[0]
        rows[:count, :] = ref[...].astype(F32)
        for block in range(2):
            tiles = [rows[pl.ds(2 * tile + block, outputs // 2, stride=2 * PAIR_TILES), :] for tile in range(PAIR_TILES)]
            line = jnp.concatenate(tiles, 1)
            for extra in range(2):
                place = pl.ds(base + extra, outputs // 2, stride=2)
                for owner in range(4):
                    part = unpack_rows(line, 4 * extra + owner)
                    dense[block, owner, 0, place, :] = part[:, :LANES]
                    dense[block, owner, 1, place, :] = part[:, LANES:]
    blank = jnp.zeros((LANES, QUARTER), BF16)
    for block in range(2):
        for owner in range(4):
            value = jnp.concatenate([dense[block, owner, 0], dense[block, owner, 1]], 1)
            natural = value[:, :QUARTER].astype(BF16)
            weights[block][owner, 0:DENSE] = natural[:DENSE]
            weights[block][owner, DENSE:LANES] = blank[: LANES - DENSE]
            weights[block][owner, LANES : LANES + POOL] = natural[DENSE:]
            weights[block][owner, LANES + POOL :] = blank[: LANES - POOL]
        for position in range(4):
            owner = me[0] ^ position
            value = jnp.concatenate([dense[block, owner, 0], dense[block, owner, 1]], 1)
            sent[position][block] = value.T[:QUARTER].astype(BF16)
    wide_lane = lax.broadcasted_iota(jnp.int32, (WIDE // 4, LANES), 1)
    narrow_lane = lax.broadcasted_iota(jnp.int32, (NARROW // 4, LANES), 1)
    start = 4 * MID - LANES
    for block in range(2):
        rows[: wide.shape[0], :] = wide[...].astype(F32)
        taps[...] = jnp.zeros_like(taps)
        tiles = [rows[pl.ds(2 * tile + block, WIDE // 4, stride=2 * MID_TILES), :] for tile in range(MID_TILES)]
        tiles.append(tiles[0])
        for extra in range(4):
            for tap in range(9):
                offset = (extra * 9 + tap) * 4 * MID
                first, shift = offset // LANES, offset % LANES
                count = -(-(shift + 4 * MID) // LANES)
                value = jnp.concatenate(tiles[first : first + count], 1)
                value = pltpu.roll(value, (count * LANES - shift) % (count * LANES), 1)
                place = pl.ds(extra, WIDE // 4, stride=4)
                taps[tap, 0, place, :] = value[:, :LANES]
                taps[tap, 1, place, :] = jnp.where(wide_lane < start, value[:, LANES : 2 * LANES], 0.0)
        rows[: narrow.shape[0], :] = narrow[...].astype(F32)
        tiles = [rows[pl.ds(2 * tile + block, NARROW // 4, stride=2 * SMALL_TILES), :] for tile in range(SMALL_TILES)]
        for extra in range(4):
            for tap in range(9):
                offset = (extra * 9 + tap) * 4 * SMALL
                value = pltpu.roll(tiles[offset // LANES], (start - offset) % LANES, 1)
                value = jnp.where((narrow_lane >= start) & (narrow_lane < start + 4 * SMALL), value, 0.0)
                taps[tap, 1, pl.ds(WIDE + extra, NARROW // 4, stride=4), :] = value
        for tap in range(9):
            first, second = taps[tap, 0], taps[tap, 1]
            kernels[block][tap] = jnp.concatenate([first, second], 1)[:, : 4 * REDUCED].astype(BF16)
            turned[block][tap, :LANES] = first.T.astype(BF16)
            turned[block][tap, LANES:] = second.T[: 4 * REDUCED - LANES].astype(BF16)


def finish_kernel(early, late, first0, first1, second0, second1, *refs):
    outs, (rows,) = refs[:-1], refs[-1:]
    mid, small, plain, pool, wide, narrow, gains, shifts = outs

    def place(out, block, start, count):
        out[pl.ds(block, count, stride=2), :] = rows[start : start + count, :]

    dense = ((mid, MID), (small, SMALL), (plain, PLAIN), (pool, POOL))
    count = early.shape[0]
    rows[:count, :] = early[...].astype(F32)
    for block, start in ((1, 0), (0, KERNEL_ROWS + DENSE_ROWS)):
        place(wide, block, start, MID_ROWS)
        place(narrow, block, start + MID_ROWS, SMALL_ROWS)
    start = KERNEL_ROWS
    for out, outputs in dense:
        place(out, 1, start, outputs * CIN // LANES)
        start += outputs * CIN // LANES
    count = late.shape[0]
    rows[:count, :] = late[...].astype(F32)
    start = 0
    for out, outputs in dense:
        place(out, 0, start, outputs * CIN // LANES)
        start += outputs * CIN // LANES
    for block, first_ref, second_ref in ((0, first0, second0), (1, first1, second1)):
        first = jnp.sum(first_ref[...], 0)
        second = jnp.sum(second_ref[...], 0)
        for out, row in ((gains, 1), (shifts, 0)):
            lines = (first[row : row + 1], first[row + 2 : row + 3], second[row : row + 1])
            total = jnp.zeros((8, 2 * LANES), F32)
            for tile, lane, width, channel in NORM_LANES:
                line = jnp.concatenate([lines[tile], jnp.zeros((1, LANES), F32)], 1)
                total += shifted_lanes(jnp.broadcast_to(line, (8, 2 * LANES)), lane, width, channel)
            out[block : block + 1, :] = total[0:1, :LANES]
            out[block + 2 : block + 3, :] = total[0:1, LANES:]


def forward_first(size, me, pieces, dense, mask, table, count):
    cells = size.cells
    tile = shaped((cells, size.frames, LANES))
    z0, z1, stat = call(
        functools.partial(project_kernel, size),
        [tile, tile, shaped((count, 8, LANES))],
        [
            pltpu.VMEM((size.side + 2, size.side + 2, size.frames, LANES), F32),
            pltpu.VMEM((cells, size.frames, LANES), F32),
        ],
        [me],
        [*pieces, dense, mask],
        flops=2 * size.rows * CIN * 256,
    )
    totals = share(stat)
    (reduced,) = call(
        functools.partial(reduced_kernel, size),
        [shaped((REDUCED, size.padded), BF16)],
        [],
        [],
        [z0, totals, table, mask],
        flops=size.rows * LANES * 20,
    )
    return z0, z1, totals, reduced


def forward_second(size, me, pieces, kernel, mask, count):
    side, frames = size.side, size.frames
    field, z2, stat = call(
        functools.partial(conv_kernel, size),
        [
            shaped((side + 2, side + 2, frames, 4 * REDUCED), size.kept),
            shaped((size.cells, frames, LANES)),
            shaped((count, 8, LANES)),
        ],
        [pltpu.VMEM((4 * REDUCED, size.padded), F32)],
        [me],
        [*pieces, kernel, mask],
        flops=2 * size.rows * 9 * 256 * 256,
    )
    return field, z2, share(stat)


def backward(size, me, grads, saved, weights_at, count, spreads):
    z0, z1, totals, field, z2, totals2, table, table2, mask, kernel, pieces = saved
    g0, g2, g1 = grads
    side, frames = size.side, size.frames
    spread_rows = [pltpu.VMEM((size.rows // 4, LANES), F32)]
    (stat,) = call(
        functools.partial(second_sums_kernel, size),
        [shaped((count, 8, LANES))],
        spread_rows if spreads else [],
        [],
        [g2, z2, totals2, table2, mask],
        flops=size.rows * LANES * 30,
    )
    back2 = share(stat)
    wire = shaped((REDUCED, size.padded), BF16)
    delta2, o0, o1, o2, o3 = call(
        functools.partial(conv_back_kernel, size),
        [shaped((size.cells, frames, LANES), size.kept), wire, wire, wire, wire],
        [
            pltpu.VMEM((side + 2, side + 2, frames, LANES), size.kept),
            pltpu.VMEM((size.cells, frames, 4 * REDUCED), F32),
            pltpu.VMEM((4 * REDUCED, size.padded), F32),
        ]
        + (spread_rows if spreads else []),
        [me],
        [g2, z2, totals2, back2, table2, mask, kernel],
        flops=2 * size.rows * 9 * 256 * 256,
    )
    partial = exchange_four([o0, o1, o2, o3])
    (kernel_grad,) = call(
        functools.partial(kernel_grad_kernel, size),
        [shaped((KERNEL_ROWS, LANES), BF16)],
        [
            pltpu.VMEM((9, 2 * LANES, 4 * REDUCED), F32),
            pltpu.VMEM((9, 2, LANES, LANES), F32),
            pltpu.VMEM((KERNEL_ROWS, LANES), F32),
        ],
        [],
        [field, delta2, mask],
        flops=2 * size.rows * 9 * 256 * 256,
    )
    tile = shaped((size.cells, frames, LANES))
    i0, i1, stat = call(
        functools.partial(first_sums_kernel, size),
        [tile, tile, shaped((count, 8, LANES))],
        [pltpu.VMEM((size.cells, frames, LANES), F32)] + (spread_rows * 2 if spreads else []),
        [],
        [*partial, g0, g1, z0, z1, totals, table, mask],
        flops=size.rows * LANES * 60,
    )
    back1 = share(stat)
    (delta1,) = call(
        functools.partial(first_delta_kernel, size),
        [shaped((ROWS, size.padded), BF16)],
        [
            pltpu.VMEM((side + 2, side + 2, frames, LANES), F32),
            pltpu.VMEM((size.cells, frames, LANES), F32),
        ],
        [],
        [z0, z1, i0, i1, totals, back1, table, mask],
        flops=size.rows * LANES * 60,
    )
    deltas = gather_four(delta1)
    (dense_grad,) = call(
        functools.partial(weight_grad_kernel, size),
        [shaped((DENSE_ROWS, LANES), BF16)],
        [pltpu.VMEM((4, 2, ROWS, LANES), F32), pltpu.VMEM((DENSE_ROWS, LANES), F32)],
        [me],
        [delta1, *pieces],
        flops=2 * size.rows * CIN * 256,
    )
    scratch = [pltpu.VMEM((2, size.padded, LANES), F32)]
    if spreads:
        result = call(
            functools.partial(input_kernel, size),
            [shaped((size.cells, frames // 8, 8 * QUARTER))],
            scratch,
            [],
            [*deltas, *weights_at],
            flops=2 * size.rows * 4 * ROWS * 256,
        )
    else:
        result = call(
            functools.partial(input_half_kernel, size),
            [tile, tile, tile],
            scratch,
            [],
            [*deltas, *weights_at],
            flops=2 * size.rows * 4 * ROWS * 256,
        )
    return result, kernel_grad, dense_grad, back1, back2


def on_device(count, clips, clip_len, w_plain, w_mid, k_mid, w_small, k_small, w_pool, gains, shifts, grad_out):
    big = Size(clips.shape[1], 8 * clips.shape[0])
    low = Size(grad_out.shape[1], 8 * grad_out.shape[0])
    me = lax.axis_index("chan").astype(jnp.int32).reshape(1)
    (own,) = call(
        functools.partial(unpack_kernel, big),
        [shaped((QUARTER, big.padded), BF16)],
        [pltpu.VMEM((2, big.rows, LANES), F32)],
        [],
        [clips.transpose(1, 2, 0, 3).reshape(big.cells, clips.shape[0], 8 * QUARTER)],
    )
    pieces = gather_four(own)
    low_tile = shaped((low.cells, low.frames, LANES))
    grads = call(
        functools.partial(grad_kernel, low),
        [low_tile, low_tile, low_tile],
        [pltpu.VMEM((2, low.rows, LANES), F32)],
        [],
        [grad_out],
    )
    table = shaped((8, LANES))
    prepared = call(
        prepare_kernel,
        [shaped((3, big.frames, LANES)), shaped((3, low.frames, LANES))]
        + [table] * 4
        + [shaped((2, QUARTER, ROWS), BF16)] * 4
        + [shaped((4, 2 * LANES, QUARTER), BF16)] * 2
        + [shaped((9, LANES, 4 * REDUCED), BF16)] * 2
        + [shaped((9, 4 * REDUCED, LANES), BF16)] * 2,
        [
            pltpu.VMEM((2 * MID_ROWS, LANES), F32),
            pltpu.VMEM((2, 4, 2, ROWS, LANES), F32),
            pltpu.VMEM((9, 2, LANES, LANES), F32),
        ],
        [me, clip_len],
        [as_rows(item) for item in (w_plain, w_mid, w_small, w_pool, k_mid, k_small, gains, shifts)],
    )
    mask, mask_low, table0, second0, table1, second1 = prepared[:6]
    sent, (dense0, dense1), (kernel0, kernel1), (turned0, turned1) = (
        prepared[6:10],
        prepared[10:12],
        prepared[12:14],
        prepared[14:16],
    )
    weights_at = exchange_four(sent)

    z0, z1, totals, reduced = forward_first(big, me, pieces, dense0, mask, table0, count)
    mids = gather_four(reduced)
    half = [pltpu.VMEM((big.rows // 4, LANES), F32)]
    h0, h1 = call(
        functools.partial(first_half_kernel, big),
        [low_tile, low_tile],
        half * 2,
        [],
        [z0, z1, totals, table0, mask],
        flops=big.rows * 2 * LANES * 20,
    )
    field, z2, totals2 = forward_second(big, me, mids, turned0, mask, count)
    (own1,) = call(
        functools.partial(second_half_kernel, big),
        [shaped((QUARTER, low.padded), BF16)],
        half,
        [],
        [z2, totals2, second0, mask, h0, h1],
        flops=big.rows * LANES * 20,
    )
    saved0 = (z0, z1, totals, field, z2, totals2, table0, second0, mask, kernel0, pieces)

    pieces1 = gather_four(own1)
    z0, z1, totals, reduced = forward_first(low, me, pieces1, dense1, mask_low, table1, count)
    mids = gather_four(reduced)
    field, z2, totals2 = forward_second(low, me, mids, turned1, mask_low, count)
    (mixed,) = call(
        functools.partial(output_kernel, low),
        [shaped(grad_out.shape, BF16)],
        [pltpu.VMEM((2, low.rows, LANES), F32)],
        [],
        [z0, z1, z2, totals, totals2, table1, second1, mask_low],
        flops=low.rows * 3 * LANES * 20,
    )
    saved1 = (z0, z1, totals, field, z2, totals2, table1, second1, mask_low, kernel1, pieces1)
    first, second, third = grads
    grads, kernel_grad1, dense_grad1, first1, last1 = backward(
        low, me, (first, second, third), saved1, weights_at, count, False
    )
    (clips_grad,), kernel_grad0, dense_grad0, first0, last0 = backward(big, me, grads, saved0, weights_at, count, True)
    early = reduce_rows([kernel_grad1, dense_grad1, kernel_grad0], count)
    late = reduce_rows([dense_grad0], count)
    sizes = [outputs * CIN // 64 for outputs in (MID, SMALL, PLAIN, POOL)] + [2 * MID_ROWS, 2 * SMALL_ROWS, 4, 4]
    flats = call(
        finish_kernel,
        [shaped((rows, LANES)) for rows in sizes],
        [pltpu.VMEM((max(early.shape[0], late.shape[0]), LANES), F32)],
        [],
        [early, late, first0, first1, last0, last1],
    )
    mid, small, plain, pool, wide, narrow, gains_grad, shifts_grad = (as_flat(item) for item in flats)
    shape = (big.side, big.side, big.frames // 8, 8 * QUARTER)
    clips_grad = clips_grad.reshape(shape).transpose(2, 0, 1, 3)
    return mixed, clips_grad, plain, mid, wide, small, narrow, pool, gains_grad, shifts_grad


def solution(mesh):
    frames = P("dp", None, None, "chan")
    flat = P(None, "chan")
    return jax.shard_map(
        functools.partial(on_device, mesh.shape["dp"]),
        mesh=mesh,
        in_specs=(frames, P("dp")) + (flat,) * 8 + (frames,),
        out_specs=(frames, frames) + (flat,) * 8,
        check_vma=False,
    )
```

```python
import functools

import jax
import jax.numpy as jnp
from jax import lax
from jax.experimental import pallas as pl
from jax.experimental.pallas import tpu as pltpu
from jax.sharding import PartitionSpec as P

CIN = 832
QUARTER = 208
WIDE, NARROW = 80, 32
MID, SMALL, PLAIN, POOL = 40, 8, 64, 32
REDUCED = MID + SMALL
DENSE = REDUCED + PLAIN
ROWS = DENSE + POOL
CLIPS = 2
EPSILON = 1e-05
F32 = jnp.float32
BF16 = jnp.bfloat16
LANES = 128
LIMIT = 62
COST = 1
MID_TILES = 4 * 9 * 160 // LANES
MID_ROWS = WIDE // 4 * MID_TILES
SMALL_TILES = 4 * 9 * 32 // LANES
SMALL_ROWS = NARROW // 4 * SMALL_TILES
KERNEL_ROWS = 976
PAIR_TILES = 2 * CIN // LANES
DENSE_ROWS = 944


class Size:
    def __init__(self, side, frames):
        self.side = side
        self.frames = frames
        self.cells = side * side
        self.rows = self.cells * frames
        self.padded = -(-self.rows // LANES) * LANES
        self.band = 2 if side % 2 == 0 else side
        self.chunks = side // self.band
        self.step = self.band * side
        self.group = LANES // frames
        self.full = self.cells // self.group
        self.rest = self.cells - self.full * self.group
        self.kept = BF16 if frames % 16 == 0 else F32
        self.parts = [(0, side // 2), (side // 2, side // 2)] if side % 2 == 0 else [(0, side)]

    def lanes(self, part):
        return -(-self.parts[part][1] * self.side * self.frames // LANES) * LANES

    def cells_of(self, part):
        first, count = self.parts[part]
        return first * self.side, count * self.side

    def columns_of(self, part):
        first, count = self.cells_of(part)
        lanes, result = self.lanes(part), []
        width = 640 if lanes > 640 else lanes
        for start in range(0, lanes, width):
            skipped = start // self.frames
            held = min(width, lanes - start)
            result.append((start, held, first + skipped, min(held // self.frames, count - skipped)))
        return result


class Stream:
    def __init__(self, far, near, sems, axis, parts):
        self.far, self.near, self.sems, self.axis, self.parts = far, near, sems, axis, parts
        self.shape, self.dtype = near.shape, near.dtype

    def copy(self, part, inward):
        index = (slice(None),) * self.axis + (pl.ds(*self.parts[part]),)
        pair = (self.far.at[index], self.near.at[index])
        return pltpu.make_async_copy(*(pair if inward else pair[::-1]), self.sems.at[part])

    def ready(self, part):
        self.copy(part, True).wait()

    def flush(self, part):
        self.copy(part, False).start()

    def __getitem__(self, index):
        return self.near[index]

    def __setitem__(self, index, value):
        self.near[index] = value

    @property
    def at(self):
        return self.near.at


def even(total, count):
    return [(start * (total // count), total // count) for start in range(count)]


def cell_parts(size):
    return 0, even(size.cells, size.chunks)


def line_parts(size, part=None):
    first, count = size.parts[part] if part is not None else (0, size.side)
    return 0, [(row * size.side, size.side) for row in range(first, first + count)]


def column_parts(size, part):
    return 1, [(start, width) for start, width, _, _ in size.columns_of(part)]


def call(body, outs, scratch, scalars, args, flops=0, ins=None, puts=None, aliases=None):
    ins, puts = ins or {}, puts or {}
    aliases = {len(scalars) + index: out for index, out in (aliases or {}).items()}
    plans = [ins.get(index) for index in range(len(args))] + [puts.get(index) for index in range(len(outs))]
    arrays = list(args) + list(outs)
    buffers = []
    for array, plan in zip(arrays, plans):
        buffers.append(pltpu.VMEM(array.shape, array.dtype))
        buffers.append(pltpu.SemaphoreType.DMA((len(plan[1]) if plan else 1,)))

    def wrapped(*refs):
        numbers, refs = refs[: len(scalars)], refs[len(scalars) :]
        far, refs = refs[: len(arrays)], refs[len(arrays) :]
        own, refs = refs[: len(scratch)], refs[len(scratch) :]
        streams = []
        for index, plan in enumerate(plans):
            axis, parts = plan or (0, [(0, arrays[index].shape[0])])
            streams.append(Stream(far[index], refs[2 * index], refs[2 * index + 1], axis, parts))
        entering, leaving = streams[: len(args)], streams[len(args) :]
        for part in range(max([len(stream.parts) for stream in entering])):
            for stream in entering:
                if part < len(stream.parts):
                    stream.copy(part, True).start()
        for index, stream in enumerate(entering):
            if index not in ins:
                stream.ready(0)
        body(*numbers, *entering, *leaving, *own)
        for index, stream in enumerate(leaving):
            if index not in puts:
                stream.flush(0)
        for stream in leaving:
            for part in range(len(stream.parts)):
                stream.copy(part, False).wait()

    moved = sum(array.size * array.dtype.itemsize for array in arrays)
    return pl.pallas_call(
        wrapped,
        out_shape=outs,
        in_specs=[pl.BlockSpec(memory_space=pltpu.SMEM)] * len(scalars) + [pl.BlockSpec(memory_space=pl.ANY)] * len(args),
        out_specs=[pl.BlockSpec(memory_space=pl.ANY)] * len(outs),
        scratch_shapes=list(scratch) + buffers,
        compiler_params=pltpu.CompilerParams(vmem_limit_bytes=LIMIT * 1024 * 1024),
        cost_estimate=pl.CostEstimate(flops=COST, bytes_accessed=COST, transcendentals=0),
        input_output_aliases=aliases,
    )(*scalars, *args)


def unrolled(count, body, carry):
    for index in range(count):
        carry = body(index, carry)
    return carry


def shaped(shape, dtype=F32):
    return jax.ShapeDtypeStruct(shape, dtype)


def sigmoid(value):
    return 0.5 * jnp.tanh(0.5 * value) + 0.5


def row_table(rows):
    index = lax.broadcasted_iota(jnp.int32, (8, LANES), 0)
    table = jnp.zeros((8, LANES), F32)
    for position, row in enumerate(rows):
        table = jnp.where(index == position, row, table)
    return table


def time_box(value, mask_ref):
    cells, frames, width = value.shape
    flat = value.reshape(cells * frames, width)
    before = pltpu.roll(flat, 1, 0).reshape(value.shape)
    after = pltpu.roll(flat, cells * frames - 1, 0).reshape(value.shape)
    return value + before * mask_ref[1] + after * mask_ref[2]


def owner_rows(all_ref, owner):
    if len(all_ref.shape) == 3:
        return all_ref[...]
    return all_ref[:, pl.ds(owner, 1)].reshape(all_ref.shape[0], 8, LANES)


def norm_rows(all_ref, table_ref, tile, owner=0):
    total = jnp.sum(owner_rows(all_ref, owner), 0)
    count = total[4:5]
    mean = total[2 * tile : 2 * tile + 1] / count
    variance = total[2 * tile + 1 : 2 * tile + 2] / count - mean * mean
    inverse = lax.rsqrt(variance + EPSILON)
    gain = table_ref[2 * tile : 2 * tile + 1]
    shift = table_ref[2 * tile + 1 : 2 * tile + 2]
    return mean, inverse, gain, shift, count


def activate(value, rows, mask_ref):
    mean, inverse, gain, shift, _ = rows
    shifted = gain * ((value - mean) * inverse) + shift
    return shifted * sigmoid(shifted) * mask_ref[0]


def inner_grad(grad, value, rows, mask_ref):
    mean, inverse, gain, shift, _ = rows
    normed = (value - mean) * inverse
    shifted = gain * normed + shift
    sigma = sigmoid(shifted)
    return grad * mask_ref[0] * sigma * (1.0 + shifted * (1.0 - sigma)), normed


def norm_delta(inner, value, rows, back_ref, tile, mask_ref):
    mean, inverse, gain, _, count = rows
    total = jnp.sum(back_ref[...], 0)
    shift_grad = total[2 * tile : 2 * tile + 1] / count
    gain_grad = total[2 * tile + 1 : 2 * tile + 2] / count
    normed = (value - mean) * inverse
    return (gain * inverse) * (inner - mask_ref[0] * (shift_grad + normed * gain_grad))


def publish(stat_ref, rows):
    stat_ref[...] = jnp.broadcast_to(row_table(rows)[None], stat_ref.shape)


def collapse(value):
    return jnp.sum(value, 0, keepdims=True)


def windows():
    result = []
    for frame in range(8):
        start = frame * QUARTER
        first, offset = start // LANES, start % LANES
        result.append((first, -(-(offset + QUARTER) // LANES), offset))
    return result


def unpack_rows(line, frame):
    first, tiles, offset = windows()[frame]
    value = line[:, first * LANES : (first + tiles) * LANES]
    if offset:
        value = pltpu.roll(value, tiles * LANES - offset, 1)
    return value[:, : 2 * LANES]


def pack_rows(parts):
    tiles = [None] * 13
    for frame, value in enumerate(parts):
        first, count, offset = windows()[frame]
        if count == 3:
            value = jnp.concatenate([value, jnp.zeros((value.shape[0], LANES), value.dtype)], 1)
        if offset:
            value = pltpu.roll(value, offset, 1)
        for index in range(count):
            piece = value[:, index * LANES : (index + 1) * LANES]
            place = first + index
            tiles[place] = piece if tiles[place] is None else tiles[place] + piece
    return tiles


def assemble(first, second, third):
    blank = jnp.zeros_like(first)
    lane = lax.broadcasted_iota(jnp.int32, (first.shape[0], 2 * LANES), 1)
    plain = pltpu.roll(jnp.concatenate([first, blank], 1), 2 * LANES - REDUCED, 1)
    middle = pltpu.roll(jnp.concatenate([second, blank], 1), PLAIN, 1)
    pool = pltpu.roll(jnp.concatenate([third, blank], 1), PLAIN + WIDE + NARROW, 1)
    return jnp.where(lane < PLAIN, plain, 0.0) + middle + pool


def separate(value):
    lane = lax.broadcasted_iota(jnp.int32, (value.shape[0], LANES), 1)
    plain = pltpu.roll(value, REDUCED, 1)[:, :LANES]
    middle = pltpu.roll(value, 2 * LANES - PLAIN, 1)[:, :LANES]
    pool = pltpu.roll(value, 2 * LANES - PLAIN - WIDE - NARROW, 1)[:, :LANES]
    first = jnp.where((lane >= REDUCED) & (lane < DENSE), plain, 0.0)
    second = jnp.where(lane < WIDE + NARROW, middle, 0.0)
    third = jnp.where(lane < POOL, pool, 0.0)
    return first, second, third


def part_blocks(size, part, one, leaving=(), per=4):
    first, count = size.cells_of(part)
    total = size.lanes(part) // LANES
    for block in range(total):
        skipped = block * size.group
        one(first + skipped, min(size.group, count - skipped), slice(block * LANES, (block + 1) * LANES))
        if block % per == per - 1 or block == total - 1:
            for stream in leaving:
                stream.flush(block // per)


def block_parts(size, part, per=4):
    total = size.lanes(part) // LANES
    return 1, [(block * LANES, min(per, total - block) * LANES) for block in range(0, total, per)]


def unpack_kernel(size, part, raw, out, scratch):
    side, frames = size.side, size.frames
    pairs_of = frames // 8
    first, count = size.parts[part]
    for index in range(count):
        raw.ready(index)
        start = (first + index) * side
        value = raw[start : start + side].astype(F32).reshape(pairs_of * side, 8 * QUARTER)
        for frame in range(8):
            place = pl.ds(index * side * frames + frame, pairs_of * side, stride=8)
            piece = unpack_rows(value, frame)
            scratch[0, place, :] = piece[:, :LANES]
            scratch[1, place, :] = piece[:, LANES:]

    def one(cell, cells, lanes):
        start = (cell - first * side) * frames
        for tile, (low, high) in enumerate(((0, LANES), (LANES, QUARTER))):
            value = scratch[tile, start : start + cells * frames, :].reshape(cells, frames, LANES)
            out[low:high, lanes] = turn(size, value, cells)[: high - low].astype(BF16)

    part_blocks(size, part, one, (out,))


def grad_kernel(size, raw, first, second, third, scratch):
    side, frames = size.side, size.frames

    def line(row, carry):
        value = raw[0, row].astype(F32)
        for frame in range(8):
            place = pl.ds(row * side * frames + frame, side, stride=frames)
            part = unpack_rows(value, frame)
            scratch[0, place, :] = part[:, :LANES]
            scratch[1, place, :] = part[:, LANES:]
        return carry

    unrolled(side, line, 0)
    parts = separate(jnp.concatenate([scratch[0], scratch[1]], 1))
    for ref, part in zip((first, second, third), parts):
        ref[...] = part.reshape(ref.shape)


def dot(left, right, dims=((1,), (0,))):
    return lax.dot_general(left, right, (dims, ((), ())), preferred_element_type=F32)


def into_padded(size, flat, field):
    side = size.side
    field[...] = jnp.zeros_like(field)

    def line(row, carry):
        field[row + 1, 1 : side + 1] = flat[pl.ds(row * side, side)]
        return carry

    unrolled(side, line, 0)


def project_part(size, part, me, pieces, w_ref, z0, flat, carry):
    frames = size.frames
    total, squares = carry
    for index, (start, width, first, cells) in enumerate(size.columns_of(part)):
        value = jnp.zeros((width, 2 * LANES), F32)
        for position, x in enumerate(pieces):
            x.ready(index)
            value += dot(x[:, start : start + width], w_ref[me[0] ^ position], ((0,), (0,)))
        value = value.reshape(width // frames, frames, 2 * LANES)[:cells]
        dense = value[:, :, :LANES]
        z0[first : first + cells] = dense
        z0.flush(index)
        flat[first : first + cells] = value[:, :, LANES:]
        total += jnp.sum(dense, 0)
        squares += jnp.sum(dense * dense, 0)
    return total, squares


def project_first_kernel(size, me, x0, x1, x2, x3, w_ref, z0, flat, sums):
    blank = jnp.zeros((size.frames, LANES), F32)
    total, squares = project_part(size, 0, me, (x0, x1, x2, x3), w_ref, z0, flat, (blank, blank))
    flat.flush(0)
    sums[0] = total
    sums[1] = squares


def project_kernel(size, me, *refs):
    side, frames = size.side, size.frames
    pieces, (w_ref, mask, table), refs = refs[:4], refs[4:7], refs[7:]
    blank = jnp.zeros((frames, LANES), F32)
    carry = (blank, blank)
    if len(size.parts) > 1:
        before, flat, sums, z0, z1, stat, wire, field = refs
        carry = (sums[0], sums[1])
    else:
        before = None
        z0, z1, stat, wire, field, flat = refs
    total, squares = project_part(size, len(size.parts) - 1, me, pieces, w_ref, z0, flat, carry)
    if before is not None:
        flat.ready(0)
    valid = mask[0]
    total, squares = collapse(total * valid), collapse(squares * valid)
    count = collapse(valid) * size.cells
    mean = total / count
    if before is not None:
        before.ready(0)

    def one(cell, cells, lanes):
        source = z0 if before is None or cell >= size.cells_of(1)[0] else before
        if before is not None and cell < size.cells_of(1)[0] < cell + cells:
            middle = size.cells_of(1)[0]
            value = jnp.concatenate([before[cell:middle], z0[middle : cell + cells]], 0)
        else:
            value = source[cell : cell + cells]
        wire[:, lanes] = turn(size, value - mean, cells)[:REDUCED].astype(BF16)

    for block in range(size.padded // LANES):
        cell = block * size.group
        one(cell, min(size.group, size.cells - cell), slice(block * LANES, (block + 1) * LANES))
    into_padded(size, flat, field)
    pool_total, pool_squares = blank, blank
    for row in range(side):
        pool = pool_line(size, field, row, mask)
        z1[row * side : (row + 1) * side] = pool
        z1.flush(row)
        pool_total += jnp.sum(pool, 0)
        pool_squares += jnp.sum(pool * pool, 0)
    rows = [total, squares, collapse(pool_total * valid), collapse(pool_squares * valid), count]
    publish(stat, rows + [table[0:1], table[1:2]])


def pool_line(size, field, row, mask):
    side = size.side
    lines = field[pl.ds(row, 3)]
    column = lines[0] + lines[1] + lines[2]
    value = column[0:side] + column[1 : side + 1] + column[2 : side + 2]
    return time_box(value, mask) * (1.0 / 27.0)


def block_bounds(size):
    bounds, last = [], 0
    for part in range(size.chunks):
        until = size.full if part == size.chunks - 1 else (part + 1) * size.step // size.group
        bounds.append((last, until))
        last = until
    return bounds


def wire_parts(size):
    parts = [(low * LANES, (high - low) * LANES) for low, high in block_bounds(size)]
    if size.rest:
        parts[-1] = (parts[-1][0], parts[-1][1] + LANES)
    return 1, parts


def blocks(size, one, entering=(), leaving=()):
    for part, (low, high) in enumerate(block_bounds(size)):
        for stream in entering:
            stream.ready(part)
        for block in range(low, high):
            one(block, size.group)
        if size.rest and part == size.chunks - 1:
            one(size.full, size.rest)
        for stream in leaving:
            stream.flush(part)


def turn(size, value, cells):
    flat = value.reshape(cells * size.frames, value.shape[-1])
    if cells < size.group:
        blank = jnp.zeros((LANES - cells * size.frames, value.shape[-1]), value.dtype)
        flat = jnp.concatenate([flat, blank], 0)
    return flat.T


def lanes_of(block):
    if isinstance(block, int):
        return pl.ds(block * LANES, LANES)
    return pl.ds(pl.multiple_of(block * LANES, LANES), LANES)


def conv_kernel(size, me, group, p0, p1, p2, p3, totals, lanes_valid, kernel, mask, field, z2, stat, joined):
    side, frames, step = size.side, size.frames, size.step
    for position, piece in enumerate((p0, p1, p2, p3)):
        owner = me[0] ^ position
        every = owner_rows(totals, owner)
        total = jnp.sum(every, 0)
        sent = totals[pl.ds(group[0], 1), pl.ds(owner, 1)].reshape(8, LANES)
        mean = total[0:1] / total[4:5]
        variance = total[1:2] / total[4:5] - mean * mean
        scale = sent[5:6] * lax.rsqrt(variance + EPSILON)
        offset = (sent[0:1] / sent[4:5] - mean) * scale + sent[6:7]
        turned = row_table([scale, offset]).T
        scale, offset = turned[:REDUCED, 0:1], turned[:REDUCED, 1:2]
        shifted = piece[...].astype(F32) * scale + offset
        value = shifted * sigmoid(shifted)
        joined[pl.ds(pl.multiple_of(owner * MID, 8), MID), :] = value[:MID]
        joined[pl.ds(pl.multiple_of(4 * MID + owner * SMALL, 8), SMALL), :] = value[MID:]
    field[...] = jnp.zeros_like(field)

    def one(block, cells):
        value = (joined[:, lanes_of(block)] * lanes_valid[0:1]).T
        value = value.reshape(size.group, frames, 4 * REDUCED).astype(size.kept)
        for index in range(cells):
            cell = block * size.group + index
            row = cell // side if isinstance(cell, int) else lax.div(cell, side)
            field[row + 1, cell - row * side + 1] = value[index]

    blocks(size, one)
    field.flush(0)
    kernel.ready(0)
    blank = jnp.zeros((frames, LANES), F32)

    def chunk(index, carry):
        total, squares = carry
        value = jnp.zeros((step * frames, LANES), F32)
        for row in range(3):
            for column in range(3):
                part = field[pl.ds(index * size.band + row, size.band), column : column + side]
                part = part.reshape(step * frames, 4 * REDUCED).astype(BF16)
                value += dot(part, kernel[3 * row + column])
        value = time_box(value.reshape(step, frames, LANES), mask) * (1.0 / 3.0)
        z2[pl.ds(index * step, step)] = value
        z2.flush(index)
        return total + jnp.sum(value, 0), squares + jnp.sum(value * value, 0)

    total, squares = unrolled(size.chunks, chunk, (blank, blank))
    valid = mask[0]
    one_row = jnp.zeros((1, LANES), F32)
    rows = [collapse(total * valid), collapse(squares * valid), one_row, one_row, collapse(valid) * size.cells]
    publish(stat, rows)


def halve_into(size, value, scratch, index):
    half = size.side // 2
    value = value.reshape(2, half, 2, size.frames, LANES)
    value = value[0] + value[1]
    value = value[:, 0] + value[:, 1]
    rows = half * size.frames
    scratch[pl.ds(index * rows, rows), :] = value.reshape(rows, LANES)


def halved_rows(scratch):
    count = scratch.shape[0] // 2
    return (scratch[pl.ds(0, count, stride=2), :] + scratch[pl.ds(1, count, stride=2), :]) * 0.125


def first_half_kernel(size, me, z0, z1, totals, table, mask, h0, h1, s0, s1):
    for tile, (z, out, scratch) in enumerate(((z0, h0, s0), (z1, h1, s1))):
        rows = norm_rows(totals, table, tile, me[0])

        def chunk(index, carry, z=z, scratch=scratch, rows=rows):
            z.ready(index)
            value = activate(z[pl.ds(index * size.step, size.step)], rows, mask)
            halve_into(size, value, scratch, index)
            return carry

        unrolled(size.chunks, chunk, 0)
        out[...] = halved_rows(scratch).reshape(out.shape)


def second_half_kernel(size, z2, totals, table, mask, h0, h1, out, scratch):
    rows = norm_rows(totals, table, 0)

    def chunk(index, carry):
        z2.ready(index)
        value = activate(z2[pl.ds(index * size.step, size.step)], rows, mask)
        halve_into(size, value, scratch, index)
        return carry

    unrolled(size.chunks, chunk, 0)
    value = halved_rows(scratch)
    count = value.shape[0]
    value = assemble(h0[...].reshape(count, LANES), value, h1[...].reshape(count, LANES))
    value = jnp.concatenate([value, jnp.zeros((out.shape[1] - count, 2 * LANES), F32)], 0)
    out[...] = value.T[:QUARTER].astype(BF16)


def strided(scratch, start, count, stride):
    place = pl.ds(start, count, stride=stride)
    return jnp.concatenate([scratch[0, place, :], scratch[1, place, :]], 1)


def output_kernel(size, me, z0, z1, z2, totals, totals2, table, table2, mask, out, scratch):
    side, frames = size.side, size.frames
    parts = [
        activate(z[...], norm_rows(total, tab, tile, me[0]), mask).reshape(size.rows, LANES)
        for z, total, tab, tile in ((z0, totals, table, 0), (z2, totals2, table2, 0), (z1, totals, table, 1))
    ]
    value = assemble(*parts)
    scratch[0] = value[:, :LANES]
    scratch[1] = value[:, LANES:]

    def line(row, carry):
        start = row * side * frames
        lines = [strided(scratch, start + frame, side, frames) for frame in range(8)]
        for place, tile in enumerate(pack_rows(lines)):
            out[0, row, :, place * LANES : (place + 1) * LANES] = tile.astype(BF16)
        return carry

    unrolled(side, line, 0)


def spread(size, grad, scratch):
    value = grad[...].reshape(-1, LANES)
    count = value.shape[0]
    scratch[pl.ds(0, count, stride=2), :] = value
    scratch[pl.ds(1, count, stride=2), :] = value


def grad_chunk(size, grad, scratch, index):
    if scratch is None:
        return grad[pl.ds(index * size.step, size.step)]
    half = size.side // 2
    rows = half * size.frames
    value = scratch[pl.ds(index * rows, rows), :].reshape(half, 1, size.frames, LANES)
    value = jnp.broadcast_to(value, (half, 2, size.frames, LANES)).reshape(1, size.side, size.frames, LANES)
    value = jnp.broadcast_to(value, (2, size.side, size.frames, LANES))
    return value.reshape(size.step, size.frames, LANES)


def second_sums_kernel(size, grad, z2, totals, table, mask, stat, *scratch):
    scratch = scratch[0] if scratch else None
    if scratch is not None:
        spread(size, grad, scratch)
    rows = norm_rows(totals, table, 0)
    blank = jnp.zeros((size.frames, LANES), F32)

    def chunk(index, carry):
        shift_grad, gain_grad = carry
        z2.ready(index)
        value = z2[pl.ds(index * size.step, size.step)]
        inner, normed = inner_grad(grad_chunk(size, grad, scratch, index), value, rows, mask)
        return shift_grad + jnp.sum(inner, 0), gain_grad + jnp.sum(inner * normed, 0)

    shift_grad, gain_grad = unrolled(size.chunks, chunk, (blank, blank))
    publish(stat, [collapse(shift_grad), collapse(gain_grad)])


def conv_back_kernel(size, me, grad, z2, totals, back, table, mask, kernel, delta, o0, o1, o2, o3, field, result, turned, *scratch):
    side, frames, step = size.side, size.frames, size.step
    scratch = scratch[0] if scratch else None
    if scratch is not None:
        spread(size, grad, scratch)
    rows = norm_rows(totals, table, 0)
    field[...] = jnp.zeros_like(field)

    def first(index, carry):
        z2.ready(index)
        value = z2[pl.ds(index * step, step)]
        inner, _ = inner_grad(grad_chunk(size, grad, scratch, index), value, rows, mask)
        value = norm_delta(inner, value, rows, back, 0, mask).astype(BF16).astype(size.kept)
        delta[pl.ds(index * step, step)] = value
        delta.flush(index)
        field[pl.ds(1 + index * size.band, size.band), 1 : side + 1] = value.reshape(size.band, side, frames, LANES)
        return carry

    unrolled(size.chunks, first, 0)
    kernel.ready(0)

    def chunk(index, carry):
        value = jnp.zeros((step * frames, 4 * REDUCED), F32)
        for row in range(3):
            for column in range(3):
                part = field[pl.ds(index * size.band + 2 - row, size.band), 2 - column : 2 - column + side]
                part = part.reshape(step * frames, LANES).astype(BF16)
                value += dot(part, kernel[3 * row + column])
        result[pl.ds(index * step, step)] = value.reshape(step, frames, 4 * REDUCED)
        return carry

    unrolled(size.chunks, chunk, 0)

    def one(block, cells):
        value = turn(size, result[pl.ds(block * size.group, cells)], cells)
        turned[:, lanes_of(block)] = value

    blocks(size, one)
    for position, out in enumerate((o0, o1, o2, o3)):
        owner = me[0] ^ position
        mid = turned[pl.ds(pl.multiple_of(owner * MID, 8), MID), :]
        small = turned[pl.ds(pl.multiple_of(4 * MID + owner * SMALL, 8), SMALL), :]
        out[...] = jnp.concatenate([mid, small], 0).astype(BF16)


def kernel_grad_kernel(size, field, delta, mask, out, total, taps, flat):
    side, frames, step = size.side, size.frames, size.step
    total[...] = jnp.zeros_like(total)
    field.ready(0)
    field.ready(1)

    def chunk(index, carry):
        delta.ready(index)
        for extra in range(size.band):
            field.ready(index * size.band + 2 + extra)
        value = delta[pl.ds(index * step, step)].astype(F32)
        value = time_box(value, mask).reshape(step * frames, LANES)
        upper = value.astype(BF16).astype(F32)
        both = jnp.concatenate([upper, value - upper], 1).T.astype(BF16)
        for row in range(3):
            for column in range(3):
                part = field[pl.ds(index * size.band + row, size.band), column : column + side]
                part = part.reshape(step * frames, 4 * REDUCED).astype(BF16)
                total[3 * row + column] += dot(both, part)
        return carry

    unrolled(size.chunks, chunk, 0)
    for tap in range(9):
        value = (total[tap, :LANES] + total[tap, LANES:]) * (1.0 / 3.0)
        taps[tap, 0] = value[:, :LANES]
        taps[tap, 1, :, : 4 * REDUCED - LANES] = value[:, LANES:]
    lane = lax.broadcasted_iota(jnp.int32, (WIDE // 4, LANES), 1)
    tiles = [None] * MID_TILES

    def add(place, value):
        tiles[place] = value if tiles[place] is None else tiles[place] + value

    for extra in range(4):
        for tap in range(9):
            rows = pl.ds(extra, WIDE // 4, stride=4)
            rest = jnp.where(lane < 4 * MID - LANES, taps[tap, 1, rows, :], 0.0)
            offset = (extra * 9 + tap) * 4 * MID
            value = jnp.concatenate([taps[tap, 0, rows, :], rest, jnp.zeros_like(rest)], 1)
            value = pltpu.roll(value, offset % LANES, 1)
            for index in range(-(-(offset % LANES + 4 * MID) // LANES)):
                add(offset // LANES + index, value[:, index * LANES : (index + 1) * LANES])
    for place, tile in enumerate(tiles):
        flat[pl.ds(place, WIDE // 4, stride=MID_TILES), :] = tile
    lane = lax.broadcasted_iota(jnp.int32, (NARROW // 4, LANES), 1)
    tiles = [None] * SMALL_TILES
    start = 4 * MID - LANES
    for extra in range(4):
        for tap in range(9):
            value = taps[tap, 1, pl.ds(WIDE + extra, NARROW // 4, stride=4), :]
            value = jnp.where((lane >= start) & (lane < start + 4 * SMALL), value, 0.0)
            offset = (extra * 9 + tap) * 4 * SMALL
            value = pltpu.roll(value, (offset - start) % LANES, 1)
            add(offset // LANES, value)
    for place, tile in enumerate(tiles):
        flat[pl.ds(MID_ROWS + place, NARROW // 4, stride=SMALL_TILES), :] = tile
    flat[MID_ROWS + SMALL_ROWS :, :] = jnp.zeros((KERNEL_ROWS - MID_ROWS - SMALL_ROWS, LANES), F32)
    out[...] = flat[...].astype(BF16)


def first_sums_kernel(size, me, p0, p1, p2, p3, g0, g1, z0, z1, totals, table, mask, i0, i1, stat, field, *scratch):
    step, frames = size.step, size.frames
    s0, s1 = scratch if scratch else (None, None)
    if scratch:
        spread(size, g0, s0)
        spread(size, g1, s1)

    def one(block, cells):
        place = lanes_of(block)
        value = p0[:, place].astype(F32) + p1[:, place].astype(F32)
        value += p2[:, place].astype(F32) + p3[:, place].astype(F32)
        value = jnp.concatenate([value, jnp.zeros((LANES - REDUCED, LANES), F32)], 0).T
        value = value.reshape(size.group, frames, LANES)
        field[pl.ds(block * size.group, cells)] = value[:cells]

    blocks(size, one)
    rows0 = norm_rows(totals, table, 0, me[0])
    rows1 = norm_rows(totals, table, 1, me[0])
    blank = jnp.zeros((frames, LANES), F32)

    def chunk(index, carry):
        place = pl.ds(index * step, step)
        z0.ready(index)
        z1.ready(index)
        grad = time_box(field[place], mask) * (1.0 / 3.0) + grad_chunk(size, g0, s0, index)
        inner0, normed0 = inner_grad(grad, z0[place], rows0, mask)
        inner1, normed1 = inner_grad(grad_chunk(size, g1, s1, index), z1[place], rows1, mask)
        i0[place] = inner0
        i1[place] = inner1
        i0.flush(index)
        i1.flush(index)
        sums = (inner0, inner0 * normed0, inner1, inner1 * normed1)
        return tuple(old + jnp.sum(new, 0) for old, new in zip(carry, sums))

    sums = unrolled(size.chunks, chunk, (blank,) * 4)
    publish(stat, [collapse(item) for item in sums])


def first_delta_kernel(size, me, z0, z1, i0, i1, totals, back, table, mask, *refs):
    outs, (field, pooled) = refs[:-2], refs[-2:]
    side, step, frames = size.side, size.step, size.frames
    rows0 = norm_rows(totals, table, 0, me[0])
    rows1 = norm_rows(totals, table, 1, me[0])
    field[...] = jnp.zeros_like(field)

    def chunk(index, carry):
        place = pl.ds(index * step, step)
        i1.ready(index)
        z1.ready(index)
        value = norm_delta(i1[place], z1[place], rows1, back, 1, mask).astype(BF16).astype(F32)
        field[pl.ds(1 + index * size.band, size.band), 1 : side + 1] = value.reshape(size.band, side, frames, LANES)
        return carry

    unrolled(size.chunks, chunk, 0)

    def line(row, carry):
        pooled[pl.ds(row * side, side)] = pool_line(size, field, row, mask)
        return carry

    unrolled(side, line, 0)

    for chunk_index in range(size.chunks):
        i0.ready(chunk_index)
        z0.ready(chunk_index)
    for part, out in enumerate(outs):

        def one(cell, cells, lanes, out=out):
            place = pl.ds(cell, cells)
            value = norm_delta(i0[place], z0[place], rows0, back, 0, mask)
            out[0:DENSE, lanes] = turn(size, value, cells)[:DENSE].astype(BF16)
            out[DENSE:ROWS, lanes] = turn(size, pooled[place], cells)[:POOL].astype(BF16)

        part_blocks(size, part, one, (out,))


def weight_grad_kernel(size, me, *refs):
    count = len(size.parts)
    deltas, pieces, (out, grads, flat) = refs[:count], refs[count : 5 * count], refs[5 * count :]
    for position in range(4):
        owner = me[0] ^ position
        value = jnp.zeros((ROWS, QUARTER), F32)
        for part in range(count):
            x = pieces[4 * part + position]
            x.ready(0)
            value += dot(deltas[part][...], x[...], ((1,), (1,)))
        grads[owner, 0] = value[:, :LANES]
        rest = value[:, LANES:]
        grads[owner, 1] = jnp.concatenate([rest, jnp.zeros((ROWS, 2 * LANES - QUARTER), F32)], 1)
    parts = []
    for extra in range(2):
        rows = pl.ds(extra, ROWS // 2, stride=2)
        for owner in range(4):
            parts.append(jnp.concatenate([grads[owner, 0, rows, :], grads[owner, 1, rows, :]], 1))
    for place, tile in enumerate(pack_rows(parts)):
        flat[pl.ds(place, ROWS // 2, stride=PAIR_TILES), :] = tile
    used = ROWS // 2 * PAIR_TILES
    flat[used:, :] = jnp.zeros((DENSE_ROWS - used, LANES), F32)
    out[...] = flat[...].astype(BF16)


def input_rows(size, part, pieces, weights, block, scratch):
    for index, (start, width, _, _) in enumerate(size.columns_of(part)):
        value = jnp.zeros((width, 2 * LANES), F32)
        for weight, piece in zip(weights, pieces):
            piece.ready(index)
            value += dot(piece[:, start : start + width], weight[block], ((0,), (0,)))
        scratch[0, start : start + width, :] = value[:, :LANES]
        scratch[1, start : start + width, :] = value[:, LANES:]


def input_half_kernel(size, d0, d1, d2, d3, w0, w1, w2, w3, first, second, third, scratch):
    input_rows(size, 0, (d0, d1, d2, d3), (w0, w1, w2, w3), 1, scratch)
    value = jnp.concatenate([scratch[0, : size.rows, :], scratch[1, : size.rows, :]], 1)
    parts = separate(value * 0.125)
    for ref, part in zip((first, second, third), parts):
        ref[...] = part.reshape(ref.shape)


def input_kernel(size, part, *refs):
    side, frames = size.side, size.frames
    pairs_of = frames // 8
    pieces, weights, (out, scratch) = refs[:4], refs[4:8], refs[-2:]
    input_rows(size, part, pieces, weights, 0, scratch)
    first, count = size.parts[part]
    for index in range(count):
        start = index * side * frames
        lines = [strided(scratch, start + frame, pairs_of * side, 8) for frame in range(8)]
        cell = (first + index) * side
        for place, tile in enumerate(pack_rows(lines)):
            out[cell : cell + side, :, place * LANES : (place + 1) * LANES] = tile.reshape(side, pairs_of, LANES)
        out.flush(index)


def pairs(axis_size, shift):
    return [(index, index ^ shift) for index in range(axis_size)]


def gather_four(piece):
    other = lax.ppermute(piece, "chan", pairs(4, 2))
    core = lax.ppermute(piece, "chan", pairs(4, 1))
    both = lax.ppermute(other, "chan", pairs(4, 1))
    return piece, core, other, both


def exchange_four(pieces):
    result = [pieces[0]]
    for shift in (1, 2, 3):
        result.append(lax.ppermute(pieces[shift], "chan", pairs(4, shift)))
    return result


def share(stat):
    return lax.all_to_all(stat, "dp", 0, 0, tiled=True)


def share_all(stat, count):
    return lax.all_to_all(stat, ("dp", "chan"), 0, 0, tiled=True).reshape(count, 4, 8, LANES)


def summed_share(parts, count):
    rows = sum(part.shape[0] for part in parts)
    unit = count * 16
    total = -(-rows // unit) * unit
    if total > rows:
        parts = [*parts, jnp.zeros((total - rows, LANES), BF16)]
    whole = jnp.concatenate(parts, 0).reshape(count, total // count, LANES)
    return jnp.sum(lax.all_to_all(whole, "dp", 0, 0, tiled=True).astype(F32), 0).astype(BF16)


def all_shares(mine, count):
    whole = jnp.broadcast_to(mine[None], (count,) + mine.shape)
    return lax.all_to_all(whole, "dp", 0, 0, tiled=True).reshape(-1, LANES)


def together(*values):
    return lax.optimization_barrier(values)


def as_rows(flat):
    return flat.reshape(2, -1, LANES).transpose(1, 0, 2).reshape(-1, LANES)


def as_flat(rows):
    return rows.reshape(-1, 2, LANES).transpose(1, 0, 2).reshape(2, -1)


NORM_LANES = (
    (0, REDUCED, PLAIN, 0),
    (0, 0, MID, 64),
    (2, 0, WIDE, 104),
    (0, MID, SMALL, 184),
    (2, WIDE, NARROW, 192),
    (1, 0, POOL, 224),
)


def shifted_lanes(value, source, width, target):
    lane = lax.broadcasted_iota(jnp.int32, value.shape, 1)
    value = jnp.where((lane >= source) & (lane < source + width), value, 0.0)
    return pltpu.roll(value, (target - source) % value.shape[1], 1)


def mask_rows(length0, length1, frames, stride):
    frame = lax.broadcasted_iota(jnp.int32, (frames, LANES), 0)
    ends = (length0, length0 + length1)

    def ident(step):
        place = (frame + step) * stride
        return jnp.where(place >= ends[0], 1, 0) + jnp.where(place >= ends[1], 1, 0)

    here = ident(0)
    valid = jnp.where(frame * stride < ends[1], 1.0, 0.0)
    before = jnp.where((frame > 0) & (ident(-1) == here), 1.0, 0.0)
    after = jnp.where((frame < frames - 1) & (ident(1) == here), 1.0, 0.0)
    return valid, before, after


def prepare_kernel(me, lengths, plain, mid, small, pool, wide, narrow, gains, shifts, *refs):
    outs, (rows, dense, taps) = refs[:-3], refs[-3:]
    mask0, mask1, tables, sent, weights, kernels = outs[0], outs[1], outs[2:6], outs[6:10], outs[10:12], outs[12:14]
    turned, along = outs[14:16], outs[16:18]
    for ref, frames, stride in ((along[0], mask0.shape[1], 1), (along[1], mask1.shape[1], 2)):
        lane = lax.broadcasted_iota(jnp.int32, (8, LANES), 1)
        ref[...] = jnp.where(lax.rem(lane, frames) * stride < lengths[0] + lengths[1], 1.0, 0.0)
    for mask, stride in ((mask0, 1), (mask1, 2)):
        for index, value in enumerate(mask_rows(lengths[0], lengths[1], mask.shape[1], stride)):
            mask[index] = value
    for block in range(2):
        lines = []
        for source in (gains, shifts):
            value = source[...].astype(F32)
            line = jnp.concatenate([value[block : block + 1], value[block + 2 : block + 3]], 1)
            lines.append(jnp.broadcast_to(line, (8, 2 * LANES)))
        found = [[jnp.zeros((8, LANES), F32)] * 2 for _ in range(3)]
        for tile, lane, width, channel in NORM_LANES:
            for index, line in enumerate(lines):
                part = shifted_lanes(line, channel, width, lane)[:, :LANES]
                found[tile][index] = found[tile][index] + part
        tables[2 * block][...] = row_table([found[0][0], found[0][1], found[1][0], found[1][1]])
        tables[2 * block + 1][...] = row_table([found[2][0], found[2][1]])
    for ref, base, outputs in ((mid, 0, MID), (small, MID, SMALL), (plain, REDUCED, PLAIN), (pool, DENSE, POOL)):
        count = ref.shape[0]
        rows[:count, :] = ref[...].astype(F32)
        for block in range(2):
            tiles = [rows[pl.ds(2 * tile + block, outputs // 2, stride=2 * PAIR_TILES), :] for tile in range(PAIR_TILES)]
            line = jnp.concatenate(tiles, 1)
            for extra in range(2):
                place = pl.ds(base + extra, outputs // 2, stride=2)
                for owner in range(4):
                    part = unpack_rows(line, 4 * extra + owner)
                    dense[block, owner, 0, place, :] = part[:, :LANES]
                    dense[block, owner, 1, place, :] = part[:, LANES:]
    lane = lax.broadcasted_iota(jnp.int32, (ROWS, LANES), 1)
    blank = jnp.zeros((LANES, 2 * LANES), F32)
    for block in range(2):
        for owner in range(4):
            rest = jnp.where(lane < QUARTER - LANES, dense[block, owner, 1], 0.0)
            dense[block, owner, 1] = rest
            value = jnp.concatenate([dense[block, owner, 0], rest], 1)
            value = jnp.concatenate([value[:DENSE], blank[: LANES - DENSE], value[DENSE:], blank[: LANES - POOL]], 0)
            weights[block][owner] = value.T[:QUARTER].astype(BF16)
        for position in range(4):
            owner = me[0] ^ position
            value = jnp.concatenate([dense[block, owner, 0], dense[block, owner, 1]], 1)
            sent[position][block] = value.astype(BF16)
    wide_lane = lax.broadcasted_iota(jnp.int32, (WIDE // 4, LANES), 1)
    narrow_lane = lax.broadcasted_iota(jnp.int32, (NARROW // 4, LANES), 1)
    start = 4 * MID - LANES
    for block in range(2):
        rows[: wide.shape[0], :] = wide[...].astype(F32)
        taps[...] = jnp.zeros_like(taps)
        tiles = [rows[pl.ds(2 * tile + block, WIDE // 4, stride=2 * MID_TILES), :] for tile in range(MID_TILES)]
        tiles.append(tiles[0])
        for extra in range(4):
            for tap in range(9):
                offset = (extra * 9 + tap) * 4 * MID
                first, shift = offset // LANES, offset % LANES
                count = -(-(shift + 4 * MID) // LANES)
                value = jnp.concatenate(tiles[first : first + count], 1)
                value = pltpu.roll(value, (count * LANES - shift) % (count * LANES), 1)
                place = pl.ds(extra, WIDE // 4, stride=4)
                taps[tap, 0, place, :] = value[:, :LANES]
                taps[tap, 1, place, :] = jnp.where(wide_lane < start, value[:, LANES : 2 * LANES], 0.0)
        rows[: narrow.shape[0], :] = narrow[...].astype(F32)
        tiles = [rows[pl.ds(2 * tile + block, NARROW // 4, stride=2 * SMALL_TILES), :] for tile in range(SMALL_TILES)]
        for extra in range(4):
            for tap in range(9):
                offset = (extra * 9 + tap) * 4 * SMALL
                value = pltpu.roll(tiles[offset // LANES], (start - offset) % LANES, 1)
                value = jnp.where((narrow_lane >= start) & (narrow_lane < start + 4 * SMALL), value, 0.0)
                taps[tap, 1, pl.ds(WIDE + extra, NARROW // 4, stride=4), :] = value
        for tap in range(9):
            first, second = taps[tap, 0], taps[tap, 1]
            kernels[block][tap] = jnp.concatenate([first, second], 1)[:, : 4 * REDUCED].astype(BF16)
            turned[block][tap, :LANES] = first.T.astype(BF16)
            turned[block][tap, LANES:] = second.T[: 4 * REDUCED - LANES].astype(BF16)


def place_rows(out, sources, count, pairs_rows):
    target = pairs_rows if out.shape[0] == 2 else out.near
    for block, (ref, start) in enumerate(sources):
        target[pl.ds(block, count, stride=2), :] = ref[start : start + count, :]
    if out.shape[0] == 2:
        for index in range(count // 4):
            value = pairs_rows[index * 8 : index * 8 + 8, :]
            for part in range(4):
                place = index * 4 + part
                out[:, place * LANES : (place + 1) * LANES] = value[2 * part : 2 * part + 2]


def finish_kernels_kernel(early, wide, narrow, rows, pairs_rows):
    rows[...] = early[...].astype(F32)
    other = KERNEL_ROWS + DENSE_ROWS
    place_rows(wide, ((rows, other), (rows, 0)), MID_ROWS, pairs_rows)
    place_rows(narrow, ((rows, other + MID_ROWS), (rows, MID_ROWS)), SMALL_ROWS, pairs_rows)


def finish_kernel(early, late, first0, first1, second0, second1, *refs):
    outs, (rows, other, pairs_rows) = refs[:-3], refs[-3:]
    mid, small, plain, pool, gains, shifts = outs
    rows[...] = early[...].astype(F32)
    other[...] = late[...].astype(F32)
    start = 0
    for out, outputs in ((mid, MID), (small, SMALL), (plain, PLAIN), (pool, POOL)):
        count = outputs * CIN // LANES
        place_rows(out, ((other, start), (rows, KERNEL_ROWS + start)), count, pairs_rows)
        start += count
    for block, first_ref, second_ref in ((0, first0, second0), (1, first1, second1)):
        first = jnp.sum(first_ref[...], 0)
        second = jnp.sum(second_ref[...], 0)
        for out, row in ((gains, 1), (shifts, 0)):
            lines = (first[row : row + 1], first[row + 2 : row + 3], second[row : row + 1])
            total = jnp.zeros((8, 2 * LANES), F32)
            for tile, lane, width, channel in NORM_LANES:
                line = jnp.concatenate([lines[tile], jnp.zeros((1, LANES), F32)], 1)
                total += shifted_lanes(jnp.broadcast_to(line, (8, 2 * LANES)), lane, width, channel)
            out[block : block + 1, :] = total[0:1, :LANES]
            out[block + 2 : block + 3, :] = total[0:1, LANES:]


def project_last(size, me, pieces, dense, mask, table, everyone, before=()):
    side, cells, frames = size.side, size.cells, size.frames
    tile = shaped((cells, frames, LANES))
    last = len(size.parts) - 1
    outs = [tile, tile, shaped((everyone, 8, LANES)), shaped((REDUCED, size.padded), BF16)]
    scratch = [pltpu.VMEM((side + 2, side + 2, frames, LANES), F32)]
    ins = {index: column_parts(size, last) for index in range(4)}
    aliases = {}
    if before:
        first, count = size.cells_of(0)
        ins[7], ins[8] = (0, [(0, count)]), (0, [(0, count)])
        aliases = {7: 0}
    else:
        scratch.append(pltpu.VMEM((cells, frames, LANES), F32))
    z0_parts = (0, [(first, cells) for _, _, first, cells in size.columns_of(last)])
    return call(
        functools.partial(project_kernel, size),
        outs,
        scratch,
        [me],
        [*pieces, dense, mask, table, *before],
        flops=2 * size.rows * CIN * 256,
        ins=ins,
        puts={0: z0_parts, 1: line_parts(size)},
        aliases=aliases,
    )


def project_before(size, me, pieces, dense):
    tile = shaped((size.cells, size.frames, LANES))
    return call(
        functools.partial(project_first_kernel, size),
        [tile, tile, shaped((2, size.frames, LANES))],
        [],
        [me],
        [*pieces, dense],
        flops=size.rows * CIN * 256,
        ins={index: column_parts(size, 0) for index in range(4)},
        puts={
            0: (0, [(first, cells) for _, _, first, cells in size.columns_of(0)]),
            1: (0, [(0, size.cells_of(0)[1])]),
        },
    )


def forward_second(size, me, group, pieces, totals, along, kernel, mask, count):
    side, frames = size.side, size.frames
    field, z2, stat = call(
        functools.partial(conv_kernel, size),
        [
            shaped((side + 2, side + 2, frames, 4 * REDUCED), size.kept),
            shaped((size.cells, frames, LANES)),
            shaped((count, 8, LANES)),
        ],
        [pltpu.VMEM((4 * REDUCED, size.padded), F32)],
        [me, group],
        [*pieces, totals, along, kernel, mask],
        flops=2 * size.rows * 9 * 256 * 256,
        ins={6: (0, [(0, 9)])},
        puts={0: (0, [(0, side + 2)]), 1: cell_parts(size)},
    )
    return field, z2, share(stat)


def hop(piece, shift):
    return lax.ppermute(piece, "chan", pairs(4, shift))


def backward(size, me, grads, saved, weights_at, count, early=None):
    z0, z1, totals, field, z2, totals2, table, table2, mask, kernel, pieces = saved
    g0, g2, g1 = grads
    side, frames = size.side, size.frames
    spreads = early is not None
    spread_rows = [pltpu.VMEM((size.rows // 4, LANES), F32)]
    tile = shaped((size.cells, frames, LANES))
    (stat,) = call(
        functools.partial(second_sums_kernel, size),
        [shaped((count, 8, LANES))],
        spread_rows if spreads else [],
        [],
        [g2, z2, totals2, table2, mask],
        flops=size.rows * LANES * 30,
        ins={1: cell_parts(size)},
    )
    back2 = share(stat)
    wire = shaped((REDUCED, size.padded), BF16)
    delta2, o0, o1, o2, o3 = call(
        functools.partial(conv_back_kernel, size),
        [shaped((size.cells, frames, LANES), size.kept), wire, wire, wire, wire],
        [
            pltpu.VMEM((side + 2, side + 2, frames, LANES), size.kept),
            pltpu.VMEM((size.cells, frames, 4 * REDUCED), F32),
            pltpu.VMEM((4 * REDUCED, size.padded), F32),
        ]
        + (spread_rows if spreads else []),
        [me],
        [g2, z2, totals2, back2, table2, mask, kernel],
        flops=2 * size.rows * 9 * 256 * 256,
        ins={1: cell_parts(size), 6: (0, [(0, 9)])},
        puts={0: cell_parts(size)},
    )
    partial = exchange_four([o0, o1, o2, o3])
    (kernel_grad,) = call(
        functools.partial(kernel_grad_kernel, size),
        [shaped((KERNEL_ROWS, LANES), BF16)],
        [
            pltpu.VMEM((9, 2 * LANES, 4 * REDUCED), F32),
            pltpu.VMEM((9, 2, LANES, LANES), F32),
            pltpu.VMEM((KERNEL_ROWS, LANES), F32),
        ],
        [],
        [field, delta2, mask],
        flops=2 * size.rows * 9 * 256 * 256,
        ins={0: (0, even(side + 2, side + 2)), 1: cell_parts(size)},
    )
    partial[2], kernel_grad = together(partial[2], kernel_grad)
    i0, i1, stat = call(
        functools.partial(first_sums_kernel, size),
        [tile, tile, shaped((count, 8, LANES))],
        [pltpu.VMEM((size.cells, frames, LANES), F32)] + (spread_rows * 2 if spreads else []),
        [me],
        [*partial, g0, g1, z0, z1, totals, table, mask],
        flops=size.rows * LANES * 60,
        ins={6: cell_parts(size), 7: cell_parts(size)},
        puts={0: cell_parts(size), 1: cell_parts(size)},
    )
    back1 = share(stat)
    if spreads:
        mine = summed_share([*early, kernel_grad], count)
        back1, mine = together(back1, mine)
    deltas = call(
        functools.partial(first_delta_kernel, size),
        [shaped((ROWS, size.lanes(part)), BF16) for part in range(len(size.parts))],
        [
            pltpu.VMEM((side + 2, side + 2, frames, LANES), F32),
            pltpu.VMEM((size.cells, frames, LANES), F32),
        ],
        [me],
        [z0, z1, i0, i1, totals, back1, table, mask],
        flops=size.rows * LANES * 60,
        ins={index: cell_parts(size) for index in range(4)},
        puts={part: block_parts(size, part) for part in range(len(size.parts))},
    )
    others = [hop(delta, 2) for delta in deltas]
    cores = [hop(delta, 1) for delta in deltas]
    cores, own = together(cores, deltas)
    flat_pieces = [piece for part in pieces for piece in part]
    (dense_grad,) = call(
        functools.partial(weight_grad_kernel, size),
        [shaped((DENSE_ROWS, LANES), BF16)],
        [pltpu.VMEM((4, 2, ROWS, LANES), F32), pltpu.VMEM((DENSE_ROWS, LANES), F32)],
        [me],
        [*own, *flat_pieces],
        flops=2 * size.rows * CIN * 256,
        ins={len(own) + index: (0, [(0, QUARTER)]) for index in range(len(flat_pieces))},
    )
    others[0], dense_grad = together(others[0], dense_grad)

    def input_call(part, body, outs, other, extra=(), puts=None):
        lanes = size.lanes(part)
        return call(
            body,
            outs,
            [pltpu.VMEM((2, lanes, LANES), F32)],
            [],
            [deltas[part], cores[part], other, hop(other, 1), *weights_at, *extra],
            flops=2 * size.rows * 4 * ROWS * 256,
            ins={index: column_parts(size, part) for index in range(4)} | ({8: (0, [])} if extra else {}),
            puts=puts,
            aliases={8: 0} if extra else None,
        )

    if not spreads:
        result = input_call(0, functools.partial(input_half_kernel, size), [tile, tile, tile], others[0])
        return result, [kernel_grad, dense_grad], back1, back2
    late = summed_share([dense_grad], count)
    early = all_shares(mine, count)
    shape = shaped((size.cells, frames // 8, 8 * QUARTER))
    result = ()
    for part in range(len(size.parts)):
        if part:
            others[part], late, result = together(others[part], late, result)
            late = all_shares(late, count)
        body = functools.partial(input_kernel, size, part)
        result = input_call(part, body, [shape], others[part], result, {0: line_parts(size, part)})
    return result, (early, late), back1, back2


def on_device(count, clips, clip_len, w_plain, w_mid, k_mid, w_small, k_small, w_pool, gains, shifts, grad_out):
    big = Size(clips.shape[1], 8 * clips.shape[0])
    low = Size(grad_out.shape[1], 8 * grad_out.shape[0])
    me = lax.axis_index("chan").astype(jnp.int32).reshape(1)
    group = lax.axis_index("dp").astype(jnp.int32).reshape(1)
    everyone = 4 * count
    raw = clips.transpose(1, 2, 0, 3).reshape(big.cells, clips.shape[0], 8 * QUARTER)
    pieces = []
    for part in range(len(big.parts)):
        (own,) = call(
            functools.partial(unpack_kernel, big, part),
            [shaped((QUARTER, big.lanes(part)), BF16)],
            [pltpu.VMEM((2, big.parts[part][1] * big.side * big.frames, LANES), F32)],
            [],
            [raw],
            ins={0: line_parts(big, part)},
            puts={0: block_parts(big, part)},
        )
        pieces.append([own, hop(own, 1), hop(own, 2)])
    low_tile = shaped((low.cells, low.frames, LANES))
    grads = call(
        functools.partial(grad_kernel, low),
        [low_tile, low_tile, low_tile],
        [pltpu.VMEM((2, low.rows, LANES), F32)],
        [],
        [grad_out],
    )
    table = shaped((8, LANES))
    prepared = call(
        prepare_kernel,
        [shaped((3, big.frames, LANES)), shaped((3, low.frames, LANES))]
        + [table] * 4
        + [shaped((2, ROWS, 2 * LANES), BF16)] * 4
        + [shaped((4, QUARTER, 2 * LANES), BF16)] * 2
        + [shaped((9, LANES, 4 * REDUCED), BF16)] * 2
        + [shaped((9, 4 * REDUCED, LANES), BF16)] * 2
        + [table] * 2,
        [
            pltpu.VMEM((2 * MID_ROWS, LANES), F32),
            pltpu.VMEM((2, 4, 2, ROWS, LANES), F32),
            pltpu.VMEM((9, 2, LANES, LANES), F32),
        ],
        [me, clip_len],
        [as_rows(item) for item in (w_plain, w_mid, w_small, w_pool, k_mid, k_small, gains, shifts)],
    )
    pieces[0][2], prepared, grads = together(pieces[0][2], prepared, grads)
    mask, mask_low, table0, second0, table1, second1 = prepared[:6]
    sent, (dense0, dense1), (kernel0, kernel1), (turned0, turned1), (along, along_low) = (
        prepared[6:10],
        prepared[10:12],
        prepared[12:14],
        prepared[14:16],
        prepared[16:18],
    )
    pieces[0].append(hop(pieces[0][2], 1))
    before = project_before(big, me, pieces[0], dense0)
    pieces[1][2], before = together(pieces[1][2], before)
    pieces[1].append(hop(pieces[1][2], 1))
    z0, z1, stat, wire = project_last(big, me, pieces[1], dense0, mask, table0, everyone, before)
    mids = exchange_four([wire] * 4)
    totals = share_all(stat, count)
    half = [pltpu.VMEM((big.rows // 4, LANES), F32)]
    h0, h1 = call(
        functools.partial(first_half_kernel, big),
        [low_tile, low_tile],
        half * 2,
        [me],
        [z0, z1, totals, table0, mask],
        flops=big.rows * 2 * LANES * 20,
        ins={0: cell_parts(big), 1: cell_parts(big)},
    )
    field, z2, totals2 = forward_second(big, me, group, mids, totals, along, turned0, mask, count)
    weights_at = exchange_four(sent)
    totals2, weights_at = together(totals2, weights_at)
    (own1,) = call(
        functools.partial(second_half_kernel, big),
        [shaped((QUARTER, low.padded), BF16)],
        half,
        [],
        [z2, totals2, second0, mask, h0, h1],
        flops=big.rows * LANES * 20,
        ins={0: cell_parts(big)},
    )
    saved0 = (z0, z1, totals, field, z2, totals2, table0, second0, mask, kernel0, pieces)

    pieces1 = gather_four(own1)
    z0, z1, stat, wire = project_last(low, me, pieces1, dense1, mask_low, table1, everyone)
    mids = exchange_four([wire] * 4)
    totals = share_all(stat, count)
    field, z2, totals2 = forward_second(low, me, group, mids, totals, along_low, turned1, mask_low, count)
    (mixed,) = call(
        functools.partial(output_kernel, low),
        [shaped(grad_out.shape, BF16)],
        [pltpu.VMEM((2, low.rows, LANES), F32)],
        [me],
        [z0, z1, z2, totals, totals2, table1, second1, mask_low],
        flops=low.rows * 3 * LANES * 20,
    )
    saved1 = (z0, z1, totals, field, z2, totals2, table1, second1, mask_low, kernel1, [pieces1])
    grads, grads1, first1, last1 = backward(low, me, grads, saved1, weights_at, count)
    (clips_grad,), (early, late), first0, last0 = backward(big, me, grads, saved0, weights_at, count, grads1)

    def sized(outputs):
        rows = outputs * CIN // 64
        return shaped((rows, LANES) if rows % 16 == 0 else (2, rows * 64))

    pairs_rows = pltpu.VMEM((2 * MID_ROWS, LANES), F32)
    wide, narrow = call(
        finish_kernels_kernel,
        [shaped((2, MID_ROWS * LANES)), shaped((2 * SMALL_ROWS, LANES))],
        [pltpu.VMEM(early.shape, F32), pairs_rows],
        [],
        [early],
    )
    mid, small, plain, pool, gains_grad, shifts_grad = call(
        finish_kernel,
        [sized(outputs) for outputs in (MID, SMALL, PLAIN, POOL)] + [shaped((4, LANES))] * 2,
        [pltpu.VMEM(early.shape, F32), pltpu.VMEM(late.shape, F32), pairs_rows],
        [],
        [early, late, first0, first1, last0, last1],
    )
    flats = [plain, mid, wide, small, narrow, pool, gains_grad, shifts_grad]
    flats = [item if item.shape[0] == 2 else as_flat(item) for item in flats]
    shape = (big.side, big.side, big.frames // 8, 8 * QUARTER)
    return mixed, clips_grad.reshape(shape).transpose(2, 0, 1, 3), *flats


def solution(mesh):
    frames = P("dp", None, None, "chan")
    flat = P(None, "chan")
    return jax.shard_map(
        functools.partial(on_device, mesh.shape["dp"]),
        mesh=mesh,
        in_specs=(frames, P("dp")) + (flat,) * 8 + (frames,),
        out_specs=(frames, frames) + (flat,) * 8,
        check_vma=False,
    )
```

```python
import functools

import jax
import jax.numpy as jnp
from jax import lax
from jax.experimental import pallas as pl
from jax.experimental.pallas import tpu as pltpu
from jax.sharding import PartitionSpec as P

CIN = 832
QUARTER = 208
WIDE, NARROW = 80, 32
MID, SMALL, PLAIN, POOL = 40, 8, 64, 32
REDUCED = MID + SMALL
DENSE = REDUCED + PLAIN
ROWS = DENSE + POOL
CLIPS = 2
EPSILON = 1e-05
F32 = jnp.float32
BF16 = jnp.bfloat16
LANES = 128
LIMIT = 62
COST = 1
MID_TILES = 4 * 9 * 160 // LANES
MID_ROWS = WIDE // 4 * MID_TILES
SMALL_TILES = 4 * 9 * 32 // LANES
SMALL_ROWS = NARROW // 4 * SMALL_TILES
KERNEL_ROWS = 976
PAIR_TILES = 2 * CIN // LANES
DENSE_ROWS = 944


class Size:
    def __init__(self, side, frames):
        self.side = side
        self.frames = frames
        self.cells = side * side
        self.rows = self.cells * frames
        self.padded = -(-self.rows // LANES) * LANES
        self.band = 2 if side % 2 == 0 else side
        self.chunks = side // self.band
        self.step = self.band * side
        self.group = LANES // frames
        self.full = self.cells // self.group
        self.rest = self.cells - self.full * self.group
        self.kept = BF16 if frames % 16 == 0 else F32
        self.whole = (0, self.padded)
        first = 13 * LANES
        self.parts = [(0, first), (first, self.padded - first)] if self.padded > 2 * first - LANES - 1 else [self.whole]

    def cells_of(self, span):
        first = span[0] // self.frames
        return first, min(span[1] // self.frames, self.cells - first)

    def columns_of(self, span, width=640):
        first, count = self.cells_of(span)
        result = []
        for start in range(0, span[1], width):
            skipped, held = start // self.frames, min(width, span[1] - start)
            result.append((start, held, first + skipped, min(held // self.frames, count - skipped)))
        return result


class Stream:
    def __init__(self, far, near, sems, axis, parts):
        self.far, self.near, self.sems, self.axis, self.parts = far, near, sems, axis, parts
        self.shape, self.dtype = near.shape, near.dtype

    def copy(self, part, inward):
        index = (slice(None),) * self.axis + (pl.ds(*self.parts[part]),)
        pair = (self.far.at[index], self.near.at[index])
        return pltpu.make_async_copy(*(pair if inward else pair[::-1]), self.sems.at[part])

    def ready(self, part):
        self.copy(part, True).wait()

    def flush(self, part):
        self.copy(part, False).start()

    def __getitem__(self, index):
        return self.near[index]

    def __setitem__(self, index, value):
        self.near[index] = value

    @property
    def at(self):
        return self.near.at


def even(total, count):
    return [(start * (total // count), total // count) for start in range(count)]


def cell_parts(size):
    return 0, even(size.cells, size.chunks)


def line_parts(size, first=0, count=None):
    return 0, [(row * size.side, size.side) for row in range(first, first + (count or size.side))]


def column_parts(size, span, width=640):
    return 1, [(start, held) for start, held, _, _ in size.columns_of(span, width)]


def call(body, outs, scratch, scalars, args, flops=0, ins=None, puts=None, aliases=None, stacks=()):
    ins, puts = ins or {}, puts or {}
    places = {}
    for stack, members in enumerate(stacks):
        start = 0
        for index in members:
            places[index] = (stack, start)
            start += args[index].shape[0]
    aliases = {len(scalars) + index: out for index, out in (aliases or {}).items()}
    plans = [ins.get(index) for index in range(len(args))] + [puts.get(index) for index in range(len(outs))]
    arrays = list(args) + list(outs)
    buffers = []
    for index, (array, plan) in enumerate(zip(arrays, plans)):
        if index not in places:
            buffers.append(pltpu.VMEM(array.shape, array.dtype))
        buffers.append(pltpu.SemaphoreType.DMA((max(len(plan[1]), 1) if plan else 1,)))
    for members in stacks:
        rows = sum(args[index].shape[0] for index in members)
        buffers.append(pltpu.VMEM((rows,) + args[members[0]].shape[1:], args[members[0]].dtype))

    def wrapped(*refs):
        numbers, refs = refs[: len(scalars)], refs[len(scalars) :]
        far, refs = refs[: len(arrays)], refs[len(arrays) :]
        own, refs = refs[: len(scratch)], list(refs[len(scratch) :])
        whole = refs[len(refs) - len(stacks) :]
        streams = []
        for index, plan in enumerate(plans):
            axis, parts = plan or (0, [(0, arrays[index].shape[0])])
            if index in places:
                stack, start = places[index]
                near = whole[stack].at[pl.ds(start, arrays[index].shape[0])]
            else:
                near = refs.pop(0)
            streams.append(Stream(far[index], near, refs.pop(0), axis, parts))
        entering, leaving = streams[: len(args)], streams[len(args) :]
        for part in range(max([len(stream.parts) for stream in entering])):
            for stream in entering:
                if part < len(stream.parts):
                    stream.copy(part, True).start()
        for index, stream in enumerate(entering):
            if index not in ins:
                stream.ready(0)
        body(*numbers, *entering, *leaving, *own, *whole)
        for index, stream in enumerate(leaving):
            if index not in puts:
                stream.flush(0)
        for stream in leaving:
            for part in range(len(stream.parts)):
                stream.copy(part, False).wait()

    moved = sum(array.size * array.dtype.itemsize for array in arrays)
    return pl.pallas_call(
        wrapped,
        out_shape=outs,
        in_specs=[pl.BlockSpec(memory_space=pltpu.SMEM)] * len(scalars) + [pl.BlockSpec(memory_space=pl.ANY)] * len(args),
        out_specs=[pl.BlockSpec(memory_space=pl.ANY)] * len(outs),
        scratch_shapes=list(scratch) + buffers,
        compiler_params=pltpu.CompilerParams(vmem_limit_bytes=LIMIT * 1024 * 1024),
        cost_estimate=pl.CostEstimate(flops=COST, bytes_accessed=COST, transcendentals=0),
        input_output_aliases=aliases,
    )(*scalars, *args)


def unrolled(count, body, carry):
    for index in range(count):
        carry = body(index, carry)
    return carry


def shaped(shape, dtype=F32):
    return jax.ShapeDtypeStruct(shape, dtype)


def sigmoid(value):
    return 0.5 * jnp.tanh(0.5 * value) + 0.5


def row_table(rows):
    index = lax.broadcasted_iota(jnp.int32, (8, LANES), 0)
    table = jnp.zeros((8, LANES), F32)
    for position, row in enumerate(rows):
        table = jnp.where(index == position, row, table)
    return table


def time_box(value, mask_ref):
    cells, frames, width = value.shape
    flat = value.reshape(cells * frames, width)
    before = pltpu.roll(flat, 1, 0).reshape(value.shape)
    after = pltpu.roll(flat, cells * frames - 1, 0).reshape(value.shape)
    return value + before * mask_ref[1] + after * mask_ref[2]


def owner_rows(all_ref, owner):
    if len(all_ref.shape) == 3:
        return all_ref[...]
    return all_ref[:, pl.ds(owner, 1)].reshape(all_ref.shape[0], 8, LANES)


def norm_rows(all_ref, table_ref, tile, owner=0):
    total = jnp.sum(owner_rows(all_ref, owner), 0)
    count = total[4:5]
    mean = total[2 * tile : 2 * tile + 1] / count
    variance = total[2 * tile + 1 : 2 * tile + 2] / count - mean * mean
    inverse = lax.rsqrt(variance + EPSILON)
    gain = table_ref[2 * tile : 2 * tile + 1]
    shift = table_ref[2 * tile + 1 : 2 * tile + 2]
    return mean, inverse, gain, shift, count


def activate(value, rows, mask_ref):
    mean, inverse, gain, shift, _ = rows
    shifted = gain * ((value - mean) * inverse) + shift
    return shifted * sigmoid(shifted) * mask_ref[0]


def inner_grad(grad, value, rows, mask_ref):
    mean, inverse, gain, shift, _ = rows
    normed = (value - mean) * inverse
    shifted = gain * normed + shift
    sigma = sigmoid(shifted)
    return grad * mask_ref[0] * sigma * (1.0 + shifted * (1.0 - sigma)), normed


def norm_delta(inner, value, rows, back_ref, tile, mask_ref):
    mean, inverse, gain, _, count = rows
    total = jnp.sum(back_ref[...], 0)
    shift_grad = total[2 * tile : 2 * tile + 1] / count
    gain_grad = total[2 * tile + 1 : 2 * tile + 2] / count
    normed = (value - mean) * inverse
    return (gain * inverse) * (inner - mask_ref[0] * (shift_grad + normed * gain_grad))


def publish(stat_ref, rows):
    stat_ref[...] = jnp.broadcast_to(row_table(rows)[None], stat_ref.shape)


def collapse(value):
    return jnp.sum(value, 0, keepdims=True)


def windows():
    result = []
    for frame in range(8):
        start = frame * QUARTER
        first, offset = start // LANES, start % LANES
        result.append((first, -(-(offset + QUARTER) // LANES), offset))
    return result


def unpack_rows(line, frame):
    first, tiles, offset = windows()[frame]
    value = line[:, first * LANES : (first + tiles) * LANES]
    if offset:
        value = pltpu.roll(value, tiles * LANES - offset, 1)
    return value[:, : 2 * LANES]


def pack_rows(parts):
    tiles = [None] * 13
    for frame, value in enumerate(parts):
        first, count, offset = windows()[frame]
        if count == 3:
            value = jnp.concatenate([value, jnp.zeros((value.shape[0], LANES), value.dtype)], 1)
        if offset:
            value = pltpu.roll(value, offset, 1)
        for index in range(count):
            piece = value[:, index * LANES : (index + 1) * LANES]
            place = first + index
            tiles[place] = piece if tiles[place] is None else tiles[place] + piece
    return tiles


def assemble(first, second, third):
    blank = jnp.zeros_like(first)
    lane = lax.broadcasted_iota(jnp.int32, (first.shape[0], 2 * LANES), 1)
    plain = pltpu.roll(jnp.concatenate([first, blank], 1), 2 * LANES - REDUCED, 1)
    middle = pltpu.roll(jnp.concatenate([second, blank], 1), PLAIN, 1)
    pool = pltpu.roll(jnp.concatenate([third, blank], 1), PLAIN + WIDE + NARROW, 1)
    return jnp.where(lane < PLAIN, plain, 0.0) + middle + pool


def separate(value):
    lane = lax.broadcasted_iota(jnp.int32, (value.shape[0], LANES), 1)
    plain = pltpu.roll(value, REDUCED, 1)[:, :LANES]
    middle = pltpu.roll(value, 2 * LANES - PLAIN, 1)[:, :LANES]
    pool = pltpu.roll(value, 2 * LANES - PLAIN - WIDE - NARROW, 1)[:, :LANES]
    first = jnp.where((lane >= REDUCED) & (lane < DENSE), plain, 0.0)
    second = jnp.where(lane < WIDE + NARROW, middle, 0.0)
    third = jnp.where(lane < POOL, pool, 0.0)
    return first, second, third


def span_blocks(size, span, one, leaving=()):
    blocks_of = size.columns_of(span, LANES)
    for index, (start, _, first, cells) in enumerate(blocks_of):
        one(first, cells, slice(start, start + LANES))
        if index % 4 == 3 or index == len(blocks_of) - 1:
            for stream in leaving:
                stream.flush(index // 4)


def span_parts(size, span):
    return column_parts(size, span, 4 * LANES)


def unpack_kernel(size, raw, out, scratch):
    side, frames = size.side, size.frames
    pairs_of = frames // 8
    for row in range(side):
        raw.ready(row)
        value = raw[row * side : (row + 1) * side].astype(F32).reshape(pairs_of * side, 8 * QUARTER)
        for frame in range(8):
            place = pl.ds(row * side * frames + frame, pairs_of * side, stride=8)
            piece = unpack_rows(value, frame)
            scratch[0, place, :] = piece[:, :LANES]
            scratch[1, place, :] = piece[:, LANES:]

    def one(cell, cells, lanes):
        start = cell * frames
        for tile, (low, high) in enumerate(((0, LANES), (LANES, QUARTER))):
            value = scratch[tile, start : start + cells * frames, :].reshape(cells, frames, LANES)
            out[low:high, lanes] = turn(size, value, cells)[: high - low].astype(BF16)

    span_blocks(size, size.whole, one, (out,))


def grad_kernel(size, raw, first, second, third, scratch):
    side, frames = size.side, size.frames

    def line(row, carry):
        value = raw[0, row].astype(F32)
        for frame in range(8):
            place = pl.ds(row * side * frames + frame, side, stride=frames)
            part = unpack_rows(value, frame)
            scratch[0, place, :] = part[:, :LANES]
            scratch[1, place, :] = part[:, LANES:]
        return carry

    unrolled(side, line, 0)
    parts = separate(jnp.concatenate([scratch[0], scratch[1]], 1))
    for ref, part in zip((first, second, third), parts):
        ref[...] = part.reshape(ref.shape)


def dot(left, right, dims=((1,), (0,))):
    return lax.dot_general(left, right, (dims, ((), ())), preferred_element_type=F32)


def into_padded(size, flat, field):
    side = size.side
    field[...] = jnp.zeros_like(field)

    def line(row, carry):
        field[row + 1, 1 : side + 1] = flat[pl.ds(row * side, side)]
        return carry

    unrolled(side, line, 0)


def stacked_weights(me, positions, w_ref, stacked):
    for index, position in enumerate(positions):
        stacked[index * QUARTER : (index + 1) * QUARTER] = w_ref[me[0] ^ position]


def project_begin_kernel(size, me, x0, x1, w_ref, dense, pool, stacked, stack):
    frames = size.frames
    stacked_weights(me, (0, 1), w_ref, stacked)
    for index, (start, width, first, cells) in enumerate(size.columns_of(size.whole)):
        for x in (x0, x1):
            x.ready(index)
        value = dot(stack[:, start : start + width], stacked[...], ((0,), (0,)))
        value = value.reshape(width // frames, frames, 2 * LANES)[:cells]
        dense[first : first + cells] = value[:, :, :LANES]
        pool[first : first + cells] = value[:, :, LANES:]
        dense.flush(index)
        pool.flush(index)


def project_kernel(size, positions, me, *refs):
    side, frames = size.side, size.frames
    pieces, (w_ref, mask, table), refs = refs[: len(positions)], refs[len(positions) : len(positions) + 3], refs[len(positions) + 3 :]
    begun = refs[:2] if len(positions) < 4 else None
    z0, z1, stat, wire, field, flat, stacked, stack = refs[-8:]
    stacked_weights(me, positions, w_ref, stacked)
    blank = jnp.zeros((frames, LANES), F32)
    total, squares = blank, blank
    for index, (start, width, first, cells) in enumerate(size.columns_of(size.whole)):
        for x in pieces:
            x.ready(index)
        value = dot(stack[:, start : start + width], stacked[...], ((0,), (0,)))
        value = value.reshape(width // frames, frames, 2 * LANES)[:cells]
        dense, pool = value[:, :, :LANES], value[:, :, LANES:]
        if begun:
            for stream in begun:
                stream.ready(index)
            dense += begun[0][first : first + cells]
            pool += begun[1][first : first + cells]
        z0[first : first + cells] = dense
        z0.flush(index)
        flat[first : first + cells] = pool
        total += jnp.sum(dense, 0)
        squares += jnp.sum(dense * dense, 0)
    valid = mask[0]
    total, squares = collapse(total * valid), collapse(squares * valid)
    count = collapse(valid) * size.cells
    mean = total / count

    def one(cell, cells, lanes):
        wire[:, lanes] = turn(size, z0[cell : cell + cells] - mean, cells)[:REDUCED].astype(BF16)

    span_blocks(size, size.whole, one)
    into_padded(size, flat, field)
    pool_total, pool_squares = blank, blank
    for row in range(side):
        pool = pool_line(size, field, row, mask)
        z1[row * side : (row + 1) * side] = pool
        z1.flush(row)
        pool_total += jnp.sum(pool, 0)
        pool_squares += jnp.sum(pool * pool, 0)
    rows = [total, squares, collapse(pool_total * valid), collapse(pool_squares * valid), count]
    publish(stat, rows + [table[0:1], table[1:2]])


def normed_kernel(size, me, z0, z1, totals, table, mask, *refs):
    outs, (field, pooled) = refs[:-2], refs[-2:]
    side, frames, step = size.side, size.frames, size.step
    lane = lax.broadcasted_iota(jnp.int32, (frames, LANES), 1)
    field[...] = jnp.zeros_like(field)
    rows = [norm_rows(totals, table, tile, me[0]) for tile in range(2)]
    scales = [(gain * inverse * inverse, mean) for mean, inverse, gain, _, _ in rows]
    for index in range(size.chunks):
        z1.ready(index)
        scale, mean = scales[1]
        value = (z1[index * step : (index + 1) * step] - mean) * scale
        value = jnp.where(lane == POOL, 1.0, value) * mask[0]
        field[1 + index * size.band : 1 + (index + 1) * size.band, 1 : side + 1] = value.reshape(size.band, side, frames, LANES)
    for row in range(side):
        pooled[row * side : (row + 1) * side] = pool_line(size, field, row, mask)
    for index in range(size.chunks):
        z0.ready(index)
    for part, span in enumerate(size.parts):
        normed, shapes = outs[2 * part : 2 * part + 2]

        def one(cell, cells, lanes, normed=normed, shapes=shapes):
            scale, mean = scales[0]
            value = (z0[cell : cell + cells] - mean) * scale
            dense = turn(size, jnp.where(lane == DENSE, 1.0, value) * mask[0], cells)
            pool = turn(size, pooled[cell : cell + cells], cells)
            normed[0:DENSE, lanes] = dense[:DENSE].astype(BF16)
            normed[DENSE:ROWS, lanes] = pool[:POOL].astype(BF16)
            both = jnp.concatenate([dense[DENSE : DENSE + 8], pool[POOL : POOL + 8]], 0)
            shapes[:, lanes] = both.astype(BF16)

        span_blocks(size, span, one, (normed,))


def moments_kernel(size, me, *refs):
    (out, stack), pieces = refs[-2:], refs[-6:-2]
    lefts = refs[:-6]
    each = len(lefts) // len(size.parts)
    lefts = [lefts[part * each : (part + 1) * each] for part in range(len(size.parts))]
    lefts = [group[0][...] if each == 1 else jnp.concatenate([item[...] for item in group], 0) for group in lefts]
    value = jnp.zeros((4 * QUARTER, lefts[0].shape[0]), F32)
    for part, (left, (start, count)) in enumerate(zip(lefts, size.parts)):
        for x in pieces:
            x.ready(part)
        value += dot(stack[:, start : start + count], left, ((1,), (1,)))
    for position in range(4):
        piece = value[position * QUARTER : (position + 1) * QUARTER]
        piece = jnp.concatenate([piece, jnp.zeros((2 * LANES - QUARTER, piece.shape[1]), F32)], 0)
        out[me[0] ^ position] = piece.T


def back_columns(back, owner):
    every = owner_rows(back, owner)
    total, own = jnp.sum(every, 0), every[0]
    count = own[6:7]
    rows = [total[1:2] / count, total[3:4] / count, own[4:5] * total[0:1] / count, own[5:6] * total[2:3] / count]
    turned = row_table(rows).T
    slope = jnp.concatenate([turned[:DENSE, 0:1], turned[:POOL, 1:2]], 0)
    offset = jnp.concatenate([turned[:DENSE, 2:3], turned[:POOL, 3:4]], 0)
    return slope, offset


def weight_grad_kernel(size, me, inner, moments, back, kernels, out, grads, flat):
    slope, offset = back_columns(back, me[0])
    for owner in range(4):
        shape = moments[owner, ROWS : ROWS + 16]
        value = inner[owner] - slope * moments[owner, 0:ROWS]
        first = value[:DENSE] - offset[:DENSE] * shape[0:1]
        last = value[DENSE:] - offset[DENSE:] * shape[8:9]
        value = jnp.concatenate([first, last], 0)
        grads[owner, 0] = value[:, :LANES]
        grads[owner, 1] = value[:, LANES:]
    parts = []
    for extra in range(2):
        rows = pl.ds(extra, ROWS // 2, stride=2)
        for owner in range(4):
            parts.append(jnp.concatenate([grads[owner, 0, rows, :], grads[owner, 1, rows, :]], 1))
    for place, tile in enumerate(pack_rows(parts)):
        flat[pl.ds(place, ROWS // 2, stride=PAIR_TILES), :] = tile
    used = ROWS // 2 * PAIR_TILES
    flat[used:, :] = jnp.zeros((DENSE_ROWS - used, LANES), F32)
    out[:KERNEL_ROWS, :] = kernels[...]
    out[KERNEL_ROWS : KERNEL_ROWS + DENSE_ROWS, :] = flat[...].astype(BF16)
    rest = out.shape[0] - KERNEL_ROWS - DENSE_ROWS
    if rest:
        out[KERNEL_ROWS + DENSE_ROWS :, :] = jnp.zeros((rest, LANES), BF16)


def pool_line(size, field, row, mask):
    side = size.side
    lines = field[pl.ds(row, 3)]
    column = lines[0] + lines[1] + lines[2]
    value = column[0:side] + column[1 : side + 1] + column[2 : side + 2]
    return time_box(value, mask) * (1.0 / 27.0)


def block_bounds(size):
    bounds, last = [], 0
    for part in range(size.chunks):
        until = size.full if part == size.chunks - 1 else (part + 1) * size.step // size.group
        bounds.append((last, until))
        last = until
    return bounds


def wire_parts(size):
    parts = [(low * LANES, (high - low) * LANES) for low, high in block_bounds(size)]
    if size.rest:
        parts[-1] = (parts[-1][0], parts[-1][1] + LANES)
    return 1, parts


def blocks(size, one, entering=(), leaving=()):
    for part, (low, high) in enumerate(block_bounds(size)):
        for stream in entering:
            stream.ready(part)
        for block in range(low, high):
            one(block, size.group)
        if size.rest and part == size.chunks - 1:
            one(size.full, size.rest)
        for stream in leaving:
            stream.flush(part)


def turn(size, value, cells):
    flat = value.reshape(cells * size.frames, value.shape[-1])
    if cells < size.group:
        blank = jnp.zeros((LANES - cells * size.frames, value.shape[-1]), value.dtype)
        flat = jnp.concatenate([flat, blank], 0)
    return flat.T


def lanes_of(block):
    if isinstance(block, int):
        return pl.ds(block * LANES, LANES)
    return pl.ds(pl.multiple_of(block * LANES, LANES), LANES)


def conv_kernel(size, me, group, p0, p1, p2, p3, totals, lanes_valid, kernel, mask, field, z2, stat, joined):
    side, frames, step = size.side, size.frames, size.step
    for position, piece in enumerate((p0, p1, p2, p3)):
        owner = me[0] ^ position
        every = owner_rows(totals, owner)
        total = jnp.sum(every, 0)
        sent = totals[pl.ds(group[0], 1), pl.ds(owner, 1)].reshape(8, LANES)
        mean = total[0:1] / total[4:5]
        variance = total[1:2] / total[4:5] - mean * mean
        scale = sent[5:6] * lax.rsqrt(variance + EPSILON)
        offset = (sent[0:1] / sent[4:5] - mean) * scale + sent[6:7]
        turned = row_table([scale, offset]).T
        scale, offset = turned[:REDUCED, 0:1], turned[:REDUCED, 1:2]
        shifted = piece[...].astype(F32) * scale + offset
        value = shifted * sigmoid(shifted)
        joined[pl.ds(pl.multiple_of(owner * MID, 8), MID), :] = value[:MID]
        joined[pl.ds(pl.multiple_of(4 * MID + owner * SMALL, 8), SMALL), :] = value[MID:]
    field[...] = jnp.zeros_like(field)
    joined[4 * REDUCED :, :] = jnp.zeros((2 * LANES - 4 * REDUCED, size.padded), F32)

    def one(block, cells):
        value = (joined[:, lanes_of(block)] * lanes_valid[0:1]).T
        value = value.reshape(size.group, frames, 2 * LANES).astype(size.kept)
        for index in range(cells):
            cell = block * size.group + index
            row = cell // side if isinstance(cell, int) else lax.div(cell, side)
            field[row + 1, cell - row * side + 1] = value[index]

    blocks(size, one)
    field.flush(0)
    kernel.ready(0)
    blank = jnp.zeros((frames, LANES), F32)

    def chunk(index, carry):
        total, squares = carry
        parts = []
        for row in range(3):
            for column in range(3):
                part = field[pl.ds(index * size.band + row, size.band), column : column + side]
                parts.append(part.reshape(step * frames, 2 * LANES).astype(BF16))
        value = dot(jnp.concatenate(parts, 1), kernel[...].reshape(18 * LANES, LANES))
        value = time_box(value.reshape(step, frames, LANES), mask) * (1.0 / 3.0)
        z2[pl.ds(index * step, step)] = value
        z2.flush(index)
        return total + jnp.sum(value, 0), squares + jnp.sum(value * value, 0)

    total, squares = unrolled(size.chunks, chunk, (blank, blank))
    valid = mask[0]
    one_row = jnp.zeros((1, LANES), F32)
    rows = [collapse(total * valid), collapse(squares * valid), one_row, one_row, collapse(valid) * size.cells]
    publish(stat, rows)


def halve_into(size, value, scratch, index):
    half = size.side // 2
    value = value.reshape(2, half, 2, size.frames, LANES)
    value = value[0] + value[1]
    value = value[:, 0] + value[:, 1]
    rows = half * size.frames
    scratch[pl.ds(index * rows, rows), :] = value.reshape(rows, LANES)


def halved_rows(scratch):
    count = scratch.shape[0] // 2
    return (scratch[pl.ds(0, count, stride=2), :] + scratch[pl.ds(1, count, stride=2), :]) * 0.125


def first_half_kernel(size, me, z0, z1, totals, table, mask, h0, h1, s0, s1):
    for tile, (z, out, scratch) in enumerate(((z0, h0, s0), (z1, h1, s1))):
        rows = norm_rows(totals, table, tile, me[0])

        def chunk(index, carry, z=z, scratch=scratch, rows=rows):
            z.ready(index)
            value = activate(z[pl.ds(index * size.step, size.step)], rows, mask)
            halve_into(size, value, scratch, index)
            return carry

        unrolled(size.chunks, chunk, 0)
        out[...] = halved_rows(scratch).reshape(out.shape)


def second_half_kernel(size, z2, totals, table, mask, h0, h1, out, scratch):
    rows = norm_rows(totals, table, 0)

    def chunk(index, carry):
        z2.ready(index)
        value = activate(z2[pl.ds(index * size.step, size.step)], rows, mask)
        halve_into(size, value, scratch, index)
        return carry

    unrolled(size.chunks, chunk, 0)
    value = halved_rows(scratch)
    count = value.shape[0]
    value = assemble(h0[...].reshape(count, LANES), value, h1[...].reshape(count, LANES))
    value = jnp.concatenate([value, jnp.zeros((out.shape[1] - count, 2 * LANES), F32)], 0)
    out[...] = value.T[:QUARTER].astype(BF16)


def strided(scratch, start, count, stride):
    place = pl.ds(start, count, stride=stride)
    return jnp.concatenate([scratch[0, place, :], scratch[1, place, :]], 1)


def output_kernel(size, me, z0, z1, z2, totals, totals2, table, table2, mask, out, scratch):
    side, frames = size.side, size.frames
    parts = [
        activate(z[...], norm_rows(total, tab, tile, me[0]), mask).reshape(size.rows, LANES)
        for z, total, tab, tile in ((z0, totals, table, 0), (z2, totals2, table2, 0), (z1, totals, table, 1))
    ]
    value = assemble(*parts)
    scratch[0] = value[:, :LANES]
    scratch[1] = value[:, LANES:]

    def line(row, carry):
        start = row * side * frames
        lines = [strided(scratch, start + frame, side, frames) for frame in range(8)]
        for place, tile in enumerate(pack_rows(lines)):
            out[0, row, :, place * LANES : (place + 1) * LANES] = tile.astype(BF16)
        return carry

    unrolled(side, line, 0)


def spread(size, grad, scratch):
    value = grad[...].reshape(-1, LANES)
    count = value.shape[0]
    scratch[pl.ds(0, count, stride=2), :] = value
    scratch[pl.ds(1, count, stride=2), :] = value


def grad_chunk(size, grad, scratch, index):
    if scratch is None:
        return grad[pl.ds(index * size.step, size.step)]
    half = size.side // 2
    rows = half * size.frames
    value = scratch[pl.ds(index * rows, rows), :].reshape(half, 1, size.frames, LANES)
    value = jnp.broadcast_to(value, (half, 2, size.frames, LANES)).reshape(1, size.side, size.frames, LANES)
    value = jnp.broadcast_to(value, (2, size.side, size.frames, LANES))
    return value.reshape(size.step, size.frames, LANES)


def second_sums_kernel(size, grad, z2, totals, table, mask, stat, *scratch):
    scratch = scratch[0] if scratch else None
    if scratch is not None:
        spread(size, grad, scratch)
    rows = norm_rows(totals, table, 0)
    blank = jnp.zeros((size.frames, LANES), F32)

    def chunk(index, carry):
        shift_grad, gain_grad = carry
        z2.ready(index)
        value = z2[pl.ds(index * size.step, size.step)]
        inner, normed = inner_grad(grad_chunk(size, grad, scratch, index), value, rows, mask)
        return shift_grad + jnp.sum(inner, 0), gain_grad + jnp.sum(inner * normed, 0)

    shift_grad, gain_grad = unrolled(size.chunks, chunk, (blank, blank))
    publish(stat, [collapse(shift_grad), collapse(gain_grad)])


def conv_back_kernel(size, me, grad, z2, totals, back, table, mask, kernel, delta, o0, o1, o2, field, result, turned, *scratch):
    side, frames, step = size.side, size.frames, size.step
    scratch = scratch[0] if scratch else None
    if scratch is not None:
        spread(size, grad, scratch)
    rows = norm_rows(totals, table, 0)
    field[...] = jnp.zeros_like(field)

    def first(index, carry):
        z2.ready(index)
        value = z2[pl.ds(index * step, step)]
        inner, _ = inner_grad(grad_chunk(size, grad, scratch, index), value, rows, mask)
        value = norm_delta(inner, value, rows, back, 0, mask).astype(BF16).astype(size.kept)
        delta[pl.ds(index * step, step)] = value
        delta.flush(index)
        field[pl.ds(1 + index * size.band, size.band), 1 : side + 1] = value.reshape(size.band, side, frames, LANES)
        return carry

    unrolled(size.chunks, first, 0)
    kernel.ready(0)

    def chunk(index, carry):
        parts = []
        for row in range(3):
            for column in range(3):
                part = field[pl.ds(index * size.band + 2 - row, size.band), 2 - column : 2 - column + side]
                parts.append(part.reshape(step * frames, LANES).astype(BF16))
        value = dot(jnp.concatenate(parts, 1), kernel[...].reshape(9 * LANES, 4 * REDUCED))
        result[pl.ds(index * step, step)] = value.reshape(step, frames, 4 * REDUCED)
        return carry

    unrolled(size.chunks, chunk, 0)

    def one(block, cells):
        value = turn(size, result[pl.ds(block * size.group, cells)], cells)
        turned[:, lanes_of(block)] = value

    blocks(size, one)
    for position, (out, start) in enumerate(((o0, 0), (o1, 0), (o2, 0), (o2, REDUCED))):
        owner = me[0] ^ position
        mid = turned[pl.ds(pl.multiple_of(owner * MID, 8), MID), :]
        small = turned[pl.ds(pl.multiple_of(4 * MID + owner * SMALL, 8), SMALL), :]
        out[start : start + REDUCED] = jnp.concatenate([mid, small], 0).astype(BF16)


def kernel_grad_kernel(size, field, delta, mask, out, turned, boxed, taps, flat):
    side, frames, step = size.side, size.frames, size.step
    for index in range(size.chunks):
        delta.ready(index)
        place = slice(index * step, (index + 1) * step)
        boxed[place] = time_box(delta[place].astype(F32), mask)
    for start, _, first, cells in size.columns_of(size.whole, LANES):
        value = turn(size, boxed[first : first + cells], cells)
        upper = value.astype(BF16)
        turned[:LANES, start : start + LANES] = upper
        turned[LANES:, start : start + LANES] = (value - upper.astype(F32)).astype(BF16)
    left = turned[:, : size.rows]
    for row in range(side + 2):
        field.ready(row)
    for row in range(3):
        for column in range(3):
            part = field[row : row + side, column : column + side].reshape(size.rows, 2 * LANES).astype(BF16)
            value = dot(left, part)
            value = (value[:LANES] + value[LANES:]) * (1.0 / 3.0)
            taps[3 * row + column, 0] = value[:, :LANES]
            taps[3 * row + column, 1] = value[:, LANES:]
    lane = lax.broadcasted_iota(jnp.int32, (WIDE // 4, LANES), 1)
    tiles = [None] * MID_TILES

    def add(place, value):
        tiles[place] = value if tiles[place] is None else tiles[place] + value

    for extra in range(4):
        for tap in range(9):
            rows = pl.ds(extra, WIDE // 4, stride=4)
            rest = jnp.where(lane < 4 * MID - LANES, taps[tap, 1, rows, :], 0.0)
            offset = (extra * 9 + tap) * 4 * MID
            value = jnp.concatenate([taps[tap, 0, rows, :], rest, jnp.zeros_like(rest)], 1)
            value = pltpu.roll(value, offset % LANES, 1)
            for index in range(-(-(offset % LANES + 4 * MID) // LANES)):
                add(offset // LANES + index, value[:, index * LANES : (index + 1) * LANES])
    for place, tile in enumerate(tiles):
        flat[pl.ds(place, WIDE // 4, stride=MID_TILES), :] = tile
    lane = lax.broadcasted_iota(jnp.int32, (NARROW // 4, LANES), 1)
    tiles = [None] * SMALL_TILES
    start = 4 * MID - LANES
    for extra in range(4):
        for tap in range(9):
            value = taps[tap, 1, pl.ds(WIDE + extra, NARROW // 4, stride=4), :]
            value = jnp.where((lane >= start) & (lane < start + 4 * SMALL), value, 0.0)
            offset = (extra * 9 + tap) * 4 * SMALL
            value = pltpu.roll(value, (offset - start) % LANES, 1)
            add(offset // LANES, value)
    for place, tile in enumerate(tiles):
        flat[pl.ds(MID_ROWS + place, NARROW // 4, stride=SMALL_TILES), :] = tile
    flat[MID_ROWS + SMALL_ROWS :, :] = jnp.zeros((KERNEL_ROWS - MID_ROWS - SMALL_ROWS, LANES), F32)
    out[...] = flat[...].astype(BF16)


def first_sums_kernel(size, me, p0, p1, p2, p3, g0, g1, z0, z1, totals, table, mask, *refs):
    side, step, frames = size.side, size.step, size.frames
    count = len(size.parts)
    stat, outs, (field, padded, pooled, *scratch) = refs[0], refs[1 : 1 + count], refs[1 + count :]
    s0, s1 = scratch if scratch else (None, None)
    if scratch:
        spread(size, g0, s0)
        spread(size, g1, s1)
    padded[...] = jnp.zeros_like(padded)

    def one(block, cells):
        place = lanes_of(block)
        value = p0[:, place].astype(F32) + p1[:, place].astype(F32)
        value += p2[:REDUCED, place].astype(F32) + p3[REDUCED:, place].astype(F32)
        value = jnp.concatenate([value, jnp.zeros((LANES - REDUCED, LANES), F32)], 0).T
        value = value.reshape(size.group, frames, LANES)
        field[pl.ds(block * size.group, cells)] = value[:cells]

    blocks(size, one)
    rows0 = norm_rows(totals, table, 0, me[0])
    rows1 = norm_rows(totals, table, 1, me[0])
    blank = jnp.zeros((frames, LANES), F32)

    def chunk(index, carry):
        place = pl.ds(index * step, step)
        z0.ready(index)
        z1.ready(index)
        grad = time_box(field[place], mask) * (1.0 / 3.0) + grad_chunk(size, g0, s0, index)
        inner0, normed0 = inner_grad(grad, z0[place], rows0, mask)
        inner1, normed1 = inner_grad(grad_chunk(size, g1, s1, index), z1[place], rows1, mask)
        field[place] = scales[0] * inner0
        pool = scales[1] * inner1
        padded[1 + index * size.band : 1 + (index + 1) * size.band, 1 : side + 1] = pool.reshape(size.band, side, frames, LANES)
        sums = (inner0, inner0 * normed0, inner1, inner1 * normed1)
        return tuple(old + jnp.sum(new, 0) for old, new in zip(carry, sums))

    scales = [rows[2] * rows[1] for rows in (rows0, rows1)]
    sums = unrolled(size.chunks, chunk, (blank,) * 4)
    publish(stat, [collapse(item) for item in sums] + scales + [rows0[4]])
    stat.flush(0)
    for row in range(side):
        pooled[row * side : (row + 1) * side] = pool_line(size, padded, row, mask)
    for out, span in zip(outs, size.parts):

        def turned(cell, cells, lanes, out=out):
            out[0:DENSE, lanes] = turn(size, field[cell : cell + cells], cells)[:DENSE].astype(BF16)
            out[DENSE:ROWS, lanes] = turn(size, pooled[cell : cell + cells], cells)[:POOL].astype(BF16)

        span_blocks(size, span, turned, (out,))


def input_rows(size, me, groups, weights, block, back, scratch, stacked):
    flat_row, pool_row = jnp.zeros((1, 2 * LANES), F32), jnp.zeros((1, 2 * LANES), F32)
    for position, weight in enumerate(weights):
        slope, offset = back_columns(back, me[0] ^ position)
        stacked[position * ROWS : (position + 1) * ROWS] = weight[block]
        value = weight[block].astype(F32)
        stacked[(position + 4) * ROWS : (position + 5) * ROWS] = (value * -slope).astype(BF16)
        value = value * offset
        flat_row -= collapse(value[:DENSE])
        pool_row -= collapse(value[DENSE:])
    index = lax.broadcasted_iota(jnp.int32, (16, 2 * LANES), 0)
    fixed = jnp.where(index == 0, flat_row, 0.0) + jnp.where(index == 8, pool_row, 0.0)
    stacked[8 * ROWS :] = fixed.astype(BF16)
    for streams, stack, columns in groups:
        for part, start, width, row in columns:
            for stream in streams:
                stream.ready(part)
            value = dot(stack[:, start : start + width], stacked[...], ((0,), (0,)))
            scratch[0, row : row + width, :] = value[:, :LANES]
            scratch[1, row : row + width, :] = value[:, LANES:]


def input_half_kernel(size, me, *refs):
    streams, weights, (back,) = refs[:9], refs[9:13], refs[13:14]
    first, second, third, scratch, stacked, stack = refs[14:]
    columns = [(part, start, width, start) for part, (start, width, _, _) in enumerate(size.columns_of(size.whole))]
    input_rows(size, me, [(streams, stack, columns)], weights, 1, back, scratch, stacked)
    value = jnp.concatenate([scratch[0, : size.rows, :], scratch[1, : size.rows, :]], 1)
    parts = separate(value * 0.125)
    for ref, part in zip((first, second, third), parts):
        ref[...] = part.reshape(ref.shape)


def input_plan(size, part):
    bounds = [0]
    for span in size.parts:
        first, count = size.cells_of(span)
        bounds.append((first + count) // size.side)
    low, high = bounds[part], bounds[part + 1]
    start = low * size.side * size.frames // LANES * LANES
    return low, high, start


def input_kernel(size, part, me, *refs):
    side, frames = size.side, size.frames
    pairs_of = frames // 8
    low, high, base = input_plan(size, part)
    own = 9 * (2 if part else 1)
    pieces, weights, back = refs[:own], refs[own : own + 4], refs[own + 4]
    out, scratch, stacked = refs[own + 5 + (1 if part else 0) :][:3]
    stacks = refs[own + 5 + (1 if part else 0) + 3 :]
    begin = size.parts[part][0]
    columns = [(index, start, width, begin + start - base) for index, (start, width, _, _) in enumerate(size.columns_of(size.parts[part]))]
    groups = [(pieces[:9], stacks[0], columns)]
    if part:
        tail = (0, base - size.parts[part - 1][0], begin - base, 0)
        groups.append((pieces[9:], stacks[1], [tail]))
    input_rows(size, me, groups, weights, 0, back, scratch, stacked)
    for index, row in enumerate(range(low, high)):
        start = row * side * frames - base
        lines = [strided(scratch, start + frame, pairs_of * side, 8) for frame in range(8)]
        cell = row * side
        for place, tile in enumerate(pack_rows(lines)):
            out[cell : cell + side, :, place * LANES : (place + 1) * LANES] = tile.reshape(side, pairs_of, LANES)
        out.flush(index)


def pairs(axis_size, shift):
    return [(index, index ^ shift) for index in range(axis_size)]


def gather_four(piece):
    other = lax.ppermute(piece, "chan", pairs(4, 2))
    core = lax.ppermute(piece, "chan", pairs(4, 1))
    both = lax.ppermute(other, "chan", pairs(4, 1))
    return piece, core, other, both


def exchange_four(pieces):
    result = [pieces[0]]
    for shift in (1, 2, 3):
        result.append(lax.ppermute(pieces[shift], "chan", pairs(4, shift)))
    return result


def share(stat):
    return lax.all_to_all(stat, "dp", 0, 0, tiled=True)


def share_all(stat, count):
    return lax.all_to_all(stat, ("dp", "chan"), 0, 0, tiled=True).reshape(count, 4, 8, LANES)


def swap_shares(rows, count):
    return lax.all_to_all(rows.reshape(count, -1, LANES), "dp", 0, 0, tiled=True)


def all_shares(swapped):
    mine = jnp.sum(swapped.astype(F32), 0).astype(BF16)
    whole = jnp.broadcast_to(mine[None], swapped.shape)
    return lax.all_to_all(whole, "dp", 0, 0, tiled=True).reshape(-1, LANES)


def together(*values):
    return lax.optimization_barrier(values)


def as_rows(flat):
    return flat.reshape(2, -1, LANES).transpose(1, 0, 2).reshape(-1, LANES)


def as_flat(rows):
    return rows.reshape(-1, 2, LANES).transpose(1, 0, 2).reshape(2, -1)


NORM_LANES = (
    (0, REDUCED, PLAIN, 0),
    (0, 0, MID, 64),
    (2, 0, WIDE, 104),
    (0, MID, SMALL, 184),
    (2, WIDE, NARROW, 192),
    (1, 0, POOL, 224),
)


def shifted_lanes(value, source, width, target):
    lane = lax.broadcasted_iota(jnp.int32, value.shape, 1)
    value = jnp.where((lane >= source) & (lane < source + width), value, 0.0)
    return pltpu.roll(value, (target - source) % value.shape[1], 1)


def mask_rows(length0, length1, frames, stride):
    frame = lax.broadcasted_iota(jnp.int32, (frames, LANES), 0)
    ends = (length0, length0 + length1)

    def ident(step):
        place = (frame + step) * stride
        return jnp.where(place >= ends[0], 1, 0) + jnp.where(place >= ends[1], 1, 0)

    here = ident(0)
    valid = jnp.where(frame * stride < ends[1], 1.0, 0.0)
    before = jnp.where((frame > 0) & (ident(-1) == here), 1.0, 0.0)
    after = jnp.where((frame < frames - 1) & (ident(1) == here), 1.0, 0.0)
    return valid, before, after


def prepare_kernel(me, lengths, plain, mid, small, pool, wide, narrow, gains, shifts, *refs):
    outs, (rows, dense, taps) = refs[:-3], refs[-3:]
    mask0, mask1, tables, sent, weights, kernels = outs[0], outs[1], outs[2:6], outs[6:10], outs[10:12], outs[12:14]
    turned, along = outs[14:16], outs[16:18]
    for ref, frames, stride in ((along[0], mask0.shape[1], 1), (along[1], mask1.shape[1], 2)):
        lane = lax.broadcasted_iota(jnp.int32, (8, LANES), 1)
        ref[...] = jnp.where(lax.rem(lane, frames) * stride < lengths[0] + lengths[1], 1.0, 0.0)
    for mask, stride in ((mask0, 1), (mask1, 2)):
        for index, value in enumerate(mask_rows(lengths[0], lengths[1], mask.shape[1], stride)):
            mask[index] = value
    for block in range(2):
        lines = []
        for source in (gains, shifts):
            value = source[...].astype(F32)
            line = jnp.concatenate([value[block : block + 1], value[block + 2 : block + 3]], 1)
            lines.append(jnp.broadcast_to(line, (8, 2 * LANES)))
        found = [[jnp.zeros((8, LANES), F32)] * 2 for _ in range(3)]
        for tile, lane, width, channel in NORM_LANES:
            for index, line in enumerate(lines):
                part = shifted_lanes(line, channel, width, lane)[:, :LANES]
                found[tile][index] = found[tile][index] + part
        tables[2 * block][...] = row_table([found[0][0], found[0][1], found[1][0], found[1][1]])
        tables[2 * block + 1][...] = row_table([found[2][0], found[2][1]])
    for ref, base, outputs in ((mid, 0, MID), (small, MID, SMALL), (plain, REDUCED, PLAIN), (pool, DENSE, POOL)):
        count = ref.shape[0]
        rows[:count, :] = ref[...].astype(F32)
        for block in range(2):
            tiles = [rows[pl.ds(2 * tile + block, outputs // 2, stride=2 * PAIR_TILES), :] for tile in range(PAIR_TILES)]
            line = jnp.concatenate(tiles, 1)
            for extra in range(2):
                place = pl.ds(base + extra, outputs // 2, stride=2)
                for owner in range(4):
                    part = unpack_rows(line, 4 * extra + owner)
                    dense[block, owner, 0, place, :] = part[:, :LANES]
                    dense[block, owner, 1, place, :] = part[:, LANES:]
    lane = lax.broadcasted_iota(jnp.int32, (ROWS, LANES), 1)
    blank = jnp.zeros((LANES, 2 * LANES), F32)
    for block in range(2):
        for owner in range(4):
            rest = jnp.where(lane < QUARTER - LANES, dense[block, owner, 1], 0.0)
            dense[block, owner, 1] = rest
            value = jnp.concatenate([dense[block, owner, 0], rest], 1)
            value = jnp.concatenate([value[:DENSE], blank[: LANES - DENSE], value[DENSE:], blank[: LANES - POOL]], 0)
            weights[block][owner] = value.T[:QUARTER].astype(BF16)
        for position in range(4):
            owner = me[0] ^ position
            value = jnp.concatenate([dense[block, owner, 0], dense[block, owner, 1]], 1)
            sent[position][block] = value.astype(BF16)
    wide_lane = lax.broadcasted_iota(jnp.int32, (WIDE // 4, LANES), 1)
    narrow_lane = lax.broadcasted_iota(jnp.int32, (NARROW // 4, LANES), 1)
    start = 4 * MID - LANES
    for block in range(2):
        rows[: wide.shape[0], :] = wide[...].astype(F32)
        taps[...] = jnp.zeros_like(taps)
        tiles = [rows[pl.ds(2 * tile + block, WIDE // 4, stride=2 * MID_TILES), :] for tile in range(MID_TILES)]
        tiles.append(tiles[0])
        for extra in range(4):
            for tap in range(9):
                offset = (extra * 9 + tap) * 4 * MID
                first, shift = offset // LANES, offset % LANES
                count = -(-(shift + 4 * MID) // LANES)
                value = jnp.concatenate(tiles[first : first + count], 1)
                value = pltpu.roll(value, (count * LANES - shift) % (count * LANES), 1)
                place = pl.ds(extra, WIDE // 4, stride=4)
                taps[tap, 0, place, :] = value[:, :LANES]
                taps[tap, 1, place, :] = jnp.where(wide_lane < start, value[:, LANES : 2 * LANES], 0.0)
        rows[: narrow.shape[0], :] = narrow[...].astype(F32)
        tiles = [rows[pl.ds(2 * tile + block, NARROW // 4, stride=2 * SMALL_TILES), :] for tile in range(SMALL_TILES)]
        for extra in range(4):
            for tap in range(9):
                offset = (extra * 9 + tap) * 4 * SMALL
                value = pltpu.roll(tiles[offset // LANES], (start - offset) % LANES, 1)
                value = jnp.where((narrow_lane >= start) & (narrow_lane < start + 4 * SMALL), value, 0.0)
                taps[tap, 1, pl.ds(WIDE + extra, NARROW // 4, stride=4), :] = value
        for tap in range(9):
            first, second = taps[tap, 0], taps[tap, 1]
            kernels[block][tap] = jnp.concatenate([first, second], 1)[:, : 4 * REDUCED].astype(BF16)
            turned[block][tap, :LANES] = first.T.astype(BF16)
            turned[block][tap, LANES:] = second.T.astype(BF16)


def place_rows(out, sources, count, pairs_rows):
    target = pairs_rows if out.shape[0] == 2 else out.near
    for block, (ref, start) in enumerate(sources):
        target[pl.ds(block, count, stride=2), :] = ref[start : start + count, :]
    if out.shape[0] == 2:
        for index in range(count // 4):
            value = pairs_rows[index * 8 : index * 8 + 8, :]
            for part in range(4):
                place = index * 4 + part
                out[:, place * LANES : (place + 1) * LANES] = value[2 * part : 2 * part + 2]


def finish_kernel(me, early, late, first0, first1, second0, second1, *refs):
    outs, (rows, other, pairs_rows) = refs[:-3], refs[-3:]
    mid, small, plain, pool, wide, narrow, gains, shifts = outs
    rows[...] = early[...].astype(F32)
    late.ready(0)
    other[...] = late[...].astype(F32)
    place_rows(wide, ((other, 0), (rows, 0)), MID_ROWS, pairs_rows)
    wide.flush(0)
    place_rows(narrow, ((other, MID_ROWS), (rows, MID_ROWS)), SMALL_ROWS, pairs_rows)
    start = KERNEL_ROWS
    for out, outputs in ((mid, MID), (small, SMALL), (plain, PLAIN), (pool, POOL)):
        count = outputs * CIN // LANES
        place_rows(out, ((other, start), (rows, start)), count, pairs_rows)
        start += count
    for block, first_ref, second_ref in ((0, first0, second0), (1, first1, second1)):
        first = jnp.sum(owner_rows(first_ref, me[0]), 0)
        second = jnp.sum(second_ref[...], 0)
        for out, row in ((gains, 1), (shifts, 0)):
            lines = (first[row : row + 1], first[row + 2 : row + 3], second[row : row + 1])
            total = jnp.zeros((8, 2 * LANES), F32)
            for tile, lane, width, channel in NORM_LANES:
                line = jnp.concatenate([lines[tile], jnp.zeros((1, LANES), F32)], 1)
                total += shifted_lanes(jnp.broadcast_to(line, (8, 2 * LANES)), lane, width, channel)
            out[block : block + 1, :] = total[0:1, :LANES]
            out[block + 2 : block + 3, :] = total[0:1, LANES:]


def project(size, me, pieces, positions, dense, mask, table, everyone, begun=()):
    side, cells, frames = size.side, size.cells, size.frames
    tile = shaped((cells, frames, LANES))
    count = len(positions)
    column_cells = (0, [(first, held) for _, _, first, held in size.columns_of(size.whole)])
    ins = {index: column_parts(size, size.whole) for index in range(count)}
    ins |= {count + 3 + index: column_cells for index in range(len(begun))}
    return call(
        functools.partial(project_kernel, size, positions),
        [tile, tile, shaped((everyone, 8, LANES)), shaped((REDUCED, size.padded), BF16)],
        [
            pltpu.VMEM((side + 2, side + 2, frames, LANES), F32),
            pltpu.VMEM((cells, frames, LANES), F32),
            pltpu.VMEM((count * QUARTER, 2 * LANES), BF16),
        ],
        [me],
        [*pieces, dense, mask, table, *begun],
        ins=ins,
        puts={0: column_cells, 1: line_parts(size)},
        stacks=[range(count)],
    )


def project_begin(size, me, pieces, dense):
    tile = shaped((size.cells, size.frames, LANES))
    column_cells = (0, [(first, held) for _, _, first, held in size.columns_of(size.whole)])
    return call(
        functools.partial(project_begin_kernel, size),
        [tile, tile],
        [pltpu.VMEM((2 * QUARTER, 2 * LANES), BF16)],
        [me],
        [*pieces, dense],
        ins={index: column_parts(size, size.whole) for index in range(2)},
        puts={0: column_cells, 1: column_cells},
        stacks=[range(2)],
    )


def normed_wires(size, me, z0, z1, totals, table, mask):
    outs, puts = [], {}
    for part, (_, lanes) in enumerate(size.parts):
        outs += [shaped((ROWS, lanes), BF16), shaped((16, lanes), BF16)]
        puts[2 * part] = span_parts(size, size.parts[part])
    wires = call(
        functools.partial(normed_kernel, size),
        outs,
        [
            pltpu.VMEM((size.side + 2, size.side + 2, size.frames, LANES), F32),
            pltpu.VMEM((size.cells, size.frames, LANES), F32),
        ],
        [me],
        [z0, z1, totals, table, mask],
        ins={0: cell_parts(size), 1: cell_parts(size)},
        puts=puts,
    )
    return wires[0::2], wires[1::2]


def moments(size, me, lefts, pieces):
    rows = sum(item.shape[0] for item in lefts[0])
    flat = [item for group in lefts for item in group]
    (result,) = call(
        functools.partial(moments_kernel, size),
        [shaped((4, rows, 2 * LANES))],
        [],
        [me],
        [*flat, *pieces],
        ins={len(flat) + index: (1, size.parts) for index in range(4)},
        stacks=[range(len(flat), len(flat) + 4)],
    )
    return result


def forward_second(size, me, group, pieces, totals, along, kernel, mask, count):
    side, frames = size.side, size.frames
    field, z2, stat = call(
        functools.partial(conv_kernel, size),
        [
            shaped((side + 2, side + 2, frames, 2 * LANES), size.kept),
            shaped((size.cells, frames, LANES)),
            shaped((count, 8, LANES)),
        ],
        [pltpu.VMEM((2 * LANES, size.padded), F32)],
        [me, group],
        [*pieces, totals, along, kernel, mask],
        flops=2 * size.rows * 9 * 256 * 256,
        ins={6: (0, [(0, 9)])},
        puts={0: (0, [(0, side + 2)]), 1: cell_parts(size)},
    )
    return field, z2, stat


def hop(piece, shift):
    return lax.ppermute(piece, "chan", pairs(4, shift))


def second_sums(size, grads, saved, count):
    z2, totals2, table2, mask = saved[4], saved[5], saved[7], saved[8]
    return call(
        functools.partial(second_sums_kernel, size),
        [shaped((count, 8, LANES))],
        spread_rows(size),
        [],
        [grads[1], z2, totals2, table2, mask],
        ins={1: cell_parts(size)},
    )


def spread_rows(size):
    return [pltpu.VMEM((size.rows // 4, LANES), F32)] if size.side % 2 == 0 else []


def weight_grad(size, me, inner, moment, back1, kernels, count):
    unit = count * 16
    total = -(-(KERNEL_ROWS + DENSE_ROWS) // unit) * unit
    (result,) = call(
        functools.partial(weight_grad_kernel, size),
        [shaped((total, LANES), BF16)],
        [pltpu.VMEM((4, 2, ROWS, LANES), F32), pltpu.VMEM((DENSE_ROWS, LANES), F32)],
        [me],
        [inner, moment, back1, kernels],
    )
    return result


def backward(size, me, grads, back2, saved, normed, weights_at, count, waiting=None, early=None, moment=None):
    z0, z1, totals, field, z2, totals2, table, table2, mask, kernel, pieces, _, shapes = saved
    g0, g2, g1 = grads
    side, frames = size.side, size.frames
    spreads = early is not None
    tile = shaped((size.cells, frames, LANES))
    wire = shaped((REDUCED, size.padded), BF16)
    delta2, o0, o1, o2 = call(
        functools.partial(conv_back_kernel, size),
        [shaped((size.cells, frames, LANES), size.kept), wire, wire, shaped((2 * REDUCED, size.padded), BF16)],
        [
            pltpu.VMEM((side + 2, side + 2, frames, LANES), size.kept),
            pltpu.VMEM((size.cells, frames, 4 * REDUCED), F32),
            pltpu.VMEM((4 * REDUCED, size.padded), F32),
        ]
        + spread_rows(size),
        [me],
        [g2, z2, totals2, back2, table2, mask, kernel],
        flops=2 * size.rows * 9 * 256 * 256,
        ins={1: cell_parts(size), 6: (0, [(0, 9)])},
        puts={0: cell_parts(size)},
    )
    partial = [o0, hop(o1, 1), hop(o2, 2)]
    (kernel_grad,) = call(
        functools.partial(kernel_grad_kernel, size),
        [shaped((KERNEL_ROWS, LANES), BF16)],
        [
            pltpu.VMEM((2 * LANES, size.padded), BF16),
            pltpu.VMEM((size.cells, frames, LANES), F32),
            pltpu.VMEM((9, 2, LANES, LANES), F32),
            pltpu.VMEM((KERNEL_ROWS, LANES), F32),
        ],
        [],
        [field, delta2, mask],
        flops=2 * size.rows * 9 * 256 * 256,
        ins={0: (0, even(side + 2, side + 2)), 1: cell_parts(size)},
    )
    if spreads:
        swapped = swap_shares(early, count)
        partial[2], kernel_grad, swapped = together(partial[2], kernel_grad, swapped)
    else:
        partial[2], kernel_grad = together(partial[2], kernel_grad)
    if not spreads:
        partial[1], waiting, normed = together(partial[1], waiting, normed)
    partial.append(hop(partial[2], 1))
    stat, *wires = call(
        functools.partial(first_sums_kernel, size),
        [shaped((4 * count, 8, LANES))] + [shaped((ROWS, lanes), BF16) for _, lanes in size.parts],
        [
            pltpu.VMEM((size.cells, frames, LANES), F32),
            pltpu.VMEM((side + 2, side + 2, frames, LANES), F32),
            pltpu.VMEM((size.cells, frames, LANES), F32),
        ]
        + spread_rows(size) * 2,
        [me],
        [*partial, g0, g1, z0, z1, totals, table, mask],
        ins={6: cell_parts(size), 7: cell_parts(size)},
        puts={0: (0, [(0, 4 * count)])} | {1 + part: span_parts(size, span) for part, span in enumerate(size.parts)},
    )
    others, cores = [hop(wire, 2) for wire in wires], [hop(wire, 1) for wire in wires]
    back1 = share_all(stat, count)
    inner = moments(size, me, [[wire] for wire in wires], pieces)
    if spreads:
        early = all_shares(swapped)
        stat, early = together(stat, early)
        back1 = share_all(stat, count)
        back1, inner, others[0] = together(back1, inner, others[0])
        dense_grad = weight_grad(size, me, inner, moment, back1, kernel_grad, count)
        swapped = swap_shares(dense_grad, count)
    else:
        back1, others[0] = together(back1, others[0])

    def four(part):
        return [wires[part], cores[part], others[part], hop(others[part], 1)]

    scratch = [pltpu.VMEM((2, size.parts[0][1] + LANES, LANES), F32), pltpu.VMEM((8 * ROWS + 16, 2 * LANES), BF16)]
    if not spreads:
        result = call(
            functools.partial(input_half_kernel, size),
            [tile, tile, tile],
            scratch,
            [me],
            [*four(0), *normed[0], shapes[0], *weights_at, back1],
            ins={index: column_parts(size, size.whole) for index in range(9)},
            stacks=[range(9)],
        )
        return result, inner, kernel_grad, back1
    shape = shaped((size.cells, frames // 8, 8 * QUARTER))
    result, sets = (), []
    for part, span in enumerate(size.parts):
        if part:
            others[part], swapped, result, early = together(others[part], swapped, result, early)
            late = all_shares(swapped)
        sets.append([*four(part), *normed[part], shapes[part]])
        low, high, base = input_plan(size, part)
        args = list(sets[part])
        ins = {index: column_parts(size, span) for index in range(9)}
        stacks = [range(9)]
        if part:
            before = size.parts[part - 1]
            tail = (1, [(base - before[0], span[0] - base)])
            ins |= {len(args) + index: tail for index in range(9)}
            stacks.append(range(9, 18))
            args += sets[part - 1]
        args += [*weights_at, back1]
        if part:
            ins[len(args)] = (0, [])
        result = call(
            functools.partial(input_kernel, size, part),
            [shape],
            scratch,
            [me],
            [*args, *result],
            ins=ins,
            puts={0: line_parts(size, low, high - low)},
            aliases={len(args): 0} if part else None,
            stacks=stacks,
        )
    return result, early, late, back1


def on_device(count, clips, clip_len, w_plain, w_mid, k_mid, w_small, k_small, w_pool, gains, shifts, grad_out):
    big = Size(clips.shape[1], 8 * clips.shape[0])
    low = Size(grad_out.shape[1], 8 * grad_out.shape[0])
    me = lax.axis_index("chan").astype(jnp.int32).reshape(1)
    group = lax.axis_index("dp").astype(jnp.int32).reshape(1)
    everyone = 4 * count
    raw = clips.transpose(1, 2, 0, 3).reshape(big.cells, clips.shape[0], 8 * QUARTER)
    (own,) = call(
        functools.partial(unpack_kernel, big),
        [shaped((QUARTER, big.padded), BF16)],
        [pltpu.VMEM((2, big.rows, LANES), F32)],
        [],
        [raw],
        ins={0: line_parts(big)},
        puts={0: span_parts(big, big.whole)},
    )
    other, core = hop(own, 2), hop(own, 1)
    low_tile = shaped((low.cells, low.frames, LANES))
    grads = call(
        functools.partial(grad_kernel, low),
        [low_tile, low_tile, low_tile],
        [pltpu.VMEM((2, low.rows, LANES), F32)],
        [],
        [grad_out],
    )
    table = shaped((8, LANES))
    prepared = call(
        prepare_kernel,
        [shaped((3, big.frames, LANES)), shaped((3, low.frames, LANES))]
        + [table] * 4
        + [shaped((2, ROWS, 2 * LANES), BF16)] * 4
        + [shaped((4, QUARTER, 2 * LANES), BF16)] * 2
        + [shaped((9, LANES, 4 * REDUCED), BF16)] * 2
        + [shaped((9, 2 * LANES, LANES), BF16)] * 2
        + [table] * 2,
        [
            pltpu.VMEM((2 * MID_ROWS, LANES), F32),
            pltpu.VMEM((2, 4, 2, ROWS, LANES), F32),
            pltpu.VMEM((9, 2, LANES, LANES), F32),
        ],
        [me, clip_len],
        [as_rows(item) for item in (w_plain, w_mid, w_small, w_pool, k_mid, k_small, gains, shifts)],
    )
    mask, mask_low, table0, second0, table1, second1 = prepared[:6]
    sent, (dense0, dense1), (kernel0, kernel1), (turned0, turned1), (along, along_low) = (
        prepared[6:10],
        prepared[10:12],
        prepared[12:14],
        prepared[14:16],
        prepared[16:18],
    )
    begun = project_begin(big, me, [own, core], dense0)
    other, begun, grads = together(other, begun, grads)
    pieces = [own, core, other, hop(other, 1)]
    z0, z1, stat, wire = project(big, me, pieces[2:], (2, 3), dense0, mask, table0, everyone, begun)
    mids = [wire, hop(wire, 1), hop(wire, 2)]
    totals = share_all(stat, count)
    totals, mids[2] = together(totals, mids[2])
    mids.append(hop(mids[2], 1))
    half = [pltpu.VMEM((big.rows // 4, LANES), F32)]
    h0, h1 = call(
        functools.partial(first_half_kernel, big),
        [low_tile, low_tile],
        half * 2,
        [me],
        [z0, z1, totals, table0, mask],
        flops=big.rows * 2 * LANES * 20,
        ins={0: cell_parts(big), 1: cell_parts(big)},
    )
    field, z2, stat = forward_second(big, me, group, mids, totals, along, turned0, mask, count)
    totals2 = share(stat)
    weights_at = exchange_four(sent)
    totals2, weights_at = together(totals2, weights_at)
    (own1,) = call(
        functools.partial(second_half_kernel, big),
        [shaped((QUARTER, low.padded), BF16)],
        half,
        [],
        [z2, totals2, second0, mask, h0, h1],
        flops=big.rows * LANES * 20,
        ins={0: cell_parts(big)},
    )
    pieces1 = gather_four(own1)
    y0, y1, stat, wire = project(low, me, pieces1, (0, 1, 2, 3), dense1, mask_low, table1, everyone)
    mids = exchange_four([wire] * 4)
    totals1 = share_all(stat, count)
    normed, shapes = normed_wires(big, me, z0, z1, totals, table0, mask)
    totals1, normed, shapes = together(totals1, normed, shapes)
    field1, y2, stat = forward_second(low, me, group, mids, totals1, along_low, turned1, mask_low, count)
    stat, normed = together(stat, normed)
    totals3 = share(stat)
    moment = moments(big, me, list(zip(normed, shapes)), pieces)
    normed = [[wire, hop(wire, 1), hop(wire, 2)] for wire in normed]
    totals3, moment, normed[0] = together(totals3, moment, normed[0])
    (mixed,) = call(
        functools.partial(output_kernel, low),
        [shaped(grad_out.shape, BF16)],
        [pltpu.VMEM((2, low.rows, LANES), F32)],
        [me],
        [y0, y1, y2, totals1, totals3, table1, second1, mask_low],
    )
    normed1, shapes1 = normed_wires(low, me, y0, y1, totals1, table1, mask_low)
    saved1 = (y0, y1, totals1, field1, y2, totals3, table1, second1, mask_low, kernel1, pieces1, normed1, shapes1)
    (back2,) = second_sums(low, grads, saved1, count)
    back2 = share(back2)
    back2, mixed, normed, normed1 = together(back2, mixed, normed, normed1)
    normed = [[*wires, hop(wires[2], 1)] for wires in normed]
    moment1 = moments(low, me, list(zip(normed1, shapes1)), pieces1)
    normed1 = [gather_four(wire) for wire in normed1]
    grads, inputs1, kernel_grad1, first1 = backward(low, me, grads, back2, saved1, normed1, weights_at, count, normed)
    last1 = back2

    saved0 = (z0, z1, totals, field, z2, totals2, table0, second0, mask, kernel0, pieces, normed, shapes)
    (back2,) = second_sums(big, grads, saved0, count)
    back2 = share(back2)
    dense_grad1 = weight_grad(low, me, inputs1, moment1, first1, kernel_grad1, count)
    back2, dense_grad1 = together(back2, dense_grad1)
    last0 = back2
    (clips_grad,), early, late, first0 = backward(
        big, me, grads, back2, saved0, normed, weights_at, count, None, dense_grad1, moment
    )

    def sized(outputs):
        rows = outputs * CIN // 64
        return shaped((rows, LANES) if rows % 16 == 0 else (2, rows * 64))

    pairs_rows = pltpu.VMEM((2 * MID_ROWS, LANES), F32)
    outs = [sized(outputs) for outputs in (MID, SMALL, PLAIN, POOL)]
    outs += [shaped((2, MID_ROWS * LANES)), shaped((2 * SMALL_ROWS, LANES))] + [shaped((4, LANES))] * 2
    mid, small, plain, pool, wide, narrow, gains_grad, shifts_grad = call(
        finish_kernel,
        outs,
        [pltpu.VMEM(early.shape, F32), pltpu.VMEM(late.shape, F32), pairs_rows],
        [me],
        [early, late, first0, first1, last0, last1],
        ins={1: (0, [(0, late.shape[0])])},
        puts={4: (0, [(0, 2)])},
    )
    flats = [plain, mid, wide, small, narrow, pool, gains_grad, shifts_grad]
    flats = [item if item.shape[0] == 2 else as_flat(item) for item in flats]
    shape = (big.side, big.side, big.frames // 8, 8 * QUARTER)
    return mixed, clips_grad.reshape(shape).transpose(2, 0, 1, 3), *flats


def solution(mesh):
    frames = P("dp", None, None, "chan")
    flat = P(None, "chan")
    return jax.shard_map(
        functools.partial(on_device, mesh.shape["dp"]),
        mesh=mesh,
        in_specs=(frames, P("dp")) + (flat,) * 8 + (frames,),
        out_specs=(frames, frames) + (flat,) * 8,
        check_vma=False,
    )
```

```python
import functools

import jax
import jax.numpy as jnp
from jax import lax
from jax.experimental import pallas as pl
from jax.experimental.pallas import tpu as pltpu
from jax.sharding import PartitionSpec as P

CIN = 832
QUARTER = 208
WIDE, NARROW = 80, 32
MID, SMALL, PLAIN, POOL = 40, 8, 64, 32
REDUCED = MID + SMALL
DENSE = REDUCED + PLAIN
ROWS = DENSE + POOL
CLIPS = 2
EPSILON = 1e-05
F32 = jnp.float32
BF16 = jnp.bfloat16
LANES = 128
LIMIT = 64
COST = 1
MID_TILES = 4 * 9 * 160 // LANES
MID_ROWS = WIDE // 4 * MID_TILES
SMALL_TILES = 4 * 9 * 32 // LANES
SMALL_ROWS = NARROW // 4 * SMALL_TILES
KERNEL_ROWS = 976
PAIR_TILES = 2 * CIN // LANES
DENSE_ROWS = 944


class Size:
    def __init__(self, side, frames):
        self.side = side
        self.frames = frames
        self.cells = side * side
        self.rows = self.cells * frames
        self.padded = -(-self.rows // LANES) * LANES
        self.band = 2 if side % 2 == 0 else side
        self.chunks = side // self.band
        self.step = self.band * side
        self.group = LANES // frames
        self.full = self.cells // self.group
        self.rest = self.cells - self.full * self.group
        self.kept = BF16 if frames % 16 == 0 else F32
        self.whole = (0, self.padded)
        first = 13 * LANES
        self.parts = [(0, first), (first, self.padded - first)] if self.padded > 2 * first - LANES - 1 else [self.whole]

    def cells_of(self, span):
        first = span[0] // self.frames
        return first, min(span[1] // self.frames, self.cells - first)

    def columns_of(self, span, width=640):
        first, count = self.cells_of(span)
        result = []
        for start in range(0, span[1], width):
            skipped, held = start // self.frames, min(width, span[1] - start)
            result.append((start, held, first + skipped, min(held // self.frames, count - skipped)))
        return result


class Stream:
    def __init__(self, far, near, sems, axis, parts):
        self.far, self.near, self.sems, self.axis, self.parts = far, near, sems, axis, parts
        self.shape, self.dtype = near.shape, near.dtype

    def copy(self, part, inward):
        if isinstance(part, int):
            start, count = self.parts[part]
        else:
            first, count = self.parts[0]
            start = first + part * count
        index = (slice(None),) * self.axis + (pl.ds(start, count),)
        pair = (self.far.at[index], self.near.at[index])
        return pltpu.make_async_copy(*(pair if inward else pair[::-1]), self.sems.at[part])

    def ready(self, part):
        self.copy(part, True).wait()

    def flush(self, part):
        self.copy(part, False).start()

    def __getitem__(self, index):
        return self.near[index]

    def __setitem__(self, index, value):
        self.near[index] = value

    @property
    def at(self):
        return self.near.at


def even(total, count):
    return [(start * (total // count), total // count) for start in range(count)]


def cell_parts(size):
    return 0, even(size.cells, size.chunks)


def line_parts(size, first=0, count=None):
    return 0, [(row * size.side, size.side) for row in range(first, first + (count or size.side))]


def column_parts(size, span, width=640):
    return 1, [(start, held) for start, held, _, _ in size.columns_of(span, width)]


def call(body, outs, scratch, scalars, args, flops=0, ins=None, puts=None, aliases=None, stacks=()):
    ins, puts = ins or {}, puts or {}
    places = {}
    for stack, members in enumerate(stacks):
        start = 0
        for index in members:
            places[index] = (stack, start)
            start += args[index].shape[0]
    aliases = {len(scalars) + index: out for index, out in (aliases or {}).items()}
    plans = [ins.get(index) for index in range(len(args))] + [puts.get(index) for index in range(len(outs))]
    arrays = list(args) + list(outs)
    buffers = []
    for index, (array, plan) in enumerate(zip(arrays, plans)):
        if index not in places:
            buffers.append(pltpu.VMEM(array.shape, array.dtype))
        buffers.append(pltpu.SemaphoreType.DMA((max(len(plan[1]), 1) if plan else 1,)))
    for members in stacks:
        rows = sum(args[index].shape[0] for index in members)
        buffers.append(pltpu.VMEM((rows,) + args[members[0]].shape[1:], args[members[0]].dtype))

    def wrapped(*refs):
        numbers, refs = refs[: len(scalars)], refs[len(scalars) :]
        far, refs = refs[: len(arrays)], refs[len(arrays) :]
        own, refs = refs[: len(scratch)], list(refs[len(scratch) :])
        whole = refs[len(refs) - len(stacks) :]
        streams = []
        for index, plan in enumerate(plans):
            axis, parts = plan or (0, [(0, arrays[index].shape[0])])
            if index in places:
                stack, start = places[index]
                near = whole[stack].at[pl.ds(start, arrays[index].shape[0])]
            else:
                near = refs.pop(0)
            streams.append(Stream(far[index], near, refs.pop(0), axis, parts))
        entering, leaving = streams[: len(args)], streams[len(args) :]
        for part in range(max([len(stream.parts) for stream in entering])):
            for stream in entering:
                if part < len(stream.parts):
                    stream.copy(part, True).start()
        for index, stream in enumerate(entering):
            if index not in ins:
                stream.ready(0)
        body(*numbers, *entering, *leaving, *own, *whole)
        for index, stream in enumerate(leaving):
            if index not in puts:
                stream.flush(0)
        for stream in leaving:
            for part in range(len(stream.parts)):
                stream.copy(part, False).wait()

    moved = sum(array.size * array.dtype.itemsize for array in arrays)
    return pl.pallas_call(
        wrapped,
        out_shape=outs,
        in_specs=[pl.BlockSpec(memory_space=pltpu.SMEM)] * len(scalars) + [pl.BlockSpec(memory_space=pl.ANY)] * len(args),
        out_specs=[pl.BlockSpec(memory_space=pl.ANY)] * len(outs),
        scratch_shapes=list(scratch) + buffers,
        compiler_params=pltpu.CompilerParams(vmem_limit_bytes=LIMIT * 1024 * 1024),
        cost_estimate=pl.CostEstimate(flops=COST, bytes_accessed=COST, transcendentals=0),
        input_output_aliases=aliases,
    )(*scalars, *args)


def unrolled(count, body, carry):
    for index in range(count):
        carry = body(index, carry)
    return carry


def rolled(count, body, carry):
    if count == 1:
        return body(0, carry)
    return lax.fori_loop(0, count, body, carry)


def shaped(shape, dtype=F32):
    return jax.ShapeDtypeStruct(shape, dtype)


def sigmoid(value):
    return 0.5 * jnp.tanh(0.5 * value) + 0.5


def row_table(rows):
    index = lax.broadcasted_iota(jnp.int32, (8, LANES), 0)
    table = jnp.zeros((8, LANES), F32)
    for position, row in enumerate(rows):
        table = jnp.where(index == position, row, table)
    return table


def time_box(value, mask_ref):
    cells, frames, width = value.shape
    flat = value.reshape(cells * frames, width)
    before = pltpu.roll(flat, 1, 0).reshape(value.shape)
    after = pltpu.roll(flat, cells * frames - 1, 0).reshape(value.shape)
    return value + before * mask_ref[1] + after * mask_ref[2]


def owner_rows(all_ref, owner):
    if len(all_ref.shape) == 3:
        return all_ref[...]
    return all_ref[:, pl.ds(owner, 1)].reshape(all_ref.shape[0], 8, LANES)


def norm_rows(all_ref, table_ref, tile, owner=0):
    total = jnp.sum(owner_rows(all_ref, owner), 0)
    count = total[4:5]
    mean = total[2 * tile : 2 * tile + 1] / count
    variance = total[2 * tile + 1 : 2 * tile + 2] / count - mean * mean
    inverse = lax.rsqrt(variance + EPSILON)
    gain = table_ref[2 * tile : 2 * tile + 1]
    shift = table_ref[2 * tile + 1 : 2 * tile + 2]
    return mean, inverse, gain, shift, count


def activate(value, rows, mask_ref):
    mean, inverse, gain, shift, _ = rows
    shifted = gain * ((value - mean) * inverse) + shift
    return shifted * sigmoid(shifted) * mask_ref[0]


def inner_grad(grad, value, rows, mask_ref):
    mean, inverse, gain, shift, _ = rows
    normed = (value - mean) * inverse
    shifted = gain * normed + shift
    sigma = sigmoid(shifted)
    return grad * mask_ref[0] * sigma * (1.0 + shifted * (1.0 - sigma)), normed


def norm_delta(inner, value, rows, back_ref, tile, mask_ref):
    mean, inverse, gain, _, count = rows
    total = jnp.sum(back_ref[...], 0)
    shift_grad = total[2 * tile : 2 * tile + 1] / count
    gain_grad = total[2 * tile + 1 : 2 * tile + 2] / count
    normed = (value - mean) * inverse
    return (gain * inverse) * (inner - mask_ref[0] * (shift_grad + normed * gain_grad))


def publish(stat_ref, rows):
    stat_ref[...] = jnp.broadcast_to(row_table(rows)[None], stat_ref.shape)


def collapse(value):
    return jnp.sum(value, 0, keepdims=True)


def windows():
    result = []
    for frame in range(8):
        start = frame * QUARTER
        first, offset = start // LANES, start % LANES
        result.append((first, -(-(offset + QUARTER) // LANES), offset))
    return result


def unpack_rows(line, frame):
    first, tiles, offset = windows()[frame]
    value = line[:, first * LANES : (first + tiles) * LANES]
    if offset:
        value = pltpu.roll(value, tiles * LANES - offset, 1)
    return value[:, : 2 * LANES]


def pack_rows(parts):
    tiles = [None] * 13
    for frame, value in enumerate(parts):
        first, count, offset = windows()[frame]
        if count == 3:
            value = jnp.concatenate([value, jnp.zeros((value.shape[0], LANES), value.dtype)], 1)
        if offset:
            value = pltpu.roll(value, offset, 1)
        for index in range(count):
            piece = value[:, index * LANES : (index + 1) * LANES]
            place = first + index
            tiles[place] = piece if tiles[place] is None else tiles[place] + piece
    return tiles


def assemble(first, second, third):
    blank = jnp.zeros_like(first)
    lane = lax.broadcasted_iota(jnp.int32, (first.shape[0], 2 * LANES), 1)
    plain = pltpu.roll(jnp.concatenate([first, blank], 1), 2 * LANES - REDUCED, 1)
    middle = pltpu.roll(jnp.concatenate([second, blank], 1), PLAIN, 1)
    pool = pltpu.roll(jnp.concatenate([third, blank], 1), PLAIN + WIDE + NARROW, 1)
    return jnp.where(lane < PLAIN, plain, 0.0) + middle + pool


def separate(value):
    lane = lax.broadcasted_iota(jnp.int32, (value.shape[0], LANES), 1)
    plain = pltpu.roll(value, REDUCED, 1)[:, :LANES]
    middle = pltpu.roll(value, 2 * LANES - PLAIN, 1)[:, :LANES]
    pool = pltpu.roll(value, 2 * LANES - PLAIN - WIDE - NARROW, 1)[:, :LANES]
    first = jnp.where((lane >= REDUCED) & (lane < DENSE), plain, 0.0)
    second = jnp.where(lane < WIDE + NARROW, middle, 0.0)
    third = jnp.where(lane < POOL, pool, 0.0)
    return first, second, third


def span_blocks(size, span, one, leaving=(), rolled=False):
    first, count = size.cells_of(span)
    total, whole = span[1] // LANES, count // size.group

    def block(index, cells):
        start = index * LANES
        start = start if isinstance(start, int) else pl.multiple_of(start, LANES)
        one(first + index * size.group, cells, pl.ds(start, LANES))

    def four(index, carry):
        for extra in range(4):
            block(index * 4 + extra, size.group)
        for stream in leaving:
            stream.flush(index)
        return carry

    groups = whole // 4 if rolled else 0
    if rolled:
        lax.fori_loop(0, groups, four, 0)
    for index in range(groups * 4, total):
        block(index, min(size.group, count - index * size.group))
        if index % 4 == 3 or index == total - 1:
            for stream in leaving:
                stream.flush(index // 4)


def span_parts(size, span):
    return column_parts(size, span, 4 * LANES)


def unpack_kernel(size, raw, out, scratch):
    side, frames = size.side, size.frames
    pairs_of = frames // 8
    def line(row, carry):
        raw.ready(row)
        value = raw[pl.ds(row * side, side)].astype(F32).reshape(pairs_of * side, 8 * QUARTER)
        for frame in range(8):
            place = pl.ds(row * side * frames + frame, pairs_of * side, stride=8)
            piece = unpack_rows(value, frame)
            scratch[0, place, :] = piece[:, :LANES]
            scratch[1, place, :] = piece[:, LANES:]
        return carry

    lax.fori_loop(0, side, line, 0)

    def one(cell, cells, lanes):
        start = cell * frames
        for tile, (low, high) in enumerate(((0, LANES), (LANES, QUARTER))):
            value = scratch[tile, pl.ds(start, cells * frames), :].reshape(cells, frames, LANES)
            out[low:high, lanes] = turn(size, value, cells)[: high - low].astype(BF16)

    span_blocks(size, size.whole, one, (out,))


def grad_kernel(size, raw, first, second, third, scratch):
    side, frames = size.side, size.frames

    def line(row, carry):
        value = raw[0, row].astype(F32)
        for frame in range(8):
            place = pl.ds(row * side * frames + frame, side, stride=frames)
            part = unpack_rows(value, frame)
            scratch[0, place, :] = part[:, :LANES]
            scratch[1, place, :] = part[:, LANES:]
        return carry

    unrolled(side, line, 0)
    parts = separate(jnp.concatenate([scratch[0], scratch[1]], 1))
    for ref, part in zip((first, second, third), parts):
        ref[...] = part.reshape(ref.shape)


def dot(left, right, dims=((1,), (0,))):
    return lax.dot_general(left, right, (dims, ((), ())), preferred_element_type=F32)


def into_padded(size, flat, field):
    side = size.side
    field[...] = jnp.zeros_like(field)

    def line(row, carry):
        field[row + 1, 1 : side + 1] = flat[pl.ds(row * side, side)]
        return carry

    unrolled(side, line, 0)


def stacked_weights(me, positions, w_ref, stacked):
    for index, position in enumerate(positions):
        stacked[index * QUARTER : (index + 1) * QUARTER] = w_ref[me[0] ^ position]


def each_column(size, body, carry):
    plan = size.columns_of(size.whole)
    _, width, _, cells = plan[0]

    def step(index, carry):
        return body(index, pl.multiple_of(index * width, LANES), width, index * cells, cells, carry)

    if len(plan) > 1:
        carry = lax.fori_loop(0, len(plan) - 1, step, carry)
    return body(len(plan) - 1, *plan[-1], carry)


def project_begin_kernel(size, me, x0, x1, w_ref, dense, pool, stacked, stack):
    frames = size.frames
    stacked_weights(me, (0, 1), w_ref, stacked)

    def column(index, start, width, first, cells, carry):
        for x in (x0, x1):
            x.ready(index)
        value = dot(stack[:, pl.ds(start, width)], stacked[...], ((0,), (0,)))
        value = value.reshape(width // frames, frames, 2 * LANES)[:cells]
        dense[pl.ds(first, cells)] = value[:, :, :LANES]
        pool[pl.ds(first, cells)] = value[:, :, LANES:]
        dense.flush(index)
        pool.flush(index)
        return carry

    each_column(size, column, 0)


def project_kernel(size, positions, me, *refs):
    side, frames = size.side, size.frames
    pieces, (w_ref, mask, table), refs = refs[: len(positions)], refs[len(positions) : len(positions) + 3], refs[len(positions) + 3 :]
    begun = refs[:2] if len(positions) < 4 else None
    z0, z1, stat, wire, field, flat, stacked, stack = refs[-8:]
    stacked_weights(me, positions, w_ref, stacked)
    blank = jnp.zeros((frames, LANES), F32)
    total, squares = blank, blank

    def column(index, start, width, first, cells, carry):
        total, squares = carry
        for x in pieces:
            x.ready(index)
        value = dot(stack[:, pl.ds(start, width)], stacked[...], ((0,), (0,)))
        value = value.reshape(width // frames, frames, 2 * LANES)[:cells]
        dense, pool = value[:, :, :LANES], value[:, :, LANES:]
        place = pl.ds(first, cells)
        if begun:
            for stream in begun:
                stream.ready(index)
            dense += begun[0][place]
            pool += begun[1][place]
        z0[place] = dense
        z0.flush(index)
        flat[place] = pool
        return total + jnp.sum(dense, 0), squares + jnp.sum(dense * dense, 0)

    total, squares = each_column(size, column, (total, squares))
    valid = mask[0]
    total, squares = collapse(total * valid), collapse(squares * valid)
    count = collapse(valid) * size.cells
    mean = total / count

    def one(cell, cells, lanes):
        wire[:, lanes] = turn(size, z0[pl.ds(cell, cells)] - mean, cells)[:REDUCED].astype(BF16)

    span_blocks(size, size.whole, one, (), True)
    into_padded(size, flat, field)

    def line(row, carry):
        pool_total, pool_squares = carry
        pool = pool_line(size, field, row, mask)
        z1[pl.ds(row * side, side)] = pool
        z1.flush(row)
        return pool_total + jnp.sum(pool, 0), pool_squares + jnp.sum(pool * pool, 0)

    pool_total, pool_squares = lax.fori_loop(0, side, line, (blank, blank))
    rows = [total, squares, collapse(pool_total * valid), collapse(pool_squares * valid), count]
    publish(stat, rows + [table[0:1], table[1:2]])


def normed_kernel(size, me, z0, z1, totals, table, mask, *refs):
    outs, (field, pooled) = refs[:-2], refs[-2:]
    side, frames, step = size.side, size.frames, size.step
    lane = lax.broadcasted_iota(jnp.int32, (frames, LANES), 1)
    field[...] = jnp.zeros_like(field)
    rows = [norm_rows(totals, table, tile, me[0]) for tile in range(2)]
    scales = [(gain * inverse * inverse, mean) for mean, inverse, gain, _, _ in rows]

    def chunk(index, carry):
        z1.ready(index)
        scale, mean = scales[1]
        value = (z1[pl.ds(index * step, step)] - mean) * scale
        value = jnp.where(lane == POOL, 1.0, value) * mask[0]
        field[pl.ds(1 + index * size.band, size.band), 1 : side + 1] = value.reshape(size.band, side, frames, LANES)
        return carry

    rolled(size.chunks, chunk, 0)
    pool_lines(size, field, pooled, mask)
    for index in range(size.chunks):
        z0.ready(index)
    for part, span in enumerate(size.parts):
        normed, shapes = outs[2 * part : 2 * part + 2]

        def one(cell, cells, lanes, normed=normed, shapes=shapes):
            scale, mean = scales[0]
            value = (z0[pl.ds(cell, cells)] - mean) * scale
            dense = turn(size, jnp.where(lane == DENSE, 1.0, value) * mask[0], cells)
            pool = turn(size, pooled[pl.ds(cell, cells)], cells)
            normed[0:DENSE, lanes] = dense[:DENSE].astype(BF16)
            normed[DENSE:ROWS, lanes] = pool[:POOL].astype(BF16)
            both = jnp.concatenate([dense[DENSE : DENSE + 8], pool[POOL : POOL + 8]], 0)
            shapes[:, lanes] = both.astype(BF16)

        span_blocks(size, span, one, (normed,), True)


def pool_lines(size, field, pooled, mask):
    def line(row, carry):
        pooled[pl.ds(row * size.side, size.side)] = pool_line(size, field, row, mask)
        return carry

    lax.fori_loop(0, size.side, line, 0)


def moments_kernel(size, me, *refs):
    (out, stack), pieces = refs[-2:], refs[-6:-2]
    lefts = refs[:-6]
    each = len(lefts) // len(size.parts)
    lefts = [lefts[part * each : (part + 1) * each] for part in range(len(size.parts))]
    lefts = [group[0][...] if each == 1 else jnp.concatenate([item[...] for item in group], 0) for group in lefts]
    value = jnp.zeros((4 * QUARTER, lefts[0].shape[0]), F32)
    for part, (left, (start, count)) in enumerate(zip(lefts, size.parts)):
        for x in pieces:
            x.ready(part)
        value += dot(stack[:, start : start + count], left, ((1,), (1,)))
    for position in range(4):
        piece = value[position * QUARTER : (position + 1) * QUARTER]
        piece = jnp.concatenate([piece, jnp.zeros((2 * LANES - QUARTER, piece.shape[1]), F32)], 0)
        out[me[0] ^ position] = piece.T


def back_columns(back, owner):
    if len(back.shape) == 2:
        return columns_of_table(back[...])
    return columns_of_table(back_table(back, owner))


def back_table(back, owner):
    every = owner_rows(back, owner)
    total, own = jnp.sum(every, 0), every[0]
    count = own[6:7]
    rows = [total[1:2] / count, total[3:4] / count, own[4:5] * total[0:1] / count, own[5:6] * total[2:3] / count]
    return row_table(rows)


def columns_of_table(table):
    turned = table.T
    slope = jnp.concatenate([turned[:DENSE, 0:1], turned[:POOL, 1:2]], 0)
    offset = jnp.concatenate([turned[:DENSE, 2:3], turned[:POOL, 3:4]], 0)
    return slope, offset


def weight_grad_kernel(size, me, inner, moments, back, kernels, out, table, grads, flat):
    table[...] = back_table(back, me[0])
    slope, offset = columns_of_table(table[...])
    for owner in range(4):
        shape = moments[owner, ROWS : ROWS + 16]
        value = inner[owner] - slope * moments[owner, 0:ROWS]
        first = value[:DENSE] - offset[:DENSE] * shape[0:1]
        last = value[DENSE:] - offset[DENSE:] * shape[8:9]
        value = jnp.concatenate([first, last], 0)
        grads[owner, 0] = value[:, :LANES]
        grads[owner, 1] = value[:, LANES:]
    parts = []
    for extra in range(2):
        rows = pl.ds(extra, ROWS // 2, stride=2)
        for owner in range(4):
            parts.append(jnp.concatenate([grads[owner, 0, rows, :], grads[owner, 1, rows, :]], 1))
    for place, tile in enumerate(pack_rows(parts)):
        flat[pl.ds(place, ROWS // 2, stride=PAIR_TILES), :] = tile
    used = ROWS // 2 * PAIR_TILES
    flat[used:, :] = jnp.zeros((DENSE_ROWS - used, LANES), F32)
    out[:KERNEL_ROWS, :] = kernels[...]
    out[KERNEL_ROWS : KERNEL_ROWS + DENSE_ROWS, :] = flat[...].astype(BF16)
    rest = out.shape[0] - KERNEL_ROWS - DENSE_ROWS
    if rest:
        out[KERNEL_ROWS + DENSE_ROWS :, :] = jnp.zeros((rest, LANES), BF16)


def pool_line(size, field, row, mask):
    side = size.side
    lines = field[pl.ds(row, 3)]
    column = lines[0] + lines[1] + lines[2]
    value = column[0:side] + column[1 : side + 1] + column[2 : side + 2]
    return time_box(value, mask) * (1.0 / 27.0)


def turn(size, value, cells):
    flat = value.reshape(cells * size.frames, value.shape[-1])
    if cells < size.group:
        blank = jnp.zeros((LANES - cells * size.frames, value.shape[-1]), value.dtype)
        flat = jnp.concatenate([flat, blank], 0)
    return flat.T


def conv_kernel(size, me, group, p0, p1, p2, p3, totals, lanes_valid, kernel, mask, field, z2, stat, joined):
    side, frames, step = size.side, size.frames, size.step
    for position, piece in enumerate((p0, p1, p2, p3)):
        owner = me[0] ^ position
        every = owner_rows(totals, owner)
        total = jnp.sum(every, 0)
        sent = totals[pl.ds(group[0], 1), pl.ds(owner, 1)].reshape(8, LANES)
        mean = total[0:1] / total[4:5]
        variance = total[1:2] / total[4:5] - mean * mean
        scale = sent[5:6] * lax.rsqrt(variance + EPSILON)
        offset = (sent[0:1] / sent[4:5] - mean) * scale + sent[6:7]
        turned = row_table([scale, offset]).T
        scale, offset = turned[:REDUCED, 0:1], turned[:REDUCED, 1:2]
        shifted = piece[...].astype(F32) * scale + offset
        value = shifted * sigmoid(shifted)
        joined[pl.ds(pl.multiple_of(owner * MID, 8), MID), :] = value[:MID]
        joined[pl.ds(pl.multiple_of(4 * MID + owner * SMALL, 8), SMALL), :] = value[MID:]
    field[...] = jnp.zeros_like(field)
    joined[4 * REDUCED :, :] = jnp.zeros((2 * LANES - 4 * REDUCED, size.padded), F32)

    def one(first, cells, lanes):
        value = (joined[:, lanes] * lanes_valid[0:1]).T
        value = value.reshape(size.group, frames, 2 * LANES).astype(size.kept)
        for index in range(cells):
            cell = first + index
            row = cell // side if isinstance(cell, int) else lax.div(cell, side)
            field[row + 1, cell - row * side + 1] = value[index]

    span_blocks(size, size.whole, one)
    field.flush(0)
    kernel.ready(0)
    blank = jnp.zeros((frames, LANES), F32)

    def chunk(index, carry):
        total, squares = carry
        parts = []
        for row in range(3):
            for column in range(3):
                part = field[pl.ds(index * size.band + row, size.band), column : column + side]
                parts.append(part.reshape(step * frames, 2 * LANES).astype(BF16))
        value = dot(jnp.concatenate(parts, 1), kernel[...].reshape(18 * LANES, LANES))
        value = time_box(value.reshape(step, frames, LANES), mask) * (1.0 / 3.0)
        z2[pl.ds(index * step, step)] = value
        z2.flush(index)
        return total + jnp.sum(value, 0), squares + jnp.sum(value * value, 0)

    total, squares = unrolled(size.chunks, chunk, (blank, blank))
    valid = mask[0]
    one_row = jnp.zeros((1, LANES), F32)
    rows = [collapse(total * valid), collapse(squares * valid), one_row, one_row, collapse(valid) * size.cells]
    publish(stat, rows)


def halve_into(size, value, scratch, index):
    half = size.side // 2
    value = value.reshape(2, half, 2, size.frames, LANES)
    value = value[0] + value[1]
    value = value[:, 0] + value[:, 1]
    rows = half * size.frames
    scratch[pl.ds(index * rows, rows), :] = value.reshape(rows, LANES)


def halved_rows(scratch):
    count = scratch.shape[0] // 2
    return (scratch[pl.ds(0, count, stride=2), :] + scratch[pl.ds(1, count, stride=2), :]) * 0.125


def first_half_kernel(size, me, z0, z1, totals, table, mask, h0, h1, s0, s1):
    for tile, (z, out, scratch) in enumerate(((z0, h0, s0), (z1, h1, s1))):
        rows = norm_rows(totals, table, tile, me[0])

        def chunk(index, carry, z=z, scratch=scratch, rows=rows):
            z.ready(index)
            value = activate(z[pl.ds(index * size.step, size.step)], rows, mask)
            halve_into(size, value, scratch, index)
            return carry

        rolled(size.chunks, chunk, 0)
        out[...] = halved_rows(scratch).reshape(out.shape)


def second_half_kernel(size, z2, totals, table, mask, h0, h1, out, scratch):
    rows = norm_rows(totals, table, 0)

    def chunk(index, carry):
        z2.ready(index)
        value = activate(z2[pl.ds(index * size.step, size.step)], rows, mask)
        halve_into(size, value, scratch, index)
        return carry

    rolled(size.chunks, chunk, 0)
    value = halved_rows(scratch)
    count = value.shape[0]
    value = assemble(h0[...].reshape(count, LANES), value, h1[...].reshape(count, LANES))
    value = jnp.concatenate([value, jnp.zeros((out.shape[1] - count, 2 * LANES), F32)], 0)
    out[...] = value.T[:QUARTER].astype(BF16)


def strided(scratch, start, count, stride):
    place = pl.ds(start, count, stride=stride)
    return jnp.concatenate([scratch[0, place, :], scratch[1, place, :]], 1)


def output_kernel(size, me, z0, z1, z2, totals, totals2, table, table2, mask, out, scratch):
    side, frames = size.side, size.frames
    parts = [
        activate(z[...], norm_rows(total, tab, tile, me[0]), mask).reshape(size.rows, LANES)
        for z, total, tab, tile in ((z0, totals, table, 0), (z2, totals2, table2, 0), (z1, totals, table, 1))
    ]
    value = assemble(*parts)
    scratch[0] = value[:, :LANES]
    scratch[1] = value[:, LANES:]

    def line(row, carry):
        start = row * side * frames
        lines = [strided(scratch, start + frame, side, frames) for frame in range(8)]
        for place, tile in enumerate(pack_rows(lines)):
            out[0, row, :, place * LANES : (place + 1) * LANES] = tile.astype(BF16)
        return carry

    unrolled(side, line, 0)


def spread(size, grad, scratch):
    value = grad[...].reshape(-1, LANES)
    count = value.shape[0]
    scratch[pl.ds(0, count, stride=2), :] = value
    scratch[pl.ds(1, count, stride=2), :] = value


def grad_chunk(size, grad, scratch, index):
    if scratch is None:
        return grad[pl.ds(index * size.step, size.step)]
    half = size.side // 2
    rows = half * size.frames
    value = scratch[pl.ds(index * rows, rows), :].reshape(half, 1, size.frames, LANES)
    value = jnp.broadcast_to(value, (half, 2, size.frames, LANES)).reshape(1, size.side, size.frames, LANES)
    value = jnp.broadcast_to(value, (2, size.side, size.frames, LANES))
    return value.reshape(size.step, size.frames, LANES)


def second_sums_kernel(size, grad, z2, totals, table, mask, stat, *scratch):
    scratch = scratch[0] if scratch else None
    if scratch is not None:
        spread(size, grad, scratch)
    rows = norm_rows(totals, table, 0)
    blank = jnp.zeros((size.frames, LANES), F32)

    def chunk(index, carry):
        shift_grad, gain_grad = carry
        z2.ready(index)
        value = z2[pl.ds(index * size.step, size.step)]
        inner, normed = inner_grad(grad_chunk(size, grad, scratch, index), value, rows, mask)
        return shift_grad + jnp.sum(inner, 0), gain_grad + jnp.sum(inner * normed, 0)

    shift_grad, gain_grad = rolled(size.chunks, chunk, (blank, blank))
    publish(stat, [collapse(shift_grad), collapse(gain_grad)])


def conv_back_kernel(size, me, grad, z2, totals, back, table, mask, kernel, delta, o0, o1, o2, field, result, turned, *scratch):
    side, frames, step = size.side, size.frames, size.step
    scratch = scratch[0] if scratch else None
    if scratch is not None:
        spread(size, grad, scratch)
    rows = norm_rows(totals, table, 0)
    field[...] = jnp.zeros_like(field)

    def first(index, carry):
        z2.ready(index)
        value = z2[pl.ds(index * step, step)]
        inner, _ = inner_grad(grad_chunk(size, grad, scratch, index), value, rows, mask)
        value = norm_delta(inner, value, rows, back, 0, mask).astype(BF16).astype(size.kept)
        delta[pl.ds(index * step, step)] = value
        delta.flush(index)
        field[pl.ds(1 + index * size.band, size.band), 1 : side + 1] = value.reshape(size.band, side, frames, LANES)
        return carry

    unrolled(size.chunks, first, 0)
    kernel.ready(0)

    def chunk(index, carry):
        parts = []
        for row in range(3):
            for column in range(3):
                part = field[pl.ds(index * size.band + 2 - row, size.band), 2 - column : 2 - column + side]
                parts.append(part.reshape(step * frames, LANES).astype(BF16))
        value = dot(jnp.concatenate(parts, 1), kernel[...].reshape(9 * LANES, 4 * REDUCED))
        result[pl.ds(index * step, step)] = value.reshape(step, frames, 4 * REDUCED)
        return carry

    unrolled(size.chunks, chunk, 0)

    def one(cell, cells, lanes):
        turned[:, lanes] = turn(size, result[pl.ds(cell, cells)], cells)

    span_blocks(size, size.whole, one)
    for position, (out, start) in enumerate(((o0, 0), (o1, 0), (o2, 0), (o2, REDUCED))):
        owner = me[0] ^ position
        mid = turned[pl.ds(pl.multiple_of(owner * MID, 8), MID), :]
        small = turned[pl.ds(pl.multiple_of(4 * MID + owner * SMALL, 8), SMALL), :]
        out[start : start + REDUCED] = jnp.concatenate([mid, small], 0).astype(BF16)


def kernel_grad_kernel(size, field, delta, mask, out, turned, boxed, taps, flat):
    side, frames, step = size.side, size.frames, size.step

    def chunk(index, carry):
        delta.ready(index)
        place = pl.ds(index * step, step)
        boxed[place] = time_box(delta[place].astype(F32), mask)
        return carry

    rolled(size.chunks, chunk, 0)

    def one(cell, cells, lanes):
        value = turn(size, boxed[pl.ds(cell, cells)], cells)
        upper = value.astype(BF16)
        turned[:LANES, lanes] = upper
        turned[LANES:, lanes] = (value - upper.astype(F32)).astype(BF16)

    span_blocks(size, size.whole, one, (), True)
    for row in range(side + 2):
        field.ready(row)

    def tap(index, carry):
        row = index // 3
        part = field[pl.ds(row, side), pl.ds(index - 3 * row, side)].reshape(size.rows, 2 * LANES).astype(BF16)
        value = dot(turned[:, : size.rows], part)
        value = (value[:LANES] + value[LANES:]) * (1.0 / 3.0)
        taps[index, 0] = value[:, :LANES]
        taps[index, 1] = value[:, LANES:]
        return carry

    for index in range(9):
        tap(index, 0)
    lane = lax.broadcasted_iota(jnp.int32, (WIDE // 4, LANES), 1)
    tiles = [None] * MID_TILES

    def add(place, value):
        tiles[place] = value if tiles[place] is None else tiles[place] + value

    for extra in range(4):
        for tap in range(9):
            rows = pl.ds(extra, WIDE // 4, stride=4)
            rest = jnp.where(lane < 4 * MID - LANES, taps[tap, 1, rows, :], 0.0)
            offset = (extra * 9 + tap) * 4 * MID
            value = jnp.concatenate([taps[tap, 0, rows, :], rest, jnp.zeros_like(rest)], 1)
            value = pltpu.roll(value, offset % LANES, 1)
            for index in range(-(-(offset % LANES + 4 * MID) // LANES)):
                add(offset // LANES + index, value[:, index * LANES : (index + 1) * LANES])
    for place, tile in enumerate(tiles):
        flat[pl.ds(place, WIDE // 4, stride=MID_TILES), :] = tile
    lane = lax.broadcasted_iota(jnp.int32, (NARROW // 4, LANES), 1)
    tiles = [None] * SMALL_TILES
    start = 4 * MID - LANES
    for extra in range(4):
        for tap in range(9):
            value = taps[tap, 1, pl.ds(WIDE + extra, NARROW // 4, stride=4), :]
            value = jnp.where((lane >= start) & (lane < start + 4 * SMALL), value, 0.0)
            offset = (extra * 9 + tap) * 4 * SMALL
            value = pltpu.roll(value, (offset - start) % LANES, 1)
            add(offset // LANES, value)
    for place, tile in enumerate(tiles):
        flat[pl.ds(MID_ROWS + place, NARROW // 4, stride=SMALL_TILES), :] = tile
    flat[MID_ROWS + SMALL_ROWS :, :] = jnp.zeros((KERNEL_ROWS - MID_ROWS - SMALL_ROWS, LANES), F32)
    out[...] = flat[...].astype(BF16)


def first_sums_kernel(size, me, p0, p1, p2, p3, g0, g1, z0, z1, totals, table, mask, *refs):
    side, step, frames = size.side, size.step, size.frames
    count = len(size.parts)
    stat, outs, (field, padded, pooled, *scratch) = refs[0], refs[1 : 1 + count], refs[1 + count :]
    s0, s1 = scratch if scratch else (None, None)
    if scratch:
        spread(size, g0, s0)
        spread(size, g1, s1)
    padded[...] = jnp.zeros_like(padded)

    def one(cell, cells, place):
        value = p0[:, place].astype(F32) + p1[:, place].astype(F32)
        value += p2[:REDUCED, place].astype(F32) + p3[REDUCED:, place].astype(F32)
        value = jnp.concatenate([value, jnp.zeros((LANES - REDUCED, LANES), F32)], 0).T
        value = value.reshape(size.group, frames, LANES)
        field[pl.ds(cell, cells)] = value[:cells]

    span_blocks(size, size.whole, one)
    rows0 = norm_rows(totals, table, 0, me[0])
    rows1 = norm_rows(totals, table, 1, me[0])
    blank = jnp.zeros((frames, LANES), F32)

    def chunk(index, carry):
        place = pl.ds(index * step, step)
        z0.ready(index)
        z1.ready(index)
        grad = time_box(field[place], mask) * (1.0 / 3.0) + grad_chunk(size, g0, s0, index)
        inner0, normed0 = inner_grad(grad, z0[place], rows0, mask)
        inner1, normed1 = inner_grad(grad_chunk(size, g1, s1, index), z1[place], rows1, mask)
        field[place] = scales[0] * inner0
        pool = scales[1] * inner1
        padded[pl.ds(1 + index * size.band, size.band), 1 : side + 1] = pool.reshape(size.band, side, frames, LANES)
        sums = (inner0, inner0 * normed0, inner1, inner1 * normed1)
        return tuple(old + jnp.sum(new, 0) for old, new in zip(carry, sums))

    scales = [rows[2] * rows[1] for rows in (rows0, rows1)]
    sums = unrolled(size.chunks, chunk, (blank,) * 4)
    publish(stat, [collapse(item) for item in sums] + scales + [rows0[4]])
    stat.flush(0)
    pool_lines(size, padded, pooled, mask)
    for out, span in zip(outs, size.parts):

        def turned(cell, cells, lanes, out=out):
            out[0:DENSE, lanes] = turn(size, field[pl.ds(cell, cells)], cells)[:DENSE].astype(BF16)
            out[DENSE:ROWS, lanes] = turn(size, pooled[pl.ds(cell, cells)], cells)[:POOL].astype(BF16)

        span_blocks(size, span, turned, (out,))


def input_rows(size, me, groups, weights, block, back, scratch, stacked):
    flat_row, pool_row = jnp.zeros((1, 2 * LANES), F32), jnp.zeros((1, 2 * LANES), F32)
    for position, weight in enumerate(weights):
        slope, offset = back_columns(back[position] if len(back) == 4 else back[0], me[0] ^ position)
        stacked[position * ROWS : (position + 1) * ROWS] = weight[block]
        value = weight[block].astype(F32)
        stacked[(position + 4) * ROWS : (position + 5) * ROWS] = (value * -slope).astype(BF16)
        value = value * offset
        flat_row -= collapse(value[:DENSE])
        pool_row -= collapse(value[DENSE:])
    index = lax.broadcasted_iota(jnp.int32, (16, 2 * LANES), 0)
    fixed = jnp.where(index == 0, flat_row, 0.0) + jnp.where(index == 8, pool_row, 0.0)
    stacked[8 * ROWS :] = fixed.astype(BF16)
    for streams, stack, columns in groups:
        for part, start, width, row in columns:
            for stream in streams:
                stream.ready(part)
            value = dot(stack[:, start : start + width], stacked[...], ((0,), (0,)))
            scratch[0, row : row + width, :] = value[:, :LANES]
            scratch[1, row : row + width, :] = value[:, LANES:]


def input_half_kernel(size, me, *refs):
    streams, weights, (back,) = refs[:9], refs[9:13], refs[13:14]
    first, second, third, scratch, stacked, stack = refs[14:]
    columns = [(part, start, width, start) for part, (start, width, _, _) in enumerate(size.columns_of(size.whole))]
    input_rows(size, me, [(streams, stack, columns)], weights, 1, (back,), scratch, stacked)
    value = jnp.concatenate([scratch[0, : size.rows, :], scratch[1, : size.rows, :]], 1)
    parts = separate(value * 0.125)
    for ref, part in zip((first, second, third), parts):
        ref[...] = part.reshape(ref.shape)


def input_plan(size, part):
    bounds = [0]
    for span in size.parts:
        first, count = size.cells_of(span)
        bounds.append((first + count) // size.side)
    low, high = bounds[part], bounds[part + 1]
    start = low * size.side * size.frames // LANES * LANES
    return low, high, start


def input_kernel(size, part, me, *refs):
    side, frames = size.side, size.frames
    pairs_of = frames // 8
    low, high, base = input_plan(size, part)
    own = 9 * (2 if part else 1)
    pieces, weights, back = refs[:own], refs[own : own + 4], refs[own + 4 : own + 8]
    refs = refs[own + 8 + (1 if part else 0) :]
    (out, scratch, stacked), stacks = refs[:3], refs[3:]
    begin = size.parts[part][0]
    columns = [(index, start, width, begin + start - base) for index, (start, width, _, _) in enumerate(size.columns_of(size.parts[part]))]
    groups = [(pieces[:9], stacks[0], columns)]
    if part:
        tail = (0, base - size.parts[part - 1][0], begin - base, 0)
        groups.append((pieces[9:], stacks[1], [tail]))
    input_rows(size, me, groups, weights, 0, back, scratch, stacked)

    def line(index, carry):
        row = low + index
        start = row * side * frames - base
        lines = [strided(scratch, start + frame, pairs_of * side, 8) for frame in range(8)]
        for place, tile in enumerate(pack_rows(lines)):
            lanes = slice(place * LANES, (place + 1) * LANES)
            out[pl.ds(row * side, side), :, lanes] = tile.reshape(side, pairs_of, LANES)
        out.flush(index)
        return carry

    for index in range(high - low):
        line(index, 0)


def pairs(axis_size, shift):
    return [(index, index ^ shift) for index in range(axis_size)]


def gather_four(piece):
    other = lax.ppermute(piece, "chan", pairs(4, 2))
    core = lax.ppermute(piece, "chan", pairs(4, 1))
    both = lax.ppermute(other, "chan", pairs(4, 1))
    return piece, core, other, both


def exchange_four(pieces):
    result = [pieces[0]]
    for shift in (1, 2, 3):
        result.append(lax.ppermute(pieces[shift], "chan", pairs(4, shift)))
    return result


def share(stat):
    return lax.all_to_all(stat, "dp", 0, 0, tiled=True)


def share_all(stat, count):
    return lax.all_to_all(stat, ("dp", "chan"), 0, 0, tiled=True).reshape(count, 4, 8, LANES)


def swap_shares(rows, count):
    return lax.all_to_all(rows.reshape(count, -1, LANES), "dp", 0, 0, tiled=True)


def shares_kernel(*refs):
    *swapped, out = refs
    start = 0
    for ref in swapped:
        count = ref.shape[1]
        value = jnp.sum(ref[...].astype(F32), 0).astype(BF16)
        for device in range(out.shape[0]):
            out[device, start : start + count] = value
        start += count


def all_shares(swapped):
    rows = sum(item.shape[1] for item in swapped)
    (whole,) = call(shares_kernel, [shaped((swapped[0].shape[0], rows, LANES), BF16)], [], [], swapped)
    return lax.all_to_all(whole, "dp", 0, 0, tiled=True)


def together(*values):
    return lax.optimization_barrier(values)


def as_rows(flat):
    return flat.reshape(2, -1, LANES).transpose(1, 0, 2).reshape(-1, LANES)


def as_flat(rows):
    return rows.reshape(-1, 2, LANES).transpose(1, 0, 2).reshape(2, -1)


NORM_LANES = (
    (0, REDUCED, PLAIN, 0),
    (0, 0, MID, 64),
    (2, 0, WIDE, 104),
    (0, MID, SMALL, 184),
    (2, WIDE, NARROW, 192),
    (1, 0, POOL, 224),
)


def shifted_lanes(value, source, width, target):
    lane = lax.broadcasted_iota(jnp.int32, value.shape, 1)
    value = jnp.where((lane >= source) & (lane < source + width), value, 0.0)
    return pltpu.roll(value, (target - source) % value.shape[1], 1)


def mask_rows(length0, length1, frames, stride):
    frame = lax.broadcasted_iota(jnp.int32, (frames, LANES), 0)
    ends = (length0, length0 + length1)

    def ident(step):
        place = (frame + step) * stride
        return jnp.where(place >= ends[0], 1, 0) + jnp.where(place >= ends[1], 1, 0)

    here = ident(0)
    valid = jnp.where(frame * stride < ends[1], 1.0, 0.0)
    before = jnp.where((frame > 0) & (ident(-1) == here), 1.0, 0.0)
    after = jnp.where((frame < frames - 1) & (ident(1) == here), 1.0, 0.0)
    return valid, before, after


def prepare_kernel(me, lengths, plain, mid, small, pool, wide, narrow, gains, shifts, *refs):
    outs, (rows, dense, taps) = refs[:-3], refs[-3:]
    mask0, mask1, tables, sent, weights, kernels = outs[0], outs[1], outs[2:6], outs[6:10], outs[10:12], outs[12:14]
    turned, along = outs[14:16], outs[16:18]
    for ref, frames, stride in ((along[0], mask0.shape[1], 1), (along[1], mask1.shape[1], 2)):
        lane = lax.broadcasted_iota(jnp.int32, (8, LANES), 1)
        ref[...] = jnp.where(lax.rem(lane, frames) * stride < lengths[0] + lengths[1], 1.0, 0.0)
    for mask, stride in ((mask0, 1), (mask1, 2)):
        for index, value in enumerate(mask_rows(lengths[0], lengths[1], mask.shape[1], stride)):
            mask[index] = value
    for block in range(2):
        lines = []
        for source in (gains, shifts):
            value = source[...].astype(F32)
            line = jnp.concatenate([value[block : block + 1], value[block + 2 : block + 3]], 1)
            lines.append(jnp.broadcast_to(line, (8, 2 * LANES)))
        found = [[jnp.zeros((8, LANES), F32)] * 2 for _ in range(3)]
        for tile, lane, width, channel in NORM_LANES:
            for index, line in enumerate(lines):
                part = shifted_lanes(line, channel, width, lane)[:, :LANES]
                found[tile][index] = found[tile][index] + part
        tables[2 * block][...] = row_table([found[0][0], found[0][1], found[1][0], found[1][1]])
        tables[2 * block + 1][...] = row_table([found[2][0], found[2][1]])
    for ref, base, outputs in ((mid, 0, MID), (small, MID, SMALL), (plain, REDUCED, PLAIN), (pool, DENSE, POOL)):
        count = ref.shape[0]
        rows[:count, :] = ref[...].astype(F32)
        for block in range(2):
            tiles = [rows[pl.ds(2 * tile + block, outputs // 2, stride=2 * PAIR_TILES), :] for tile in range(PAIR_TILES)]
            line = jnp.concatenate(tiles, 1)
            for extra in range(2):
                place = pl.ds(base + extra, outputs // 2, stride=2)
                for owner in range(4):
                    part = unpack_rows(line, 4 * extra + owner)
                    dense[block, owner, 0, place, :] = part[:, :LANES]
                    dense[block, owner, 1, place, :] = part[:, LANES:]
    lane = lax.broadcasted_iota(jnp.int32, (ROWS, LANES), 1)
    blank = jnp.zeros((LANES, 2 * LANES), F32)
    for block in range(2):
        for owner in range(4):
            rest = jnp.where(lane < QUARTER - LANES, dense[block, owner, 1], 0.0)
            dense[block, owner, 1] = rest
            value = jnp.concatenate([dense[block, owner, 0], rest], 1)
            value = jnp.concatenate([value[:DENSE], blank[: LANES - DENSE], value[DENSE:], blank[: LANES - POOL]], 0)
            weights[block][owner] = value.T[:QUARTER].astype(BF16)
        for position in range(4):
            owner = me[0] ^ position
            value = jnp.concatenate([dense[block, owner, 0], dense[block, owner, 1]], 1)
            sent[position][block] = value.astype(BF16)
    wide_lane = lax.broadcasted_iota(jnp.int32, (WIDE // 4, LANES), 1)
    narrow_lane = lax.broadcasted_iota(jnp.int32, (NARROW // 4, LANES), 1)
    start = 4 * MID - LANES
    for block in range(2):
        rows[: wide.shape[0], :] = wide[...].astype(F32)
        taps[...] = jnp.zeros_like(taps)
        tiles = [rows[pl.ds(2 * tile + block, WIDE // 4, stride=2 * MID_TILES), :] for tile in range(MID_TILES)]
        tiles.append(tiles[0])
        for extra in range(4):
            for tap in range(9):
                offset = (extra * 9 + tap) * 4 * MID
                first, shift = offset // LANES, offset % LANES
                count = -(-(shift + 4 * MID) // LANES)
                value = jnp.concatenate(tiles[first : first + count], 1)
                value = pltpu.roll(value, (count * LANES - shift) % (count * LANES), 1)
                place = pl.ds(extra, WIDE // 4, stride=4)
                taps[tap, 0, place, :] = value[:, :LANES]
                taps[tap, 1, place, :] = jnp.where(wide_lane < start, value[:, LANES : 2 * LANES], 0.0)
        rows[: narrow.shape[0], :] = narrow[...].astype(F32)
        tiles = [rows[pl.ds(2 * tile + block, NARROW // 4, stride=2 * SMALL_TILES), :] for tile in range(SMALL_TILES)]
        for extra in range(4):
            for tap in range(9):
                offset = (extra * 9 + tap) * 4 * SMALL
                value = pltpu.roll(tiles[offset // LANES], (start - offset) % LANES, 1)
                value = jnp.where((narrow_lane >= start) & (narrow_lane < start + 4 * SMALL), value, 0.0)
                taps[tap, 1, pl.ds(WIDE + extra, NARROW // 4, stride=4), :] = value
        for tap in range(9):
            first, second = taps[tap, 0], taps[tap, 1]
            kernels[block][tap] = jnp.concatenate([first, second], 1)[:, : 4 * REDUCED].astype(BF16)
            turned[block][tap, :LANES] = first.T.astype(BF16)
            turned[block][tap, LANES:] = second.T.astype(BF16)


def place_rows(out, sources, count, pairs_rows):
    target = pairs_rows if out.shape[0] == 2 else out.near
    for block, (ref, start) in enumerate(sources):
        target[pl.ds(block, count, stride=2), :] = ref[start : start + count, :]
    if out.shape[0] == 2:
        for index in range(count // 4):
            value = pairs_rows[index * 8 : index * 8 + 8, :]
            for part in range(4):
                place = index * 4 + part
                out[:, place * LANES : (place + 1) * LANES] = value[2 * part : 2 * part + 2]


def finish_kernel(me, early, late, first0, first1, second0, second1, *refs):
    outs, (rows, other, pairs_rows) = refs[:-3], refs[-3:]
    mid, small, plain, pool, wide, narrow, gains, shifts = outs
    share = late.shape[1]
    for device in range(late.shape[0]):
        place = slice(device * share, (device + 1) * share)
        rows[place] = early[device].astype(F32)
    late.ready(0)
    for device in range(late.shape[0]):
        place = slice(device * share, (device + 1) * share)
        other[place] = late[device].astype(F32)
    place_rows(wide, ((other, 0), (rows, 0)), MID_ROWS, pairs_rows)
    wide.flush(0)
    place_rows(narrow, ((other, MID_ROWS), (rows, MID_ROWS)), SMALL_ROWS, pairs_rows)
    start = KERNEL_ROWS
    for out, outputs in ((mid, MID), (small, SMALL), (plain, PLAIN), (pool, POOL)):
        count = outputs * CIN // LANES
        place_rows(out, ((other, start), (rows, start)), count, pairs_rows)
        start += count
    for block, first_ref, second_ref in ((0, first0, second0), (1, first1, second1)):
        first = jnp.sum(owner_rows(first_ref, me[0]), 0)
        second = jnp.sum(second_ref[...], 0)
        for out, row in ((gains, 1), (shifts, 0)):
            lines = (first[row : row + 1], first[row + 2 : row + 3], second[row : row + 1])
            total = jnp.zeros((8, 2 * LANES), F32)
            for tile, lane, width, channel in NORM_LANES:
                line = jnp.concatenate([lines[tile], jnp.zeros((1, LANES), F32)], 1)
                total += shifted_lanes(jnp.broadcast_to(line, (8, 2 * LANES)), lane, width, channel)
            out[block : block + 1, :] = total[0:1, :LANES]
            out[block + 2 : block + 3, :] = total[0:1, LANES:]


def project(size, me, pieces, positions, dense, mask, table, everyone, begun=()):
    side, cells, frames = size.side, size.cells, size.frames
    tile = shaped((cells, frames, LANES))
    count = len(positions)
    column_cells = (0, [(first, held) for _, _, first, held in size.columns_of(size.whole)])
    ins = {index: column_parts(size, size.whole) for index in range(count)}
    ins |= {count + 3 + index: column_cells for index in range(len(begun))}
    return call(
        functools.partial(project_kernel, size, positions),
        [tile, tile, shaped((everyone, 8, LANES)), shaped((REDUCED, size.padded), BF16)],
        [
            pltpu.VMEM((side + 2, side + 2, frames, LANES), F32),
            pltpu.VMEM((cells, frames, LANES), F32),
            pltpu.VMEM((count * QUARTER, 2 * LANES), BF16),
        ],
        [me],
        [*pieces, dense, mask, table, *begun],
        ins=ins,
        puts={0: column_cells, 1: line_parts(size)},
        stacks=[range(count)],
    )


def project_begin(size, me, pieces, dense):
    tile = shaped((size.cells, size.frames, LANES))
    column_cells = (0, [(first, held) for _, _, first, held in size.columns_of(size.whole)])
    return call(
        functools.partial(project_begin_kernel, size),
        [tile, tile],
        [pltpu.VMEM((2 * QUARTER, 2 * LANES), BF16)],
        [me],
        [*pieces, dense],
        ins={index: column_parts(size, size.whole) for index in range(2)},
        puts={0: column_cells, 1: column_cells},
        stacks=[range(2)],
    )


def normed_wires(size, me, z0, z1, totals, table, mask):
    outs, puts = [], {}
    for part, (_, lanes) in enumerate(size.parts):
        outs += [shaped((ROWS, lanes), BF16), shaped((16, lanes), BF16)]
        puts[2 * part] = span_parts(size, size.parts[part])
    wires = call(
        functools.partial(normed_kernel, size),
        outs,
        [
            pltpu.VMEM((size.side + 2, size.side + 2, size.frames, LANES), F32),
            pltpu.VMEM((size.cells, size.frames, LANES), F32),
        ],
        [me],
        [z0, z1, totals, table, mask],
        ins={0: cell_parts(size), 1: cell_parts(size)},
        puts=puts,
    )
    return wires[0::2], wires[1::2]


def moments(size, me, lefts, pieces):
    rows = sum(item.shape[0] for item in lefts[0])
    flat = [item for group in lefts for item in group]
    (result,) = call(
        functools.partial(moments_kernel, size),
        [shaped((4, rows, 2 * LANES))],
        [],
        [me],
        [*flat, *pieces],
        ins={len(flat) + index: (1, size.parts) for index in range(4)},
        stacks=[range(len(flat), len(flat) + 4)],
    )
    return result


def forward_second(size, me, group, pieces, totals, along, kernel, mask, count):
    side, frames = size.side, size.frames
    field, z2, stat = call(
        functools.partial(conv_kernel, size),
        [
            shaped((side + 2, side + 2, frames, 2 * LANES), size.kept),
            shaped((size.cells, frames, LANES)),
            shaped((count, 8, LANES)),
        ],
        [pltpu.VMEM((2 * LANES, size.padded), F32)],
        [me, group],
        [*pieces, totals, along, kernel, mask],
        flops=2 * size.rows * 9 * 256 * 256,
        ins={6: (0, [(0, 9)])},
        puts={0: (0, [(0, side + 2)]), 1: cell_parts(size)},
    )
    return field, z2, stat


def hop(piece, shift):
    return lax.ppermute(piece, "chan", pairs(4, shift))


def second_sums(size, grads, saved, count):
    z2, totals2, table2, mask = saved[4], saved[5], saved[7], saved[8]
    return call(
        functools.partial(second_sums_kernel, size),
        [shaped((count, 8, LANES))],
        spread_rows(size),
        [],
        [grads[1], z2, totals2, table2, mask],
        ins={1: cell_parts(size)},
    )


def spread_rows(size):
    return [pltpu.VMEM((size.rows // 4, LANES), F32)] if size.side % 2 == 0 else []


def weight_grad(size, me, inner, moment, back1, kernels, count):
    unit = count * 16
    total = -(-(KERNEL_ROWS + DENSE_ROWS) // unit) * unit
    return call(
        functools.partial(weight_grad_kernel, size),
        [shaped((total, LANES), BF16), shaped((8, LANES))],
        [pltpu.VMEM((4, 2, ROWS, LANES), F32), pltpu.VMEM((DENSE_ROWS, LANES), F32)],
        [me],
        [inner, moment, back1, kernels],
    )


def backward(size, me, grads, back2, saved, normed, weights_at, count, early=None, moment=None):
    z0, z1, totals, field, z2, totals2, table, table2, mask, kernel, pieces, _, shapes = saved
    g0, g2, g1 = grads
    side, frames = size.side, size.frames
    spreads = early is not None
    tile = shaped((size.cells, frames, LANES))
    wire = shaped((REDUCED, size.padded), BF16)
    delta2, o0, o1, o2 = call(
        functools.partial(conv_back_kernel, size),
        [shaped((size.cells, frames, LANES), size.kept), wire, wire, shaped((2 * REDUCED, size.padded), BF16)],
        [
            pltpu.VMEM((side + 2, side + 2, frames, LANES), size.kept),
            pltpu.VMEM((size.cells, frames, 4 * REDUCED), F32),
            pltpu.VMEM((4 * REDUCED, size.padded), F32),
        ]
        + spread_rows(size),
        [me],
        [g2, z2, totals2, back2, table2, mask, kernel],
        flops=2 * size.rows * 9 * 256 * 256,
        ins={1: cell_parts(size), 6: (0, [(0, 9)])},
        puts={0: cell_parts(size)},
    )
    if spreads:
        o2, normed = together(o2, normed)
        normed = [[*wires, hop(wires[2], 1)] for wires in normed]
    partial = [o0, hop(o1, 1), hop(o2, 2)]
    (kernel_grad,) = call(
        functools.partial(kernel_grad_kernel, size),
        [shaped((KERNEL_ROWS, LANES), BF16)],
        [
            pltpu.VMEM((2 * LANES, size.padded), BF16),
            pltpu.VMEM((size.cells, frames, LANES), F32),
            pltpu.VMEM((9, 2, LANES, LANES), F32),
            pltpu.VMEM((KERNEL_ROWS, LANES), F32),
        ],
        [],
        [field, delta2, mask],
        flops=2 * size.rows * 9 * 256 * 256,
        ins={0: (0, even(side + 2, side + 2)), 1: cell_parts(size)},
    )
    if spreads:
        early, o1 = together(early, o1)
        swapped = swap_shares(early, count)
        partial[2], kernel_grad = together(partial[2], kernel_grad)
    else:
        partial[2], kernel_grad = together(partial[2], kernel_grad)
    if not spreads:
        partial[1], normed = together(partial[1], normed)
    partial.append(hop(partial[2], 1))
    if spreads:
        partial[3], swapped = together(partial[3], swapped)
    devices = count if spreads else 4 * count
    stat, *wires = call(
        functools.partial(first_sums_kernel, size),
        [shaped((devices, 8, LANES))] + [shaped((ROWS, lanes), BF16) for _, lanes in size.parts],
        [
            pltpu.VMEM((size.cells, frames, LANES), F32),
            pltpu.VMEM((side + 2, side + 2, frames, LANES), F32),
            pltpu.VMEM((size.cells, frames, LANES), F32),
        ]
        + spread_rows(size) * 2,
        [me],
        [*partial, g0, g1, z0, z1, totals, table, mask],
        ins={6: cell_parts(size), 7: cell_parts(size)},
        puts={0: (0, [(0, devices)])} | {1 + part: span_parts(size, span) for part, span in enumerate(size.parts)},
    )
    others, cores = [hop(wire, 2) for wire in wires[:1]] + [None] * (len(wires) - 1), [hop(wire, 1) for wire in wires]
    inner = moments(size, me, [[wire] for wire in wires], pieces)
    if spreads:
        early = all_shares([swapped])
        stat, early = together(stat, early)
        back1 = share(stat)
        back1, inner, others[0] = together(back1, inner, others[0])
        dense_grad, table_own = weight_grad(size, me, inner, moment, back1, kernel_grad, count)
        tables = exchange_four([table_own] * 4)
        tables, last = together(tables, wires[1])
        others[1] = hop(last, 2)
        swapped = swap_shares(dense_grad, count)
    else:
        back1 = share_all(stat, count)
        back1, others[0], moment = together(back1, others[0], moment)

    def four(part):
        return [wires[part], cores[part], others[part], hop(others[part], 1)]

    scratch = [pltpu.VMEM((2, size.parts[0][1] + LANES, LANES), F32), pltpu.VMEM((8 * ROWS + 16, 2 * LANES), BF16)]
    if not spreads:
        result = call(
            functools.partial(input_half_kernel, size),
            [tile, tile, tile],
            scratch,
            [me],
            [*four(0), *normed[0], shapes[0], *weights_at, back1],
            ins={index: column_parts(size, size.whole) for index in range(9)},
            stacks=[range(9)],
        )
        return result, inner, kernel_grad, back1, moment
    shape = shaped((size.cells, frames // 8, 8 * QUARTER))
    result, sets = (), []
    for part, span in enumerate(size.parts):
        if part:
            swapped, result = together(swapped, result)
            late = all_shares([swapped])
        sets.append([*four(part), *normed[part], shapes[part]])
        low, high, base = input_plan(size, part)
        args = list(sets[part])
        ins = {index: column_parts(size, span) for index in range(9)}
        stacks = [range(9)]
        if part:
            before = size.parts[part - 1]
            tail = (1, [(base - before[0], span[0] - base)])
            ins |= {len(args) + index: tail for index in range(9)}
            stacks.append(range(9, 18))
            args += sets[part - 1]
        args += [*weights_at, *tables]
        if part:
            ins[len(args)] = (0, [])
        result = call(
            functools.partial(input_kernel, size, part),
            [shape],
            scratch,
            [me],
            [*args, *result],
            ins=ins,
            puts={0: line_parts(size, low, high - low)},
            aliases={len(args): 0} if part else None,
            stacks=stacks,
        )
    return result, (early, late), back1


def on_device(count, clips, clip_len, w_plain, w_mid, k_mid, w_small, k_small, w_pool, gains, shifts, grad_out):
    big = Size(clips.shape[1], 8 * clips.shape[0])
    low = Size(grad_out.shape[1], 8 * grad_out.shape[0])
    me = lax.axis_index("chan").astype(jnp.int32).reshape(1)
    group = lax.axis_index("dp").astype(jnp.int32).reshape(1)
    everyone = 4 * count
    raw = clips.transpose(1, 2, 0, 3).reshape(big.cells, clips.shape[0], 8 * QUARTER)
    (own,) = call(
        functools.partial(unpack_kernel, big),
        [shaped((QUARTER, big.padded), BF16)],
        [pltpu.VMEM((2, big.rows, LANES), F32)],
        [],
        [raw],
        ins={0: line_parts(big)},
        puts={0: span_parts(big, big.whole)},
    )
    other, core = hop(own, 2), hop(own, 1)
    low_tile = shaped((low.cells, low.frames, LANES))
    grads = call(
        functools.partial(grad_kernel, low),
        [low_tile, low_tile, low_tile],
        [pltpu.VMEM((2, low.rows, LANES), F32)],
        [],
        [grad_out],
    )
    table = shaped((8, LANES))
    prepared = call(
        prepare_kernel,
        [shaped((3, big.frames, LANES)), shaped((3, low.frames, LANES))]
        + [table] * 4
        + [shaped((2, ROWS, 2 * LANES), BF16)] * 4
        + [shaped((4, QUARTER, 2 * LANES), BF16)] * 2
        + [shaped((9, LANES, 4 * REDUCED), BF16)] * 2
        + [shaped((9, 2 * LANES, LANES), BF16)] * 2
        + [table] * 2,
        [
            pltpu.VMEM((2 * MID_ROWS, LANES), F32),
            pltpu.VMEM((2, 4, 2, ROWS, LANES), F32),
            pltpu.VMEM((9, 2, LANES, LANES), F32),
        ],
        [me, clip_len],
        [as_rows(item) for item in (w_plain, w_mid, w_small, w_pool, k_mid, k_small, gains, shifts)],
    )
    mask, mask_low, table0, second0, table1, second1 = prepared[:6]
    sent, (dense0, dense1), (kernel0, kernel1), (turned0, turned1), (along, along_low) = (
        prepared[6:10],
        prepared[10:12],
        prepared[12:14],
        prepared[14:16],
        prepared[16:18],
    )
    begun = project_begin(big, me, [own, core], dense0)
    other, begun, grads = together(other, begun, grads)
    pieces = [own, core, other, hop(other, 1)]
    z0, z1, stat, wire = project(big, me, pieces[2:], (2, 3), dense0, mask, table0, everyone, begun)
    mids = [wire, hop(wire, 1), hop(wire, 2)]
    totals = share_all(stat, count)
    totals, mids[2] = together(totals, mids[2])
    mids.append(hop(mids[2], 1))
    half = [pltpu.VMEM((big.rows // 4, LANES), F32)]
    h0, h1 = call(
        functools.partial(first_half_kernel, big),
        [low_tile, low_tile],
        half * 2,
        [me],
        [z0, z1, totals, table0, mask],
        flops=big.rows * 2 * LANES * 20,
        ins={0: cell_parts(big), 1: cell_parts(big)},
    )
    field, z2, stat = forward_second(big, me, group, mids, totals, along, turned0, mask, count)
    totals2 = share(stat)
    weights_at = exchange_four(sent)
    totals2, weights_at = together(totals2, weights_at)
    (own1,) = call(
        functools.partial(second_half_kernel, big),
        [shaped((QUARTER, low.padded), BF16)],
        half,
        [],
        [z2, totals2, second0, mask, h0, h1],
        flops=big.rows * LANES * 20,
        ins={0: cell_parts(big)},
    )
    pieces1 = gather_four(own1)
    y0, y1, stat, wire = project(low, me, pieces1, (0, 1, 2, 3), dense1, mask_low, table1, everyone)
    mids = exchange_four([wire] * 4)
    totals1 = share_all(stat, count)
    normed, shapes = normed_wires(big, me, z0, z1, totals, table0, mask)
    totals1, normed, shapes = together(totals1, normed, shapes)
    field1, y2, stat = forward_second(low, me, group, mids, totals1, along_low, turned1, mask_low, count)
    totals3 = share(stat)
    normed1, shapes1 = normed_wires(low, me, y0, y1, totals1, table1, mask_low)
    totals3, normed1 = together(totals3, normed1)
    (mixed,) = call(
        functools.partial(output_kernel, low),
        [shaped(grad_out.shape, BF16)],
        [pltpu.VMEM((2, low.rows, LANES), F32)],
        [me],
        [y0, y1, y2, totals1, totals3, table1, second1, mask_low],
    )
    saved1 = (y0, y1, totals1, field1, y2, totals3, table1, second1, mask_low, kernel1, pieces1, normed1, shapes1)
    (back2,) = second_sums(low, grads, saved1, count)
    back2 = share(back2)
    moment1 = moments(low, me, list(zip(normed1, shapes1)), pieces1)
    normed1 = [[wire, hop(wire, 1), hop(wire, 2)] for wire in normed1]
    back2, mixed, normed1, moment1 = together(back2, mixed, normed1, moment1)
    normed1 = [[*wires, hop(wires[2], 1)] for wires in normed1]
    moment = moments(big, me, list(zip(normed, shapes)), pieces)
    grads, inputs1, kernel_grad1, first1, moment = backward(
        low, me, grads, back2, saved1, normed1, weights_at, count, None, moment
    )
    last1 = back2

    saved0 = (z0, z1, totals, field, z2, totals2, table0, second0, mask, kernel0, pieces, normed, shapes)
    (back2,) = second_sums(big, grads, saved0, count)
    back2, normed = together(back2, normed)
    back2 = share(back2)
    normed = [[wire, hop(wire, 1), hop(wire, 2)] for wire in normed]
    dense_grad1, _ = weight_grad(low, me, inputs1, moment1, first1, kernel_grad1, count)
    back2, dense_grad1, normed[0] = together(back2, dense_grad1, normed[0])
    last0 = back2
    (clips_grad,), (early, late), first0 = backward(
        big, me, grads, back2, saved0, normed, weights_at, count, dense_grad1, moment
    )

    def sized(outputs):
        rows = outputs * CIN // 64
        return shaped((rows, LANES) if rows % 16 == 0 else (2, rows * 64))

    pairs_rows = pltpu.VMEM((2 * MID_ROWS, LANES), F32)
    outs = [sized(outputs) for outputs in (MID, SMALL, PLAIN, POOL)]
    outs += [shaped((2, MID_ROWS * LANES)), shaped((2 * SMALL_ROWS, LANES))] + [shaped((4, LANES))] * 2
    mid, small, plain, pool, wide, narrow, gains_grad, shifts_grad = call(
        finish_kernel,
        outs,
        [pltpu.VMEM((count * late.shape[1], LANES), F32)] * 2 + [pairs_rows],
        [me],
        [early, late, first0, first1, last0, last1],
        ins={1: (0, [(0, count)])},
        puts={4: (0, [(0, 2)])},
    )
    flats = [plain, mid, wide, small, narrow, pool, gains_grad, shifts_grad]
    flats = [item if item.shape[0] == 2 else as_flat(item) for item in flats]
    shape = (big.side, big.side, big.frames // 8, 8 * QUARTER)
    return mixed, clips_grad.reshape(shape).transpose(2, 0, 1, 3), *flats


def solution(mesh):
    frames = P("dp", None, None, "chan")
    flat = P(None, "chan")
    return jax.shard_map(
        functools.partial(on_device, mesh.shape["dp"]),
        mesh=mesh,
        in_specs=(frames, P("dp")) + (flat,) * 8 + (frames,),
        out_specs=(frames, frames) + (flat,) * 8,
        check_vma=False,
    )
```

```python
import functools

import jax
import jax.numpy as jnp
from jax import lax
from jax.experimental import pallas as pl
from jax.experimental.pallas import tpu as pltpu
from jax.sharding import PartitionSpec as P

CIN = 832
QUARTER = 208
WIDE, NARROW = 80, 32
MID, SMALL, PLAIN, POOL = 40, 8, 64, 32
REDUCED = MID + SMALL
DENSE = REDUCED + PLAIN
ROWS = DENSE + POOL
CLIPS = 2
EPSILON = 1e-05
F32 = jnp.float32
BF16 = jnp.bfloat16
LANES = 128
LIMIT = 64
COST = 1
MID_TILES = 4 * 9 * 160 // LANES
MID_ROWS = WIDE // 4 * MID_TILES
SMALL_TILES = 4 * 9 * 32 // LANES
SMALL_ROWS = NARROW // 4 * SMALL_TILES
KERNEL_ROWS = 976
PAIR_TILES = 2 * CIN // LANES
DENSE_ROWS = 944


class Size:
    def __init__(self, side, frames):
        self.side = side
        self.frames = frames
        self.cells = side * side
        self.rows = self.cells * frames
        self.padded = -(-self.rows // LANES) * LANES
        self.band = 2 if side % 2 == 0 else side
        self.chunks = side // self.band
        self.step = self.band * side
        self.group = LANES // frames
        self.full = self.cells // self.group
        self.rest = self.cells - self.full * self.group
        self.kept = BF16 if frames % 16 == 0 else F32
        self.whole = (0, self.padded)
        first = 13 * LANES
        self.parts = [(0, first), (first, self.padded - first)] if self.padded > 2 * first - LANES - 1 else [self.whole]

    def cells_of(self, span):
        first = span[0] // self.frames
        return first, min(span[1] // self.frames, self.cells - first)

    def columns_of(self, span, width=640):
        first, count = self.cells_of(span)
        result = []
        for start in range(0, span[1], width):
            skipped, held = start // self.frames, min(width, span[1] - start)
            result.append((start, held, first + skipped, min(held // self.frames, count - skipped)))
        return result


class Stream:
    def __init__(self, far, near, sems, axis, parts):
        self.far, self.near, self.sems, self.axis, self.parts = far, near, sems, axis, parts
        self.shape, self.dtype = near.shape, near.dtype

    def copy(self, part, inward):
        if isinstance(part, int):
            start, count = self.parts[part]
        else:
            first, count = self.parts[0]
            start = first + part * count
        index = (slice(None),) * self.axis + (pl.ds(start, count),)
        pair = (self.far.at[index], self.near.at[index])
        return pltpu.make_async_copy(*(pair if inward else pair[::-1]), self.sems.at[part])

    def ready(self, part):
        self.copy(part, True).wait()

    def flush(self, part):
        self.copy(part, False).start()

    def __getitem__(self, index):
        return self.near[index]

    def __setitem__(self, index, value):
        self.near[index] = value

    @property
    def at(self):
        return self.near.at


def even(total, count):
    return [(start * (total // count), total // count) for start in range(count)]


def cell_parts(size):
    return 0, even(size.cells, size.chunks)


def line_parts(size, first=0, count=None):
    return 0, [(row * size.side, size.side) for row in range(first, first + (count or size.side))]


def column_parts(size, span, width=640):
    return 1, [(start, held) for start, held, _, _ in size.columns_of(span, width)]


def call(body, outs, scratch, scalars, args, flops=0, ins=None, puts=None, aliases=None, stacks=()):
    ins, puts = ins or {}, puts or {}
    places = {}
    for stack, members in enumerate(stacks):
        start = 0
        for index in members:
            places[index] = (stack, start)
            start += args[index].shape[0]
    aliases = {len(scalars) + index: out for index, out in (aliases or {}).items()}
    plans = [ins.get(index) for index in range(len(args))] + [puts.get(index) for index in range(len(outs))]
    arrays = list(args) + list(outs)
    buffers = []
    for index, (array, plan) in enumerate(zip(arrays, plans)):
        if index not in places:
            buffers.append(pltpu.VMEM(array.shape, array.dtype))
        buffers.append(pltpu.SemaphoreType.DMA((max(len(plan[1]), 1) if plan else 1,)))
    for members in stacks:
        rows = sum(args[index].shape[0] for index in members)
        buffers.append(pltpu.VMEM((rows,) + args[members[0]].shape[1:], args[members[0]].dtype))

    def wrapped(*refs):
        numbers, refs = refs[: len(scalars)], refs[len(scalars) :]
        far, refs = refs[: len(arrays)], refs[len(arrays) :]
        own, refs = refs[: len(scratch)], list(refs[len(scratch) :])
        whole = refs[len(refs) - len(stacks) :]
        streams = []
        for index, plan in enumerate(plans):
            axis, parts = plan or (0, [(0, arrays[index].shape[0])])
            if index in places:
                stack, start = places[index]
                near = whole[stack].at[pl.ds(start, arrays[index].shape[0])]
            else:
                near = refs.pop(0)
            streams.append(Stream(far[index], near, refs.pop(0), axis, parts))
        entering, leaving = streams[: len(args)], streams[len(args) :]
        for part in range(max([len(stream.parts) for stream in entering])):
            for stream in entering:
                if part < len(stream.parts):
                    stream.copy(part, True).start()
        for index, stream in enumerate(entering):
            if index not in ins:
                stream.ready(0)
        body(*numbers, *entering, *leaving, *own, *whole)
        for index, stream in enumerate(leaving):
            if index not in puts:
                stream.flush(0)
        for stream in leaving:
            for part in range(len(stream.parts)):
                stream.copy(part, False).wait()

    moved = sum(array.size * array.dtype.itemsize for array in arrays)
    return pl.pallas_call(
        wrapped,
        out_shape=outs,
        in_specs=[pl.BlockSpec(memory_space=pltpu.SMEM)] * len(scalars) + [pl.BlockSpec(memory_space=pl.ANY)] * len(args),
        out_specs=[pl.BlockSpec(memory_space=pl.ANY)] * len(outs),
        scratch_shapes=list(scratch) + buffers,
        compiler_params=pltpu.CompilerParams(vmem_limit_bytes=LIMIT * 1024 * 1024),
        cost_estimate=pl.CostEstimate(flops=COST, bytes_accessed=COST, transcendentals=0),
        input_output_aliases=aliases,
    )(*scalars, *args)


def unrolled(count, body, carry):
    for index in range(count):
        carry = body(index, carry)
    return carry


def rolled(count, body, carry):
    if count == 1:
        return body(0, carry)
    return lax.fori_loop(0, count, body, carry)


def shaped(shape, dtype=F32):
    return jax.ShapeDtypeStruct(shape, dtype)


def sigmoid(value):
    return 0.5 * jnp.tanh(0.5 * value) + 0.5


def row_table(rows):
    index = lax.broadcasted_iota(jnp.int32, (8, LANES), 0)
    table = jnp.zeros((8, LANES), F32)
    for position, row in enumerate(rows):
        table = jnp.where(index == position, row, table)
    return table


def time_box(value, mask_ref):
    cells, frames, width = value.shape
    flat = value.reshape(cells * frames, width)
    before = pltpu.roll(flat, 1, 0).reshape(value.shape)
    after = pltpu.roll(flat, cells * frames - 1, 0).reshape(value.shape)
    return value + before * mask_ref[1] + after * mask_ref[2]


def owner_rows(all_ref, owner):
    if len(all_ref.shape) == 3:
        return all_ref[...]
    return all_ref[:, pl.ds(owner, 1)].reshape(all_ref.shape[0], 8, LANES)


def norm_rows(all_ref, table_ref, tile, owner=0):
    total = jnp.sum(owner_rows(all_ref, owner), 0)
    count = total[4:5]
    mean = total[2 * tile : 2 * tile + 1] / count
    variance = total[2 * tile + 1 : 2 * tile + 2] / count - mean * mean
    inverse = lax.rsqrt(variance + EPSILON)
    gain = table_ref[2 * tile : 2 * tile + 1]
    shift = table_ref[2 * tile + 1 : 2 * tile + 2]
    return mean, inverse, gain, shift, count


def activate(value, rows, mask_ref):
    mean, inverse, gain, shift, _ = rows
    shifted = gain * ((value - mean) * inverse) + shift
    return shifted * sigmoid(shifted) * mask_ref[0]


def inner_grad(grad, value, rows, mask_ref):
    mean, inverse, gain, shift, _ = rows
    normed = (value - mean) * inverse
    shifted = gain * normed + shift
    sigma = sigmoid(shifted)
    return grad * mask_ref[0] * sigma * (1.0 + shifted * (1.0 - sigma)), normed


def norm_delta(inner, value, rows, back_ref, tile, mask_ref):
    mean, inverse, gain, _, count = rows
    total = jnp.sum(back_ref[...], 0)
    shift_grad = total[2 * tile : 2 * tile + 1] / count
    gain_grad = total[2 * tile + 1 : 2 * tile + 2] / count
    normed = (value - mean) * inverse
    return (gain * inverse) * (inner - mask_ref[0] * (shift_grad + normed * gain_grad))


def publish(stat_ref, rows):
    stat_ref[...] = jnp.broadcast_to(row_table(rows)[None], stat_ref.shape)


def collapse(value):
    return jnp.sum(value, 0, keepdims=True)


def windows():
    result = []
    for frame in range(8):
        start = frame * QUARTER
        first, offset = start // LANES, start % LANES
        result.append((first, -(-(offset + QUARTER) // LANES), offset))
    return result


def unpack_rows(line, frame):
    first, tiles, offset = windows()[frame]
    value = line[:, first * LANES : (first + tiles) * LANES]
    if offset:
        value = pltpu.roll(value, tiles * LANES - offset, 1)
    return value[:, : 2 * LANES]


def pack_rows(parts):
    tiles = [None] * 13
    for frame, value in enumerate(parts):
        first, count, offset = windows()[frame]
        if count == 3:
            value = jnp.concatenate([value, jnp.zeros((value.shape[0], LANES), value.dtype)], 1)
        if offset:
            value = pltpu.roll(value, offset, 1)
        for index in range(count):
            piece = value[:, index * LANES : (index + 1) * LANES]
            place = first + index
            tiles[place] = piece if tiles[place] is None else tiles[place] + piece
    return tiles


def assemble(first, second, third):
    blank = jnp.zeros_like(first)
    lane = lax.broadcasted_iota(jnp.int32, (first.shape[0], 2 * LANES), 1)
    plain = pltpu.roll(jnp.concatenate([first, blank], 1), 2 * LANES - REDUCED, 1)
    middle = pltpu.roll(jnp.concatenate([second, blank], 1), PLAIN, 1)
    pool = pltpu.roll(jnp.concatenate([third, blank], 1), PLAIN + WIDE + NARROW, 1)
    return jnp.where(lane < PLAIN, plain, 0.0) + middle + pool


def separate(value):
    lane = lax.broadcasted_iota(jnp.int32, (value.shape[0], LANES), 1)
    plain = pltpu.roll(value, REDUCED, 1)[:, :LANES]
    middle = pltpu.roll(value, 2 * LANES - PLAIN, 1)[:, :LANES]
    pool = pltpu.roll(value, 2 * LANES - PLAIN - WIDE - NARROW, 1)[:, :LANES]
    first = jnp.where((lane >= REDUCED) & (lane < DENSE), plain, 0.0)
    second = jnp.where(lane < WIDE + NARROW, middle, 0.0)
    third = jnp.where(lane < POOL, pool, 0.0)
    return first, second, third


def span_blocks(size, span, one, leaving=(), rolled=False):
    first, count = size.cells_of(span)
    total, whole = span[1] // LANES, count // size.group

    def block(index, cells):
        start = index * LANES
        start = start if isinstance(start, int) else pl.multiple_of(start, LANES)
        one(first + index * size.group, cells, pl.ds(start, LANES))

    def four(index, carry):
        for extra in range(4):
            block(index * 4 + extra, size.group)
        for stream in leaving:
            stream.flush(index)
        return carry

    groups = whole // 4 if rolled else 0
    if rolled:
        lax.fori_loop(0, groups, four, 0)
    for index in range(groups * 4, total):
        block(index, min(size.group, count - index * size.group))
        if index % 4 == 3 or index == total - 1:
            for stream in leaving:
                stream.flush(index // 4)


def span_parts(size, span):
    return column_parts(size, span, 4 * LANES)


def unpack_kernel(size, raw, out, scratch):
    side, frames = size.side, size.frames
    pairs_of = frames // 8
    def line(row, carry):
        raw.ready(row)
        value = raw[pl.ds(row * side, side)].astype(F32).reshape(pairs_of * side, 8 * QUARTER)
        for frame in range(8):
            place = pl.ds(row * side * frames + frame, pairs_of * side, stride=8)
            piece = unpack_rows(value, frame)
            scratch[0, place, :] = piece[:, :LANES]
            scratch[1, place, :] = piece[:, LANES:]
        return carry

    lax.fori_loop(0, side, line, 0)

    def one(cell, cells, lanes):
        start = cell * frames
        for tile, (low, high) in enumerate(((0, LANES), (LANES, QUARTER))):
            value = scratch[tile, pl.ds(start, cells * frames), :].reshape(cells, frames, LANES)
            out[low:high, lanes] = turn(size, value, cells)[: high - low].astype(BF16)

    span_blocks(size, size.whole, one, (out,))


def grad_kernel(size, raw, first, second, third, scratch):
    side, frames = size.side, size.frames

    def line(row, carry):
        value = raw[0, row].astype(F32)
        for frame in range(8):
            place = pl.ds(row * side * frames + frame, side, stride=frames)
            part = unpack_rows(value, frame)
            scratch[0, place, :] = part[:, :LANES]
            scratch[1, place, :] = part[:, LANES:]
        return carry

    unrolled(side, line, 0)
    parts = separate(jnp.concatenate([scratch[0], scratch[1]], 1))
    for ref, part in zip((first, second, third), parts):
        ref[...] = part.reshape(ref.shape)


def dot(left, right, dims=((1,), (0,))):
    return lax.dot_general(left, right, (dims, ((), ())), preferred_element_type=F32)


def into_padded(size, flat, field):
    side = size.side
    field[...] = jnp.zeros_like(field)

    def line(row, carry):
        field[row + 1, 1 : side + 1] = flat[pl.ds(row * side, side)]
        return carry

    unrolled(side, line, 0)


def stacked_weights(me, positions, w_ref, stacked):
    for index, position in enumerate(positions):
        stacked[index * QUARTER : (index + 1) * QUARTER] = w_ref[me[0] ^ position]


def each_column(size, body, carry):
    plan = size.columns_of(size.whole)
    _, width, _, cells = plan[0]

    def step(index, carry):
        return body(index, pl.multiple_of(index * width, LANES), width, index * cells, cells, carry)

    if len(plan) > 1:
        carry = lax.fori_loop(0, len(plan) - 1, step, carry)
    return body(len(plan) - 1, *plan[-1], carry)


def project_begin_kernel(size, me, x0, x1, w_ref, dense, pool, stacked, stack):
    frames = size.frames
    stacked_weights(me, (0, 1), w_ref, stacked)

    def column(index, start, width, first, cells, carry):
        for x in (x0, x1):
            x.ready(index)
        value = dot(stack[:, pl.ds(start, width)], stacked[...], ((0,), (0,)))
        value = value.reshape(width // frames, frames, 2 * LANES)[:cells]
        dense[pl.ds(first, cells)] = value[:, :, :LANES]
        pool[pl.ds(first, cells)] = value[:, :, LANES:]
        dense.flush(index)
        pool.flush(index)
        return carry

    each_column(size, column, 0)


def project_kernel(size, positions, me, *refs):
    side, frames = size.side, size.frames
    pieces, (w_ref, mask, table), refs = refs[: len(positions)], refs[len(positions) : len(positions) + 3], refs[len(positions) + 3 :]
    begun = refs[:2] if len(positions) < 4 else None
    z0, z1, stat, wire, field, flat, stacked, stack = refs[-8:]
    stacked_weights(me, positions, w_ref, stacked)
    blank = jnp.zeros((frames, LANES), F32)
    total, squares = blank, blank

    def column(index, start, width, first, cells, carry):
        total, squares = carry
        for x in pieces:
            x.ready(index)
        value = dot(stack[:, pl.ds(start, width)], stacked[...], ((0,), (0,)))
        value = value.reshape(width // frames, frames, 2 * LANES)[:cells]
        dense, pool = value[:, :, :LANES], value[:, :, LANES:]
        place = pl.ds(first, cells)
        if begun:
            for stream in begun:
                stream.ready(index)
            dense += begun[0][place]
            pool += begun[1][place]
        z0[place] = dense
        z0.flush(index)
        flat[place] = pool
        return total + jnp.sum(dense, 0), squares + jnp.sum(dense * dense, 0)

    total, squares = each_column(size, column, (total, squares))
    valid = mask[0]
    total, squares = collapse(total * valid), collapse(squares * valid)
    count = collapse(valid) * size.cells
    mean = total / count

    def one(cell, cells, lanes):
        wire[:, lanes] = turn(size, z0[pl.ds(cell, cells)] - mean, cells)[:REDUCED].astype(BF16)

    span_blocks(size, size.whole, one, (), True)
    into_padded(size, flat, field)

    def line(row, carry):
        pool_total, pool_squares = carry
        pool = pool_line(size, field, row, mask)
        z1[pl.ds(row * side, side)] = pool
        z1.flush(row)
        return pool_total + jnp.sum(pool, 0), pool_squares + jnp.sum(pool * pool, 0)

    pool_total, pool_squares = lax.fori_loop(0, side, line, (blank, blank))
    rows = [total, squares, collapse(pool_total * valid), collapse(pool_squares * valid), count]
    publish(stat, rows + [table[0:1], table[1:2]])


def normed_kernel(size, me, z0, z1, totals, table, mask, *refs):
    outs, (field, pooled) = refs[:-2], refs[-2:]
    side, frames, step = size.side, size.frames, size.step
    lane = lax.broadcasted_iota(jnp.int32, (frames, LANES), 1)
    field[...] = jnp.zeros_like(field)
    rows = [norm_rows(totals, table, tile, me[0]) for tile in range(2)]
    scales = [(gain * inverse * inverse, mean) for mean, inverse, gain, _, _ in rows]

    def chunk(index, carry):
        z1.ready(index)
        scale, mean = scales[1]
        value = (z1[pl.ds(index * step, step)] - mean) * scale
        value = jnp.where(lane == POOL, 1.0, value) * mask[0]
        field[pl.ds(1 + index * size.band, size.band), 1 : side + 1] = value.reshape(size.band, side, frames, LANES)
        return carry

    rolled(size.chunks, chunk, 0)
    pool_lines(size, field, pooled, mask)
    for index in range(size.chunks):
        z0.ready(index)
    for part, span in enumerate(size.parts):
        normed, shapes = outs[2 * part : 2 * part + 2]

        def one(cell, cells, lanes, normed=normed, shapes=shapes):
            scale, mean = scales[0]
            value = (z0[pl.ds(cell, cells)] - mean) * scale
            dense = turn(size, jnp.where(lane == DENSE, 1.0, value) * mask[0], cells)
            pool = turn(size, pooled[pl.ds(cell, cells)], cells)
            normed[0:DENSE, lanes] = dense[:DENSE].astype(BF16)
            normed[DENSE:ROWS, lanes] = pool[:POOL].astype(BF16)
            both = jnp.concatenate([dense[DENSE : DENSE + 8], pool[POOL : POOL + 8]], 0)
            shapes[:, lanes] = both.astype(BF16)

        span_blocks(size, span, one, (normed,), True)


def pool_lines(size, field, pooled, mask):
    def line(row, carry):
        pooled[pl.ds(row * size.side, size.side)] = pool_line(size, field, row, mask)
        return carry

    lax.fori_loop(0, size.side, line, 0)


def moments_kernel(size, me, *refs):
    (out, stack), pieces = refs[-2:], refs[-6:-2]
    lefts = refs[:-6]
    each = len(lefts) // len(size.parts)
    lefts = [lefts[part * each : (part + 1) * each] for part in range(len(size.parts))]
    lefts = [group[0][...] if each == 1 else jnp.concatenate([item[...] for item in group], 0) for group in lefts]
    value = jnp.zeros((4 * QUARTER, lefts[0].shape[0]), F32)
    for part, (left, (start, count)) in enumerate(zip(lefts, size.parts)):
        for x in pieces:
            x.ready(part)
        value += dot(stack[:, start : start + count], left, ((1,), (1,)))
    for position in range(4):
        piece = value[position * QUARTER : (position + 1) * QUARTER]
        piece = jnp.concatenate([piece, jnp.zeros((2 * LANES - QUARTER, piece.shape[1]), F32)], 0)
        out[me[0] ^ position] = piece.T


def back_columns(back, owner):
    if len(back.shape) == 2:
        return columns_of_table(back[...])
    return columns_of_table(back_table(back, owner))


def back_table(back, owner):
    every = owner_rows(back, owner)
    total, own = jnp.sum(every, 0), every[0]
    count = own[6:7]
    rows = [total[1:2] / count, total[3:4] / count, own[4:5] * total[0:1] / count, own[5:6] * total[2:3] / count]
    return row_table(rows)


def columns_of_table(table):
    turned = table.T
    slope = jnp.concatenate([turned[:DENSE, 0:1], turned[:POOL, 1:2]], 0)
    offset = jnp.concatenate([turned[:DENSE, 2:3], turned[:POOL, 3:4]], 0)
    return slope, offset


def weight_grad_kernel(size, me, inner, moments, back, kernels, out, table, grads, flat):
    table[...] = back_table(back, me[0])
    slope, offset = columns_of_table(table[...])
    for owner in range(4):
        shape = moments[owner, ROWS : ROWS + 16]
        value = inner[owner] - slope * moments[owner, 0:ROWS]
        first = value[:DENSE] - offset[:DENSE] * shape[0:1]
        last = value[DENSE:] - offset[DENSE:] * shape[8:9]
        value = jnp.concatenate([first, last], 0)
        grads[owner, 0] = value[:, :LANES]
        grads[owner, 1] = value[:, LANES:]
    parts = []
    for extra in range(2):
        rows = pl.ds(extra, ROWS // 2, stride=2)
        for owner in range(4):
            parts.append(jnp.concatenate([grads[owner, 0, rows, :], grads[owner, 1, rows, :]], 1))
    for place, tile in enumerate(pack_rows(parts)):
        flat[pl.ds(place, ROWS // 2, stride=PAIR_TILES), :] = tile
    used = ROWS // 2 * PAIR_TILES
    flat[used:, :] = jnp.zeros((DENSE_ROWS - used, LANES), F32)
    out[:KERNEL_ROWS, :] = kernels[...]
    out[KERNEL_ROWS : KERNEL_ROWS + DENSE_ROWS, :] = flat[...].astype(BF16)
    rest = out.shape[0] - KERNEL_ROWS - DENSE_ROWS
    if rest:
        out[KERNEL_ROWS + DENSE_ROWS :, :] = jnp.zeros((rest, LANES), BF16)


def pool_line(size, field, row, mask):
    side = size.side
    lines = field[pl.ds(row, 3)]
    column = lines[0] + lines[1] + lines[2]
    value = column[0:side] + column[1 : side + 1] + column[2 : side + 2]
    return time_box(value, mask) * (1.0 / 27.0)


def turn(size, value, cells):
    flat = value.reshape(cells * size.frames, value.shape[-1])
    if cells < size.group:
        blank = jnp.zeros((LANES - cells * size.frames, value.shape[-1]), value.dtype)
        flat = jnp.concatenate([flat, blank], 0)
    return flat.T


def conv_kernel(size, me, group, p0, p1, p2, p3, totals, lanes_valid, kernel, mask, field, z2, stat, joined):
    side, frames, step = size.side, size.frames, size.step
    for position, piece in enumerate((p0, p1, p2, p3)):
        owner = me[0] ^ position
        every = owner_rows(totals, owner)
        total = jnp.sum(every, 0)
        sent = totals[pl.ds(group[0], 1), pl.ds(owner, 1)].reshape(8, LANES)
        mean = total[0:1] / total[4:5]
        variance = total[1:2] / total[4:5] - mean * mean
        scale = sent[5:6] * lax.rsqrt(variance + EPSILON)
        offset = (sent[0:1] / sent[4:5] - mean) * scale + sent[6:7]
        turned = row_table([scale, offset]).T
        scale, offset = turned[:REDUCED, 0:1], turned[:REDUCED, 1:2]
        shifted = piece[...].astype(F32) * scale + offset
        value = shifted * sigmoid(shifted)
        joined[pl.ds(pl.multiple_of(owner * MID, 8), MID), :] = value[:MID]
        joined[pl.ds(pl.multiple_of(4 * MID + owner * SMALL, 8), SMALL), :] = value[MID:]
    field[...] = jnp.zeros_like(field)
    joined[4 * REDUCED :, :] = jnp.zeros((2 * LANES - 4 * REDUCED, size.padded), F32)

    def one(first, cells, lanes):
        value = (joined[:, lanes] * lanes_valid[0:1]).T
        value = value.reshape(size.group, frames, 2 * LANES).astype(size.kept)
        for index in range(cells):
            cell = first + index
            row = cell // side if isinstance(cell, int) else lax.div(cell, side)
            field[row + 1, cell - row * side + 1] = value[index]

    span_blocks(size, size.whole, one)
    field.flush(0)
    kernel.ready(0)
    blank = jnp.zeros((frames, LANES), F32)

    def chunk(index, carry):
        total, squares = carry
        parts = []
        for row in range(3):
            for column in range(3):
                part = field[pl.ds(index * size.band + row, size.band), column : column + side]
                parts.append(part.reshape(step * frames, 2 * LANES).astype(BF16))
        value = dot(jnp.concatenate(parts, 1), kernel[...].reshape(18 * LANES, LANES))
        value = time_box(value.reshape(step, frames, LANES), mask) * (1.0 / 3.0)
        z2[pl.ds(index * step, step)] = value
        z2.flush(index)
        return total + jnp.sum(value, 0), squares + jnp.sum(value * value, 0)

    total, squares = unrolled(size.chunks, chunk, (blank, blank))
    valid = mask[0]
    one_row = jnp.zeros((1, LANES), F32)
    rows = [collapse(total * valid), collapse(squares * valid), one_row, one_row, collapse(valid) * size.cells]
    publish(stat, rows)


def halve_into(size, value, scratch, index):
    half = size.side // 2
    value = value.reshape(2, half, 2, size.frames, LANES)
    value = value[0] + value[1]
    value = value[:, 0] + value[:, 1]
    rows = half * size.frames
    scratch[pl.ds(index * rows, rows), :] = value.reshape(rows, LANES)


def halved_rows(scratch):
    count = scratch.shape[0] // 2
    return (scratch[pl.ds(0, count, stride=2), :] + scratch[pl.ds(1, count, stride=2), :]) * 0.125


def first_half_kernel(size, me, z0, z1, totals, table, mask, h0, h1, s0, s1):
    for tile, (z, out, scratch) in enumerate(((z0, h0, s0), (z1, h1, s1))):
        rows = norm_rows(totals, table, tile, me[0])

        def chunk(index, carry, z=z, scratch=scratch, rows=rows):
            z.ready(index)
            value = activate(z[pl.ds(index * size.step, size.step)], rows, mask)
            halve_into(size, value, scratch, index)
            return carry

        rolled(size.chunks, chunk, 0)
        out[...] = halved_rows(scratch).reshape(out.shape)


def second_half_kernel(size, z2, totals, table, mask, h0, h1, out, scratch):
    rows = norm_rows(totals, table, 0)

    def chunk(index, carry):
        z2.ready(index)
        value = activate(z2[pl.ds(index * size.step, size.step)], rows, mask)
        halve_into(size, value, scratch, index)
        return carry

    rolled(size.chunks, chunk, 0)
    value = halved_rows(scratch)
    count = value.shape[0]
    value = assemble(h0[...].reshape(count, LANES), value, h1[...].reshape(count, LANES))
    value = jnp.concatenate([value, jnp.zeros((out.shape[1] - count, 2 * LANES), F32)], 0)
    out[...] = value.T[:QUARTER].astype(BF16)


def strided(scratch, start, count, stride):
    place = pl.ds(start, count, stride=stride)
    return jnp.concatenate([scratch[0, place, :], scratch[1, place, :]], 1)


def output_kernel(size, me, z0, z1, z2, totals, totals2, table, table2, mask, out, scratch):
    side, frames = size.side, size.frames
    parts = [
        activate(z[...], norm_rows(total, tab, tile, me[0]), mask).reshape(size.rows, LANES)
        for z, total, tab, tile in ((z0, totals, table, 0), (z2, totals2, table2, 0), (z1, totals, table, 1))
    ]
    value = assemble(*parts)
    scratch[0] = value[:, :LANES]
    scratch[1] = value[:, LANES:]

    def line(row, carry):
        start = row * side * frames
        lines = [strided(scratch, start + frame, side, frames) for frame in range(8)]
        for place, tile in enumerate(pack_rows(lines)):
            out[0, row, :, place * LANES : (place + 1) * LANES] = tile.astype(BF16)
        return carry

    unrolled(side, line, 0)


def spread(size, grad, scratch):
    value = grad[...].reshape(-1, LANES)
    count = value.shape[0]
    scratch[pl.ds(0, count, stride=2), :] = value
    scratch[pl.ds(1, count, stride=2), :] = value


def grad_chunk(size, grad, scratch, index):
    if scratch is None:
        return grad[pl.ds(index * size.step, size.step)]
    half = size.side // 2
    rows = half * size.frames
    value = scratch[pl.ds(index * rows, rows), :].reshape(half, 1, size.frames, LANES)
    value = jnp.broadcast_to(value, (half, 2, size.frames, LANES)).reshape(1, size.side, size.frames, LANES)
    value = jnp.broadcast_to(value, (2, size.side, size.frames, LANES))
    return value.reshape(size.step, size.frames, LANES)


def second_sums_kernel(size, grad, z2, totals, table, mask, stat, *scratch):
    scratch = scratch[0] if scratch else None
    if scratch is not None:
        spread(size, grad, scratch)
    rows = norm_rows(totals, table, 0)
    blank = jnp.zeros((size.frames, LANES), F32)

    def chunk(index, carry):
        shift_grad, gain_grad = carry
        z2.ready(index)
        value = z2[pl.ds(index * size.step, size.step)]
        inner, normed = inner_grad(grad_chunk(size, grad, scratch, index), value, rows, mask)
        return shift_grad + jnp.sum(inner, 0), gain_grad + jnp.sum(inner * normed, 0)

    shift_grad, gain_grad = rolled(size.chunks, chunk, (blank, blank))
    publish(stat, [collapse(shift_grad), collapse(gain_grad)])


def conv_back_kernel(size, me, grad, z2, totals, back, table, mask, kernel, delta, o0, o1, o2, field, result, turned, *scratch):
    side, frames, step = size.side, size.frames, size.step
    scratch = scratch[0] if scratch else None
    if scratch is not None:
        spread(size, grad, scratch)
    rows = norm_rows(totals, table, 0)
    field[...] = jnp.zeros_like(field)

    def first(index, carry):
        z2.ready(index)
        value = z2[pl.ds(index * step, step)]
        inner, _ = inner_grad(grad_chunk(size, grad, scratch, index), value, rows, mask)
        value = norm_delta(inner, value, rows, back, 0, mask).astype(BF16).astype(size.kept)
        delta[pl.ds(index * step, step)] = value
        delta.flush(index)
        field[pl.ds(1 + index * size.band, size.band), 1 : side + 1] = value.reshape(size.band, side, frames, LANES)
        return carry

    unrolled(size.chunks, first, 0)
    kernel.ready(0)

    def chunk(index, carry):
        parts = []
        for row in range(3):
            for column in range(3):
                part = field[pl.ds(index * size.band + 2 - row, size.band), 2 - column : 2 - column + side]
                parts.append(part.reshape(step * frames, LANES).astype(BF16))
        value = dot(jnp.concatenate(parts, 1), kernel[...].reshape(9 * LANES, 4 * REDUCED))
        result[pl.ds(index * step, step)] = value.reshape(step, frames, 4 * REDUCED)
        return carry

    unrolled(size.chunks, chunk, 0)

    def one(cell, cells, lanes):
        turned[:, lanes] = turn(size, result[pl.ds(cell, cells)], cells)

    span_blocks(size, size.whole, one)
    for position, (out, start) in enumerate(((o0, 0), (o1, 0), (o2, 0), (o2, REDUCED))):
        owner = me[0] ^ position
        mid = turned[pl.ds(pl.multiple_of(owner * MID, 8), MID), :]
        small = turned[pl.ds(pl.multiple_of(4 * MID + owner * SMALL, 8), SMALL), :]
        out[start : start + REDUCED] = jnp.concatenate([mid, small], 0).astype(BF16)


def kernel_grad_kernel(size, field, delta, mask, out, turned, boxed, taps, flat):
    side, frames, step = size.side, size.frames, size.step

    def chunk(index, carry):
        delta.ready(index)
        place = pl.ds(index * step, step)
        boxed[place] = time_box(delta[place].astype(F32), mask)
        return carry

    rolled(size.chunks, chunk, 0)

    def one(cell, cells, lanes):
        value = turn(size, boxed[pl.ds(cell, cells)], cells)
        upper = value.astype(BF16)
        turned[:LANES, lanes] = upper
        turned[LANES:, lanes] = (value - upper.astype(F32)).astype(BF16)

    span_blocks(size, size.whole, one, (), True)
    for row in range(side + 2):
        field.ready(row)

    def tap(index, carry):
        row = index // 3
        part = field[pl.ds(row, side), pl.ds(index - 3 * row, side)].reshape(size.rows, 2 * LANES).astype(BF16)
        value = dot(turned[:, : size.rows], part)
        value = (value[:LANES] + value[LANES:]) * (1.0 / 3.0)
        taps[index, 0] = value[:, :LANES]
        taps[index, 1] = value[:, LANES:]
        return carry

    for index in range(9):
        tap(index, 0)
    lane = lax.broadcasted_iota(jnp.int32, (WIDE // 4, LANES), 1)
    tiles = [None] * MID_TILES

    def add(place, value):
        tiles[place] = value if tiles[place] is None else tiles[place] + value

    for extra in range(4):
        for tap in range(9):
            rows = pl.ds(extra, WIDE // 4, stride=4)
            rest = jnp.where(lane < 4 * MID - LANES, taps[tap, 1, rows, :], 0.0)
            offset = (extra * 9 + tap) * 4 * MID
            value = jnp.concatenate([taps[tap, 0, rows, :], rest, jnp.zeros_like(rest)], 1)
            value = pltpu.roll(value, offset % LANES, 1)
            for index in range(-(-(offset % LANES + 4 * MID) // LANES)):
                add(offset // LANES + index, value[:, index * LANES : (index + 1) * LANES])
    for place, tile in enumerate(tiles):
        flat[pl.ds(place, WIDE // 4, stride=MID_TILES), :] = tile
    lane = lax.broadcasted_iota(jnp.int32, (NARROW // 4, LANES), 1)
    tiles = [None] * SMALL_TILES
    start = 4 * MID - LANES
    for extra in range(4):
        for tap in range(9):
            value = taps[tap, 1, pl.ds(WIDE + extra, NARROW // 4, stride=4), :]
            value = jnp.where((lane >= start) & (lane < start + 4 * SMALL), value, 0.0)
            offset = (extra * 9 + tap) * 4 * SMALL
            value = pltpu.roll(value, (offset - start) % LANES, 1)
            add(offset // LANES, value)
    for place, tile in enumerate(tiles):
        flat[pl.ds(MID_ROWS + place, NARROW // 4, stride=SMALL_TILES), :] = tile
    flat[MID_ROWS + SMALL_ROWS :, :] = jnp.zeros((KERNEL_ROWS - MID_ROWS - SMALL_ROWS, LANES), F32)
    out[...] = flat[...].astype(BF16)


def first_sums_kernel(size, me, p0, p1, p2, p3, g0, g1, z0, z1, totals, table, mask, *refs):
    side, step, frames = size.side, size.step, size.frames
    count = len(size.parts)
    stat, outs, (field, padded, pooled, *scratch) = refs[0], refs[1 : 1 + count], refs[1 + count :]
    s0, s1 = scratch if scratch else (None, None)
    if scratch:
        spread(size, g0, s0)
        spread(size, g1, s1)
    padded[...] = jnp.zeros_like(padded)

    def one(cell, cells, place):
        value = p0[:, place].astype(F32) + p1[:, place].astype(F32)
        value += p2[:REDUCED, place].astype(F32) + p3[REDUCED:, place].astype(F32)
        value = jnp.concatenate([value, jnp.zeros((LANES - REDUCED, LANES), F32)], 0).T
        value = value.reshape(size.group, frames, LANES)
        field[pl.ds(cell, cells)] = value[:cells]

    span_blocks(size, size.whole, one)
    rows0 = norm_rows(totals, table, 0, me[0])
    rows1 = norm_rows(totals, table, 1, me[0])
    blank = jnp.zeros((frames, LANES), F32)

    def chunk(index, carry):
        place = pl.ds(index * step, step)
        z0.ready(index)
        z1.ready(index)
        grad = time_box(field[place], mask) * (1.0 / 3.0) + grad_chunk(size, g0, s0, index)
        inner0, normed0 = inner_grad(grad, z0[place], rows0, mask)
        inner1, normed1 = inner_grad(grad_chunk(size, g1, s1, index), z1[place], rows1, mask)
        field[place] = scales[0] * inner0
        pool = scales[1] * inner1
        padded[pl.ds(1 + index * size.band, size.band), 1 : side + 1] = pool.reshape(size.band, side, frames, LANES)
        sums = (inner0, inner0 * normed0, inner1, inner1 * normed1)
        return tuple(old + jnp.sum(new, 0) for old, new in zip(carry, sums))

    scales = [rows[2] * rows[1] for rows in (rows0, rows1)]
    sums = unrolled(size.chunks, chunk, (blank,) * 4)
    publish(stat, [collapse(item) for item in sums] + scales + [rows0[4]])
    stat.flush(0)
    pool_lines(size, padded, pooled, mask)
    for out, span in zip(outs, size.parts):

        def turned(cell, cells, lanes, out=out):
            out[0:DENSE, lanes] = turn(size, field[pl.ds(cell, cells)], cells)[:DENSE].astype(BF16)
            out[DENSE:ROWS, lanes] = turn(size, pooled[pl.ds(cell, cells)], cells)[:POOL].astype(BF16)

        span_blocks(size, span, turned, (out,))


def input_rows(size, me, groups, weights, block, back, scratch, stacked):
    flat_row, pool_row = jnp.zeros((1, 2 * LANES), F32), jnp.zeros((1, 2 * LANES), F32)
    for position, weight in enumerate(weights):
        slope, offset = back_columns(back[position] if len(back) == 4 else back[0], me[0] ^ position)
        stacked[position * ROWS : (position + 1) * ROWS] = weight[block]
        value = weight[block].astype(F32)
        stacked[(position + 4) * ROWS : (position + 5) * ROWS] = (value * -slope).astype(BF16)
        value = value * offset
        flat_row -= collapse(value[:DENSE])
        pool_row -= collapse(value[DENSE:])
    index = lax.broadcasted_iota(jnp.int32, (16, 2 * LANES), 0)
    fixed = jnp.where(index == 0, flat_row, 0.0) + jnp.where(index == 8, pool_row, 0.0)
    stacked[8 * ROWS :] = fixed.astype(BF16)
    for streams, stack, columns in groups:
        for part, start, width, row in columns:
            for stream in streams:
                stream.ready(part)
            value = dot(stack[:, start : start + width], stacked[...], ((0,), (0,)))
            scratch[0, row : row + width, :] = value[:, :LANES]
            scratch[1, row : row + width, :] = value[:, LANES:]


def input_half_kernel(size, me, *refs):
    streams, weights, (back,) = refs[:9], refs[9:13], refs[13:14]
    first, second, third, scratch, stacked, stack = refs[14:]
    columns = [(part, start, width, start) for part, (start, width, _, _) in enumerate(size.columns_of(size.whole))]
    input_rows(size, me, [(streams, stack, columns)], weights, 1, (back,), scratch, stacked)
    value = jnp.concatenate([scratch[0, : size.rows, :], scratch[1, : size.rows, :]], 1)
    parts = separate(value * 0.125)
    for ref, part in zip((first, second, third), parts):
        ref[...] = part.reshape(ref.shape)


def input_half_sums_kernel(size, above, me, *refs):
    pieces, (z2, totals, table, mask), refs = refs[:14], refs[14:18], refs[18:]
    (first, second, third, stat), (scratch, stacked, wide), (stack,) = refs[:4], refs[4:7], refs[7:]
    input_half_kernel(size, me, *pieces, first, second, third, scratch, stacked, stack)
    second_sums_kernel(above, second, z2, totals, table, mask, stat, wide)


def input_plan(size, part):
    bounds = [0]
    for span in size.parts:
        first, count = size.cells_of(span)
        bounds.append((first + count) // size.side)
    low, high = bounds[part], bounds[part + 1]
    start = low * size.side * size.frames // LANES * LANES
    return low, high, start


def input_kernel(size, part, me, *refs):
    side, frames = size.side, size.frames
    pairs_of = frames // 8
    low, high, base = input_plan(size, part)
    own = 9 * (2 if part else 1)
    pieces, weights, back = refs[:own], refs[own : own + 4], refs[own + 4 : own + 8]
    refs = refs[own + 8 + (1 if part else 0) :]
    (out, scratch, stacked), stacks = refs[:3], refs[3:]
    begin = size.parts[part][0]
    columns = [(index, start, width, begin + start - base) for index, (start, width, _, _) in enumerate(size.columns_of(size.parts[part]))]
    groups = [(pieces[:9], stacks[0], columns)]
    if part:
        tail = (0, base - size.parts[part - 1][0], begin - base, 0)
        groups.append((pieces[9:], stacks[1], [tail]))
    input_rows(size, me, groups, weights, 0, back, scratch, stacked)

    def line(index, carry):
        row = low + index
        start = row * side * frames - base
        lines = [strided(scratch, start + frame, pairs_of * side, 8) for frame in range(8)]
        for place, tile in enumerate(pack_rows(lines)):
            lanes = slice(place * LANES, (place + 1) * LANES)
            out[pl.ds(row * side, side), :, lanes] = tile.reshape(side, pairs_of, LANES)
        out.flush(index)
        return carry

    for index in range(high - low):
        line(index, 0)


def pairs(axis_size, shift):
    return [(index, index ^ shift) for index in range(axis_size)]


def gather_four(piece):
    other = lax.ppermute(piece, "chan", pairs(4, 2))
    core = lax.ppermute(piece, "chan", pairs(4, 1))
    both = lax.ppermute(other, "chan", pairs(4, 1))
    return piece, core, other, both


def exchange_four(pieces):
    result = [pieces[0]]
    for shift in (1, 2, 3):
        result.append(lax.ppermute(pieces[shift], "chan", pairs(4, shift)))
    return result


def share(stat):
    return lax.all_to_all(stat, "dp", 0, 0, tiled=True)


def share_all(stat, count):
    return lax.all_to_all(stat, ("dp", "chan"), 0, 0, tiled=True).reshape(count, 4, 8, LANES)


def swap_shares(rows, count):
    return lax.all_to_all(rows.reshape(count, -1, LANES), "dp", 0, 0, tiled=True)


def shares_kernel(*refs):
    *swapped, out = refs
    start = 0
    for ref in swapped:
        count = ref.shape[1]
        value = jnp.sum(ref[...].astype(F32), 0).astype(BF16)
        for device in range(out.shape[0]):
            out[device, start : start + count] = value
        start += count


def all_shares(swapped):
    rows = sum(item.shape[1] for item in swapped)
    (whole,) = call(shares_kernel, [shaped((swapped[0].shape[0], rows, LANES), BF16)], [], [], swapped)
    return lax.all_to_all(whole, "dp", 0, 0, tiled=True)


def other_of(rows, bit, count):
    return lax.ppermute(rows, "dp", pairs(count, 1 << bit))


def joined_halves(group, bit, mine, others):
    low = (group[0] >> bit) & 1
    return jnp.where(low == 0, jnp.concatenate([mine, others], 0), jnp.concatenate([others, mine], 0))


def together(*values):
    return lax.optimization_barrier(values)


def as_rows(flat):
    return flat.reshape(2, -1, LANES).transpose(1, 0, 2).reshape(-1, LANES)


def as_flat(rows):
    return rows.reshape(-1, 2, LANES).transpose(1, 0, 2).reshape(2, -1)


NORM_LANES = (
    (0, REDUCED, PLAIN, 0),
    (0, 0, MID, 64),
    (2, 0, WIDE, 104),
    (0, MID, SMALL, 184),
    (2, WIDE, NARROW, 192),
    (1, 0, POOL, 224),
)


def shifted_lanes(value, source, width, target):
    lane = lax.broadcasted_iota(jnp.int32, value.shape, 1)
    value = jnp.where((lane >= source) & (lane < source + width), value, 0.0)
    return pltpu.roll(value, (target - source) % value.shape[1], 1)


def mask_rows(length0, length1, frames, stride):
    frame = lax.broadcasted_iota(jnp.int32, (frames, LANES), 0)
    ends = (length0, length0 + length1)

    def ident(step):
        place = (frame + step) * stride
        return jnp.where(place >= ends[0], 1, 0) + jnp.where(place >= ends[1], 1, 0)

    here = ident(0)
    valid = jnp.where(frame * stride < ends[1], 1.0, 0.0)
    before = jnp.where((frame > 0) & (ident(-1) == here), 1.0, 0.0)
    after = jnp.where((frame < frames - 1) & (ident(1) == here), 1.0, 0.0)
    return valid, before, after


def prepare_kernel(me, lengths, plain, mid, small, pool, wide, narrow, gains, shifts, *refs):
    outs, (rows, dense, taps) = refs[:-3], refs[-3:]
    mask0, mask1, tables, sent, weights, kernels = outs[0], outs[1], outs[2:6], outs[6:10], outs[10:12], outs[12:14]
    turned, along = outs[14:16], outs[16:18]
    for ref, frames, stride in ((along[0], mask0.shape[1], 1), (along[1], mask1.shape[1], 2)):
        lane = lax.broadcasted_iota(jnp.int32, (8, LANES), 1)
        ref[...] = jnp.where(lax.rem(lane, frames) * stride < lengths[0] + lengths[1], 1.0, 0.0)
    for mask, stride in ((mask0, 1), (mask1, 2)):
        for index, value in enumerate(mask_rows(lengths[0], lengths[1], mask.shape[1], stride)):
            mask[index] = value
    for block in range(2):
        lines = []
        for source in (gains, shifts):
            value = source[...].astype(F32)
            line = jnp.concatenate([value[block : block + 1], value[block + 2 : block + 3]], 1)
            lines.append(jnp.broadcast_to(line, (8, 2 * LANES)))
        found = [[jnp.zeros((8, LANES), F32)] * 2 for _ in range(3)]
        for tile, lane, width, channel in NORM_LANES:
            for index, line in enumerate(lines):
                part = shifted_lanes(line, channel, width, lane)[:, :LANES]
                found[tile][index] = found[tile][index] + part
        tables[2 * block][...] = row_table([found[0][0], found[0][1], found[1][0], found[1][1]])
        tables[2 * block + 1][...] = row_table([found[2][0], found[2][1]])
    for ref, base, outputs in ((mid, 0, MID), (small, MID, SMALL), (plain, REDUCED, PLAIN), (pool, DENSE, POOL)):
        count = ref.shape[0]
        rows[:count, :] = ref[...].astype(F32)
        for block in range(2):
            tiles = [rows[pl.ds(2 * tile + block, outputs // 2, stride=2 * PAIR_TILES), :] for tile in range(PAIR_TILES)]
            line = jnp.concatenate(tiles, 1)
            for extra in range(2):
                place = pl.ds(base + extra, outputs // 2, stride=2)
                for owner in range(4):
                    part = unpack_rows(line, 4 * extra + owner)
                    dense[block, owner, 0, place, :] = part[:, :LANES]
                    dense[block, owner, 1, place, :] = part[:, LANES:]
    lane = lax.broadcasted_iota(jnp.int32, (ROWS, LANES), 1)
    blank = jnp.zeros((LANES, 2 * LANES), F32)
    for block in range(2):
        for owner in range(4):
            rest = jnp.where(lane < QUARTER - LANES, dense[block, owner, 1], 0.0)
            dense[block, owner, 1] = rest
            value = jnp.concatenate([dense[block, owner, 0], rest], 1)
            value = jnp.concatenate([value[:DENSE], blank[: LANES - DENSE], value[DENSE:], blank[: LANES - POOL]], 0)
            weights[block][owner] = value.T[:QUARTER].astype(BF16)
        for position in range(4):
            owner = me[0] ^ position
            value = jnp.concatenate([dense[block, owner, 0], dense[block, owner, 1]], 1)
            sent[position][block] = value.astype(BF16)
    wide_lane = lax.broadcasted_iota(jnp.int32, (WIDE // 4, LANES), 1)
    narrow_lane = lax.broadcasted_iota(jnp.int32, (NARROW // 4, LANES), 1)
    start = 4 * MID - LANES
    for block in range(2):
        rows[: wide.shape[0], :] = wide[...].astype(F32)
        taps[...] = jnp.zeros_like(taps)
        tiles = [rows[pl.ds(2 * tile + block, WIDE // 4, stride=2 * MID_TILES), :] for tile in range(MID_TILES)]
        tiles.append(tiles[0])
        for extra in range(4):
            for tap in range(9):
                offset = (extra * 9 + tap) * 4 * MID
                first, shift = offset // LANES, offset % LANES
                count = -(-(shift + 4 * MID) // LANES)
                value = jnp.concatenate(tiles[first : first + count], 1)
                value = pltpu.roll(value, (count * LANES - shift) % (count * LANES), 1)
                place = pl.ds(extra, WIDE // 4, stride=4)
                taps[tap, 0, place, :] = value[:, :LANES]
                taps[tap, 1, place, :] = jnp.where(wide_lane < start, value[:, LANES : 2 * LANES], 0.0)
        rows[: narrow.shape[0], :] = narrow[...].astype(F32)
        tiles = [rows[pl.ds(2 * tile + block, NARROW // 4, stride=2 * SMALL_TILES), :] for tile in range(SMALL_TILES)]
        for extra in range(4):
            for tap in range(9):
                offset = (extra * 9 + tap) * 4 * SMALL
                value = pltpu.roll(tiles[offset // LANES], (start - offset) % LANES, 1)
                value = jnp.where((narrow_lane >= start) & (narrow_lane < start + 4 * SMALL), value, 0.0)
                taps[tap, 1, pl.ds(WIDE + extra, NARROW // 4, stride=4), :] = value
        for tap in range(9):
            first, second = taps[tap, 0], taps[tap, 1]
            kernels[block][tap] = jnp.concatenate([first, second], 1)[:, : 4 * REDUCED].astype(BF16)
            turned[block][tap, :LANES] = first.T.astype(BF16)
            turned[block][tap, LANES:] = second.T.astype(BF16)


def place_rows(out, sources, count, pairs_rows):
    target = pairs_rows if out.shape[0] == 2 else out.near
    for block, (ref, start) in enumerate(sources):
        target[pl.ds(block, count, stride=2), :] = ref[start : start + count, :]
    if out.shape[0] == 2:
        for index in range(count // 4):
            value = pairs_rows[index * 8 : index * 8 + 8, :]
            for part in range(4):
                place = index * 4 + part
                out[:, place * LANES : (place + 1) * LANES] = value[2 * part : 2 * part + 2]


def finish_kernel(me, group, early, halves, late, first0, first1, second0, second1, *refs):
    outs, (rows, other, pairs_rows) = refs[:-3], refs[-3:]
    mid, small, plain, pool, wide, narrow, gains, shifts = outs
    count, share = late.shape[:2]
    bits = count.bit_length() - 1
    low = group[0] & 1
    for index in range(count // 2):
        device = sum(((index >> bit) & 1) << (bits - 1 - bit) for bit in range(bits))
        place = slice(index * share, (index + 1) * share)
        rows[pl.ds(pl.multiple_of((device + low) * share, 16), share)] = early[place].astype(F32)
        rows[pl.ds(pl.multiple_of((device + 1 - low) * share, 16), share)] = halves[place].astype(F32)
    late.ready(0)
    for device in range(late.shape[0]):
        place = slice(device * share, (device + 1) * share)
        other[place] = late[device].astype(F32)
    place_rows(wide, ((other, 0), (rows, 0)), MID_ROWS, pairs_rows)
    wide.flush(0)
    place_rows(narrow, ((other, MID_ROWS), (rows, MID_ROWS)), SMALL_ROWS, pairs_rows)
    start = KERNEL_ROWS
    for out, outputs in ((mid, MID), (small, SMALL), (plain, PLAIN), (pool, POOL)):
        count = outputs * CIN // LANES
        place_rows(out, ((other, start), (rows, start)), count, pairs_rows)
        start += count
    for block, first_ref, second_ref in ((0, first0, second0), (1, first1, second1)):
        first = jnp.sum(owner_rows(first_ref, me[0]), 0)
        second = jnp.sum(second_ref[...], 0)
        for out, row in ((gains, 1), (shifts, 0)):
            lines = (first[row : row + 1], first[row + 2 : row + 3], second[row : row + 1])
            total = jnp.zeros((8, 2 * LANES), F32)
            for tile, lane, width, channel in NORM_LANES:
                line = jnp.concatenate([lines[tile], jnp.zeros((1, LANES), F32)], 1)
                total += shifted_lanes(jnp.broadcast_to(line, (8, 2 * LANES)), lane, width, channel)
            out[block : block + 1, :] = total[0:1, :LANES]
            out[block + 2 : block + 3, :] = total[0:1, LANES:]


def project(size, me, pieces, positions, dense, mask, table, everyone, begun=()):
    side, cells, frames = size.side, size.cells, size.frames
    tile = shaped((cells, frames, LANES))
    count = len(positions)
    column_cells = (0, [(first, held) for _, _, first, held in size.columns_of(size.whole)])
    ins = {index: column_parts(size, size.whole) for index in range(count)}
    ins |= {count + 3 + index: column_cells for index in range(len(begun))}
    return call(
        functools.partial(project_kernel, size, positions),
        [tile, tile, shaped((everyone, 8, LANES)), shaped((REDUCED, size.padded), BF16)],
        [
            pltpu.VMEM((side + 2, side + 2, frames, LANES), F32),
            pltpu.VMEM((cells, frames, LANES), F32),
            pltpu.VMEM((count * QUARTER, 2 * LANES), BF16),
        ],
        [me],
        [*pieces, dense, mask, table, *begun],
        ins=ins,
        puts={0: column_cells, 1: line_parts(size)},
        stacks=[range(count)],
    )


def project_begin(size, me, pieces, dense):
    tile = shaped((size.cells, size.frames, LANES))
    column_cells = (0, [(first, held) for _, _, first, held in size.columns_of(size.whole)])
    return call(
        functools.partial(project_begin_kernel, size),
        [tile, tile],
        [pltpu.VMEM((2 * QUARTER, 2 * LANES), BF16)],
        [me],
        [*pieces, dense],
        ins={index: column_parts(size, size.whole) for index in range(2)},
        puts={0: column_cells, 1: column_cells},
        stacks=[range(2)],
    )


def normed_wires(size, me, z0, z1, totals, table, mask):
    outs, puts = [], {}
    for part, (_, lanes) in enumerate(size.parts):
        outs += [shaped((ROWS, lanes), BF16), shaped((16, lanes), BF16)]
        puts[2 * part] = span_parts(size, size.parts[part])
    wires = call(
        functools.partial(normed_kernel, size),
        outs,
        [
            pltpu.VMEM((size.side + 2, size.side + 2, size.frames, LANES), F32),
            pltpu.VMEM((size.cells, size.frames, LANES), F32),
        ],
        [me],
        [z0, z1, totals, table, mask],
        ins={0: cell_parts(size), 1: cell_parts(size)},
        puts=puts,
    )
    return wires[0::2], wires[1::2]


def moments(size, me, lefts, pieces):
    rows = sum(item.shape[0] for item in lefts[0])
    flat = [item for group in lefts for item in group]
    (result,) = call(
        functools.partial(moments_kernel, size),
        [shaped((4, rows, 2 * LANES))],
        [],
        [me],
        [*flat, *pieces],
        ins={len(flat) + index: (1, size.parts) for index in range(4)},
        stacks=[range(len(flat), len(flat) + 4)],
    )
    return result


def forward_second(size, me, group, pieces, totals, along, kernel, mask, count):
    side, frames = size.side, size.frames
    field, z2, stat = call(
        functools.partial(conv_kernel, size),
        [
            shaped((side + 2, side + 2, frames, 2 * LANES), size.kept),
            shaped((size.cells, frames, LANES)),
            shaped((count, 8, LANES)),
        ],
        [pltpu.VMEM((2 * LANES, size.padded), F32)],
        [me, group],
        [*pieces, totals, along, kernel, mask],
        flops=2 * size.rows * 9 * 256 * 256,
        ins={6: (0, [(0, 9)])},
        puts={0: (0, [(0, side + 2)]), 1: cell_parts(size)},
    )
    return field, z2, stat


def hop(piece, shift):
    return lax.ppermute(piece, "chan", pairs(4, shift))


def second_sums(size, grads, saved, count):
    z2, totals2, table2, mask = saved[4], saved[5], saved[7], saved[8]
    return call(
        functools.partial(second_sums_kernel, size),
        [shaped((count, 8, LANES))],
        spread_rows(size),
        [],
        [grads[1], z2, totals2, table2, mask],
        ins={1: cell_parts(size)},
    )


def spread_rows(size):
    return [pltpu.VMEM((size.rows // 4, LANES), F32)] if size.side % 2 == 0 else []


def weight_grad(size, me, inner, moment, back1, kernels, count):
    unit = count * 16
    total = -(-(KERNEL_ROWS + DENSE_ROWS) // unit) * unit
    return call(
        functools.partial(weight_grad_kernel, size),
        [shaped((total, LANES), BF16), shaped((8, LANES))],
        [pltpu.VMEM((4, 2, ROWS, LANES), F32), pltpu.VMEM((DENSE_ROWS, LANES), F32)],
        [me],
        [inner, moment, back1, kernels],
    )


def backward(size, me, grads, back2, saved, normed, weights_at, count, early=None, moment=None, group=None, above=None):
    z0, z1, totals, field, z2, totals2, table, table2, mask, kernel, pieces, _, shapes = saved
    g0, g2, g1 = grads
    side, frames = size.side, size.frames
    spreads = early is not None
    tile = shaped((size.cells, frames, LANES))
    wire = shaped((REDUCED, size.padded), BF16)
    delta2, o0, o1, o2 = call(
        functools.partial(conv_back_kernel, size),
        [shaped((size.cells, frames, LANES), size.kept), wire, wire, shaped((2 * REDUCED, size.padded), BF16)],
        [
            pltpu.VMEM((side + 2, side + 2, frames, LANES), size.kept),
            pltpu.VMEM((size.cells, frames, 4 * REDUCED), F32),
            pltpu.VMEM((4 * REDUCED, size.padded), F32),
        ]
        + spread_rows(size),
        [me],
        [g2, z2, totals2, back2, table2, mask, kernel],
        flops=2 * size.rows * 9 * 256 * 256,
        ins={1: cell_parts(size), 6: (0, [(0, 9)])},
        puts={0: cell_parts(size)},
    )
    if spreads:
        o2, normed = together(o2, normed)
        normed = [[*wires, hop(wires[2], 1)] for wires in normed]
    partial = [o0, hop(o1, 1), hop(o2, 2)]
    (kernel_grad,) = call(
        functools.partial(kernel_grad_kernel, size),
        [shaped((KERNEL_ROWS, LANES), BF16)],
        [
            pltpu.VMEM((2 * LANES, size.padded), BF16),
            pltpu.VMEM((size.cells, frames, LANES), F32),
            pltpu.VMEM((9, 2, LANES, LANES), F32),
            pltpu.VMEM((KERNEL_ROWS, LANES), F32),
        ],
        [],
        [field, delta2, mask],
        flops=2 * size.rows * 9 * 256 * 256,
        ins={0: (0, even(side + 2, side + 2)), 1: cell_parts(size)},
    )
    if spreads:
        early, o1 = together(early, o1)
        swapped = swap_shares(early, count)
        partial[2], kernel_grad = together(partial[2], kernel_grad)
    else:
        partial[2], kernel_grad = together(partial[2], kernel_grad)
    if not spreads:
        partial[1], normed = together(partial[1], normed)
    partial.append(hop(partial[2], 1))
    if spreads:
        partial[3], swapped = together(partial[3], swapped)
    devices = count if spreads else 4 * count
    stat, *wires = call(
        functools.partial(first_sums_kernel, size),
        [shaped((devices, 8, LANES))] + [shaped((ROWS, lanes), BF16) for _, lanes in size.parts],
        [
            pltpu.VMEM((size.cells, frames, LANES), F32),
            pltpu.VMEM((side + 2, side + 2, frames, LANES), F32),
            pltpu.VMEM((size.cells, frames, LANES), F32),
        ]
        + spread_rows(size) * 2,
        [me],
        [*partial, g0, g1, z0, z1, totals, table, mask],
        ins={6: cell_parts(size), 7: cell_parts(size)},
        puts={0: (0, [(0, devices)])} | {1 + part: span_parts(size, span) for part, span in enumerate(size.parts)},
    )
    others, cores = [hop(wire, 2) for wire in wires[:1]] + [None] * (len(wires) - 1), [hop(wire, 1) for wire in wires]
    inner = moments(size, me, [[wire] for wire in wires], pieces)
    if spreads:
        bits = count.bit_length() - 1
        back1 = share(stat)
        early = jnp.sum(swapped.astype(F32), 0).astype(BF16)
        halves = other_of(early, bits - 1, count)
        back1, inner, others[0], halves = together(back1, inner, others[0], halves)
        dense_grad, table_own = weight_grad(size, me, inner, moment, back1, kernel_grad, count)
        tables = exchange_four([table_own] * 4)
        tables, last = together(tables, wires[1])
        others[1] = hop(last, 2)
        swapped = swap_shares(dense_grad, count)
    else:
        back1 = share_all(stat, count)
        back1, others[0], moment = together(back1, others[0], moment)

    def four(part):
        return [wires[part], cores[part], others[part], hop(others[part], 1)]

    scratch = [pltpu.VMEM((2, size.parts[0][1] + LANES, LANES), F32), pltpu.VMEM((8 * ROWS + 16, 2 * LANES), BF16)]
    if not spreads:
        top, top_args = above
        result = call(
            functools.partial(input_half_sums_kernel, size, top),
            [tile, tile, tile, shaped((count, 8, LANES))],
            scratch + spread_rows(top),
            [me],
            [*four(0), *normed[0], shapes[0], *weights_at, back1, *top_args],
            ins={index: column_parts(size, size.whole) for index in range(9)} | {14: cell_parts(top)},
            stacks=[range(9)],
        )
        return result, inner, kernel_grad, back1, moment
    shape = shaped((size.cells, frames // 8, 8 * QUARTER))
    result, sets = (), []
    for part, span in enumerate(size.parts):
        if part:
            for bit in range(bits - 1, 0, -1):
                early = joined_halves(group, bit, early, halves)
                halves = other_of(early, bit - 1, count)
                if bit == 2:
                    swapped, halves = together(swapped, halves)
            late = all_shares([swapped])
        sets.append([*four(part), *normed[part], shapes[part]])
        low, high, base = input_plan(size, part)
        args = list(sets[part])
        ins = {index: column_parts(size, span) for index in range(9)}
        stacks = [range(9)]
        if part:
            before = size.parts[part - 1]
            tail = (1, [(base - before[0], span[0] - base)])
            ins |= {len(args) + index: tail for index in range(9)}
            stacks.append(range(9, 18))
            args += sets[part - 1]
        args += [*weights_at, *tables]
        if part:
            ins[len(args)] = (0, [])
        result = call(
            functools.partial(input_kernel, size, part),
            [shape],
            scratch,
            [me],
            [*args, *result],
            ins=ins,
            puts={0: line_parts(size, low, high - low)},
            aliases={len(args): 0} if part else None,
            stacks=stacks,
        )
    return result, (early, halves, late), back1


def on_device(count, clips, clip_len, w_plain, w_mid, k_mid, w_small, k_small, w_pool, gains, shifts, grad_out):
    big = Size(clips.shape[1], 8 * clips.shape[0])
    low = Size(grad_out.shape[1], 8 * grad_out.shape[0])
    me = lax.axis_index("chan").astype(jnp.int32).reshape(1)
    group = lax.axis_index("dp").astype(jnp.int32).reshape(1)
    everyone = 4 * count
    raw = clips.transpose(1, 2, 0, 3).reshape(big.cells, clips.shape[0], 8 * QUARTER)
    (own,) = call(
        functools.partial(unpack_kernel, big),
        [shaped((QUARTER, big.padded), BF16)],
        [pltpu.VMEM((2, big.rows, LANES), F32)],
        [],
        [raw],
        ins={0: line_parts(big)},
        puts={0: span_parts(big, big.whole)},
    )
    other, core = hop(own, 2), hop(own, 1)
    low_tile = shaped((low.cells, low.frames, LANES))
    grads = call(
        functools.partial(grad_kernel, low),
        [low_tile, low_tile, low_tile],
        [pltpu.VMEM((2, low.rows, LANES), F32)],
        [],
        [grad_out],
    )
    table = shaped((8, LANES))
    prepared = call(
        prepare_kernel,
        [shaped((3, big.frames, LANES)), shaped((3, low.frames, LANES))]
        + [table] * 4
        + [shaped((2, ROWS, 2 * LANES), BF16)] * 4
        + [shaped((4, QUARTER, 2 * LANES), BF16)] * 2
        + [shaped((9, LANES, 4 * REDUCED), BF16)] * 2
        + [shaped((9, 2 * LANES, LANES), BF16)] * 2
        + [table] * 2,
        [
            pltpu.VMEM((2 * MID_ROWS, LANES), F32),
            pltpu.VMEM((2, 4, 2, ROWS, LANES), F32),
            pltpu.VMEM((9, 2, LANES, LANES), F32),
        ],
        [me, clip_len],
        [as_rows(item) for item in (w_plain, w_mid, w_small, w_pool, k_mid, k_small, gains, shifts)],
    )
    mask, mask_low, table0, second0, table1, second1 = prepared[:6]
    sent, (dense0, dense1), (kernel0, kernel1), (turned0, turned1), (along, along_low) = (
        prepared[6:10],
        prepared[10:12],
        prepared[12:14],
        prepared[14:16],
        prepared[16:18],
    )
    begun = project_begin(big, me, [own, core], dense0)
    other, begun, grads = together(other, begun, grads)
    pieces = [own, core, other, hop(other, 1)]
    z0, z1, stat, wire = project(big, me, pieces[2:], (2, 3), dense0, mask, table0, everyone, begun)
    mids = [wire, hop(wire, 1), hop(wire, 2)]
    totals = share_all(stat, count)
    totals, mids[2] = together(totals, mids[2])
    mids.append(hop(mids[2], 1))
    half = [pltpu.VMEM((big.rows // 4, LANES), F32)]
    h0, h1 = call(
        functools.partial(first_half_kernel, big),
        [low_tile, low_tile],
        half * 2,
        [me],
        [z0, z1, totals, table0, mask],
        flops=big.rows * 2 * LANES * 20,
        ins={0: cell_parts(big), 1: cell_parts(big)},
    )
    field, z2, stat = forward_second(big, me, group, mids, totals, along, turned0, mask, count)
    totals2 = share(stat)
    weights_at = exchange_four(sent)
    totals2, weights_at = together(totals2, weights_at)
    (own1,) = call(
        functools.partial(second_half_kernel, big),
        [shaped((QUARTER, low.padded), BF16)],
        half,
        [],
        [z2, totals2, second0, mask, h0, h1],
        flops=big.rows * LANES * 20,
        ins={0: cell_parts(big)},
    )
    pieces1 = gather_four(own1)
    y0, y1, stat, wire = project(low, me, pieces1, (0, 1, 2, 3), dense1, mask_low, table1, everyone)
    mids = exchange_four([wire] * 4)
    totals1 = share_all(stat, count)
    normed, shapes = normed_wires(big, me, z0, z1, totals, table0, mask)
    totals1, normed, shapes = together(totals1, normed, shapes)
    field1, y2, stat = forward_second(low, me, group, mids, totals1, along_low, turned1, mask_low, count)
    totals3 = share(stat)
    normed1, shapes1 = normed_wires(low, me, y0, y1, totals1, table1, mask_low)
    totals3, normed1 = together(totals3, normed1)
    (mixed,) = call(
        functools.partial(output_kernel, low),
        [shaped(grad_out.shape, BF16)],
        [pltpu.VMEM((2, low.rows, LANES), F32)],
        [me],
        [y0, y1, y2, totals1, totals3, table1, second1, mask_low],
    )
    saved1 = (y0, y1, totals1, field1, y2, totals3, table1, second1, mask_low, kernel1, pieces1, normed1, shapes1)
    (back2,) = second_sums(low, grads, saved1, count)
    back2 = share(back2)
    moment1 = moments(low, me, list(zip(normed1, shapes1)), pieces1)
    normed1 = [[wire, hop(wire, 1), hop(wire, 2)] for wire in normed1]
    back2, mixed, normed1, moment1 = together(back2, mixed, normed1, moment1)
    normed1 = [[*wires, hop(wires[2], 1)] for wires in normed1]
    moment = moments(big, me, list(zip(normed, shapes)), pieces)
    grads, inputs1, kernel_grad1, first1, moment = backward(
        low, me, grads, back2, saved1, normed1, weights_at, count, None, moment, above=(big, (z2, totals2, second0, mask))
    )
    last1 = back2
    *grads, back2 = grads

    saved0 = (z0, z1, totals, field, z2, totals2, table0, second0, mask, kernel0, pieces, normed, shapes)
    back2, normed = together(back2, normed)
    back2 = share(back2)
    normed = [[wire, hop(wire, 1), hop(wire, 2)] for wire in normed]
    dense_grad1, _ = weight_grad(low, me, inputs1, moment1, first1, kernel_grad1, count)
    back2, dense_grad1, normed[0] = together(back2, dense_grad1, normed[0])
    last0 = back2
    (clips_grad,), (early, halves, late), first0 = backward(
        big, me, grads, back2, saved0, normed, weights_at, count, dense_grad1, moment, group
    )

    def sized(outputs):
        rows = outputs * CIN // 64
        return shaped((rows, LANES) if rows % 16 == 0 else (2, rows * 64))

    pairs_rows = pltpu.VMEM((2 * MID_ROWS, LANES), F32)
    outs = [sized(outputs) for outputs in (MID, SMALL, PLAIN, POOL)]
    outs += [shaped((2, MID_ROWS * LANES)), shaped((2 * SMALL_ROWS, LANES))] + [shaped((4, LANES))] * 2
    mid, small, plain, pool, wide, narrow, gains_grad, shifts_grad = call(
        finish_kernel,
        outs,
        [pltpu.VMEM((count * late.shape[1], LANES), F32)] * 2 + [pairs_rows],
        [me, group],
        [early, halves, late, first0, first1, last0, last1],
        ins={2: (0, [(0, count)])},
        puts={4: (0, [(0, 2)])},
    )
    flats = [plain, mid, wide, small, narrow, pool, gains_grad, shifts_grad]
    flats = [item if item.shape[0] == 2 else as_flat(item) for item in flats]
    shape = (big.side, big.side, big.frames // 8, 8 * QUARTER)
    return mixed, clips_grad.reshape(shape).transpose(2, 0, 1, 3), *flats


def solution(mesh):
    frames = P("dp", None, None, "chan")
    flat = P(None, "chan")
    return jax.shard_map(
        functools.partial(on_device, mesh.shape["dp"]),
        mesh=mesh,
        in_specs=(frames, P("dp")) + (flat,) * 8 + (frames,),
        out_specs=(frames, frames) + (flat,) * 8,
        check_vma=False,
    )
```

```python
import functools

import jax
import jax.numpy as jnp
from jax import lax
from jax.experimental import pallas as pl
from jax.experimental.pallas import tpu as pltpu
from jax.sharding import PartitionSpec as P

CIN = 832
QUARTER = 208
WIDE, NARROW = 80, 32
MID, SMALL, PLAIN, POOL = 40, 8, 64, 32
REDUCED = MID + SMALL
DENSE = REDUCED + PLAIN
ROWS = DENSE + POOL
CLIPS = 2
EPSILON = 1e-05
F32 = jnp.float32
BF16 = jnp.bfloat16
LANES = 128
LIMIT = 64
ROOM = 64
COST = 1
MID_TILES = 4 * 9 * 160 // LANES
MID_ROWS = WIDE // 4 * MID_TILES
SMALL_TILES = 4 * 9 * 32 // LANES
SMALL_ROWS = NARROW // 4 * SMALL_TILES
KERNEL_ROWS = 976
PAIR_TILES = 2 * CIN // LANES
DENSE_ROWS = 944


class Size:
    def __init__(self, side, frames):
        self.side = side
        self.frames = frames
        self.cells = side * side
        self.rows = self.cells * frames
        self.padded = -(-self.rows // LANES) * LANES
        self.band = 2 if side % 2 == 0 else side
        self.chunks = side // self.band
        self.step = self.band * side
        self.group = LANES // frames
        self.full = self.cells // self.group
        self.rest = self.cells - self.full * self.group
        self.kept = BF16 if frames % 16 == 0 else F32
        self.whole = (0, self.padded)
        first = 13 * LANES
        self.parts = [(0, first), (first, self.padded - first)] if self.padded > 2 * first - LANES - 1 else [self.whole]

    def cells_of(self, span):
        first = span[0] // self.frames
        return first, min(span[1] // self.frames, self.cells - first)

    def columns_of(self, span, width=640):
        first, count = self.cells_of(span)
        result = []
        for start in range(0, span[1], width):
            skipped, held = start // self.frames, min(width, span[1] - start)
            result.append((start, held, first + skipped, min(held // self.frames, count - skipped)))
        return result


class Stream:
    def __init__(self, far, near, sems, axis, parts):
        self.far, self.near, self.sems, self.axis, self.parts = far, near, sems, axis, parts
        self.shape, self.dtype = near.shape, near.dtype

    def copy(self, part, inward):
        if isinstance(part, int):
            start, count = self.parts[part]
        else:
            first, count = self.parts[0]
            start = first + part * count
        index = (slice(None),) * self.axis + (pl.ds(start, count),)
        pair = (self.far.at[index], self.near.at[index])
        return pltpu.make_async_copy(*(pair if inward else pair[::-1]), self.sems.at[part])

    def ready(self, part):
        self.copy(part, True).wait()

    def flush(self, part):
        self.copy(part, False).start()

    def __getitem__(self, index):
        return self.near[index]

    def __setitem__(self, index, value):
        self.near[index] = value

    @property
    def at(self):
        return self.near.at


def even(total, count):
    return [(start * (total // count), total // count) for start in range(count)]


def cell_parts(size):
    return 0, even(size.cells, size.chunks)


def line_parts(size, first=0, count=None):
    return 0, [(row * size.side, size.side) for row in range(first, first + (count or size.side))]


def column_parts(size, span, width=640):
    return 1, [(start, held) for start, held, _, _ in size.columns_of(span, width)]


def call(body, outs, scratch, scalars, args, flops=0, ins=None, puts=None, aliases=None, stacks=()):
    ins, puts = ins or {}, puts or {}
    places = {}
    for stack, members in enumerate(stacks):
        start = 0
        for index in members:
            places[index] = (stack, start)
            start += args[index].shape[0]
    aliases = {len(scalars) + index: out for index, out in (aliases or {}).items()}
    plans = [ins.get(index) for index in range(len(args))] + [puts.get(index) for index in range(len(outs))]
    arrays = list(args) + list(outs)
    buffers = []
    for index, (array, plan) in enumerate(zip(arrays, plans)):
        if index not in places:
            buffers.append(pltpu.VMEM(array.shape, array.dtype))
        buffers.append(pltpu.SemaphoreType.DMA((max(len(plan[1]), 1) if plan else 1,)))
    for members in stacks:
        rows = sum(args[index].shape[0] for index in members)
        buffers.append(pltpu.VMEM((rows,) + args[members[0]].shape[1:], args[members[0]].dtype))

    def wrapped(*refs):
        numbers, refs = refs[: len(scalars)], refs[len(scalars) :]
        far, refs = refs[: len(arrays)], refs[len(arrays) :]
        own, refs = refs[: len(scratch)], list(refs[len(scratch) :])
        whole = refs[len(refs) - len(stacks) :]
        streams = []
        for index, plan in enumerate(plans):
            axis, parts = plan or (0, [(0, arrays[index].shape[0])])
            if index in places:
                stack, start = places[index]
                near = whole[stack].at[pl.ds(start, arrays[index].shape[0])]
            else:
                near = refs.pop(0)
            streams.append(Stream(far[index], near, refs.pop(0), axis, parts))
        entering, leaving = streams[: len(args)], streams[len(args) :]
        for part in range(max([len(stream.parts) for stream in entering])):
            for stream in entering:
                if part < len(stream.parts):
                    stream.copy(part, True).start()
        for index, stream in enumerate(entering):
            if index not in ins:
                stream.ready(0)
        body(*numbers, *entering, *leaving, *own, *whole)
        for index, stream in enumerate(leaving):
            if index not in puts:
                stream.flush(0)
        for stream in leaving:
            for part in range(len(stream.parts)):
                stream.copy(part, False).wait()

    moved = sum(array.size * array.dtype.itemsize for array in arrays)
    return pl.pallas_call(
        wrapped,
        out_shape=outs,
        in_specs=[pl.BlockSpec(memory_space=pltpu.SMEM)] * len(scalars) + [pl.BlockSpec(memory_space=pl.ANY)] * len(args),
        out_specs=[pl.BlockSpec(memory_space=pl.ANY)] * len(outs),
        scratch_shapes=list(scratch) + buffers,
        compiler_params=pltpu.CompilerParams(vmem_limit_bytes=LIMIT * 1024 * 1024),
        cost_estimate=pl.CostEstimate(flops=COST, bytes_accessed=COST, transcendentals=0),
        input_output_aliases=aliases,
    )(*scalars, *args)


def unrolled(count, body, carry):
    for index in range(count):
        carry = body(index, carry)
    return carry


def rolled(count, body, carry):
    if count == 1:
        return body(0, carry)
    return lax.fori_loop(0, count, body, carry)


def shaped(shape, dtype=F32):
    return jax.ShapeDtypeStruct(shape, dtype)


def sigmoid(value):
    return 0.5 * jnp.tanh(0.5 * value) + 0.5


def row_table(rows):
    index = lax.broadcasted_iota(jnp.int32, (8, LANES), 0)
    table = jnp.zeros((8, LANES), F32)
    for position, row in enumerate(rows):
        table = jnp.where(index == position, row, table)
    return table


def time_box(value, mask_ref):
    cells, frames, width = value.shape
    flat = value.reshape(cells * frames, width)
    before = pltpu.roll(flat, 1, 0).reshape(value.shape)
    after = pltpu.roll(flat, cells * frames - 1, 0).reshape(value.shape)
    return value + before * mask_ref[1] + after * mask_ref[2]


def owner_rows(all_ref, owner):
    if len(all_ref.shape) == 3:
        return all_ref[...]
    return all_ref[:, pl.ds(owner, 1)].reshape(all_ref.shape[0], 8, LANES)


def norm_rows(all_ref, table_ref, tile, owner=0):
    total = jnp.sum(owner_rows(all_ref, owner), 0)
    count = total[4:5]
    mean = total[2 * tile : 2 * tile + 1] / count
    variance = total[2 * tile + 1 : 2 * tile + 2] / count - mean * mean
    inverse = lax.rsqrt(variance + EPSILON)
    gain = table_ref[2 * tile : 2 * tile + 1]
    shift = table_ref[2 * tile + 1 : 2 * tile + 2]
    return mean, inverse, gain, shift, count


def activate(value, rows, mask_ref):
    mean, inverse, gain, shift, _ = rows
    shifted = gain * ((value - mean) * inverse) + shift
    return shifted * sigmoid(shifted) * mask_ref[0]


def inner_grad(grad, value, rows, mask_ref):
    mean, inverse, gain, shift, _ = rows
    normed = (value - mean) * inverse
    shifted = gain * normed + shift
    sigma = sigmoid(shifted)
    return grad * mask_ref[0] * sigma * (1.0 + shifted * (1.0 - sigma)), normed


def norm_delta(inner, value, rows, back_ref, tile, mask_ref):
    mean, inverse, gain, _, count = rows
    total = jnp.sum(back_ref[...], 0)
    shift_grad = total[2 * tile : 2 * tile + 1] / count
    gain_grad = total[2 * tile + 1 : 2 * tile + 2] / count
    normed = (value - mean) * inverse
    return (gain * inverse) * (inner - mask_ref[0] * (shift_grad + normed * gain_grad))


def publish(stat_ref, rows):
    stat_ref[...] = jnp.broadcast_to(row_table(rows)[None], stat_ref.shape)


def collapse(value):
    return jnp.sum(value, 0, keepdims=True)


def windows():
    result = []
    for frame in range(8):
        start = frame * QUARTER
        first, offset = start // LANES, start % LANES
        result.append((first, -(-(offset + QUARTER) // LANES), offset))
    return result


def unpack_rows(line, frame):
    first, tiles, offset = windows()[frame]
    value = line[:, first * LANES : (first + tiles) * LANES]
    if offset:
        value = pltpu.roll(value, tiles * LANES - offset, 1)
    return value[:, : 2 * LANES]


def pack_rows(parts):
    tiles = [None] * 13
    for frame, value in enumerate(parts):
        first, count, offset = windows()[frame]
        if count == 3:
            value = jnp.concatenate([value, jnp.zeros((value.shape[0], LANES), value.dtype)], 1)
        if offset:
            value = pltpu.roll(value, offset, 1)
        for index in range(count):
            piece = value[:, index * LANES : (index + 1) * LANES]
            place = first + index
            tiles[place] = piece if tiles[place] is None else tiles[place] + piece
    return tiles


def assemble(first, second, third):
    blank = jnp.zeros_like(first)
    lane = lax.broadcasted_iota(jnp.int32, (first.shape[0], 2 * LANES), 1)
    plain = pltpu.roll(jnp.concatenate([first, blank], 1), 2 * LANES - REDUCED, 1)
    middle = pltpu.roll(jnp.concatenate([second, blank], 1), PLAIN, 1)
    pool = pltpu.roll(jnp.concatenate([third, blank], 1), PLAIN + WIDE + NARROW, 1)
    return jnp.where(lane < PLAIN, plain, 0.0) + middle + pool


def separate(value):
    lane = lax.broadcasted_iota(jnp.int32, (value.shape[0], LANES), 1)
    plain = pltpu.roll(value, REDUCED, 1)[:, :LANES]
    middle = pltpu.roll(value, 2 * LANES - PLAIN, 1)[:, :LANES]
    pool = pltpu.roll(value, 2 * LANES - PLAIN - WIDE - NARROW, 1)[:, :LANES]
    first = jnp.where((lane >= REDUCED) & (lane < DENSE), plain, 0.0)
    second = jnp.where(lane < WIDE + NARROW, middle, 0.0)
    third = jnp.where(lane < POOL, pool, 0.0)
    return first, second, third


def span_blocks(size, span, one, leaving=(), rolled=False):
    first, count = size.cells_of(span)
    total, whole = span[1] // LANES, count // size.group

    def block(index, cells):
        start = index * LANES
        start = start if isinstance(start, int) else pl.multiple_of(start, LANES)
        one(first + index * size.group, cells, pl.ds(start, LANES))

    def four(index, carry):
        for extra in range(4):
            block(index * 4 + extra, size.group)
        for stream in leaving:
            stream.flush(index)
        return carry

    groups = whole // 4 if rolled else 0
    if rolled:
        lax.fori_loop(0, groups, four, 0)
    for index in range(groups * 4, total):
        block(index, min(size.group, count - index * size.group))
        if index % 4 == 3 or index == total - 1:
            for stream in leaving:
                stream.flush(index // 4)


def span_parts(size, span):
    return column_parts(size, span, 4 * LANES)


def unpack_kernel(size, raw, out, scratch):
    side, frames = size.side, size.frames
    pairs_of = frames // 8
    def line(row, carry):
        raw.ready(row)
        value = raw[pl.ds(row * side, side)].astype(F32).reshape(pairs_of * side, 8 * QUARTER)
        for frame in range(8):
            place = pl.ds(row * side * frames + frame, pairs_of * side, stride=8)
            piece = unpack_rows(value, frame)
            scratch[0, place, :] = piece[:, :LANES]
            scratch[1, place, :] = piece[:, LANES:]
        return carry

    lax.fori_loop(0, side, line, 0)

    def one(cell, cells, lanes):
        start = cell * frames
        for tile, (low, high) in enumerate(((0, LANES), (LANES, QUARTER))):
            value = scratch[tile, pl.ds(start, cells * frames), :].reshape(cells, frames, LANES)
            out[low:high, lanes] = turn(size, value, cells)[: high - low].astype(BF16)

    span_blocks(size, size.whole, one, (out,))


def grad_kernel(size, raw, first, second, third, scratch):
    side, frames = size.side, size.frames

    def line(row, carry):
        value = raw[0, row].astype(F32)
        for frame in range(8):
            place = pl.ds(row * side * frames + frame, side, stride=frames)
            part = unpack_rows(value, frame)
            scratch[0, place, :] = part[:, :LANES]
            scratch[1, place, :] = part[:, LANES:]
        return carry

    unrolled(side, line, 0)
    parts = separate(jnp.concatenate([scratch[0, : size.rows], scratch[1, : size.rows]], 1))
    for ref, part in zip((first, second, third), parts):
        ref[...] = part.reshape(ref.shape)


def dot(left, right, dims=((1,), (0,))):
    return lax.dot_general(left, right, (dims, ((), ())), preferred_element_type=F32)


def into_padded(size, flat, field):
    side = size.side
    field[...] = jnp.zeros_like(field)

    def line(row, carry):
        field[row + 1, 1 : side + 1] = flat[pl.ds(row * side, side)]
        return carry

    unrolled(side, line, 0)


def stacked_weights(me, positions, w_ref, stacked):
    for index, position in enumerate(positions):
        stacked[index * QUARTER : (index + 1) * QUARTER] = w_ref[me[0] ^ position]


def each_column(size, body, carry):
    plan = size.columns_of(size.whole)
    _, width, _, cells = plan[0]

    def step(index, carry):
        return body(index, pl.multiple_of(index * width, LANES), width, index * cells, cells, carry)

    if len(plan) > 1:
        carry = lax.fori_loop(0, len(plan) - 1, step, carry)
    return body(len(plan) - 1, *plan[-1], carry)


def project_begin_kernel(size, me, x0, x1, w_ref, dense, pool, stacked, stack):
    frames = size.frames
    stacked_weights(me, (0, 1), w_ref, stacked)

    def column(index, start, width, first, cells, carry):
        for x in (x0, x1):
            x.ready(index)
        value = dot(stack[:, pl.ds(start, width)], stacked[...], ((0,), (0,)))
        value = value.reshape(width // frames, frames, 2 * LANES)[:cells]
        dense[pl.ds(first, cells)] = value[:, :, :LANES]
        pool[pl.ds(first, cells)] = value[:, :, LANES:]
        dense.flush(index)
        pool.flush(index)
        return carry

    each_column(size, column, 0)


def project_kernel(size, positions, me, *refs):
    side, frames = size.side, size.frames
    pieces, (w_ref, mask, table), refs = refs[: len(positions)], refs[len(positions) : len(positions) + 3], refs[len(positions) + 3 :]
    begun = refs[:2] if len(positions) < 4 else None
    z0, z1, stat, wire, field, flat, stacked, stack = refs[-8:]
    stacked_weights(me, positions, w_ref, stacked)
    blank = jnp.zeros((frames, LANES), F32)
    total, squares = blank, blank

    def column(index, start, width, first, cells, carry):
        total, squares = carry
        for x in pieces:
            x.ready(index)
        value = dot(stack[:, pl.ds(start, width)], stacked[...], ((0,), (0,)))
        value = value.reshape(width // frames, frames, 2 * LANES)[:cells]
        dense, pool = value[:, :, :LANES], value[:, :, LANES:]
        place = pl.ds(first, cells)
        if begun:
            for stream in begun:
                stream.ready(index)
            dense += begun[0][place]
            pool += begun[1][place]
        z0[place] = dense
        z0.flush(index)
        flat[place] = pool
        return total + jnp.sum(dense, 0), squares + jnp.sum(dense * dense, 0)

    total, squares = each_column(size, column, (total, squares))
    valid = mask[0]
    total, squares = collapse(total * valid), collapse(squares * valid)
    count = collapse(valid) * size.cells
    mean = total / count

    def one(cell, cells, lanes):
        wire[:, lanes] = turn(size, z0[pl.ds(cell, cells)] - mean, cells)[:REDUCED].astype(BF16)

    span_blocks(size, size.whole, one, (), True)
    into_padded(size, flat, field)

    def line(row, carry):
        pool_total, pool_squares = carry
        pool = pool_line(size, field, row, mask)
        z1[pl.ds(row * side, side)] = pool
        z1.flush(row)
        return pool_total + jnp.sum(pool, 0), pool_squares + jnp.sum(pool * pool, 0)

    pool_total, pool_squares = lax.fori_loop(0, side, line, (blank, blank))
    rows = [total, squares, collapse(pool_total * valid), collapse(pool_squares * valid), count]
    publish(stat, rows + [table[0:1], table[1:2]])


def normed_kernel(size, me, z0, z1, totals, table, mask, *refs):
    outs, (field, pooled) = refs[:-2], refs[-2:]
    side, frames, step = size.side, size.frames, size.step
    lane = lax.broadcasted_iota(jnp.int32, (frames, LANES), 1)
    field[...] = jnp.zeros_like(field)
    rows = [norm_rows(totals, table, tile, me[0]) for tile in range(2)]
    scales = [(gain * inverse * inverse, mean) for mean, inverse, gain, _, _ in rows]

    def chunk(index, carry):
        z1.ready(index)
        scale, mean = scales[1]
        value = (z1[pl.ds(index * step, step)] - mean) * scale
        value = jnp.where(lane == POOL, 1.0, value) * mask[0]
        field[pl.ds(1 + index * size.band, size.band), 1 : side + 1] = value.reshape(size.band, side, frames, LANES)
        return carry

    rolled(size.chunks, chunk, 0)
    pool_lines(size, field, pooled, mask)
    for index in range(size.chunks):
        z0.ready(index)
    for part, span in enumerate(size.parts):
        normed, shapes = outs[2 * part : 2 * part + 2]

        def one(cell, cells, lanes, normed=normed, shapes=shapes):
            scale, mean = scales[0]
            value = (z0[pl.ds(cell, cells)] - mean) * scale
            dense = turn(size, jnp.where(lane == DENSE, 1.0, value) * mask[0], cells)
            pool = turn(size, pooled[pl.ds(cell, cells)], cells)
            normed[0:DENSE, lanes] = dense[:DENSE].astype(BF16)
            normed[DENSE:ROWS, lanes] = pool[:POOL].astype(BF16)
            both = jnp.concatenate([dense[DENSE : DENSE + 8], pool[POOL : POOL + 8]], 0)
            shapes[:, lanes] = both.astype(BF16)

        span_blocks(size, span, one, (normed,), True)


def pool_lines(size, field, pooled, mask):
    def line(row, carry):
        pooled[pl.ds(row * size.side, size.side)] = pool_line(size, field, row, mask)
        return carry

    lax.fori_loop(0, size.side, line, 0)


def moments_kernel(size, me, *refs):
    (out, stack), pieces = refs[-2:], refs[-6:-2]
    lefts = refs[:-6]
    each = len(lefts) // len(size.parts)
    lefts = [lefts[part * each : (part + 1) * each] for part in range(len(size.parts))]
    lefts = [group[0][...] if each == 1 else jnp.concatenate([item[...] for item in group], 0) for group in lefts]
    value = jnp.zeros((4 * QUARTER, lefts[0].shape[0]), F32)
    for part, (left, (start, count)) in enumerate(zip(lefts, size.parts)):
        for x in pieces:
            x.ready(part)
        value += dot(stack[:, start : start + count], left, ((1,), (1,)))
    for position in range(4):
        piece = value[position * QUARTER : (position + 1) * QUARTER]
        piece = jnp.concatenate([piece, jnp.zeros((2 * LANES - QUARTER, piece.shape[1]), F32)], 0)
        out[me[0] ^ position] = piece.T


def back_columns(back, owner):
    if len(back.shape) == 2:
        return columns_of_table(back[...])
    return columns_of_table(back_table(back, owner))


def back_table(back, owner):
    every = owner_rows(back, owner)
    total, own = jnp.sum(every, 0), every[0]
    count = own[6:7]
    rows = [total[1:2] / count, total[3:4] / count, own[4:5] * total[0:1] / count, own[5:6] * total[2:3] / count]
    return row_table(rows)


def columns_of_table(table):
    turned = table.T
    slope = jnp.concatenate([turned[:DENSE, 0:1], turned[:POOL, 1:2]], 0)
    offset = jnp.concatenate([turned[:DENSE, 2:3], turned[:POOL, 3:4]], 0)
    return slope, offset


def weight_grad_kernel(size, me, inner, moments, back, kernels, out, table, grads, flat):
    table[...] = back_table(back, me[0])
    slope, offset = columns_of_table(table[...])
    for owner in range(4):
        shape = moments[owner, ROWS : ROWS + 16]
        value = inner[owner] - slope * moments[owner, 0:ROWS]
        first = value[:DENSE] - offset[:DENSE] * shape[0:1]
        last = value[DENSE:] - offset[DENSE:] * shape[8:9]
        value = jnp.concatenate([first, last], 0)
        grads[owner, 0] = value[:, :LANES]
        grads[owner, 1] = value[:, LANES:]
    parts = []
    for extra in range(2):
        rows = pl.ds(extra, ROWS // 2, stride=2)
        for owner in range(4):
            parts.append(jnp.concatenate([grads[owner, 0, rows, :], grads[owner, 1, rows, :]], 1))
    for place, tile in enumerate(pack_rows(parts)):
        flat[pl.ds(place, ROWS // 2, stride=PAIR_TILES), :] = tile
    used = ROWS // 2 * PAIR_TILES
    flat[used:, :] = jnp.zeros((DENSE_ROWS - used, LANES), F32)
    out[:KERNEL_ROWS, :] = kernels[...]
    out[KERNEL_ROWS : KERNEL_ROWS + DENSE_ROWS, :] = flat[...].astype(BF16)
    rest = out.shape[0] - KERNEL_ROWS - DENSE_ROWS
    if rest:
        out[KERNEL_ROWS + DENSE_ROWS :, :] = jnp.zeros((rest, LANES), BF16)


def pool_line(size, field, row, mask):
    side = size.side
    lines = field[pl.ds(row, 3)]
    column = lines[0] + lines[1] + lines[2]
    value = column[0:side] + column[1 : side + 1] + column[2 : side + 2]
    return time_box(value, mask) * (1.0 / 27.0)


def turn(size, value, cells):
    flat = value.reshape(cells * size.frames, value.shape[-1])
    if cells < size.group:
        blank = jnp.zeros((LANES - cells * size.frames, value.shape[-1]), value.dtype)
        flat = jnp.concatenate([flat, blank], 0)
    return flat.T


def conv_kernel(size, me, group, p0, p1, p2, p3, totals, lanes_valid, kernel, mask, field, z2, stat, joined):
    side, frames, step = size.side, size.frames, size.step
    for position, piece in enumerate((p0, p1, p2, p3)):
        owner = me[0] ^ position
        every = owner_rows(totals, owner)
        total = jnp.sum(every, 0)
        sent = totals[pl.ds(group[0], 1), pl.ds(owner, 1)].reshape(8, LANES)
        mean = total[0:1] / total[4:5]
        variance = total[1:2] / total[4:5] - mean * mean
        scale = sent[5:6] * lax.rsqrt(variance + EPSILON)
        offset = (sent[0:1] / sent[4:5] - mean) * scale + sent[6:7]
        turned = row_table([scale, offset]).T
        scale, offset = turned[:REDUCED, 0:1], turned[:REDUCED, 1:2]
        shifted = piece[...].astype(F32) * scale + offset
        value = shifted * sigmoid(shifted)
        joined[pl.ds(pl.multiple_of(owner * MID, 8), MID), :] = value[:MID]
        joined[pl.ds(pl.multiple_of(4 * MID + owner * SMALL, 8), SMALL), :] = value[MID:]
    field[...] = jnp.zeros_like(field)
    joined[4 * REDUCED :, :] = jnp.zeros((2 * LANES - 4 * REDUCED, size.padded), F32)

    def one(first, cells, lanes):
        value = (joined[:, lanes] * lanes_valid[0:1]).T
        value = value.reshape(size.group, frames, 2 * LANES).astype(size.kept)
        for index in range(cells):
            cell = first + index
            row = cell // side if isinstance(cell, int) else lax.div(cell, side)
            field[row + 1, cell - row * side + 1] = value[index]

    span_blocks(size, size.whole, one)
    field.flush(0)
    kernel.ready(0)
    blank = jnp.zeros((frames, LANES), F32)

    def chunk(index, carry):
        total, squares = carry
        parts = []
        for row in range(3):
            for column in range(3):
                part = field[pl.ds(index * size.band + row, size.band), column : column + side]
                parts.append(part.reshape(step * frames, 2 * LANES).astype(BF16))
        value = dot(jnp.concatenate(parts, 1), kernel[...].reshape(18 * LANES, LANES))
        value = time_box(value.reshape(step, frames, LANES), mask) * (1.0 / 3.0)
        z2[pl.ds(index * step, step)] = value
        z2.flush(index)
        return total + jnp.sum(value, 0), squares + jnp.sum(value * value, 0)

    total, squares = unrolled(size.chunks, chunk, (blank, blank))
    valid = mask[0]
    one_row = jnp.zeros((1, LANES), F32)
    rows = [collapse(total * valid), collapse(squares * valid), one_row, one_row, collapse(valid) * size.cells]
    publish(stat, rows)


def halve_into(size, value, scratch, index):
    half = size.side // 2
    value = value.reshape(2, half, 2, size.frames, LANES)
    value = value[0] + value[1]
    value = value[:, 0] + value[:, 1]
    rows = half * size.frames
    scratch[pl.ds(index * rows, rows), :] = value.reshape(rows, LANES)


def halved_rows(scratch):
    count = scratch.shape[0] // 2
    return (scratch[pl.ds(0, count, stride=2), :] + scratch[pl.ds(1, count, stride=2), :]) * 0.125


def first_half_kernel(size, me, z0, z1, totals, table, mask, h0, h1, s0, s1):
    for tile, (z, out, scratch) in enumerate(((z0, h0, s0), (z1, h1, s1))):
        rows = norm_rows(totals, table, tile, me[0])

        def chunk(index, carry, z=z, scratch=scratch, rows=rows):
            z.ready(index)
            value = activate(z[pl.ds(index * size.step, size.step)], rows, mask)
            halve_into(size, value, scratch, index)
            return carry

        rolled(size.chunks, chunk, 0)
        out[...] = halved_rows(scratch).reshape(out.shape)


def second_half_kernel(size, z2, totals, table, mask, h0, h1, out, scratch):
    rows = norm_rows(totals, table, 0)

    def chunk(index, carry):
        z2.ready(index)
        value = activate(z2[pl.ds(index * size.step, size.step)], rows, mask)
        halve_into(size, value, scratch, index)
        return carry

    rolled(size.chunks, chunk, 0)
    value = halved_rows(scratch)
    count = value.shape[0]
    value = assemble(h0[...].reshape(count, LANES), value, h1[...].reshape(count, LANES))
    value = jnp.concatenate([value, jnp.zeros((out.shape[1] - count, 2 * LANES), F32)], 0)
    out[...] = value.T[:QUARTER].astype(BF16)


def strided(scratch, start, count, stride):
    place = pl.ds(start, count, stride=stride)
    return jnp.concatenate([scratch[0, place, :], scratch[1, place, :]], 1)


def output_kernel(size, me, z0, z1, z2, totals, totals2, table, table2, mask, out, scratch):
    side, frames = size.side, size.frames
    parts = [
        activate(z[...], norm_rows(total, tab, tile, me[0]), mask).reshape(size.rows, LANES)
        for z, total, tab, tile in ((z0, totals, table, 0), (z2, totals2, table2, 0), (z1, totals, table, 1))
    ]
    value = assemble(*parts)
    scratch[0, : size.rows] = value[:, :LANES]
    scratch[1, : size.rows] = value[:, LANES:]

    def line(row, carry):
        start = row * side * frames
        lines = [strided(scratch, start + frame, side, frames) for frame in range(8)]
        for place, tile in enumerate(pack_rows(lines)):
            out[0, row, :, place * LANES : (place + 1) * LANES] = tile.astype(BF16)
        return carry

    unrolled(side, line, 0)


def spread(size, grad, scratch):
    value = grad[...].reshape(-1, LANES)
    count = value.shape[0]
    scratch[pl.ds(0, count, stride=2), :] = value
    scratch[pl.ds(1, count, stride=2), :] = value


def grad_chunk(size, grad, scratch, index):
    if scratch is None:
        return grad[pl.ds(index * size.step, size.step)]
    half = size.side // 2
    rows = half * size.frames
    value = scratch[pl.ds(index * rows, rows), :].reshape(half, 1, size.frames, LANES)
    value = jnp.broadcast_to(value, (half, 2, size.frames, LANES)).reshape(1, size.side, size.frames, LANES)
    value = jnp.broadcast_to(value, (2, size.side, size.frames, LANES))
    return value.reshape(size.step, size.frames, LANES)


def second_sums_kernel(size, grad, z2, totals, table, mask, stat, *scratch):
    scratch = scratch[0] if scratch else None
    if scratch is not None:
        spread(size, grad, scratch)
    rows = norm_rows(totals, table, 0)
    blank = jnp.zeros((size.frames, LANES), F32)

    def chunk(index, carry):
        shift_grad, gain_grad = carry
        z2.ready(index)
        value = z2[pl.ds(index * size.step, size.step)]
        inner, normed = inner_grad(grad_chunk(size, grad, scratch, index), value, rows, mask)
        return shift_grad + jnp.sum(inner, 0), gain_grad + jnp.sum(inner * normed, 0)

    shift_grad, gain_grad = rolled(size.chunks, chunk, (blank, blank))
    publish(stat, [collapse(shift_grad), collapse(gain_grad)])


def conv_back_kernel(size, me, grad, z2, totals, back, table, mask, kernel, delta, o0, o1, o2, field, result, turned, *scratch):
    side, frames, step = size.side, size.frames, size.step
    scratch = scratch[0] if scratch else None
    if scratch is not None:
        spread(size, grad, scratch)
    rows = norm_rows(totals, table, 0)
    field[...] = jnp.zeros_like(field)

    def first(index, carry):
        z2.ready(index)
        value = z2[pl.ds(index * step, step)]
        inner, _ = inner_grad(grad_chunk(size, grad, scratch, index), value, rows, mask)
        value = norm_delta(inner, value, rows, back, 0, mask).astype(BF16).astype(size.kept)
        delta[pl.ds(index * step, step)] = value
        delta.flush(index)
        field[pl.ds(1 + index * size.band, size.band), 1 : side + 1] = value.reshape(size.band, side, frames, LANES)
        return carry

    unrolled(size.chunks, first, 0)
    kernel.ready(0)

    def chunk(index, carry):
        parts = []
        for row in range(3):
            for column in range(3):
                part = field[pl.ds(index * size.band + 2 - row, size.band), 2 - column : 2 - column + side]
                parts.append(part.reshape(step * frames, LANES).astype(BF16))
        value = dot(jnp.concatenate(parts, 1), kernel[...].reshape(9 * LANES, 4 * REDUCED))
        result[pl.ds(index * step, step)] = value.reshape(step, frames, 4 * REDUCED)
        return carry

    unrolled(size.chunks, chunk, 0)

    def one(cell, cells, lanes):
        turned[:, lanes] = turn(size, result[pl.ds(cell, cells)], cells)

    span_blocks(size, size.whole, one)
    for position, (out, start) in enumerate(((o0, 0), (o1, 0), (o2, 0), (o2, REDUCED))):
        owner = me[0] ^ position
        mid = turned[pl.ds(pl.multiple_of(owner * MID, 8), MID), :]
        small = turned[pl.ds(pl.multiple_of(4 * MID + owner * SMALL, 8), SMALL), :]
        out[start : start + REDUCED] = jnp.concatenate([mid, small], 0).astype(BF16)


def kernel_grad_kernel(size, field, delta, mask, out, turned, boxed, taps, flat):
    side, frames, step = size.side, size.frames, size.step

    def chunk(index, carry):
        delta.ready(index)
        place = pl.ds(index * step, step)
        boxed[place] = time_box(delta[place].astype(F32), mask)
        return carry

    rolled(size.chunks, chunk, 0)

    def one(cell, cells, lanes):
        value = turn(size, boxed[pl.ds(cell, cells)], cells)
        upper = value.astype(BF16)
        turned[:LANES, lanes] = upper
        turned[LANES:, lanes] = (value - upper.astype(F32)).astype(BF16)

    span_blocks(size, size.whole, one, (), True)
    for row in range(side + 2):
        field.ready(row)

    def tap(index, carry):
        row = index // 3
        part = field[pl.ds(row, side), pl.ds(index - 3 * row, side)].reshape(size.rows, 2 * LANES).astype(BF16)
        value = dot(turned[:, : size.rows], part)
        value = (value[:LANES] + value[LANES:]) * (1.0 / 3.0)
        taps[index, 0] = value[:, :LANES]
        taps[index, 1] = value[:, LANES:]
        return carry

    for index in range(9):
        tap(index, 0)
    lane = lax.broadcasted_iota(jnp.int32, (WIDE // 4, LANES), 1)
    tiles = [None] * MID_TILES

    def add(place, value):
        tiles[place] = value if tiles[place] is None else tiles[place] + value

    for extra in range(4):
        for tap in range(9):
            rows = pl.ds(extra, WIDE // 4, stride=4)
            rest = jnp.where(lane < 4 * MID - LANES, taps[tap, 1, rows, :], 0.0)
            offset = (extra * 9 + tap) * 4 * MID
            value = jnp.concatenate([taps[tap, 0, rows, :], rest, jnp.zeros_like(rest)], 1)
            value = pltpu.roll(value, offset % LANES, 1)
            for index in range(-(-(offset % LANES + 4 * MID) // LANES)):
                add(offset // LANES + index, value[:, index * LANES : (index + 1) * LANES])
    for place, tile in enumerate(tiles):
        flat[pl.ds(place, WIDE // 4, stride=MID_TILES), :] = tile
    lane = lax.broadcasted_iota(jnp.int32, (NARROW // 4, LANES), 1)
    tiles = [None] * SMALL_TILES
    start = 4 * MID - LANES
    for extra in range(4):
        for tap in range(9):
            value = taps[tap, 1, pl.ds(WIDE + extra, NARROW // 4, stride=4), :]
            value = jnp.where((lane >= start) & (lane < start + 4 * SMALL), value, 0.0)
            offset = (extra * 9 + tap) * 4 * SMALL
            value = pltpu.roll(value, (offset - start) % LANES, 1)
            add(offset // LANES, value)
    for place, tile in enumerate(tiles):
        flat[pl.ds(MID_ROWS + place, NARROW // 4, stride=SMALL_TILES), :] = tile
    flat[MID_ROWS + SMALL_ROWS : KERNEL_ROWS, :] = jnp.zeros((KERNEL_ROWS - MID_ROWS - SMALL_ROWS, LANES), F32)
    out[...] = flat[:KERNEL_ROWS].astype(BF16)


def first_sums_kernel(size, me, p0, p1, p2, p3, g0, g1, z0, z1, totals, table, mask, *refs):
    side, step, frames = size.side, size.step, size.frames
    count = len(size.parts)
    stat, outs, (field, padded, pooled, *scratch) = refs[0], refs[1 : 1 + count], refs[1 + count :]
    s0, s1 = scratch if scratch else (None, None)
    if scratch:
        spread(size, g0, s0)
        spread(size, g1, s1)
    padded[...] = jnp.zeros_like(padded)

    def one(cell, cells, place):
        value = p0[:, place].astype(F32) + p1[:, place].astype(F32)
        value += p2[:REDUCED, place].astype(F32) + p3[REDUCED:, place].astype(F32)
        value = jnp.concatenate([value, jnp.zeros((LANES - REDUCED, LANES), F32)], 0).T
        value = value.reshape(size.group, frames, LANES)
        field[pl.ds(cell, cells)] = value[:cells]

    span_blocks(size, size.whole, one)
    rows0 = norm_rows(totals, table, 0, me[0])
    rows1 = norm_rows(totals, table, 1, me[0])
    blank = jnp.zeros((frames, LANES), F32)

    def chunk(index, carry):
        place = pl.ds(index * step, step)
        z0.ready(index)
        z1.ready(index)
        grad = time_box(field[place], mask) * (1.0 / 3.0) + grad_chunk(size, g0, s0, index)
        inner0, normed0 = inner_grad(grad, z0[place], rows0, mask)
        inner1, normed1 = inner_grad(grad_chunk(size, g1, s1, index), z1[place], rows1, mask)
        field[place] = scales[0] * inner0
        pool = scales[1] * inner1
        padded[pl.ds(1 + index * size.band, size.band), 1 : side + 1] = pool.reshape(size.band, side, frames, LANES)
        sums = (inner0, inner0 * normed0, inner1, inner1 * normed1)
        return tuple(old + jnp.sum(new, 0) for old, new in zip(carry, sums))

    scales = [rows[2] * rows[1] for rows in (rows0, rows1)]
    sums = unrolled(size.chunks, chunk, (blank,) * 4)
    publish(stat, [collapse(item) for item in sums] + scales + [rows0[4]])
    stat.flush(0)
    pool_lines(size, padded, pooled, mask)
    for out, span in zip(outs, size.parts):

        def turned(cell, cells, lanes, out=out):
            out[0:DENSE, lanes] = turn(size, field[pl.ds(cell, cells)], cells)[:DENSE].astype(BF16)
            out[DENSE:ROWS, lanes] = turn(size, pooled[pl.ds(cell, cells)], cells)[:POOL].astype(BF16)

        span_blocks(size, span, turned, (out,))


def input_rows(size, me, groups, weights, block, back, scratch, stacked):
    flat_row, pool_row = jnp.zeros((1, 2 * LANES), F32), jnp.zeros((1, 2 * LANES), F32)
    for position, weight in enumerate(weights):
        slope, offset = back_columns(back[position] if len(back) == 4 else back[0], me[0] ^ position)
        stacked[position * ROWS : (position + 1) * ROWS] = weight[block]
        value = weight[block].astype(F32)
        stacked[(position + 4) * ROWS : (position + 5) * ROWS] = (value * -slope).astype(BF16)
        value = value * offset
        flat_row -= collapse(value[:DENSE])
        pool_row -= collapse(value[DENSE:])
    index = lax.broadcasted_iota(jnp.int32, (16, 2 * LANES), 0)
    fixed = jnp.where(index == 0, flat_row, 0.0) + jnp.where(index == 8, pool_row, 0.0)
    stacked[8 * ROWS :] = fixed.astype(BF16)
    for streams, stack, columns in groups:
        for part, start, width, row in columns:
            for stream in streams:
                stream.ready(part)
            value = dot(stack[:, start : start + width], stacked[...], ((0,), (0,)))
            scratch[0, row : row + width, :] = value[:, :LANES]
            scratch[1, row : row + width, :] = value[:, LANES:]


def input_half_kernel(size, me, *refs):
    streams, weights, (back,) = refs[:9], refs[9:13], refs[13:14]
    first, second, third, scratch, stacked, stack = refs[14:]
    columns = [(part, start, width, start) for part, (start, width, _, _) in enumerate(size.columns_of(size.whole))]
    input_rows(size, me, [(streams, stack, columns)], weights, 1, (back,), scratch, stacked)
    value = jnp.concatenate([scratch[0, : size.rows, :], scratch[1, : size.rows, :]], 1)
    parts = separate(value * 0.125)
    for ref, part in zip((first, second, third), parts):
        ref[...] = part.reshape(ref.shape)


def input_half_sums_kernel(size, above, me, *refs):
    pieces, (z2, totals, table, mask), refs = refs[:14], refs[14:18], refs[18:]
    (first, second, third, stat), (scratch, stacked, wide), (stack,) = refs[:4], refs[4:7], refs[7:]
    input_half_kernel(size, me, *pieces, first, second, third, scratch, stacked, stack)
    second_sums_kernel(above, second, z2, totals, table, mask, stat, wide)


def input_plan(size, part):
    bounds = [0]
    for span in size.parts:
        first, count = size.cells_of(span)
        bounds.append((first + count) // size.side)
    low, high = bounds[part], bounds[part + 1]
    start = low * size.side * size.frames // LANES * LANES
    return low, high, start


def input_kernel(size, part, me, *refs):
    side, frames = size.side, size.frames
    pairs_of = frames // 8
    low, high, base = input_plan(size, part)
    own = 9 * (2 if part else 1)
    pieces, weights, back = refs[:own], refs[own : own + 4], refs[own + 4 : own + 8]
    refs = refs[own + 8 + (1 if part else 0) :]
    (out, scratch, stacked), stacks = refs[:3], refs[3:]
    begin = size.parts[part][0]
    columns = [(index, start, width, begin + start - base) for index, (start, width, _, _) in enumerate(size.columns_of(size.parts[part]))]
    groups = [(pieces[:9], stacks[0], columns)]
    if part:
        tail = (0, base - size.parts[part - 1][0], begin - base, 0)
        groups.append((pieces[9:], stacks[1], [tail]))
    input_rows(size, me, groups, weights, 0, back, scratch, stacked)

    def line(index, carry):
        row = low + index
        start = row * side * frames - base
        lines = [strided(scratch, start + frame, pairs_of * side, 8) for frame in range(8)]
        for place, tile in enumerate(pack_rows(lines)):
            lanes = slice(place * LANES, (place + 1) * LANES)
            out[pl.ds(row * side, side), :, lanes] = tile.reshape(side, pairs_of, LANES)
        out.flush(index)
        return carry

    for index in range(high - low):
        line(index, 0)


def pairs(axis_size, shift):
    return [(index, index ^ shift) for index in range(axis_size)]


def gather_four(piece):
    other = lax.ppermute(piece, "chan", pairs(4, 2))
    core = lax.ppermute(piece, "chan", pairs(4, 1))
    both = lax.ppermute(other, "chan", pairs(4, 1))
    return piece, core, other, both


def exchange_four(pieces):
    result = [pieces[0]]
    for shift in (1, 2, 3):
        result.append(lax.ppermute(pieces[shift], "chan", pairs(4, shift)))
    return result


def share(stat):
    return lax.all_to_all(stat, "dp", 0, 0, tiled=True)


def share_all(stat, count):
    return lax.all_to_all(stat, ("dp", "chan"), 0, 0, tiled=True).reshape(count, 4, 8, LANES)


def swap_shares(rows, count):
    return lax.all_to_all(rows.reshape(count, -1, LANES), "dp", 0, 0, tiled=True)


def shares_kernel(*refs):
    *swapped, out = refs
    start = 0
    for ref in swapped:
        count = ref.shape[1]
        value = jnp.sum(ref[...].astype(F32), 0).astype(BF16)
        for device in range(out.shape[0]):
            out[device, start : start + count] = value
        start += count


def all_shares(swapped):
    rows = sum(item.shape[1] for item in swapped)
    (whole,) = call(shares_kernel, [shaped((swapped[0].shape[0], rows, LANES), BF16)], [], [], swapped)
    return lax.all_to_all(whole, "dp", 0, 0, tiled=True)


def other_of(rows, bit, count):
    return lax.ppermute(rows, "dp", pairs(count, 1 << bit))


def joined_halves(group, bit, mine, others):
    low = (group[0] >> bit) & 1
    return jnp.where(low == 0, jnp.concatenate([mine, others], 0), jnp.concatenate([others, mine], 0))


def together(*values):
    return lax.optimization_barrier(values)


def as_rows(flat):
    return flat.reshape(2, -1, LANES).transpose(1, 0, 2).reshape(-1, LANES)


def as_flat(rows):
    return rows.reshape(-1, 2, LANES).transpose(1, 0, 2).reshape(2, -1)


NORM_LANES = (
    (0, REDUCED, PLAIN, 0),
    (0, 0, MID, 64),
    (2, 0, WIDE, 104),
    (0, MID, SMALL, 184),
    (2, WIDE, NARROW, 192),
    (1, 0, POOL, 224),
)


def shifted_lanes(value, source, width, target):
    lane = lax.broadcasted_iota(jnp.int32, value.shape, 1)
    value = jnp.where((lane >= source) & (lane < source + width), value, 0.0)
    return pltpu.roll(value, (target - source) % value.shape[1], 1)


def mask_rows(length0, length1, frames, stride):
    frame = lax.broadcasted_iota(jnp.int32, (frames, LANES), 0)
    ends = (length0, length0 + length1)

    def ident(step):
        place = (frame + step) * stride
        return jnp.where(place >= ends[0], 1, 0) + jnp.where(place >= ends[1], 1, 0)

    here = ident(0)
    valid = jnp.where(frame * stride < ends[1], 1.0, 0.0)
    before = jnp.where((frame > 0) & (ident(-1) == here), 1.0, 0.0)
    after = jnp.where((frame < frames - 1) & (ident(1) == here), 1.0, 0.0)
    return valid, before, after


def prepare_kernel(me, lengths, plain, mid, small, pool, wide, narrow, gains, shifts, *refs):
    outs, (rows, dense, taps) = refs[:-3], refs[-3:]
    mask0, mask1, tables, sent, weights, kernels = outs[0], outs[1], outs[2:6], outs[6:10], outs[10:12], outs[12:14]
    turned, along = outs[14:16], outs[16:18]
    for ref, frames, stride in ((along[0], mask0.shape[1], 1), (along[1], mask1.shape[1], 2)):
        lane = lax.broadcasted_iota(jnp.int32, (8, LANES), 1)
        ref[...] = jnp.where(lax.rem(lane, frames) * stride < lengths[0] + lengths[1], 1.0, 0.0)
    for mask, stride in ((mask0, 1), (mask1, 2)):
        for index, value in enumerate(mask_rows(lengths[0], lengths[1], mask.shape[1], stride)):
            mask[index] = value
    for block in range(2):
        lines = []
        for source in (gains, shifts):
            value = source[...].astype(F32)
            line = jnp.concatenate([value[block : block + 1], value[block + 2 : block + 3]], 1)
            lines.append(jnp.broadcast_to(line, (8, 2 * LANES)))
        found = [[jnp.zeros((8, LANES), F32)] * 2 for _ in range(3)]
        for tile, lane, width, channel in NORM_LANES:
            for index, line in enumerate(lines):
                part = shifted_lanes(line, channel, width, lane)[:, :LANES]
                found[tile][index] = found[tile][index] + part
        tables[2 * block][...] = row_table([found[0][0], found[0][1], found[1][0], found[1][1]])
        tables[2 * block + 1][...] = row_table([found[2][0], found[2][1]])
    for ref, base, outputs in ((mid, 0, MID), (small, MID, SMALL), (plain, REDUCED, PLAIN), (pool, DENSE, POOL)):
        count = ref.shape[0]
        rows[:count, :] = ref[...].astype(F32)
        for block in range(2):
            tiles = [rows[pl.ds(2 * tile + block, outputs // 2, stride=2 * PAIR_TILES), :] for tile in range(PAIR_TILES)]
            line = jnp.concatenate(tiles, 1)
            for extra in range(2):
                place = pl.ds(base + extra, outputs // 2, stride=2)
                for owner in range(4):
                    part = unpack_rows(line, 4 * extra + owner)
                    dense[block, owner, 0, place, :] = part[:, :LANES]
                    dense[block, owner, 1, place, :] = part[:, LANES:]
    lane = lax.broadcasted_iota(jnp.int32, (ROWS, LANES), 1)
    blank = jnp.zeros((LANES, 2 * LANES), F32)
    for block in range(2):
        for owner in range(4):
            rest = jnp.where(lane < QUARTER - LANES, dense[block, owner, 1], 0.0)
            dense[block, owner, 1] = rest
            value = jnp.concatenate([dense[block, owner, 0], rest], 1)
            value = jnp.concatenate([value[:DENSE], blank[: LANES - DENSE], value[DENSE:], blank[: LANES - POOL]], 0)
            weights[block][owner] = value.T[:QUARTER].astype(BF16)
        for position in range(4):
            owner = me[0] ^ position
            value = jnp.concatenate([dense[block, owner, 0], dense[block, owner, 1]], 1)
            sent[position][block] = value.astype(BF16)
    wide_lane = lax.broadcasted_iota(jnp.int32, (WIDE // 4, LANES), 1)
    narrow_lane = lax.broadcasted_iota(jnp.int32, (NARROW // 4, LANES), 1)
    start = 4 * MID - LANES
    for block in range(2):
        rows[: wide.shape[0], :] = wide[...].astype(F32)
        taps[...] = jnp.zeros_like(taps)
        tiles = [rows[pl.ds(2 * tile + block, WIDE // 4, stride=2 * MID_TILES), :] for tile in range(MID_TILES)]
        tiles.append(tiles[0])
        for extra in range(4):
            for tap in range(9):
                offset = (extra * 9 + tap) * 4 * MID
                first, shift = offset // LANES, offset % LANES
                count = -(-(shift + 4 * MID) // LANES)
                value = jnp.concatenate(tiles[first : first + count], 1)
                value = pltpu.roll(value, (count * LANES - shift) % (count * LANES), 1)
                place = pl.ds(extra, WIDE // 4, stride=4)
                taps[tap, 0, place, :] = value[:, :LANES]
                taps[tap, 1, place, :] = jnp.where(wide_lane < start, value[:, LANES : 2 * LANES], 0.0)
        rows[: narrow.shape[0], :] = narrow[...].astype(F32)
        tiles = [rows[pl.ds(2 * tile + block, NARROW // 4, stride=2 * SMALL_TILES), :] for tile in range(SMALL_TILES)]
        for extra in range(4):
            for tap in range(9):
                offset = (extra * 9 + tap) * 4 * SMALL
                value = pltpu.roll(tiles[offset // LANES], (start - offset) % LANES, 1)
                value = jnp.where((narrow_lane >= start) & (narrow_lane < start + 4 * SMALL), value, 0.0)
                taps[tap, 1, pl.ds(WIDE + extra, NARROW // 4, stride=4), :] = value
        for tap in range(9):
            first, second = taps[tap, 0], taps[tap, 1]
            kernels[block][tap] = jnp.concatenate([first, second], 1)[:, : 4 * REDUCED].astype(BF16)
            turned[block][tap, :LANES] = first.T.astype(BF16)
            turned[block][tap, LANES:] = second.T.astype(BF16)


def place_rows(out, sources, count, pairs_rows):
    target = pairs_rows if out.shape[0] == 2 else out.near
    for block, (ref, start) in enumerate(sources):
        target[pl.ds(block, count, stride=2), :] = ref[start : start + count, :]
    if out.shape[0] == 2:
        for index in range(count // 4):
            value = pairs_rows[index * 8 : index * 8 + 8, :]
            for part in range(4):
                place = index * 4 + part
                out[:, place * LANES : (place + 1) * LANES] = value[2 * part : 2 * part + 2]


def finish_kernel(me, group, early, halves, late, first0, first1, second0, second1, *refs):
    outs, (rows, other, pairs_rows) = refs[:-3], refs[-3:]
    mid, small, plain, pool, wide, narrow, gains, shifts = outs
    count, share = late.shape[:2]
    bits = count.bit_length() - 1
    low = group[0] & 1
    for index in range(count // 2):
        device = sum(((index >> bit) & 1) << (bits - 1 - bit) for bit in range(bits))
        place = slice(index * share, (index + 1) * share)
        rows[pl.ds(pl.multiple_of((device + low) * share, 16), share)] = early[place].astype(F32)
        rows[pl.ds(pl.multiple_of((device + 1 - low) * share, 16), share)] = halves[place].astype(F32)
    late.ready(0)
    for device in range(late.shape[0]):
        place = slice(device * share, (device + 1) * share)
        other[place] = late[device].astype(F32)
    place_rows(wide, ((other, 0), (rows, 0)), MID_ROWS, pairs_rows)
    wide.flush(0)
    place_rows(narrow, ((other, MID_ROWS), (rows, MID_ROWS)), SMALL_ROWS, pairs_rows)
    start = KERNEL_ROWS
    for out, outputs in ((mid, MID), (small, SMALL), (plain, PLAIN), (pool, POOL)):
        count = outputs * CIN // LANES
        place_rows(out, ((other, start), (rows, start)), count, pairs_rows)
        start += count
    for block, first_ref, second_ref in ((0, first0, second0), (1, first1, second1)):
        first = jnp.sum(owner_rows(first_ref, me[0]), 0)
        second = jnp.sum(second_ref[...], 0)
        for out, row in ((gains, 1), (shifts, 0)):
            lines = (first[row : row + 1], first[row + 2 : row + 3], second[row : row + 1])
            total = jnp.zeros((8, 2 * LANES), F32)
            for tile, lane, width, channel in NORM_LANES:
                line = jnp.concatenate([lines[tile], jnp.zeros((1, LANES), F32)], 1)
                total += shifted_lanes(jnp.broadcast_to(line, (8, 2 * LANES)), lane, width, channel)
            out[block : block + 1, :] = total[0:1, :LANES]
            out[block + 2 : block + 3, :] = total[0:1, LANES:]


def project(size, me, pieces, positions, dense, mask, table, everyone, begun=()):
    side, cells, frames = size.side, size.cells, size.frames
    tile = shaped((cells, frames, LANES))
    count = len(positions)
    column_cells = (0, [(first, held) for _, _, first, held in size.columns_of(size.whole)])
    ins = {index: column_parts(size, size.whole) for index in range(count)}
    ins |= {count + 3 + index: column_cells for index in range(len(begun))}
    return call(
        functools.partial(project_kernel, size, positions),
        [tile, tile, shaped((everyone, 8, LANES)), shaped((REDUCED, size.padded), BF16)],
        [
            pltpu.VMEM((side + 2, side + 2, frames, LANES), F32),
            pltpu.VMEM((cells, frames, LANES), F32),
            pltpu.VMEM((count * QUARTER, 2 * LANES), BF16),
        ],
        [me],
        [*pieces, dense, mask, table, *begun],
        ins=ins,
        puts={0: column_cells, 1: line_parts(size)},
        stacks=[range(count)],
    )


def project_begin(size, me, pieces, dense):
    tile = shaped((size.cells, size.frames, LANES))
    column_cells = (0, [(first, held) for _, _, first, held in size.columns_of(size.whole)])
    return call(
        functools.partial(project_begin_kernel, size),
        [tile, tile],
        [pltpu.VMEM((2 * QUARTER, 2 * LANES), BF16)],
        [me],
        [*pieces, dense],
        ins={index: column_parts(size, size.whole) for index in range(2)},
        puts={0: column_cells, 1: column_cells},
        stacks=[range(2)],
    )


def normed_wires(size, me, z0, z1, totals, table, mask):
    outs, puts = [], {}
    for part, (_, lanes) in enumerate(size.parts):
        outs += [shaped((ROWS, lanes), BF16), shaped((16, lanes), BF16)]
        puts[2 * part] = span_parts(size, size.parts[part])
    wires = call(
        functools.partial(normed_kernel, size),
        outs,
        [
            pltpu.VMEM((size.side + 2, size.side + 2, size.frames, LANES), F32),
            pltpu.VMEM((size.cells, size.frames, LANES), F32),
        ],
        [me],
        [z0, z1, totals, table, mask],
        ins={0: cell_parts(size), 1: cell_parts(size)},
        puts=puts,
    )
    return wires[0::2], wires[1::2]


def moments(size, me, lefts, pieces):
    rows = sum(item.shape[0] for item in lefts[0])
    flat = [item for group in lefts for item in group]
    (result,) = call(
        functools.partial(moments_kernel, size),
        [shaped((4, rows, 2 * LANES))],
        [],
        [me],
        [*flat, *pieces],
        ins={len(flat) + index: (1, size.parts) for index in range(4)},
        stacks=[range(len(flat), len(flat) + 4)],
    )
    return result


def forward_second(size, me, group, pieces, totals, along, kernel, mask, count):
    side, frames = size.side, size.frames
    field, z2, stat = call(
        functools.partial(conv_kernel, size),
        [
            shaped((side + 2, side + 2, frames, 2 * LANES), size.kept),
            shaped((size.cells, frames, LANES)),
            shaped((count, 8, LANES)),
        ],
        [pltpu.VMEM((2 * LANES, size.padded), F32)],
        [me, group],
        [*pieces, totals, along, kernel, mask],
        flops=2 * size.rows * 9 * 256 * 256,
        ins={6: (0, [(0, 9)])},
        puts={0: (0, [(0, side + 2)]), 1: cell_parts(size)},
    )
    return field, z2, stat


def hop(piece, shift):
    return lax.ppermute(piece, "chan", pairs(4, shift))


def second_sums(size, grads, saved, count):
    z2, totals2, table2, mask = saved[4], saved[5], saved[7], saved[8]
    return call(
        functools.partial(second_sums_kernel, size),
        [shaped((count, 8, LANES))],
        spread_rows(size),
        [],
        [grads[1], z2, totals2, table2, mask],
        ins={1: cell_parts(size)},
    )


def spread_rows(size):
    return [pltpu.VMEM((size.rows // 4, LANES), F32)] if size.side % 2 == 0 else []


def weight_grad(size, me, inner, moment, back1, kernels, count):
    unit = count * 16
    total = -(-(KERNEL_ROWS + DENSE_ROWS) // unit) * unit
    return call(
        functools.partial(weight_grad_kernel, size),
        [shaped((total, LANES), BF16), shaped((8, LANES))],
        [pltpu.VMEM((4, 2, ROWS, LANES), F32), pltpu.VMEM((DENSE_ROWS, LANES), F32)],
        [me],
        [inner, moment, back1, kernels],
    )


def backward(size, me, grads, back2, saved, normed, weights_at, count, early=None, moment=None, group=None, above=None):
    z0, z1, totals, field, z2, totals2, table, table2, mask, kernel, pieces, _, shapes = saved
    g0, g2, g1 = grads
    side, frames = size.side, size.frames
    spreads = early is not None
    tile = shaped((size.cells, frames, LANES))
    wire = shaped((REDUCED, size.padded), BF16)
    delta2, o0, o1, o2 = call(
        functools.partial(conv_back_kernel, size),
        [shaped((size.cells, frames, LANES), size.kept), wire, wire, shaped((2 * REDUCED, size.padded), BF16)],
        [
            pltpu.VMEM((side + 2, side + 2, frames, LANES), size.kept),
            pltpu.VMEM((size.cells, frames, 4 * REDUCED), F32),
            pltpu.VMEM((4 * REDUCED, size.padded), F32),
        ]
        + spread_rows(size),
        [me],
        [g2, z2, totals2, back2, table2, mask, kernel],
        flops=2 * size.rows * 9 * 256 * 256,
        ins={1: cell_parts(size), 6: (0, [(0, 9)])},
        puts={0: cell_parts(size)},
    )
    if spreads:
        o2, normed = together(o2, normed)
        normed = [[*wires, hop(wires[2], 1)] for wires in normed]
    partial = [o0, hop(o1, 1), hop(o2, 2)]
    (kernel_grad,) = call(
        functools.partial(kernel_grad_kernel, size),
        [shaped((KERNEL_ROWS, LANES), BF16)],
        [
            pltpu.VMEM((2 * LANES, size.padded), BF16),
            pltpu.VMEM((size.cells, frames, LANES), F32),
            pltpu.VMEM((9, 2, LANES, LANES), F32),
            pltpu.VMEM((KERNEL_ROWS + 3 * ROOM, LANES), F32),
        ],
        [],
        [field, delta2, mask],
        flops=2 * size.rows * 9 * 256 * 256,
        ins={0: (0, even(side + 2, side + 2)), 1: cell_parts(size)},
    )
    if spreads:
        early, o1 = together(early, o1)
        swapped = swap_shares(early, count)
        partial[2], kernel_grad = together(partial[2], kernel_grad)
    else:
        partial[2], kernel_grad = together(partial[2], kernel_grad)
    if not spreads:
        partial[1], normed = together(partial[1], normed)
    partial.append(hop(partial[2], 1))
    if spreads:
        partial[3], swapped = together(partial[3], swapped)
    devices = count if spreads else 4 * count
    stat, *wires = call(
        functools.partial(first_sums_kernel, size),
        [shaped((devices, 8, LANES))] + [shaped((ROWS, lanes), BF16) for _, lanes in size.parts],
        [
            pltpu.VMEM((size.cells, frames, LANES), F32),
            pltpu.VMEM((side + 2, side + 2, frames, LANES), F32),
            pltpu.VMEM((size.cells, frames, LANES), F32),
        ]
        + spread_rows(size) * 2,
        [me],
        [*partial, g0, g1, z0, z1, totals, table, mask],
        ins={6: cell_parts(size), 7: cell_parts(size)},
        puts={0: (0, [(0, devices)])} | {1 + part: span_parts(size, span) for part, span in enumerate(size.parts)},
    )
    others, cores = [hop(wire, 2) for wire in wires[:1]] + [None] * (len(wires) - 1), [hop(wire, 1) for wire in wires]
    inner = moments(size, me, [[wire] for wire in wires], pieces)
    if spreads:
        bits = count.bit_length() - 1
        back1 = share(stat)
        early = jnp.sum(swapped.astype(F32), 0).astype(BF16)
        halves = other_of(early, bits - 1, count)
        back1, inner, others[0], halves = together(back1, inner, others[0], halves)
        dense_grad, table_own = weight_grad(size, me, inner, moment, back1, kernel_grad, count)
        tables = exchange_four([table_own] * 4)
        tables, last = together(tables, wires[1])
        others[1] = hop(last, 2)
        swapped = swap_shares(dense_grad, count)
    else:
        back1 = share_all(stat, count)
        back1, others[0], moment = together(back1, others[0], moment)

    def four(part):
        return [wires[part], cores[part], others[part], hop(others[part], 1)]

    scratch = [pltpu.VMEM((2, size.parts[0][1] + LANES, LANES), F32), pltpu.VMEM((8 * ROWS + 16, 2 * LANES), BF16)]
    if not spreads:
        top, top_args = above
        result = call(
            functools.partial(input_half_sums_kernel, size, top),
            [tile, tile, tile, shaped((count, 8, LANES))],
            scratch + spread_rows(top),
            [me],
            [*four(0), *normed[0], shapes[0], *weights_at, back1, *top_args],
            ins={index: column_parts(size, size.whole) for index in range(9)} | {14: cell_parts(top)},
            stacks=[range(9)],
        )
        return result, inner, kernel_grad, back1, moment
    shape = shaped((size.cells, frames // 8, 8 * QUARTER))
    result, sets = (), []
    for part, span in enumerate(size.parts):
        if part:
            for bit in range(bits - 1, 0, -1):
                early = joined_halves(group, bit, early, halves)
                halves = other_of(early, bit - 1, count)
                if bit == 2:
                    swapped, halves = together(swapped, halves)
            late = all_shares([swapped])
        sets.append([*four(part), *normed[part], shapes[part]])
        low, high, base = input_plan(size, part)
        args = list(sets[part])
        ins = {index: column_parts(size, span) for index in range(9)}
        stacks = [range(9)]
        if part:
            before = size.parts[part - 1]
            tail = (1, [(base - before[0], span[0] - base)])
            ins |= {len(args) + index: tail for index in range(9)}
            stacks.append(range(9, 18))
            args += sets[part - 1]
        args += [*weights_at, *tables]
        if part:
            ins[len(args)] = (0, [])
        result = call(
            functools.partial(input_kernel, size, part),
            [shape],
            scratch,
            [me],
            [*args, *result],
            ins=ins,
            puts={0: line_parts(size, low, high - low)},
            aliases={len(args): 0} if part else None,
            stacks=stacks,
        )
    return result, (early, halves, late), back1


def on_device(count, clips, clip_len, w_plain, w_mid, k_mid, w_small, k_small, w_pool, gains, shifts, grad_out):
    big = Size(clips.shape[1], 8 * clips.shape[0])
    low = Size(grad_out.shape[1], 8 * grad_out.shape[0])
    me = lax.axis_index("chan").astype(jnp.int32).reshape(1)
    group = lax.axis_index("dp").astype(jnp.int32).reshape(1)
    everyone = 4 * count
    raw = clips.transpose(1, 2, 0, 3).reshape(big.cells, clips.shape[0], 8 * QUARTER)
    (own,) = call(
        functools.partial(unpack_kernel, big),
        [shaped((QUARTER, big.padded), BF16)],
        [pltpu.VMEM((2, big.rows + ROOM, LANES), F32)],
        [],
        [raw],
        ins={0: line_parts(big)},
        puts={0: span_parts(big, big.whole)},
    )
    other, core = hop(own, 2), hop(own, 1)
    low_tile = shaped((low.cells, low.frames, LANES))
    grads = call(
        functools.partial(grad_kernel, low),
        [low_tile, low_tile, low_tile],
        [pltpu.VMEM((2, low.rows + ROOM, LANES), F32)],
        [],
        [grad_out],
    )
    table = shaped((8, LANES))
    prepared = call(
        prepare_kernel,
        [shaped((3, big.frames, LANES)), shaped((3, low.frames, LANES))]
        + [table] * 4
        + [shaped((2, ROWS, 2 * LANES), BF16)] * 4
        + [shaped((4, QUARTER, 2 * LANES), BF16)] * 2
        + [shaped((9, LANES, 4 * REDUCED), BF16)] * 2
        + [shaped((9, 2 * LANES, LANES), BF16)] * 2
        + [table] * 2,
        [
            pltpu.VMEM((2 * MID_ROWS + 6 * ROOM, LANES), F32),
            pltpu.VMEM((2, 4, 2, ROWS, LANES), F32),
            pltpu.VMEM((9, 2, LANES, LANES), F32),
        ],
        [me, clip_len],
        [as_rows(item) for item in (w_plain, w_mid, w_small, w_pool, k_mid, k_small, gains, shifts)],
    )
    mask, mask_low, table0, second0, table1, second1 = prepared[:6]
    sent, (dense0, dense1), (kernel0, kernel1), (turned0, turned1), (along, along_low) = (
        prepared[6:10],
        prepared[10:12],
        prepared[12:14],
        prepared[14:16],
        prepared[16:18],
    )
    begun = project_begin(big, me, [own, core], dense0)
    other, begun, grads = together(other, begun, grads)
    pieces = [own, core, other, hop(other, 1)]
    z0, z1, stat, wire = project(big, me, pieces[2:], (2, 3), dense0, mask, table0, everyone, begun)
    mids = [wire, hop(wire, 1), hop(wire, 2)]
    totals = share_all(stat, count)
    totals, mids[2] = together(totals, mids[2])
    mids.append(hop(mids[2], 1))
    half = [pltpu.VMEM((big.rows // 4, LANES), F32)]
    h0, h1 = call(
        functools.partial(first_half_kernel, big),
        [low_tile, low_tile],
        half * 2,
        [me],
        [z0, z1, totals, table0, mask],
        flops=big.rows * 2 * LANES * 20,
        ins={0: cell_parts(big), 1: cell_parts(big)},
    )
    field, z2, stat = forward_second(big, me, group, mids, totals, along, turned0, mask, count)
    totals2 = share(stat)
    weights_at = exchange_four(sent)
    totals2, weights_at = together(totals2, weights_at)
    (own1,) = call(
        functools.partial(second_half_kernel, big),
        [shaped((QUARTER, low.padded), BF16)],
        half,
        [],
        [z2, totals2, second0, mask, h0, h1],
        flops=big.rows * LANES * 20,
        ins={0: cell_parts(big)},
    )
    pieces1 = gather_four(own1)
    y0, y1, stat, wire = project(low, me, pieces1, (0, 1, 2, 3), dense1, mask_low, table1, everyone)
    mids = exchange_four([wire] * 4)
    totals1 = share_all(stat, count)
    normed, shapes = normed_wires(big, me, z0, z1, totals, table0, mask)
    totals1, normed, shapes = together(totals1, normed, shapes)
    field1, y2, stat = forward_second(low, me, group, mids, totals1, along_low, turned1, mask_low, count)
    totals3 = share(stat)
    normed1, shapes1 = normed_wires(low, me, y0, y1, totals1, table1, mask_low)
    totals3, normed1 = together(totals3, normed1)
    (mixed,) = call(
        functools.partial(output_kernel, low),
        [shaped(grad_out.shape, BF16)],
        [pltpu.VMEM((2, low.rows + ROOM, LANES), F32)],
        [me],
        [y0, y1, y2, totals1, totals3, table1, second1, mask_low],
    )
    saved1 = (y0, y1, totals1, field1, y2, totals3, table1, second1, mask_low, kernel1, pieces1, normed1, shapes1)
    (back2,) = second_sums(low, grads, saved1, count)
    back2 = share(back2)
    moment1 = moments(low, me, list(zip(normed1, shapes1)), pieces1)
    normed1 = [[wire, hop(wire, 1), hop(wire, 2)] for wire in normed1]
    back2, mixed, normed1, moment1 = together(back2, mixed, normed1, moment1)
    normed1 = [[*wires, hop(wires[2], 1)] for wires in normed1]
    moment = moments(big, me, list(zip(normed, shapes)), pieces)
    grads, inputs1, kernel_grad1, first1, moment = backward(
        low, me, grads, back2, saved1, normed1, weights_at, count, None, moment, above=(big, (z2, totals2, second0, mask))
    )
    last1 = back2
    *grads, back2 = grads

    saved0 = (z0, z1, totals, field, z2, totals2, table0, second0, mask, kernel0, pieces, normed, shapes)
    back2, normed = together(back2, normed)
    back2 = share(back2)
    normed = [[wire, hop(wire, 1), hop(wire, 2)] for wire in normed]
    dense_grad1, _ = weight_grad(low, me, inputs1, moment1, first1, kernel_grad1, count)
    back2, dense_grad1, normed[0] = together(back2, dense_grad1, normed[0])
    last0 = back2
    (clips_grad,), (early, halves, late), first0 = backward(
        big, me, grads, back2, saved0, normed, weights_at, count, dense_grad1, moment, group
    )

    def sized(outputs):
        rows = outputs * CIN // 64
        return shaped((rows, LANES) if rows % 16 == 0 else (2, rows * 64))

    pairs_rows = pltpu.VMEM((2 * MID_ROWS + ROOM, LANES), F32)
    outs = [sized(outputs) for outputs in (MID, SMALL, PLAIN, POOL)]
    outs += [shaped((2, MID_ROWS * LANES)), shaped((2 * SMALL_ROWS, LANES))] + [shaped((4, LANES))] * 2
    mid, small, plain, pool, wide, narrow, gains_grad, shifts_grad = call(
        finish_kernel,
        outs,
        [pltpu.VMEM((count * late.shape[1], LANES), F32)] * 2 + [pairs_rows],
        [me, group],
        [early, halves, late, first0, first1, last0, last1],
        ins={2: (0, [(0, count)])},
        puts={4: (0, [(0, 2)])},
    )
    flats = [plain, mid, wide, small, narrow, pool, gains_grad, shifts_grad]
    flats = [item if item.shape[0] == 2 else as_flat(item) for item in flats]
    shape = (big.side, big.side, big.frames // 8, 8 * QUARTER)
    return mixed, clips_grad.reshape(shape).transpose(2, 0, 1, 3), *flats


def solution(mesh):
    frames = P("dp", None, None, "chan")
    flat = P(None, "chan")
    return jax.shard_map(
        functools.partial(on_device, mesh.shape["dp"]),
        mesh=mesh,
        in_specs=(frames, P("dp")) + (flat,) * 8 + (frames,),
        out_specs=(frames, frames) + (flat,) * 8,
        check_vma=False,
    )
```

```python
import functools

import jax
import jax.numpy as jnp
from jax import lax
from jax.experimental import pallas as pl
from jax.experimental.pallas import tpu as pltpu
from jax.sharding import PartitionSpec as P

CIN = 832
QUARTER = 208
WIDE, NARROW = 80, 32
MID, SMALL, PLAIN, POOL = 40, 8, 64, 32
REDUCED = MID + SMALL
DENSE = REDUCED + PLAIN
ROWS = DENSE + POOL
CLIPS = 2
EPSILON = 1e-05
F32 = jnp.float32
BF16 = jnp.bfloat16
LANES = 128
LIMIT = 64
ROOM = 64
COST = 1
MID_TILES = 4 * 9 * 160 // LANES
MID_ROWS = WIDE // 4 * MID_TILES
SMALL_TILES = 4 * 9 * 32 // LANES
SMALL_ROWS = NARROW // 4 * SMALL_TILES
KERNEL_ROWS = 976
PAIR_TILES = 2 * CIN // LANES
DENSE_ROWS = 944


class Size:
    def __init__(self, side, frames):
        self.side = side
        self.frames = frames
        self.cells = side * side
        self.rows = self.cells * frames
        self.padded = -(-self.rows // LANES) * LANES
        self.band = 2 if side % 2 == 0 else side
        self.chunks = side // self.band
        self.step = self.band * side
        self.group = LANES // frames
        self.full = self.cells // self.group
        self.rest = self.cells - self.full * self.group
        self.kept = BF16 if frames % 16 == 0 else F32
        self.whole = (0, self.padded)
        first = 13 * LANES
        self.parts = [(0, first), (first, self.padded - first)] if self.padded > 2 * first - LANES - 1 else [self.whole]

    def cells_of(self, span):
        first = span[0] // self.frames
        return first, min(span[1] // self.frames, self.cells - first)

    def columns_of(self, span, width=640):
        first, count = self.cells_of(span)
        result = []
        for start in range(0, span[1], width):
            skipped, held = start // self.frames, min(width, span[1] - start)
            result.append((start, held, first + skipped, min(held // self.frames, count - skipped)))
        return result


class Stream:
    def __init__(self, far, near, sems, axis, parts, window=None):
        self.far, self.near, self.sems, self.axis, self.parts = far, near, sems, axis, parts
        self.window = window
        self.shape, self.dtype = near.shape, near.dtype

    def copy(self, part, inward):
        if isinstance(part, int):
            start, count = self.parts[part]
        else:
            first, count = self.parts[0]
            start = first + part * count
        index = (slice(None),) * self.axis + (pl.ds(start, count),)
        away = (pl.ds(*self.window),) + index[1:] if self.window else index
        pair = (self.far.at[away], self.near.at[index])
        return pltpu.make_async_copy(*(pair if inward else pair[::-1]), self.sems.at[part])

    def ready(self, part):
        self.copy(part, True).wait()

    def flush(self, part):
        self.copy(part, False).start()

    def __getitem__(self, index):
        return self.near[index]

    def __setitem__(self, index, value):
        self.near[index] = value

    @property
    def at(self):
        return self.near.at


def even(total, count):
    return [(start * (total // count), total // count) for start in range(count)]


def cell_parts(size):
    return 0, even(size.cells, size.chunks)


def line_parts(size, first=0, count=None):
    return 0, [(row * size.side, size.side) for row in range(first, first + (count or size.side))]


def column_parts(size, span, width=640):
    return 1, [(start, held) for start, held, _, _ in size.columns_of(span, width)]


def call(body, outs, scratch, scalars, args, flops=0, ins=None, puts=None, aliases=None, stacks=()):
    ins, puts = ins or {}, puts or {}
    places = {}

    def height(index):
        plan = ins.get(index)
        return plan[2][1] if plan and len(plan) > 2 else args[index].shape[0]

    for stack, members in enumerate(stacks):
        start = 0
        for index in members:
            places[index] = (stack, start)
            start += height(index)
    aliases = {len(scalars) + index: out for index, out in (aliases or {}).items()}
    plans = [ins.get(index) for index in range(len(args))] + [puts.get(index) for index in range(len(outs))]
    arrays = list(args) + list(outs)
    buffers = []
    for index, (array, plan) in enumerate(zip(arrays, plans)):
        if index not in places:
            rows = height(index) if index < len(args) else array.shape[0]
            buffers.append(pltpu.VMEM((rows,) + array.shape[1:], array.dtype))
        buffers.append(pltpu.SemaphoreType.DMA((max(len(plan[1]), 1) if plan else 1,)))
    for members in stacks:
        rows = sum(height(index) for index in members)
        buffers.append(pltpu.VMEM((rows,) + args[members[0]].shape[1:], args[members[0]].dtype))

    def wrapped(*refs):
        numbers, refs = refs[: len(scalars)], refs[len(scalars) :]
        far, refs = refs[: len(arrays)], refs[len(arrays) :]
        own, refs = refs[: len(scratch)], list(refs[len(scratch) :])
        whole = refs[len(refs) - len(stacks) :]
        streams = []
        for index, plan in enumerate(plans):
            axis, parts, *window = plan or (0, [(0, arrays[index].shape[0])])
            if index in places:
                stack, start = places[index]
                near = whole[stack].at[pl.ds(start, height(index))]
            else:
                near = refs.pop(0)
            streams.append(Stream(far[index], near, refs.pop(0), axis, parts, *window))
        entering, leaving = streams[: len(args)], streams[len(args) :]
        for part in range(max([len(stream.parts) for stream in entering])):
            for stream in entering:
                if part < len(stream.parts):
                    stream.copy(part, True).start()
        for index, stream in enumerate(entering):
            if index not in ins:
                stream.ready(0)
        body(*numbers, *entering, *leaving, *own, *whole)
        for index, stream in enumerate(leaving):
            if index not in puts:
                stream.flush(0)
        for stream in leaving:
            for part in range(len(stream.parts)):
                stream.copy(part, False).wait()

    moved = sum(array.size * array.dtype.itemsize for array in arrays)
    return pl.pallas_call(
        wrapped,
        out_shape=outs,
        in_specs=[pl.BlockSpec(memory_space=pltpu.SMEM)] * len(scalars) + [pl.BlockSpec(memory_space=pl.ANY)] * len(args),
        out_specs=[pl.BlockSpec(memory_space=pl.ANY)] * len(outs),
        scratch_shapes=list(scratch) + buffers,
        compiler_params=pltpu.CompilerParams(vmem_limit_bytes=LIMIT * 1024 * 1024),
        cost_estimate=pl.CostEstimate(flops=COST, bytes_accessed=COST, transcendentals=0),
        input_output_aliases=aliases,
    )(*scalars, *args)


def unrolled(count, body, carry):
    for index in range(count):
        carry = body(index, carry)
    return carry


def rolled(count, body, carry):
    if count == 1:
        return body(0, carry)
    return lax.fori_loop(0, count, body, carry)


def shaped(shape, dtype=F32):
    return jax.ShapeDtypeStruct(shape, dtype)


def sigmoid(value):
    return 0.5 * jnp.tanh(0.5 * value) + 0.5


def row_table(rows):
    index = lax.broadcasted_iota(jnp.int32, (8, LANES), 0)
    table = jnp.zeros((8, LANES), F32)
    for position, row in enumerate(rows):
        table = jnp.where(index == position, row, table)
    return table


def time_box(value, mask_ref):
    cells, frames, width = value.shape
    flat = value.reshape(cells * frames, width)
    before = pltpu.roll(flat, 1, 0).reshape(value.shape)
    after = pltpu.roll(flat, cells * frames - 1, 0).reshape(value.shape)
    return value + before * mask_ref[1] + after * mask_ref[2]


def owner_rows(all_ref, owner):
    if len(all_ref.shape) == 3:
        return all_ref[...]
    return all_ref[:, pl.ds(owner, 1)].reshape(all_ref.shape[0], 8, LANES)


def norm_rows(all_ref, table_ref, tile, owner=0):
    total = jnp.sum(owner_rows(all_ref, owner), 0)
    count = total[4:5]
    mean = total[2 * tile : 2 * tile + 1] / count
    variance = total[2 * tile + 1 : 2 * tile + 2] / count - mean * mean
    inverse = lax.rsqrt(variance + EPSILON)
    gain = table_ref[2 * tile : 2 * tile + 1]
    shift = table_ref[2 * tile + 1 : 2 * tile + 2]
    return mean, inverse, gain, shift, count


def activate(value, rows, mask_ref):
    mean, inverse, gain, shift, _ = rows
    shifted = gain * ((value - mean) * inverse) + shift
    return shifted * sigmoid(shifted) * mask_ref[0]


def inner_grad(grad, value, rows, mask_ref):
    mean, inverse, gain, shift, _ = rows
    normed = (value - mean) * inverse
    shifted = gain * normed + shift
    sigma = sigmoid(shifted)
    return grad * mask_ref[0] * sigma * (1.0 + shifted * (1.0 - sigma)), normed


def norm_delta(inner, value, rows, back_ref, tile, mask_ref):
    mean, inverse, gain, _, count = rows
    total = jnp.sum(back_ref[...], 0)
    shift_grad = total[2 * tile : 2 * tile + 1] / count
    gain_grad = total[2 * tile + 1 : 2 * tile + 2] / count
    normed = (value - mean) * inverse
    return (gain * inverse) * (inner - mask_ref[0] * (shift_grad + normed * gain_grad))


def publish(stat_ref, rows):
    stat_ref[...] = jnp.broadcast_to(row_table(rows)[None], stat_ref.shape)


def collapse(value):
    return jnp.sum(value, 0, keepdims=True)


def windows():
    result = []
    for frame in range(8):
        start = frame * QUARTER
        first, offset = start // LANES, start % LANES
        result.append((first, -(-(offset + QUARTER) // LANES), offset))
    return result


def unpack_rows(line, frame):
    first, tiles, offset = windows()[frame]
    value = line[:, first * LANES : (first + tiles) * LANES]
    if offset:
        value = pltpu.roll(value, tiles * LANES - offset, 1)
    return value[:, : 2 * LANES]


def pack_rows(parts):
    tiles = [None] * 13
    for frame, value in enumerate(parts):
        first, count, offset = windows()[frame]
        if count == 3:
            value = jnp.concatenate([value, jnp.zeros((value.shape[0], LANES), value.dtype)], 1)
        if offset:
            value = pltpu.roll(value, offset, 1)
        for index in range(count):
            piece = value[:, index * LANES : (index + 1) * LANES]
            place = first + index
            tiles[place] = piece if tiles[place] is None else tiles[place] + piece
    return tiles


def assemble(first, second, third):
    blank = jnp.zeros_like(first)
    lane = lax.broadcasted_iota(jnp.int32, (first.shape[0], 2 * LANES), 1)
    plain = pltpu.roll(jnp.concatenate([first, blank], 1), 2 * LANES - REDUCED, 1)
    middle = pltpu.roll(jnp.concatenate([second, blank], 1), PLAIN, 1)
    pool = pltpu.roll(jnp.concatenate([third, blank], 1), PLAIN + WIDE + NARROW, 1)
    return jnp.where(lane < PLAIN, plain, 0.0) + middle + pool


def separate(value):
    lane = lax.broadcasted_iota(jnp.int32, (value.shape[0], LANES), 1)
    plain = pltpu.roll(value, REDUCED, 1)[:, :LANES]
    middle = pltpu.roll(value, 2 * LANES - PLAIN, 1)[:, :LANES]
    pool = pltpu.roll(value, 2 * LANES - PLAIN - WIDE - NARROW, 1)[:, :LANES]
    first = jnp.where((lane >= REDUCED) & (lane < DENSE), plain, 0.0)
    second = jnp.where(lane < WIDE + NARROW, middle, 0.0)
    third = jnp.where(lane < POOL, pool, 0.0)
    return first, second, third


def span_blocks(size, span, one, leaving=(), rolled=False):
    first, count = size.cells_of(span)
    total, whole = span[1] // LANES, count // size.group

    def block(index, cells):
        start = index * LANES
        start = start if isinstance(start, int) else pl.multiple_of(start, LANES)
        one(first + index * size.group, cells, pl.ds(start, LANES))

    def four(index, carry):
        for extra in range(4):
            block(index * 4 + extra, size.group)
        for stream in leaving:
            stream.flush(index)
        return carry

    groups = whole // 4 if rolled else 0
    if rolled:
        lax.fori_loop(0, groups, four, 0)
    for index in range(groups * 4, total):
        block(index, min(size.group, count - index * size.group))
        if index % 4 == 3 or index == total - 1:
            for stream in leaving:
                stream.flush(index // 4)


def span_parts(size, span):
    return column_parts(size, span, 4 * LANES)


def unpack_kernel(size, raw, out, scratch):
    side, frames = size.side, size.frames
    pairs_of = frames // 8
    def line(row, carry):
        raw.ready(row)
        value = raw[pl.ds(row * side, side)].astype(F32).reshape(pairs_of * side, 8 * QUARTER)
        for frame in range(8):
            place = pl.ds(row * side * frames + frame, pairs_of * side, stride=8)
            piece = unpack_rows(value, frame)
            scratch[0, place, :] = piece[:, :LANES]
            scratch[1, place, :] = piece[:, LANES:]
        return carry

    lax.fori_loop(0, side, line, 0)

    def one(cell, cells, lanes):
        start = cell * frames
        for tile, (low, high) in enumerate(((0, LANES), (LANES, QUARTER))):
            value = scratch[tile, pl.ds(start, cells * frames), :].reshape(cells, frames, LANES)
            out[low:high, lanes] = turn(size, value, cells)[: high - low].astype(BF16)

    span_blocks(size, size.whole, one, (out,))


def grad_kernel(size, raw, first, second, third, scratch):
    side, frames = size.side, size.frames

    def line(row, carry):
        value = raw[0, row].astype(F32)
        for frame in range(8):
            place = pl.ds(row * side * frames + frame, side, stride=frames)
            part = unpack_rows(value, frame)
            scratch[0, place, :] = part[:, :LANES]
            scratch[1, place, :] = part[:, LANES:]
        return carry

    unrolled(side, line, 0)
    parts = separate(jnp.concatenate([scratch[0, : size.rows], scratch[1, : size.rows]], 1))
    for ref, part in zip((first, second, third), parts):
        ref[...] = part.reshape(ref.shape)


def dot(left, right, dims=((1,), (0,))):
    return lax.dot_general(left, right, (dims, ((), ())), preferred_element_type=F32)


def into_padded(size, flat, field):
    side = size.side
    field[...] = jnp.zeros_like(field)

    def line(row, carry):
        field[row + 1, 1 : side + 1] = flat[pl.ds(row * side, side)]
        return carry

    unrolled(side, line, 0)


def stacked_weights(me, positions, w_ref, stacked):
    for index, position in enumerate(positions):
        stacked[index * QUARTER : (index + 1) * QUARTER] = w_ref[me[0] ^ position]


def each_column(size, body, carry):
    plan = size.columns_of(size.whole)
    _, width, _, cells = plan[0]

    def step(index, carry):
        return body(index, pl.multiple_of(index * width, LANES), width, index * cells, cells, carry)

    if len(plan) > 1:
        carry = lax.fori_loop(0, len(plan) - 1, step, carry)
    return body(len(plan) - 1, *plan[-1], carry)


def project_begin_kernel(size, me, x0, x1, w_ref, dense, pool, stacked, stack):
    frames = size.frames
    stacked_weights(me, (0, 1), w_ref, stacked)

    def column(index, start, width, first, cells, carry):
        for x in (x0, x1):
            x.ready(index)
        value = dot(stack[:, pl.ds(start, width)], stacked[...], ((0,), (0,)))
        value = value.reshape(width // frames, frames, 2 * LANES)[:cells]
        dense[pl.ds(first, cells)] = value[:, :, :LANES]
        pool[pl.ds(first, cells)] = value[:, :, LANES:]
        dense.flush(index)
        pool.flush(index)
        return carry

    each_column(size, column, 0)


def project_kernel(size, positions, me, *refs):
    side, frames = size.side, size.frames
    pieces, (w_ref, mask, table), refs = refs[: len(positions)], refs[len(positions) : len(positions) + 3], refs[len(positions) + 3 :]
    begun = refs[:2] if len(positions) < 4 else None
    z0, z1, stat, wire, field, flat, stacked, stack = refs[-8:]
    stacked_weights(me, positions, w_ref, stacked)
    blank = jnp.zeros((frames, LANES), F32)
    total, squares = blank, blank

    def column(index, start, width, first, cells, carry):
        total, squares = carry
        for x in pieces:
            x.ready(index)
        value = dot(stack[:, pl.ds(start, width)], stacked[...], ((0,), (0,)))
        value = value.reshape(width // frames, frames, 2 * LANES)[:cells]
        dense, pool = value[:, :, :LANES], value[:, :, LANES:]
        place = pl.ds(first, cells)
        if begun:
            for stream in begun:
                stream.ready(index)
            dense += begun[0][place]
            pool += begun[1][place]
        z0[place] = dense
        z0.flush(index)
        flat[place] = pool
        return total + jnp.sum(dense, 0), squares + jnp.sum(dense * dense, 0)

    total, squares = each_column(size, column, (total, squares))
    valid = mask[0]
    total, squares = collapse(total * valid), collapse(squares * valid)
    count = collapse(valid) * size.cells
    mean = total / count

    def one(cell, cells, lanes):
        wire[:, lanes] = turn(size, z0[pl.ds(cell, cells)] - mean, cells)[:REDUCED].astype(BF16)

    span_blocks(size, size.whole, one, (), True)
    into_padded(size, flat, field)

    def line(row, carry):
        pool_total, pool_squares = carry
        pool = pool_line(size, field, row, mask)
        z1[pl.ds(row * side, side)] = pool
        z1.flush(row)
        return pool_total + jnp.sum(pool, 0), pool_squares + jnp.sum(pool * pool, 0)

    pool_total, pool_squares = lax.fori_loop(0, side, line, (blank, blank))
    rows = [total, squares, collapse(pool_total * valid), collapse(pool_squares * valid), count]
    publish(stat, rows + [table[0:1], table[1:2]])


def normed_kernel(size, me, z0, z1, totals, table, mask, *refs):
    outs, (field, pooled) = refs[:-2], refs[-2:]
    side, frames, step = size.side, size.frames, size.step
    lane = lax.broadcasted_iota(jnp.int32, (frames, LANES), 1)
    field[...] = jnp.zeros_like(field)
    rows = [norm_rows(totals, table, tile, me[0]) for tile in range(2)]
    scales = [(gain * inverse * inverse, mean) for mean, inverse, gain, _, _ in rows]

    def chunk(index, carry):
        z1.ready(index)
        scale, mean = scales[1]
        value = (z1[pl.ds(index * step, step)] - mean) * scale
        value = jnp.where(lane == POOL, 1.0, value) * mask[0]
        field[pl.ds(1 + index * size.band, size.band), 1 : side + 1] = value.reshape(size.band, side, frames, LANES)
        return carry

    rolled(size.chunks, chunk, 0)
    pool_lines(size, field, pooled, mask)
    for index in range(size.chunks):
        z0.ready(index)
    for part, span in enumerate(size.parts):
        normed, shapes = outs[2 * part : 2 * part + 2]

        def one(cell, cells, lanes, normed=normed, shapes=shapes):
            scale, mean = scales[0]
            value = (z0[pl.ds(cell, cells)] - mean) * scale
            dense = turn(size, jnp.where(lane == DENSE, 1.0, value) * mask[0], cells)
            pool = turn(size, pooled[pl.ds(cell, cells)], cells)
            normed[0:DENSE, lanes] = dense[:DENSE].astype(BF16)
            normed[DENSE:ROWS, lanes] = pool[:POOL].astype(BF16)
            both = jnp.concatenate([dense[DENSE : DENSE + 8], pool[POOL : POOL + 8]], 0)
            shapes[:, lanes] = both.astype(BF16)

        span_blocks(size, span, one, (normed,), True)


def pool_lines(size, field, pooled, mask):
    def line(row, carry):
        pooled[pl.ds(row * size.side, size.side)] = pool_line(size, field, row, mask)
        return carry

    lax.fori_loop(0, size.side, line, 0)


def moments_kernel(size, me, *refs):
    (out, stack), pieces = refs[-2:], refs[-6:-2]
    lefts = refs[:-6]
    each = len(lefts) // len(size.parts)
    lefts = [lefts[part * each : (part + 1) * each] for part in range(len(size.parts))]
    lefts = [group[0][...] if each == 1 else jnp.concatenate([item[...] for item in group], 0) for group in lefts]
    value = jnp.zeros((4 * QUARTER, lefts[0].shape[0]), F32)
    for part, (left, (start, count)) in enumerate(zip(lefts, size.parts)):
        for x in pieces:
            x.ready(part)
        value += dot(stack[:, start : start + count], left, ((1,), (1,)))
    for position in range(4):
        piece = value[position * QUARTER : (position + 1) * QUARTER]
        piece = jnp.concatenate([piece, jnp.zeros((2 * LANES - QUARTER, piece.shape[1]), F32)], 0)
        out[me[0] ^ position] = piece.T


def back_columns(back, owner):
    if len(back.shape) == 2:
        parts = back[:, :LANES].astype(F32)
        return columns_of_table(parts[:8] + parts[8:])
    return columns_of_table(back_table(back, owner))


def back_table(back, owner):
    every = owner_rows(back, owner)
    total, own = jnp.sum(every, 0), every[0]
    count = own[6:7]
    rows = [total[1:2] / count, total[3:4] / count, own[4:5] * total[0:1] / count, own[5:6] * total[2:3] / count]
    return row_table(rows)


def columns_of_table(table):
    turned = table.T
    slope = jnp.concatenate([turned[:DENSE, 0:1], turned[:POOL, 1:2]], 0)
    offset = jnp.concatenate([turned[:DENSE, 2:3], turned[:POOL, 3:4]], 0)
    return slope, offset


def weight_grad_kernel(size, me, inner, moments, back, kernels, out, table, grads, flat):
    value = back_table(back, me[0])
    slope, offset = columns_of_table(value)
    upper = value.astype(BF16).astype(F32)
    table[...] = jnp.concatenate([upper, value - upper], 0).astype(BF16)
    for owner in range(4):
        shape = moments[owner, ROWS : ROWS + 16]
        value = inner[owner] - slope * moments[owner, 0:ROWS]
        first = value[:DENSE] - offset[:DENSE] * shape[0:1]
        last = value[DENSE:] - offset[DENSE:] * shape[8:9]
        value = jnp.concatenate([first, last], 0)
        grads[owner, 0] = value[:, :LANES]
        grads[owner, 1] = value[:, LANES:]
    parts = []
    for extra in range(2):
        rows = pl.ds(extra, ROWS // 2, stride=2)
        for owner in range(4):
            parts.append(jnp.concatenate([grads[owner, 0, rows, :], grads[owner, 1, rows, :]], 1))
    for place, tile in enumerate(pack_rows(parts)):
        flat[pl.ds(place, ROWS // 2, stride=PAIR_TILES), :] = tile
    used = ROWS // 2 * PAIR_TILES
    flat[used:, :] = jnp.zeros((DENSE_ROWS - used, LANES), F32)
    out[:KERNEL_ROWS, :] = kernels[...]
    out[KERNEL_ROWS : KERNEL_ROWS + DENSE_ROWS, :] = flat[...].astype(BF16)
    rest = out.shape[0] - KERNEL_ROWS - DENSE_ROWS
    if rest:
        out[KERNEL_ROWS + DENSE_ROWS :, :] = jnp.zeros((rest, LANES), BF16)


def pool_line(size, field, row, mask):
    side = size.side
    lines = field[pl.ds(row, 3)]
    column = lines[0] + lines[1] + lines[2]
    value = column[0:side] + column[1 : side + 1] + column[2 : side + 2]
    return time_box(value, mask) * (1.0 / 27.0)


def turn(size, value, cells):
    flat = value.reshape(cells * size.frames, value.shape[-1])
    if cells < size.group:
        blank = jnp.zeros((LANES - cells * size.frames, value.shape[-1]), value.dtype)
        flat = jnp.concatenate([flat, blank], 0)
    return flat.T


def conv_kernel(size, me, group, p0, p1, p2, p3, totals, lanes_valid, kernel, mask, field, z2, stat, joined):
    side, frames, step = size.side, size.frames, size.step
    for position, piece in enumerate((p0, p1, p2, p3)):
        owner = me[0] ^ position
        every = owner_rows(totals, owner)
        total = jnp.sum(every, 0)
        sent = totals[pl.ds(group[0], 1), pl.ds(owner, 1)].reshape(8, LANES)
        mean = total[0:1] / total[4:5]
        variance = total[1:2] / total[4:5] - mean * mean
        scale = sent[5:6] * lax.rsqrt(variance + EPSILON)
        offset = (sent[0:1] / sent[4:5] - mean) * scale + sent[6:7]
        turned = row_table([scale, offset]).T
        scale, offset = turned[:REDUCED, 0:1], turned[:REDUCED, 1:2]
        shifted = piece[...].astype(F32) * scale + offset
        value = shifted * sigmoid(shifted)
        joined[pl.ds(pl.multiple_of(owner * MID, 8), MID), :] = value[:MID]
        joined[pl.ds(pl.multiple_of(4 * MID + owner * SMALL, 8), SMALL), :] = value[MID:]
    field[...] = jnp.zeros_like(field)
    joined[4 * REDUCED :, :] = jnp.zeros((2 * LANES - 4 * REDUCED, size.padded), F32)

    def one(first, cells, lanes):
        value = (joined[:, lanes] * lanes_valid[0:1]).T
        value = value.reshape(size.group, frames, 2 * LANES).astype(size.kept)
        for index in range(cells):
            cell = first + index
            row = cell // side if isinstance(cell, int) else lax.div(cell, side)
            field[row + 1, cell - row * side + 1] = value[index]

    span_blocks(size, size.whole, one)
    field.flush(0)
    kernel.ready(0)
    blank = jnp.zeros((frames, LANES), F32)

    def chunk(index, carry):
        total, squares = carry
        parts = []
        for row in range(3):
            for column in range(3):
                part = field[pl.ds(index * size.band + row, size.band), column : column + side]
                parts.append(part.reshape(step * frames, 2 * LANES).astype(BF16))
        value = dot(jnp.concatenate(parts, 1), kernel[...].reshape(18 * LANES, LANES))
        value = time_box(value.reshape(step, frames, LANES), mask) * (1.0 / 3.0)
        z2[pl.ds(index * step, step)] = value
        z2.flush(index)
        return total + jnp.sum(value, 0), squares + jnp.sum(value * value, 0)

    total, squares = unrolled(size.chunks, chunk, (blank, blank))
    valid = mask[0]
    one_row = jnp.zeros((1, LANES), F32)
    rows = [collapse(total * valid), collapse(squares * valid), one_row, one_row, collapse(valid) * size.cells]
    publish(stat, rows)


def halve_into(size, value, scratch, index):
    half = size.side // 2
    value = value.reshape(2, half, 2, size.frames, LANES)
    value = value[0] + value[1]
    value = value[:, 0] + value[:, 1]
    rows = half * size.frames
    scratch[pl.ds(index * rows, rows), :] = value.reshape(rows, LANES)


def halved_rows(scratch):
    count = scratch.shape[0] // 2
    return (scratch[pl.ds(0, count, stride=2), :] + scratch[pl.ds(1, count, stride=2), :]) * 0.125


def first_half_kernel(size, me, z0, z1, totals, table, mask, h0, h1, s0, s1):
    for tile, (z, out, scratch) in enumerate(((z0, h0, s0), (z1, h1, s1))):
        rows = norm_rows(totals, table, tile, me[0])

        def chunk(index, carry, z=z, scratch=scratch, rows=rows):
            z.ready(index)
            value = activate(z[pl.ds(index * size.step, size.step)], rows, mask)
            halve_into(size, value, scratch, index)
            return carry

        rolled(size.chunks, chunk, 0)
        out[...] = halved_rows(scratch).reshape(out.shape)


def second_half_kernel(size, z2, totals, table, mask, h0, h1, out, scratch):
    rows = norm_rows(totals, table, 0)

    def chunk(index, carry):
        z2.ready(index)
        value = activate(z2[pl.ds(index * size.step, size.step)], rows, mask)
        halve_into(size, value, scratch, index)
        return carry

    rolled(size.chunks, chunk, 0)
    value = halved_rows(scratch)
    count = value.shape[0]
    value = assemble(h0[...].reshape(count, LANES), value, h1[...].reshape(count, LANES))
    value = jnp.concatenate([value, jnp.zeros((out.shape[1] - count, 2 * LANES), F32)], 0)
    out[...] = value.T[:QUARTER].astype(BF16)


def strided(scratch, start, count, stride):
    place = pl.ds(start, count, stride=stride)
    return jnp.concatenate([scratch[0, place, :], scratch[1, place, :]], 1)


def output_kernel(size, me, z0, z1, z2, totals, totals2, table, table2, mask, out, scratch):
    side, frames = size.side, size.frames
    parts = [
        activate(z[...], norm_rows(total, tab, tile, me[0]), mask).reshape(size.rows, LANES)
        for z, total, tab, tile in ((z0, totals, table, 0), (z2, totals2, table2, 0), (z1, totals, table, 1))
    ]
    value = assemble(*parts)
    scratch[0, : size.rows] = value[:, :LANES]
    scratch[1, : size.rows] = value[:, LANES:]

    def line(row, carry):
        start = row * side * frames
        lines = [strided(scratch, start + frame, side, frames) for frame in range(8)]
        for place, tile in enumerate(pack_rows(lines)):
            out[0, row, :, place * LANES : (place + 1) * LANES] = tile.astype(BF16)
        return carry

    unrolled(side, line, 0)


def spread(size, grad, scratch):
    value = grad[...].reshape(-1, LANES)
    count = value.shape[0]
    scratch[pl.ds(0, count, stride=2), :] = value
    scratch[pl.ds(1, count, stride=2), :] = value


def grad_chunk(size, grad, scratch, index):
    if scratch is None:
        return grad[pl.ds(index * size.step, size.step)]
    half = size.side // 2
    rows = half * size.frames
    value = scratch[pl.ds(index * rows, rows), :].reshape(half, 1, size.frames, LANES)
    value = jnp.broadcast_to(value, (half, 2, size.frames, LANES)).reshape(1, size.side, size.frames, LANES)
    value = jnp.broadcast_to(value, (2, size.side, size.frames, LANES))
    return value.reshape(size.step, size.frames, LANES)


def second_sums_kernel(size, grad, z2, totals, table, mask, stat, *scratch):
    scratch = scratch[0] if scratch else None
    if scratch is not None:
        spread(size, grad, scratch)
    rows = norm_rows(totals, table, 0)
    blank = jnp.zeros((size.frames, LANES), F32)

    def chunk(index, carry):
        shift_grad, gain_grad = carry
        z2.ready(index)
        value = z2[pl.ds(index * size.step, size.step)]
        inner, normed = inner_grad(grad_chunk(size, grad, scratch, index), value, rows, mask)
        return shift_grad + jnp.sum(inner, 0), gain_grad + jnp.sum(inner * normed, 0)

    shift_grad, gain_grad = rolled(size.chunks, chunk, (blank, blank))
    publish(stat, [collapse(shift_grad), collapse(gain_grad)])


def conv_back_kernel(size, me, grad, z2, totals, back, table, mask, kernel, delta, o0, o1, o2, field, result, turned, *scratch):
    side, frames, step = size.side, size.frames, size.step
    scratch = scratch[0] if scratch else None
    if scratch is not None:
        spread(size, grad, scratch)
    rows = norm_rows(totals, table, 0)
    field[...] = jnp.zeros_like(field)

    def first(index, carry):
        z2.ready(index)
        value = z2[pl.ds(index * step, step)]
        inner, _ = inner_grad(grad_chunk(size, grad, scratch, index), value, rows, mask)
        value = norm_delta(inner, value, rows, back, 0, mask).astype(BF16).astype(size.kept)
        delta[pl.ds(index * step, step)] = value
        delta.flush(index)
        field[pl.ds(1 + index * size.band, size.band), 1 : side + 1] = value.reshape(size.band, side, frames, LANES)
        return carry

    unrolled(size.chunks, first, 0)
    kernel.ready(0)

    def chunk(index, carry):
        parts = []
        for row in range(3):
            for column in range(3):
                part = field[pl.ds(index * size.band + 2 - row, size.band), 2 - column : 2 - column + side]
                parts.append(part.reshape(step * frames, LANES).astype(BF16))
        value = dot(jnp.concatenate(parts, 1), kernel[...].reshape(9 * LANES, 4 * REDUCED))
        result[pl.ds(index * step, step)] = value.reshape(step, frames, 4 * REDUCED)
        return carry

    unrolled(size.chunks, chunk, 0)

    def one(cell, cells, lanes):
        turned[:, lanes] = turn(size, result[pl.ds(cell, cells)], cells)

    span_blocks(size, size.whole, one)
    for position, (out, start) in enumerate(((o0, 0), (o1, 0), (o2, 0), (o2, REDUCED))):
        owner = me[0] ^ position
        mid = turned[pl.ds(pl.multiple_of(owner * MID, 8), MID), :]
        small = turned[pl.ds(pl.multiple_of(4 * MID + owner * SMALL, 8), SMALL), :]
        out[start : start + REDUCED] = jnp.concatenate([mid, small], 0).astype(BF16)


def kernel_grad_kernel(size, field, delta, mask, out, turned, boxed, taps, flat):
    side, frames, step = size.side, size.frames, size.step

    def chunk(index, carry):
        delta.ready(index)
        place = pl.ds(index * step, step)
        boxed[place] = time_box(delta[place].astype(F32), mask)
        return carry

    rolled(size.chunks, chunk, 0)

    def one(cell, cells, lanes):
        value = turn(size, boxed[pl.ds(cell, cells)], cells)
        upper = value.astype(BF16)
        turned[:LANES, lanes] = upper
        turned[LANES:, lanes] = (value - upper.astype(F32)).astype(BF16)

    span_blocks(size, size.whole, one, (), True)
    for row in range(side + 2):
        field.ready(row)

    def tap(index, carry):
        row = index // 3
        part = field[pl.ds(row, side), pl.ds(index - 3 * row, side)].reshape(size.rows, 2 * LANES).astype(BF16)
        value = dot(turned[:, : size.rows], part)
        value = (value[:LANES] + value[LANES:]) * (1.0 / 3.0)
        taps[index, 0] = value[:, :LANES]
        taps[index, 1] = value[:, LANES:]
        return carry

    for index in range(9):
        tap(index, 0)
    lane = lax.broadcasted_iota(jnp.int32, (WIDE // 4, LANES), 1)
    tiles = [None] * MID_TILES

    def add(place, value):
        tiles[place] = value if tiles[place] is None else tiles[place] + value

    for extra in range(4):
        for tap in range(9):
            rows = pl.ds(extra, WIDE // 4, stride=4)
            rest = jnp.where(lane < 4 * MID - LANES, taps[tap, 1, rows, :], 0.0)
            offset = (extra * 9 + tap) * 4 * MID
            value = jnp.concatenate([taps[tap, 0, rows, :], rest, jnp.zeros_like(rest)], 1)
            value = pltpu.roll(value, offset % LANES, 1)
            for index in range(-(-(offset % LANES + 4 * MID) // LANES)):
                add(offset // LANES + index, value[:, index * LANES : (index + 1) * LANES])
    for place, tile in enumerate(tiles):
        flat[pl.ds(place, WIDE // 4, stride=MID_TILES), :] = tile
    lane = lax.broadcasted_iota(jnp.int32, (NARROW // 4, LANES), 1)
    tiles = [None] * SMALL_TILES
    start = 4 * MID - LANES
    for extra in range(4):
        for tap in range(9):
            value = taps[tap, 1, pl.ds(WIDE + extra, NARROW // 4, stride=4), :]
            value = jnp.where((lane >= start) & (lane < start + 4 * SMALL), value, 0.0)
            offset = (extra * 9 + tap) * 4 * SMALL
            value = pltpu.roll(value, (offset - start) % LANES, 1)
            add(offset // LANES, value)
    for place, tile in enumerate(tiles):
        flat[pl.ds(MID_ROWS + place, NARROW // 4, stride=SMALL_TILES), :] = tile
    flat[MID_ROWS + SMALL_ROWS : KERNEL_ROWS, :] = jnp.zeros((KERNEL_ROWS - MID_ROWS - SMALL_ROWS, LANES), F32)
    out[...] = flat[:KERNEL_ROWS].astype(BF16)


def first_sums_kernel(size, me, p0, p1, p2, p3, g0, g1, z0, z1, totals, table, mask, *refs):
    side, step, frames = size.side, size.step, size.frames
    count = len(size.parts)
    stat, outs, (field, padded, pooled, *scratch) = refs[0], refs[1 : 1 + count], refs[1 + count :]
    s0, s1 = scratch if scratch else (None, None)
    if scratch:
        spread(size, g0, s0)
        spread(size, g1, s1)
    padded[...] = jnp.zeros_like(padded)

    def one(cell, cells, place):
        value = p0[:, place].astype(F32) + p1[:, place].astype(F32)
        value += p2[:REDUCED, place].astype(F32) + p3[REDUCED:, place].astype(F32)
        value = jnp.concatenate([value, jnp.zeros((LANES - REDUCED, LANES), F32)], 0).T
        value = value.reshape(size.group, frames, LANES)
        field[pl.ds(cell, cells)] = value[:cells]

    span_blocks(size, size.whole, one)
    rows0 = norm_rows(totals, table, 0, me[0])
    rows1 = norm_rows(totals, table, 1, me[0])
    blank = jnp.zeros((frames, LANES), F32)

    def chunk(index, carry):
        place = pl.ds(index * step, step)
        z0.ready(index)
        z1.ready(index)
        grad = time_box(field[place], mask) * (1.0 / 3.0) + grad_chunk(size, g0, s0, index)
        inner0, normed0 = inner_grad(grad, z0[place], rows0, mask)
        inner1, normed1 = inner_grad(grad_chunk(size, g1, s1, index), z1[place], rows1, mask)
        field[place] = scales[0] * inner0
        pool = scales[1] * inner1
        padded[pl.ds(1 + index * size.band, size.band), 1 : side + 1] = pool.reshape(size.band, side, frames, LANES)
        sums = (inner0, inner0 * normed0, inner1, inner1 * normed1)
        return tuple(old + jnp.sum(new, 0) for old, new in zip(carry, sums))

    scales = [rows[2] * rows[1] for rows in (rows0, rows1)]
    sums = unrolled(size.chunks, chunk, (blank,) * 4)
    publish(stat, [collapse(item) for item in sums] + scales + [rows0[4]])
    stat.flush(0)
    pool_lines(size, padded, pooled, mask)
    for out, span in zip(outs, size.parts):

        def turned(cell, cells, lanes, out=out):
            out[0:DENSE, lanes] = turn(size, field[pl.ds(cell, cells)], cells)[:DENSE].astype(BF16)
            out[DENSE:ROWS, lanes] = turn(size, pooled[pl.ds(cell, cells)], cells)[:POOL].astype(BF16)

        span_blocks(size, span, turned, (out,))


def input_weights(size, me, weights, block, back, stacked):
    flat_row, pool_row = jnp.zeros((1, 2 * LANES), F32), jnp.zeros((1, 2 * LANES), F32)
    for position, weight in enumerate(weights):
        slope, offset = back_columns(back[position] if len(back) == 4 else back[0], me[0] ^ position)
        stacked[position * ROWS : (position + 1) * ROWS] = weight[block]
        value = weight[block].astype(F32)
        stacked[(position + 4) * ROWS : (position + 5) * ROWS] = (value * -slope).astype(BF16)
        value = value * offset
        flat_row -= collapse(value[:DENSE])
        pool_row -= collapse(value[DENSE:])
    index = lax.broadcasted_iota(jnp.int32, (16, 2 * LANES), 0)
    fixed = jnp.where(index == 0, flat_row, 0.0) + jnp.where(index == 8, pool_row, 0.0)
    stacked[8 * ROWS :] = fixed.astype(BF16)


def input_columns(size, span, streams, stack, stacked, scratch):
    for part, (start, width, _, _) in enumerate(size.columns_of(span)):
        for stream in streams:
            stream.ready(part)
        value = dot(stack[:, start : start + width], stacked[...], ((0,), (0,)))
        row = span[0] + start
        scratch[0, row : row + width, :] = value[:, :LANES]
        scratch[1, row : row + width, :] = value[:, LANES:]


def input_half_kernel(size, me, *refs):
    streams, weights, (back,) = refs[:9], refs[9:13], refs[13:14]
    first, second, third, scratch, stacked, stack = refs[14:]
    input_weights(size, me, weights, 1, (back,), stacked)
    input_columns(size, size.whole, streams, stack, stacked, scratch)
    value = jnp.concatenate([scratch[0, : size.rows, :], scratch[1, : size.rows, :]], 1)
    parts = separate(value * 0.125)
    for ref, part in zip((first, second, third), parts):
        ref[...] = part.reshape(ref.shape)


def input_half_sums_kernel(size, above, me, *refs):
    pieces, (z2, totals, table, mask), refs = refs[:14], refs[14:18], refs[18:]
    (first, second, third, stat), (scratch, stacked, wide), (stack,) = refs[:4], refs[4:7], refs[7:]
    input_half_kernel(size, me, *pieces, first, second, third, scratch, stacked, stack)
    second_sums_kernel(above, second, z2, totals, table, mask, stat, wide)


def input_kernel(size, me, *refs):
    side, frames = size.side, size.frames
    pairs_of = frames // 8
    count = 9 * len(size.parts)
    pieces, weights, back = refs[:count], refs[count : count + 4], refs[count + 4 : count + 8]
    out, scratch, stacked, *stacks = refs[count + 8 :]
    for table in back:
        table.ready(0)
    input_weights(size, me, weights, 0, back, stacked)
    done = 0
    for part, span in enumerate(size.parts):
        input_columns(size, span, pieces[9 * part : 9 * part + 9], stacks[part], stacked, scratch)
        until = sum(size.cells_of(span)) // side
        for row in range(done, until):
            lines = [strided(scratch, row * side * frames + frame, pairs_of * side, 8) for frame in range(8)]
            for place, tile in enumerate(pack_rows(lines)):
                lanes = slice(place * LANES, (place + 1) * LANES)
                out[row * side : (row + 1) * side, :, lanes] = tile.reshape(side, pairs_of, LANES)
            out.flush(row)
        done = until


def pairs(axis_size, shift):
    return [(index, index ^ shift) for index in range(axis_size)]


def gather_four(piece):
    other = lax.ppermute(piece, "chan", pairs(4, 2))
    core = lax.ppermute(piece, "chan", pairs(4, 1))
    both = lax.ppermute(other, "chan", pairs(4, 1))
    return piece, core, other, both


def exchange_four(pieces):
    result = [pieces[0]]
    for shift in (1, 2, 3):
        result.append(lax.ppermute(pieces[shift], "chan", pairs(4, shift)))
    return result


def share(stat):
    return lax.all_to_all(stat, "dp", 0, 0, tiled=True)


def share_all(stat, count):
    return lax.all_to_all(stat, ("dp", "chan"), 0, 0, tiled=True).reshape(count, 4, 8, LANES)


def swap_shares(rows, count):
    return lax.all_to_all(rows.reshape(count, -1, LANES), "dp", 0, 0, tiled=True)


def shares_kernel(*refs):
    *swapped, out = refs
    start = 0
    for ref in swapped:
        count = ref.shape[1]
        value = jnp.sum(ref[...].astype(F32), 0).astype(BF16)
        for device in range(out.shape[0]):
            out[device, start : start + count] = value
        start += count


def all_shares(swapped):
    rows = sum(item.shape[1] for item in swapped)
    (whole,) = call(shares_kernel, [shaped((swapped[0].shape[0], rows, LANES), BF16)], [], [], swapped)
    return lax.all_to_all(whole, "dp", 0, 0, tiled=True)


def other_of(rows, bit, count):
    return lax.ppermute(rows, "dp", pairs(count, 1 << bit))


def joined_halves(group, bit, mine, others):
    low = (group[0] >> bit) & 1
    return jnp.where(low == 0, jnp.concatenate([mine, others], 0), jnp.concatenate([others, mine], 0))


def together(*values):
    return lax.optimization_barrier(values)


def as_rows(flat):
    return flat.reshape(2, -1, LANES).transpose(1, 0, 2).reshape(-1, LANES)


def as_flat(rows):
    return rows.reshape(-1, 2, LANES).transpose(1, 0, 2).reshape(2, -1)


NORM_LANES = (
    (0, REDUCED, PLAIN, 0),
    (0, 0, MID, 64),
    (2, 0, WIDE, 104),
    (0, MID, SMALL, 184),
    (2, WIDE, NARROW, 192),
    (1, 0, POOL, 224),
)


def shifted_lanes(value, source, width, target):
    lane = lax.broadcasted_iota(jnp.int32, value.shape, 1)
    value = jnp.where((lane >= source) & (lane < source + width), value, 0.0)
    return pltpu.roll(value, (target - source) % value.shape[1], 1)


def mask_rows(length0, length1, frames, stride):
    frame = lax.broadcasted_iota(jnp.int32, (frames, LANES), 0)
    ends = (length0, length0 + length1)

    def ident(step):
        place = (frame + step) * stride
        return jnp.where(place >= ends[0], 1, 0) + jnp.where(place >= ends[1], 1, 0)

    here = ident(0)
    valid = jnp.where(frame * stride < ends[1], 1.0, 0.0)
    before = jnp.where((frame > 0) & (ident(-1) == here), 1.0, 0.0)
    after = jnp.where((frame < frames - 1) & (ident(1) == here), 1.0, 0.0)
    return valid, before, after


def prepare_kernel(me, lengths, plain, mid, small, pool, wide, narrow, gains, shifts, *refs):
    outs, (rows, dense, taps) = refs[:-3], refs[-3:]
    mask0, mask1, tables, sent, weights, kernels = outs[0], outs[1], outs[2:6], outs[6:10], outs[10:12], outs[12:14]
    turned, along = outs[14:16], outs[16:18]
    for ref, frames, stride in ((along[0], mask0.shape[1], 1), (along[1], mask1.shape[1], 2)):
        lane = lax.broadcasted_iota(jnp.int32, (8, LANES), 1)
        ref[...] = jnp.where(lax.rem(lane, frames) * stride < lengths[0] + lengths[1], 1.0, 0.0)
    for mask, stride in ((mask0, 1), (mask1, 2)):
        for index, value in enumerate(mask_rows(lengths[0], lengths[1], mask.shape[1], stride)):
            mask[index] = value
    for block in range(2):
        lines = []
        for source in (gains, shifts):
            value = source[...].astype(F32)
            line = jnp.concatenate([value[block : block + 1], value[block + 2 : block + 3]], 1)
            lines.append(jnp.broadcast_to(line, (8, 2 * LANES)))
        found = [[jnp.zeros((8, LANES), F32)] * 2 for _ in range(3)]
        for tile, lane, width, channel in NORM_LANES:
            for index, line in enumerate(lines):
                part = shifted_lanes(line, channel, width, lane)[:, :LANES]
                found[tile][index] = found[tile][index] + part
        tables[2 * block][...] = row_table([found[0][0], found[0][1], found[1][0], found[1][1]])
        tables[2 * block + 1][...] = row_table([found[2][0], found[2][1]])
    for ref, base, outputs in ((mid, 0, MID), (small, MID, SMALL), (plain, REDUCED, PLAIN), (pool, DENSE, POOL)):
        count = ref.shape[0]
        rows[:count, :] = ref[...].astype(F32)
        for block in range(2):
            tiles = [rows[pl.ds(2 * tile + block, outputs // 2, stride=2 * PAIR_TILES), :] for tile in range(PAIR_TILES)]
            line = jnp.concatenate(tiles, 1)
            for extra in range(2):
                place = pl.ds(base + extra, outputs // 2, stride=2)
                for owner in range(4):
                    part = unpack_rows(line, 4 * extra + owner)
                    dense[block, owner, 0, place, :] = part[:, :LANES]
                    dense[block, owner, 1, place, :] = part[:, LANES:]
    lane = lax.broadcasted_iota(jnp.int32, (ROWS, LANES), 1)
    blank = jnp.zeros((LANES, 2 * LANES), F32)
    for block in range(2):
        for owner in range(4):
            rest = jnp.where(lane < QUARTER - LANES, dense[block, owner, 1], 0.0)
            dense[block, owner, 1] = rest
            value = jnp.concatenate([dense[block, owner, 0], rest], 1)
            value = jnp.concatenate([value[:DENSE], blank[: LANES - DENSE], value[DENSE:], blank[: LANES - POOL]], 0)
            weights[block][owner] = value.T[:QUARTER].astype(BF16)
        for position in range(4):
            owner = me[0] ^ position
            value = jnp.concatenate([dense[block, owner, 0], dense[block, owner, 1]], 1)
            sent[position][block] = value.astype(BF16)
    wide_lane = lax.broadcasted_iota(jnp.int32, (WIDE // 4, LANES), 1)
    narrow_lane = lax.broadcasted_iota(jnp.int32, (NARROW // 4, LANES), 1)
    start = 4 * MID - LANES
    for block in range(2):
        rows[: wide.shape[0], :] = wide[...].astype(F32)
        taps[...] = jnp.zeros_like(taps)
        tiles = [rows[pl.ds(2 * tile + block, WIDE // 4, stride=2 * MID_TILES), :] for tile in range(MID_TILES)]
        tiles.append(tiles[0])
        for extra in range(4):
            for tap in range(9):
                offset = (extra * 9 + tap) * 4 * MID
                first, shift = offset // LANES, offset % LANES
                count = -(-(shift + 4 * MID) // LANES)
                value = jnp.concatenate(tiles[first : first + count], 1)
                value = pltpu.roll(value, (count * LANES - shift) % (count * LANES), 1)
                place = pl.ds(extra, WIDE // 4, stride=4)
                taps[tap, 0, place, :] = value[:, :LANES]
                taps[tap, 1, place, :] = jnp.where(wide_lane < start, value[:, LANES : 2 * LANES], 0.0)
        rows[: narrow.shape[0], :] = narrow[...].astype(F32)
        tiles = [rows[pl.ds(2 * tile + block, NARROW // 4, stride=2 * SMALL_TILES), :] for tile in range(SMALL_TILES)]
        for extra in range(4):
            for tap in range(9):
                offset = (extra * 9 + tap) * 4 * SMALL
                value = pltpu.roll(tiles[offset // LANES], (start - offset) % LANES, 1)
                value = jnp.where((narrow_lane >= start) & (narrow_lane < start + 4 * SMALL), value, 0.0)
                taps[tap, 1, pl.ds(WIDE + extra, NARROW // 4, stride=4), :] = value
        for tap in range(9):
            first, second = taps[tap, 0], taps[tap, 1]
            kernels[block][tap] = jnp.concatenate([first, second], 1)[:, : 4 * REDUCED].astype(BF16)
            turned[block][tap, :LANES] = first.T.astype(BF16)
            turned[block][tap, LANES:] = second.T.astype(BF16)


def place_rows(out, sources, count, pairs_rows):
    target = pairs_rows if out.shape[0] == 2 else out.near
    for block, (ref, start) in enumerate(sources):
        target[pl.ds(block, count, stride=2), :] = ref[start : start + count, :]
    if out.shape[0] == 2:
        for index in range(count // 4):
            value = pairs_rows[index * 8 : index * 8 + 8, :]
            for part in range(4):
                place = index * 4 + part
                out[:, place * LANES : (place + 1) * LANES] = value[2 * part : 2 * part + 2]


def finish_kernel(me, group, early, halves, late, first0, first1, second0, second1, *refs):
    outs, (rows, other, pairs_rows) = refs[:-3], refs[-3:]
    mid, small, plain, pool, wide, narrow, gains, shifts = outs
    count, share = late.shape[:2]
    bits = count.bit_length() - 1
    low = group[0] & 1
    for index in range(count // 2):
        device = sum(((index >> bit) & 1) << (bits - 1 - bit) for bit in range(bits))
        place = slice(index * share, (index + 1) * share)
        rows[pl.ds(pl.multiple_of((device + low) * share, 16), share)] = early[place].astype(F32)
        rows[pl.ds(pl.multiple_of((device + 1 - low) * share, 16), share)] = halves[place].astype(F32)
    late.ready(0)
    for device in range(late.shape[0]):
        place = slice(device * share, (device + 1) * share)
        other[place] = late[device].astype(F32)
    place_rows(wide, ((other, 0), (rows, 0)), MID_ROWS, pairs_rows)
    wide.flush(0)
    place_rows(narrow, ((other, MID_ROWS), (rows, MID_ROWS)), SMALL_ROWS, pairs_rows)
    start = KERNEL_ROWS
    for out, outputs in ((mid, MID), (small, SMALL), (plain, PLAIN), (pool, POOL)):
        count = outputs * CIN // LANES
        place_rows(out, ((other, start), (rows, start)), count, pairs_rows)
        start += count
    for block, first_ref, second_ref in ((0, first0, second0), (1, first1, second1)):
        first = jnp.sum(owner_rows(first_ref, me[0]), 0)
        second = jnp.sum(second_ref[...], 0)
        for out, row in ((gains, 1), (shifts, 0)):
            lines = (first[row : row + 1], first[row + 2 : row + 3], second[row : row + 1])
            total = jnp.zeros((8, 2 * LANES), F32)
            for tile, lane, width, channel in NORM_LANES:
                line = jnp.concatenate([lines[tile], jnp.zeros((1, LANES), F32)], 1)
                total += shifted_lanes(jnp.broadcast_to(line, (8, 2 * LANES)), lane, width, channel)
            out[block : block + 1, :] = total[0:1, :LANES]
            out[block + 2 : block + 3, :] = total[0:1, LANES:]


def project(size, me, pieces, positions, dense, mask, table, everyone, begun=()):
    side, cells, frames = size.side, size.cells, size.frames
    tile = shaped((cells, frames, LANES))
    count = len(positions)
    column_cells = (0, [(first, held) for _, _, first, held in size.columns_of(size.whole)])
    ins = {index: column_parts(size, size.whole) for index in range(count)}
    ins |= {count + 3 + index: column_cells for index in range(len(begun))}
    return call(
        functools.partial(project_kernel, size, positions),
        [tile, tile, shaped((everyone, 8, LANES)), shaped((REDUCED, size.padded), BF16)],
        [
            pltpu.VMEM((side + 2, side + 2, frames, LANES), F32),
            pltpu.VMEM((cells, frames, LANES), F32),
            pltpu.VMEM((count * QUARTER, 2 * LANES), BF16),
        ],
        [me],
        [*pieces, dense, mask, table, *begun],
        ins=ins,
        puts={0: column_cells, 1: line_parts(size)},
        stacks=[range(count)],
    )


def project_begin(size, me, pieces, dense):
    tile = shaped((size.cells, size.frames, LANES))
    column_cells = (0, [(first, held) for _, _, first, held in size.columns_of(size.whole)])
    return call(
        functools.partial(project_begin_kernel, size),
        [tile, tile],
        [pltpu.VMEM((2 * QUARTER, 2 * LANES), BF16)],
        [me],
        [*pieces, dense],
        ins={index: column_parts(size, size.whole) for index in range(2)},
        puts={0: column_cells, 1: column_cells},
        stacks=[range(2)],
    )


def normed_wires(size, me, z0, z1, totals, table, mask):
    outs, puts = [], {}
    for part, (_, lanes) in enumerate(size.parts):
        outs += [shaped((ROWS, lanes), BF16), shaped((16, lanes), BF16)]
        puts[2 * part] = span_parts(size, size.parts[part])
    wires = call(
        functools.partial(normed_kernel, size),
        outs,
        [
            pltpu.VMEM((size.side + 2, size.side + 2, size.frames, LANES), F32),
            pltpu.VMEM((size.cells, size.frames, LANES), F32),
        ],
        [me],
        [z0, z1, totals, table, mask],
        ins={0: cell_parts(size), 1: cell_parts(size)},
        puts=puts,
    )
    return wires[0::2], wires[1::2]


def moments(size, me, lefts, pieces):
    rows = sum(item.shape[0] for item in lefts[0])
    flat = [item for group in lefts for item in group]
    (result,) = call(
        functools.partial(moments_kernel, size),
        [shaped((4, rows, 2 * LANES))],
        [],
        [me],
        [*flat, *pieces],
        ins={len(flat) + index: (1, size.parts) for index in range(4)},
        stacks=[range(len(flat), len(flat) + 4)],
    )
    return result


def forward_second(size, me, group, pieces, totals, along, kernel, mask, count):
    side, frames = size.side, size.frames
    field, z2, stat = call(
        functools.partial(conv_kernel, size),
        [
            shaped((side + 2, side + 2, frames, 2 * LANES), size.kept),
            shaped((size.cells, frames, LANES)),
            shaped((count, 8, LANES)),
        ],
        [pltpu.VMEM((2 * LANES, size.padded), F32)],
        [me, group],
        [*pieces, totals, along, kernel, mask],
        flops=2 * size.rows * 9 * 256 * 256,
        ins={6: (0, [(0, 9)])},
        puts={0: (0, [(0, side + 2)]), 1: cell_parts(size)},
    )
    return field, z2, stat


def hop(piece, shift):
    return lax.ppermute(piece, "chan", pairs(4, shift))


def second_sums(size, grads, saved, count):
    z2, totals2, table2, mask = saved[4], saved[5], saved[7], saved[8]
    return call(
        functools.partial(second_sums_kernel, size),
        [shaped((count, 8, LANES))],
        spread_rows(size),
        [],
        [grads[1], z2, totals2, table2, mask],
        ins={1: cell_parts(size)},
    )


def spread_rows(size):
    return [pltpu.VMEM((size.rows // 4, LANES), F32)] if size.side % 2 == 0 else []


def weight_grad(size, me, inner, moment, back1, kernels, count):
    unit = count * 16
    total = -(-(KERNEL_ROWS + DENSE_ROWS) // unit) * unit
    return call(
        functools.partial(weight_grad_kernel, size),
        [shaped((total, LANES), BF16), shaped((16, LANES), BF16)],
        [pltpu.VMEM((4, 2, ROWS, LANES), F32), pltpu.VMEM((DENSE_ROWS, LANES), F32)],
        [me],
        [inner, moment, back1, kernels],
    )


def backward(size, me, grads, back2, saved, normed, weights_at, count, early=None, moment=None, group=None, above=None):
    z0, z1, totals, field, z2, totals2, table, table2, mask, kernel, pieces, _, shapes = saved
    g0, g2, g1 = grads
    side, frames = size.side, size.frames
    spreads = early is not None
    tile = shaped((size.cells, frames, LANES))
    wire = shaped((REDUCED, size.padded), BF16)
    delta2, o0, o1, o2 = call(
        functools.partial(conv_back_kernel, size),
        [shaped((size.cells, frames, LANES), size.kept), wire, wire, shaped((2 * REDUCED, size.padded), BF16)],
        [
            pltpu.VMEM((side + 2, side + 2, frames, LANES), size.kept),
            pltpu.VMEM((size.cells, frames, 4 * REDUCED), F32),
            pltpu.VMEM((4 * REDUCED, size.padded), F32),
        ]
        + spread_rows(size),
        [me],
        [g2, z2, totals2, back2, table2, mask, kernel],
        flops=2 * size.rows * 9 * 256 * 256,
        ins={1: cell_parts(size), 6: (0, [(0, 9)])},
        puts={0: cell_parts(size)},
    )
    if spreads:
        o2, normed = together(o2, normed)
        normed = [[*wires, hop(wires[2], 1)] for wires in normed]
    partial = [o0, hop(o1, 1), hop(o2, 2)]
    (kernel_grad,) = call(
        functools.partial(kernel_grad_kernel, size),
        [shaped((KERNEL_ROWS, LANES), BF16)],
        [
            pltpu.VMEM((2 * LANES, size.padded), BF16),
            pltpu.VMEM((size.cells, frames, LANES), F32),
            pltpu.VMEM((9, 2, LANES, LANES), F32),
            pltpu.VMEM((KERNEL_ROWS + 3 * ROOM, LANES), F32),
        ],
        [],
        [field, delta2, mask],
        flops=2 * size.rows * 9 * 256 * 256,
        ins={0: (0, even(side + 2, side + 2)), 1: cell_parts(size)},
    )
    if spreads:
        early, o1 = together(early, o1)
        swapped = swap_shares(early, count)
        partial[2], kernel_grad = together(partial[2], kernel_grad)
    else:
        partial[2], kernel_grad = together(partial[2], kernel_grad)
    if not spreads:
        partial[1], normed = together(partial[1], normed)
    partial.append(hop(partial[2], 1))
    if spreads:
        partial[3], swapped = together(partial[3], swapped)
    devices = count if spreads else 4 * count
    stat, *wires = call(
        functools.partial(first_sums_kernel, size),
        [shaped((devices, 8, LANES))] + [shaped((ROWS, lanes), BF16) for _, lanes in size.parts],
        [
            pltpu.VMEM((size.cells, frames, LANES), F32),
            pltpu.VMEM((side + 2, side + 2, frames, LANES), F32),
            pltpu.VMEM((size.cells, frames, LANES), F32),
        ]
        + spread_rows(size) * 2,
        [me],
        [*partial, g0, g1, z0, z1, totals, table, mask],
        ins={6: cell_parts(size), 7: cell_parts(size)},
        puts={0: (0, [(0, devices)])} | {1 + part: span_parts(size, span) for part, span in enumerate(size.parts)},
    )
    others, cores = [hop(wire, 2) for wire in wires[:1]] + [None] * (len(wires) - 1), [hop(wire, 1) for wire in wires[:1]] + [None] * (len(wires) - 1)
    inner = moments(size, me, [[wire] for wire in wires], pieces)
    if spreads:
        bits = count.bit_length() - 1
        back1 = share(stat)
        early = jnp.sum(swapped.astype(F32), 0).astype(BF16)
        halves = other_of(early, bits - 1, count)
        back1, inner, others[0], halves = together(back1, inner, others[0], halves)
        dense_grad, table_own = weight_grad(size, me, inner, moment, back1, kernel_grad, count)
        room = wires[1].shape[1] - LANES
        wires[1] = jnp.concatenate([wires[1], jnp.pad(table_own, ((0, 0), (0, room)))], 0)
        others[1], cores[1] = hop(wires[1], 2), hop(wires[1], 1)
        tables = [wires[1], cores[1], others[1], hop(others[1], 1)]
        swapped = swap_shares(dense_grad, count)
    else:
        back1 = share_all(stat, count)
        back1, others[0], moment = together(back1, others[0], moment)

    def four(part):
        return [wires[part], cores[part], others[part], hop(others[part], 1)]

    scratch = [pltpu.VMEM((2, size.parts[0][1] + LANES, LANES), F32), pltpu.VMEM((8 * ROWS + 16, 2 * LANES), BF16)]
    if not spreads:
        top, top_args = above
        result = call(
            functools.partial(input_half_sums_kernel, size, top),
            [tile, tile, tile, shaped((count, 8, LANES))],
            scratch + spread_rows(top),
            [me],
            [*four(0), *normed[0], shapes[0], *weights_at, back1, *top_args],
            ins={index: column_parts(size, size.whole) for index in range(9)} | {14: cell_parts(top)},
            stacks=[range(9)],
        )
        return result, inner, kernel_grad, back1, moment
    shape = shaped((size.cells, frames // 8, 8 * QUARTER))
    for bit in range(bits - 1, 0, -1):
        early = joined_halves(group, bit, early, halves)
        halves = other_of(early, bit - 1, count)
        if bit == 2:
            swapped, halves = together(swapped, halves)
    late = all_shares([swapped])
    args, ins, stacks = [], {}, []
    for part, span in enumerate(size.parts):
        first = len(args)
        args += [*(tables if part else four(part)), *normed[part], shapes[part]]
        ins |= {first + index: column_parts(size, span) for index in range(9)}
        if part:
            ins |= {first + index: (*column_parts(size, span), (0, ROWS)) for index in range(4)}
        stacks.append(range(first, first + 9))
    args += weights_at
    ins |= {len(args) + index: (1, [(0, LANES)], (ROWS, 16)) for index in range(4)}
    args += tables
    result = call(
        functools.partial(input_kernel, size),
        [shape],
        [pltpu.VMEM((2, size.padded + ROOM, LANES), F32), pltpu.VMEM((8 * ROWS + 16, 2 * LANES), BF16)],
        [me],
        args,
        ins=ins,
        puts={0: line_parts(size)},
        stacks=stacks,
    )
    return result, (early, halves, late), back1


def on_device(count, clips, clip_len, w_plain, w_mid, k_mid, w_small, k_small, w_pool, gains, shifts, grad_out):
    big = Size(clips.shape[1], 8 * clips.shape[0])
    low = Size(grad_out.shape[1], 8 * grad_out.shape[0])
    me = lax.axis_index("chan").astype(jnp.int32).reshape(1)
    group = lax.axis_index("dp").astype(jnp.int32).reshape(1)
    everyone = 4 * count
    raw = clips.transpose(1, 2, 0, 3).reshape(big.cells, clips.shape[0], 8 * QUARTER)
    (own,) = call(
        functools.partial(unpack_kernel, big),
        [shaped((QUARTER, big.padded), BF16)],
        [pltpu.VMEM((2, big.rows + ROOM, LANES), F32)],
        [],
        [raw],
        ins={0: line_parts(big)},
        puts={0: span_parts(big, big.whole)},
    )
    other, core = hop(own, 2), hop(own, 1)
    low_tile = shaped((low.cells, low.frames, LANES))
    grads = call(
        functools.partial(grad_kernel, low),
        [low_tile, low_tile, low_tile],
        [pltpu.VMEM((2, low.rows + ROOM, LANES), F32)],
        [],
        [grad_out],
    )
    table = shaped((8, LANES))
    prepared = call(
        prepare_kernel,
        [shaped((3, big.frames, LANES)), shaped((3, low.frames, LANES))]
        + [table] * 4
        + [shaped((2, ROWS, 2 * LANES), BF16)] * 4
        + [shaped((4, QUARTER, 2 * LANES), BF16)] * 2
        + [shaped((9, LANES, 4 * REDUCED), BF16)] * 2
        + [shaped((9, 2 * LANES, LANES), BF16)] * 2
        + [table] * 2,
        [
            pltpu.VMEM((2 * MID_ROWS + 6 * ROOM, LANES), F32),
            pltpu.VMEM((2, 4, 2, ROWS, LANES), F32),
            pltpu.VMEM((9, 2, LANES, LANES), F32),
        ],
        [me, clip_len],
        [as_rows(item) for item in (w_plain, w_mid, w_small, w_pool, k_mid, k_small, gains, shifts)],
    )
    mask, mask_low, table0, second0, table1, second1 = prepared[:6]
    sent, (dense0, dense1), (kernel0, kernel1), (turned0, turned1), (along, along_low) = (
        prepared[6:10],
        prepared[10:12],
        prepared[12:14],
        prepared[14:16],
        prepared[16:18],
    )
    begun = project_begin(big, me, [own, core], dense0)
    other, begun, grads = together(other, begun, grads)
    pieces = [own, core, other, hop(other, 1)]
    z0, z1, stat, wire = project(big, me, pieces[2:], (2, 3), dense0, mask, table0, everyone, begun)
    mids = [wire, hop(wire, 1), hop(wire, 2)]
    totals = share_all(stat, count)
    totals, mids[2] = together(totals, mids[2])
    mids.append(hop(mids[2], 1))
    half = [pltpu.VMEM((big.rows // 4, LANES), F32)]
    h0, h1 = call(
        functools.partial(first_half_kernel, big),
        [low_tile, low_tile],
        half * 2,
        [me],
        [z0, z1, totals, table0, mask],
        flops=big.rows * 2 * LANES * 20,
        ins={0: cell_parts(big), 1: cell_parts(big)},
    )
    field, z2, stat = forward_second(big, me, group, mids, totals, along, turned0, mask, count)
    totals2 = share(stat)
    weights_at = exchange_four(sent)
    totals2, weights_at = together(totals2, weights_at)
    (own1,) = call(
        functools.partial(second_half_kernel, big),
        [shaped((QUARTER, low.padded), BF16)],
        half,
        [],
        [z2, totals2, second0, mask, h0, h1],
        flops=big.rows * LANES * 20,
        ins={0: cell_parts(big)},
    )
    pieces1 = gather_four(own1)
    y0, y1, stat, wire = project(low, me, pieces1, (0, 1, 2, 3), dense1, mask_low, table1, everyone)
    mids = exchange_four([wire] * 4)
    totals1 = share_all(stat, count)
    normed, shapes = normed_wires(big, me, z0, z1, totals, table0, mask)
    totals1, normed, shapes = together(totals1, normed, shapes)
    field1, y2, stat = forward_second(low, me, group, mids, totals1, along_low, turned1, mask_low, count)
    totals3 = share(stat)
    normed1, shapes1 = normed_wires(low, me, y0, y1, totals1, table1, mask_low)
    totals3, normed1 = together(totals3, normed1)
    (mixed,) = call(
        functools.partial(output_kernel, low),
        [shaped(grad_out.shape, BF16)],
        [pltpu.VMEM((2, low.rows + ROOM, LANES), F32)],
        [me],
        [y0, y1, y2, totals1, totals3, table1, second1, mask_low],
    )
    saved1 = (y0, y1, totals1, field1, y2, totals3, table1, second1, mask_low, kernel1, pieces1, normed1, shapes1)
    (back2,) = second_sums(low, grads, saved1, count)
    back2 = share(back2)
    moment1 = moments(low, me, list(zip(normed1, shapes1)), pieces1)
    normed1 = [[wire, hop(wire, 1), hop(wire, 2)] for wire in normed1]
    back2, mixed, normed1, moment1 = together(back2, mixed, normed1, moment1)
    normed1 = [[*wires, hop(wires[2], 1)] for wires in normed1]
    moment = moments(big, me, list(zip(normed, shapes)), pieces)
    grads, inputs1, kernel_grad1, first1, moment = backward(
        low, me, grads, back2, saved1, normed1, weights_at, count, None, moment, above=(big, (z2, totals2, second0, mask))
    )
    last1 = back2
    *grads, back2 = grads

    saved0 = (z0, z1, totals, field, z2, totals2, table0, second0, mask, kernel0, pieces, normed, shapes)
    back2, normed = together(back2, normed)
    back2 = share(back2)
    normed = [[wire, hop(wire, 1), hop(wire, 2)] for wire in normed]
    dense_grad1, _ = weight_grad(low, me, inputs1, moment1, first1, kernel_grad1, count)
    back2, dense_grad1, normed[0] = together(back2, dense_grad1, normed[0])
    last0 = back2
    (clips_grad,), (early, halves, late), first0 = backward(
        big, me, grads, back2, saved0, normed, weights_at, count, dense_grad1, moment, group
    )

    def sized(outputs):
        rows = outputs * CIN // 64
        return shaped((rows, LANES) if rows % 16 == 0 else (2, rows * 64))

    pairs_rows = pltpu.VMEM((2 * MID_ROWS + ROOM, LANES), F32)
    outs = [sized(outputs) for outputs in (MID, SMALL, PLAIN, POOL)]
    outs += [shaped((2, MID_ROWS * LANES)), shaped((2 * SMALL_ROWS, LANES))] + [shaped((4, LANES))] * 2
    mid, small, plain, pool, wide, narrow, gains_grad, shifts_grad = call(
        finish_kernel,
        outs,
        [pltpu.VMEM((count * late.shape[1], LANES), F32)] * 2 + [pairs_rows],
        [me, group],
        [early, halves, late, first0, first1, last0, last1],
        ins={2: (0, [(0, count)])},
        puts={4: (0, [(0, 2)])},
    )
    flats = [plain, mid, wide, small, narrow, pool, gains_grad, shifts_grad]
    flats = [item if item.shape[0] == 2 else as_flat(item) for item in flats]
    shape = (big.side, big.side, big.frames // 8, 8 * QUARTER)
    return mixed, clips_grad.reshape(shape).transpose(2, 0, 1, 3), *flats


def solution(mesh):
    frames = P("dp", None, None, "chan")
    flat = P(None, "chan")
    return jax.shard_map(
        functools.partial(on_device, mesh.shape["dp"]),
        mesh=mesh,
        in_specs=(frames, P("dp")) + (flat,) * 8 + (frames,),
        out_specs=(frames, frames) + (flat,) * 8,
        check_vma=False,
    )
```

```python
import functools

import jax
import jax.numpy as jnp
from jax import lax
from jax.experimental import pallas as pl
from jax.experimental.pallas import tpu as pltpu
from jax.sharding import PartitionSpec as P

CIN = 832
QUARTER = 208
WIDE, NARROW = 80, 32
MID, SMALL, PLAIN, POOL = 40, 8, 64, 32
REDUCED = MID + SMALL
DENSE = REDUCED + PLAIN
ROWS = DENSE + POOL
CLIPS = 2
EPSILON = 1e-05
F32 = jnp.float32
BF16 = jnp.bfloat16
LANES = 128
LIMIT = 64
ROOM = 64
COST = 1
MID_TILES = 4 * 9 * 160 // LANES
MID_ROWS = WIDE // 4 * MID_TILES
SMALL_TILES = 4 * 9 * 32 // LANES
SMALL_ROWS = NARROW // 4 * SMALL_TILES
KERNEL_ROWS = 976
PAIR_TILES = 2 * CIN // LANES
DENSE_ROWS = 944


class Size:
    def __init__(self, side, frames):
        self.side = side
        self.frames = frames
        self.cells = side * side
        self.rows = self.cells * frames
        self.padded = -(-self.rows // LANES) * LANES
        self.band = 2 if side % 2 == 0 else side
        self.chunks = side // self.band
        self.step = self.band * side
        self.group = LANES // frames
        self.full = self.cells // self.group
        self.rest = self.cells - self.full * self.group
        self.kept = BF16 if frames % 16 == 0 else F32
        self.whole = (0, self.padded)
        first = 13 * LANES
        self.parts = [(0, first), (first, self.padded - first)] if self.padded > 2 * first - LANES - 1 else [self.whole]

    def cells_of(self, span):
        first = span[0] // self.frames
        return first, min(span[1] // self.frames, self.cells - first)

    def columns_of(self, span, width=640):
        first, count = self.cells_of(span)
        result = []
        for start in range(0, span[1], width):
            skipped, held = start // self.frames, min(width, span[1] - start)
            result.append((start, held, first + skipped, min(held // self.frames, count - skipped)))
        return result


class Stream:
    def __init__(self, far, near, sems, axis, parts, window=None):
        self.far, self.near, self.sems, self.axis, self.parts = far, near, sems, axis, parts
        self.window = window
        self.shape, self.dtype = near.shape, near.dtype

    def copy(self, part, inward):
        if isinstance(part, int):
            start, count = self.parts[part]
        else:
            first, count = self.parts[0]
            start = first + part * count
        index = (slice(None),) * self.axis + (pl.ds(start, count),)
        away = (pl.ds(*self.window),) + index[1:] if self.window else index
        pair = (self.far.at[away], self.near.at[index])
        return pltpu.make_async_copy(*(pair if inward else pair[::-1]), self.sems.at[part])

    def ready(self, part):
        self.copy(part, True).wait()

    def flush(self, part):
        self.copy(part, False).start()

    def __getitem__(self, index):
        return self.near[index]

    def __setitem__(self, index, value):
        self.near[index] = value

    @property
    def at(self):
        return self.near.at


def even(total, count):
    return [(start * (total // count), total // count) for start in range(count)]


def cell_parts(size):
    return 0, even(size.cells, size.chunks)


def line_parts(size, first=0, count=None):
    return 0, [(row * size.side, size.side) for row in range(first, first + (count or size.side))]


def column_parts(size, span, width=640):
    return 1, [(start, held) for start, held, _, _ in size.columns_of(span, width)]


def call(body, outs, scratch, scalars, args, flops=0, ins=None, puts=None, aliases=None, stacks=()):
    ins, puts = ins or {}, puts or {}
    places = {}

    def height(index):
        plan = ins.get(index)
        return plan[2][1] if plan and len(plan) > 2 else args[index].shape[0]

    for stack, members in enumerate(stacks):
        start = 0
        for index in members:
            places[index] = (stack, start)
            start += height(index)
    aliases = {len(scalars) + index: out for index, out in (aliases or {}).items()}
    plans = [ins.get(index) for index in range(len(args))] + [puts.get(index) for index in range(len(outs))]
    arrays = list(args) + list(outs)
    buffers = []
    for index, (array, plan) in enumerate(zip(arrays, plans)):
        if index not in places:
            rows = height(index) if index < len(args) else array.shape[0]
            buffers.append(pltpu.VMEM((rows,) + array.shape[1:], array.dtype))
        buffers.append(pltpu.SemaphoreType.DMA((max(len(plan[1]), 1) if plan else 1,)))
    for members in stacks:
        rows = sum(height(index) for index in members)
        buffers.append(pltpu.VMEM((rows,) + args[members[0]].shape[1:], args[members[0]].dtype))

    def wrapped(*refs):
        numbers, refs = refs[: len(scalars)], refs[len(scalars) :]
        far, refs = refs[: len(arrays)], refs[len(arrays) :]
        own, refs = refs[: len(scratch)], list(refs[len(scratch) :])
        whole = refs[len(refs) - len(stacks) :]
        streams = []
        for index, plan in enumerate(plans):
            axis, parts, *window = plan or (0, [(0, arrays[index].shape[0])])
            if index in places:
                stack, start = places[index]
                near = whole[stack].at[pl.ds(start, height(index))]
            else:
                near = refs.pop(0)
            streams.append(Stream(far[index], near, refs.pop(0), axis, parts, *window))
        entering, leaving = streams[: len(args)], streams[len(args) :]
        for part in range(max([len(stream.parts) for stream in entering])):
            for stream in entering:
                if part < len(stream.parts):
                    stream.copy(part, True).start()
        for index, stream in enumerate(entering):
            if index not in ins:
                stream.ready(0)
        body(*numbers, *entering, *leaving, *own, *whole)
        for index, stream in enumerate(leaving):
            if index not in puts:
                stream.flush(0)
        for stream in leaving:
            for part in range(len(stream.parts)):
                stream.copy(part, False).wait()

    moved = sum(array.size * array.dtype.itemsize for array in arrays)
    return pl.pallas_call(
        wrapped,
        out_shape=outs,
        in_specs=[pl.BlockSpec(memory_space=pltpu.SMEM)] * len(scalars) + [pl.BlockSpec(memory_space=pl.ANY)] * len(args),
        out_specs=[pl.BlockSpec(memory_space=pl.ANY)] * len(outs),
        scratch_shapes=list(scratch) + buffers,
        compiler_params=pltpu.CompilerParams(vmem_limit_bytes=LIMIT * 1024 * 1024),
        cost_estimate=pl.CostEstimate(flops=COST, bytes_accessed=COST, transcendentals=0),
        input_output_aliases=aliases,
    )(*scalars, *args)


def unrolled(count, body, carry):
    for index in range(count):
        carry = body(index, carry)
    return carry


def rolled(count, body, carry):
    if count == 1:
        return body(0, carry)
    return lax.fori_loop(0, count, body, carry)


def shaped(shape, dtype=F32):
    return jax.ShapeDtypeStruct(shape, dtype)


def sigmoid(value):
    return 0.5 * jnp.tanh(0.5 * value) + 0.5


def row_table(rows):
    index = lax.broadcasted_iota(jnp.int32, (8, LANES), 0)
    table = jnp.zeros((8, LANES), F32)
    for position, row in enumerate(rows):
        table = jnp.where(index == position, row, table)
    return table


def time_box(value, mask_ref):
    cells, frames, width = value.shape
    flat = value.reshape(cells * frames, width)
    before = pltpu.roll(flat, 1, 0).reshape(value.shape)
    after = pltpu.roll(flat, cells * frames - 1, 0).reshape(value.shape)
    return value + before * mask_ref[1] + after * mask_ref[2]


def owner_rows(all_ref, owner):
    if len(all_ref.shape) == 3:
        return all_ref[...]
    return all_ref[:, pl.ds(owner, 1)].reshape(all_ref.shape[0], 8, LANES)


def norm_rows(all_ref, table_ref, tile, owner=0):
    total = jnp.sum(owner_rows(all_ref, owner), 0)
    count = total[4:5]
    mean = total[2 * tile : 2 * tile + 1] / count
    variance = total[2 * tile + 1 : 2 * tile + 2] / count - mean * mean
    inverse = lax.rsqrt(variance + EPSILON)
    gain = table_ref[2 * tile : 2 * tile + 1]
    shift = table_ref[2 * tile + 1 : 2 * tile + 2]
    return mean, inverse, gain, shift, count


def activate(value, rows, mask_ref):
    mean, inverse, gain, shift, _ = rows
    shifted = gain * ((value - mean) * inverse) + shift
    return shifted * sigmoid(shifted) * mask_ref[0]


def inner_grad(grad, value, rows, mask_ref):
    mean, inverse, gain, shift, _ = rows
    normed = (value - mean) * inverse
    shifted = gain * normed + shift
    sigma = sigmoid(shifted)
    return grad * mask_ref[0] * sigma * (1.0 + shifted * (1.0 - sigma)), normed


def norm_delta(inner, value, rows, back_ref, tile, mask_ref):
    mean, inverse, gain, _, count = rows
    total = jnp.sum(back_ref[...], 0)
    shift_grad = total[2 * tile : 2 * tile + 1] / count
    gain_grad = total[2 * tile + 1 : 2 * tile + 2] / count
    normed = (value - mean) * inverse
    return (gain * inverse) * (inner - mask_ref[0] * (shift_grad + normed * gain_grad))


def publish(stat_ref, rows):
    stat_ref[...] = jnp.broadcast_to(row_table(rows)[None], stat_ref.shape)


def collapse(value):
    return jnp.sum(value, 0, keepdims=True)


def windows():
    result = []
    for frame in range(8):
        start = frame * QUARTER
        first, offset = start // LANES, start % LANES
        result.append((first, -(-(offset + QUARTER) // LANES), offset))
    return result


def unpack_rows(line, frame):
    first, tiles, offset = windows()[frame]
    value = line[:, first * LANES : (first + tiles) * LANES]
    if offset:
        value = pltpu.roll(value, tiles * LANES - offset, 1)
    return value[:, : 2 * LANES]


def pack_rows(parts):
    tiles = [None] * 13
    for frame, value in enumerate(parts):
        first, count, offset = windows()[frame]
        if count == 3:
            value = jnp.concatenate([value, jnp.zeros((value.shape[0], LANES), value.dtype)], 1)
        if offset:
            value = pltpu.roll(value, offset, 1)
        for index in range(count):
            piece = value[:, index * LANES : (index + 1) * LANES]
            place = first + index
            tiles[place] = piece if tiles[place] is None else tiles[place] + piece
    return tiles


def assemble(first, second, third):
    blank = jnp.zeros_like(first)
    lane = lax.broadcasted_iota(jnp.int32, (first.shape[0], 2 * LANES), 1)
    plain = pltpu.roll(jnp.concatenate([first, blank], 1), 2 * LANES - REDUCED, 1)
    middle = pltpu.roll(jnp.concatenate([second, blank], 1), PLAIN, 1)
    pool = pltpu.roll(jnp.concatenate([third, blank], 1), PLAIN + WIDE + NARROW, 1)
    return jnp.where(lane < PLAIN, plain, 0.0) + middle + pool


def separate(value):
    lane = lax.broadcasted_iota(jnp.int32, (value.shape[0], LANES), 1)
    plain = pltpu.roll(value, REDUCED, 1)[:, :LANES]
    middle = pltpu.roll(value, 2 * LANES - PLAIN, 1)[:, :LANES]
    pool = pltpu.roll(value, 2 * LANES - PLAIN - WIDE - NARROW, 1)[:, :LANES]
    first = jnp.where((lane >= REDUCED) & (lane < DENSE), plain, 0.0)
    second = jnp.where(lane < WIDE + NARROW, middle, 0.0)
    third = jnp.where(lane < POOL, pool, 0.0)
    return first, second, third


def span_blocks(size, span, one, leaving=(), rolled=False):
    first, count = size.cells_of(span)
    total, whole = span[1] // LANES, count // size.group

    def block(index, cells):
        start = index * LANES
        start = start if isinstance(start, int) else pl.multiple_of(start, LANES)
        one(first + index * size.group, cells, pl.ds(start, LANES))

    def four(index, carry):
        for extra in range(4):
            block(index * 4 + extra, size.group)
        for stream in leaving:
            stream.flush(index)
        return carry

    groups = whole // 4 if rolled else 0
    if rolled:
        lax.fori_loop(0, groups, four, 0)
    for index in range(groups * 4, total):
        block(index, min(size.group, count - index * size.group))
        if index % 4 == 3 or index == total - 1:
            for stream in leaving:
                stream.flush(index // 4)


def span_parts(size, span):
    return column_parts(size, span, 4 * LANES)


def unpack_kernel(size, raw, out, scratch):
    side, frames = size.side, size.frames
    pairs_of = frames // 8
    def line(row, carry):
        raw.ready(row)
        value = raw[pl.ds(row * side, side)].astype(F32).reshape(pairs_of * side, 8 * QUARTER)
        for frame in range(8):
            place = pl.ds(row * side * frames + frame, pairs_of * side, stride=8)
            piece = unpack_rows(value, frame)
            scratch[0, place, :] = piece[:, :LANES]
            scratch[1, place, :] = piece[:, LANES:]
        return carry

    lax.fori_loop(0, side, line, 0)

    def one(cell, cells, lanes):
        start = cell * frames
        for tile, (low, high) in enumerate(((0, LANES), (LANES, QUARTER))):
            value = scratch[tile, pl.ds(start, cells * frames), :].reshape(cells, frames, LANES)
            out[low:high, lanes] = turn(size, value, cells)[: high - low].astype(BF16)

    span_blocks(size, size.whole, one, (out,))


def grad_kernel(size, raw, first, second, third, scratch):
    side, frames = size.side, size.frames

    def line(row, carry):
        value = raw[0, row].astype(F32)
        for frame in range(8):
            place = pl.ds(row * side * frames + frame, side, stride=frames)
            part = unpack_rows(value, frame)
            scratch[0, place, :] = part[:, :LANES]
            scratch[1, place, :] = part[:, LANES:]
        return carry

    unrolled(side, line, 0)
    parts = separate(jnp.concatenate([scratch[0, : size.rows], scratch[1, : size.rows]], 1))
    for ref, part in zip((first, second, third), parts):
        ref[...] = part.reshape(ref.shape)


def dot(left, right, dims=((1,), (0,))):
    return lax.dot_general(left, right, (dims, ((), ())), preferred_element_type=F32)


def into_padded(size, flat, field):
    side = size.side
    field[...] = jnp.zeros_like(field)

    def line(row, carry):
        field[row + 1, 1 : side + 1] = flat[pl.ds(row * side, side)]
        return carry

    unrolled(side, line, 0)


def stacked_weights(me, positions, w_ref, stacked):
    for index, position in enumerate(positions):
        stacked[index * QUARTER : (index + 1) * QUARTER] = w_ref[me[0] ^ position]


def each_column(size, body, carry):
    plan = size.columns_of(size.whole)
    _, width, _, cells = plan[0]

    def step(index, carry):
        return body(index, pl.multiple_of(index * width, LANES), width, index * cells, cells, carry)

    if len(plan) > 1:
        carry = lax.fori_loop(0, len(plan) - 1, step, carry)
    return body(len(plan) - 1, *plan[-1], carry)


def project_begin_kernel(size, me, x0, x1, w_ref, dense, pool, stacked, stack):
    frames = size.frames
    stacked_weights(me, (0, 1), w_ref, stacked)

    def column(index, start, width, first, cells, carry):
        for x in (x0, x1):
            x.ready(index)
        value = dot(stack[:, pl.ds(start, width)], stacked[...], ((0,), (0,)))
        value = value.reshape(width // frames, frames, 2 * LANES)[:cells]
        dense[pl.ds(first, cells)] = value[:, :, :LANES]
        pool[pl.ds(first, cells)] = value[:, :, LANES:]
        dense.flush(index)
        pool.flush(index)
        return carry

    each_column(size, column, 0)


def project_kernel(size, positions, me, *refs):
    side, frames = size.side, size.frames
    pieces, (w_ref, mask, table), refs = refs[: len(positions)], refs[len(positions) : len(positions) + 3], refs[len(positions) + 3 :]
    begun = refs[:2] if len(positions) < 4 else None
    z0, z1, stat, wire, field, flat, stacked, stack = refs[-8:]
    stacked_weights(me, positions, w_ref, stacked)
    blank = jnp.zeros((frames, LANES), F32)
    total, squares = blank, blank

    def column(index, start, width, first, cells, carry):
        total, squares = carry
        for x in pieces:
            x.ready(index)
        value = dot(stack[:, pl.ds(start, width)], stacked[...], ((0,), (0,)))
        value = value.reshape(width // frames, frames, 2 * LANES)[:cells]
        dense, pool = value[:, :, :LANES], value[:, :, LANES:]
        place = pl.ds(first, cells)
        if begun:
            for stream in begun:
                stream.ready(index)
            dense += begun[0][place]
            pool += begun[1][place]
        z0[place] = dense
        z0.flush(index)
        flat[place] = pool
        return total + jnp.sum(dense, 0), squares + jnp.sum(dense * dense, 0)

    total, squares = each_column(size, column, (total, squares))
    valid = mask[0]
    total, squares = collapse(total * valid), collapse(squares * valid)
    count = collapse(valid) * size.cells
    mean = total / count

    def one(cell, cells, lanes):
        wire[:, lanes] = turn(size, z0[pl.ds(cell, cells)] - mean, cells)[:REDUCED].astype(BF16)

    span_blocks(size, size.whole, one, (), True)
    into_padded(size, flat, field)

    def line(row, carry):
        pool_total, pool_squares = carry
        pool = pool_line(size, field, row, mask)
        z1[pl.ds(row * side, side)] = pool
        z1.flush(row)
        return pool_total + jnp.sum(pool, 0), pool_squares + jnp.sum(pool * pool, 0)

    pool_total, pool_squares = lax.fori_loop(0, side, line, (blank, blank))
    rows = [total, squares, collapse(pool_total * valid), collapse(pool_squares * valid), count]
    publish(stat, rows + [table[0:1], table[1:2]])


def normed_kernel(size, me, z0, z1, totals, table, mask, *refs):
    outs, (field, pooled) = refs[:-2], refs[-2:]
    side, frames, step = size.side, size.frames, size.step
    lane = lax.broadcasted_iota(jnp.int32, (frames, LANES), 1)
    field[...] = jnp.zeros_like(field)
    rows = [norm_rows(totals, table, tile, me[0]) for tile in range(2)]
    scales = [(gain * inverse * inverse, mean) for mean, inverse, gain, _, _ in rows]

    def chunk(index, carry):
        z1.ready(index)
        scale, mean = scales[1]
        value = (z1[pl.ds(index * step, step)] - mean) * scale
        value = jnp.where(lane == POOL, 1.0, value) * mask[0]
        field[pl.ds(1 + index * size.band, size.band), 1 : side + 1] = value.reshape(size.band, side, frames, LANES)
        return carry

    rolled(size.chunks, chunk, 0)
    pool_lines(size, field, pooled, mask)
    for index in range(size.chunks):
        z0.ready(index)
    for part, span in enumerate(size.parts):
        normed, shapes = outs[2 * part : 2 * part + 2]

        def one(cell, cells, lanes, normed=normed, shapes=shapes):
            scale, mean = scales[0]
            value = (z0[pl.ds(cell, cells)] - mean) * scale
            dense = turn(size, jnp.where(lane == DENSE, 1.0, value) * mask[0], cells)
            pool = turn(size, pooled[pl.ds(cell, cells)], cells)
            normed[0:DENSE, lanes] = dense[:DENSE].astype(BF16)
            normed[DENSE:ROWS, lanes] = pool[:POOL].astype(BF16)
            both = jnp.concatenate([dense[DENSE : DENSE + 8], pool[POOL : POOL + 8]], 0)
            shapes[:, lanes] = both.astype(BF16)

        span_blocks(size, span, one, (normed,), True)


def pool_lines(size, field, pooled, mask):
    def line(row, carry):
        pooled[pl.ds(row * size.side, size.side)] = pool_line(size, field, row, mask)
        return carry

    lax.fori_loop(0, size.side, line, 0)


def moments_kernel(size, me, *refs):
    (out, stack), pieces = refs[-2:], refs[-6:-2]
    lefts = refs[:-6]
    each = len(lefts) // len(size.parts)
    lefts = [lefts[part * each : (part + 1) * each] for part in range(len(size.parts))]
    lefts = [group[0][...] if each == 1 else jnp.concatenate([item[...] for item in group], 0) for group in lefts]
    value = jnp.zeros((4 * QUARTER, lefts[0].shape[0]), F32)
    for part, (left, (start, count)) in enumerate(zip(lefts, size.parts)):
        for x in pieces:
            x.ready(part)
        value += dot(stack[:, start : start + count], left, ((1,), (1,)))
    for position in range(4):
        piece = value[position * QUARTER : (position + 1) * QUARTER]
        piece = jnp.concatenate([piece, jnp.zeros((2 * LANES - QUARTER, piece.shape[1]), F32)], 0)
        out[me[0] ^ position] = piece.T


def back_columns(back, owner):
    if len(back.shape) == 2:
        parts = back[:, :LANES].astype(F32)
        return columns_of_table(parts[:8] + parts[8:])
    return columns_of_table(back_table(back, owner))


def back_table(back, owner):
    every = owner_rows(back, owner)
    total, own = jnp.sum(every, 0), every[0]
    count = own[6:7]
    rows = [total[1:2] / count, total[3:4] / count, own[4:5] * total[0:1] / count, own[5:6] * total[2:3] / count]
    return row_table(rows)


def columns_of_table(table):
    turned = table.T
    slope = jnp.concatenate([turned[:DENSE, 0:1], turned[:POOL, 1:2]], 0)
    offset = jnp.concatenate([turned[:DENSE, 2:3], turned[:POOL, 3:4]], 0)
    return slope, offset


def weight_grad_kernel(size, me, inner, moments, back, kernels, out, table, grads, flat):
    value = back_table(back, me[0])
    slope, offset = columns_of_table(value)
    upper = value.astype(BF16).astype(F32)
    table[...] = jnp.concatenate([upper, value - upper], 0).astype(BF16)
    for owner in range(4):
        shape = moments[owner, ROWS : ROWS + 16]
        value = inner[owner] - slope * moments[owner, 0:ROWS]
        first = value[:DENSE] - offset[:DENSE] * shape[0:1]
        last = value[DENSE:] - offset[DENSE:] * shape[8:9]
        value = jnp.concatenate([first, last], 0)
        grads[owner, 0] = value[:, :LANES]
        grads[owner, 1] = value[:, LANES:]
    parts = []
    for extra in range(2):
        rows = pl.ds(extra, ROWS // 2, stride=2)
        for owner in range(4):
            parts.append(jnp.concatenate([grads[owner, 0, rows, :], grads[owner, 1, rows, :]], 1))
    for place, tile in enumerate(pack_rows(parts)):
        flat[pl.ds(place, ROWS // 2, stride=PAIR_TILES), :] = tile
    used = ROWS // 2 * PAIR_TILES
    flat[used:, :] = jnp.zeros((DENSE_ROWS - used, LANES), F32)
    out[:KERNEL_ROWS, :] = kernels[...]
    out[KERNEL_ROWS : KERNEL_ROWS + DENSE_ROWS, :] = flat[...].astype(BF16)
    rest = out.shape[0] - KERNEL_ROWS - DENSE_ROWS
    if rest:
        out[KERNEL_ROWS + DENSE_ROWS :, :] = jnp.zeros((rest, LANES), BF16)


def pool_line(size, field, row, mask):
    side = size.side
    lines = field[pl.ds(row, 3)]
    column = lines[0] + lines[1] + lines[2]
    value = column[0:side] + column[1 : side + 1] + column[2 : side + 2]
    return time_box(value, mask) * (1.0 / 27.0)


def turn(size, value, cells):
    flat = value.reshape(cells * size.frames, value.shape[-1])
    if cells < size.group:
        blank = jnp.zeros((LANES - cells * size.frames, value.shape[-1]), value.dtype)
        flat = jnp.concatenate([flat, blank], 0)
    return flat.T


def conv_kernel(size, me, group, p0, p1, p2, p3, totals, lanes_valid, kernel, mask, field, z2, stat, joined):
    side, frames, step = size.side, size.frames, size.step
    for position, piece in enumerate((p0, p1, p2, p3)):
        owner = me[0] ^ position
        every = owner_rows(totals, owner)
        total = jnp.sum(every, 0)
        sent = totals[pl.ds(group[0], 1), pl.ds(owner, 1)].reshape(8, LANES)
        mean = total[0:1] / total[4:5]
        variance = total[1:2] / total[4:5] - mean * mean
        scale = sent[5:6] * lax.rsqrt(variance + EPSILON)
        offset = (sent[0:1] / sent[4:5] - mean) * scale + sent[6:7]
        turned = row_table([scale, offset]).T
        scale, offset = turned[:REDUCED, 0:1], turned[:REDUCED, 1:2]
        shifted = piece[...].astype(F32) * scale + offset
        value = shifted * sigmoid(shifted)
        joined[pl.ds(pl.multiple_of(owner * MID, 8), MID), :] = value[:MID]
        joined[pl.ds(pl.multiple_of(4 * MID + owner * SMALL, 8), SMALL), :] = value[MID:]
    field[...] = jnp.zeros_like(field)
    joined[4 * REDUCED :, :] = jnp.zeros((2 * LANES - 4 * REDUCED, size.padded), F32)

    def one(first, cells, lanes):
        value = (joined[:, lanes] * lanes_valid[0:1]).T
        value = value.reshape(size.group, frames, 2 * LANES).astype(size.kept)
        for index in range(cells):
            cell = first + index
            row = cell // side if isinstance(cell, int) else lax.div(cell, side)
            field[row + 1, cell - row * side + 1] = value[index]

    span_blocks(size, size.whole, one)
    field.flush(0)
    kernel.ready(0)
    blank = jnp.zeros((frames, LANES), F32)

    def chunk(index, carry):
        total, squares = carry
        parts = []
        for row in range(3):
            for column in range(3):
                part = field[pl.ds(index * size.band + row, size.band), column : column + side]
                parts.append(part.reshape(step * frames, 2 * LANES).astype(BF16))
        value = dot(jnp.concatenate(parts, 1), kernel[...].reshape(18 * LANES, LANES))
        value = time_box(value.reshape(step, frames, LANES), mask) * (1.0 / 3.0)
        z2[pl.ds(index * step, step)] = value
        z2.flush(index)
        return total + jnp.sum(value, 0), squares + jnp.sum(value * value, 0)

    total, squares = unrolled(size.chunks, chunk, (blank, blank))
    valid = mask[0]
    one_row = jnp.zeros((1, LANES), F32)
    rows = [collapse(total * valid), collapse(squares * valid), one_row, one_row, collapse(valid) * size.cells]
    publish(stat, rows)


def halve_into(size, value, scratch, index):
    half = size.side // 2
    value = value.reshape(2, half, 2, size.frames, LANES)
    value = value[0] + value[1]
    value = value[:, 0] + value[:, 1]
    rows = half * size.frames
    scratch[pl.ds(index * rows, rows), :] = value.reshape(rows, LANES)


def halved_rows(scratch):
    count = scratch.shape[0] // 2
    return (scratch[pl.ds(0, count, stride=2), :] + scratch[pl.ds(1, count, stride=2), :]) * 0.125


def first_half_kernel(size, me, z0, z1, totals, table, mask, h0, h1, s0, s1):
    for tile, (z, out, scratch) in enumerate(((z0, h0, s0), (z1, h1, s1))):
        rows = norm_rows(totals, table, tile, me[0])

        def chunk(index, carry, z=z, scratch=scratch, rows=rows):
            z.ready(index)
            value = activate(z[pl.ds(index * size.step, size.step)], rows, mask)
            halve_into(size, value, scratch, index)
            return carry

        rolled(size.chunks, chunk, 0)
        out[...] = halved_rows(scratch).reshape(out.shape)


def second_half_kernel(size, z2, totals, table, mask, h0, h1, out, scratch):
    rows = norm_rows(totals, table, 0)

    def chunk(index, carry):
        z2.ready(index)
        value = activate(z2[pl.ds(index * size.step, size.step)], rows, mask)
        halve_into(size, value, scratch, index)
        return carry

    rolled(size.chunks, chunk, 0)
    value = halved_rows(scratch)
    count = value.shape[0]
    value = assemble(h0[...].reshape(count, LANES), value, h1[...].reshape(count, LANES))
    value = jnp.concatenate([value, jnp.zeros((out.shape[1] - count, 2 * LANES), F32)], 0)
    out[...] = value.T[:QUARTER].astype(BF16)


def strided(scratch, start, count, stride):
    place = pl.ds(start, count, stride=stride)
    return jnp.concatenate([scratch[0, place, :], scratch[1, place, :]], 1)


def output_kernel(size, me, z0, z1, z2, totals, totals2, table, table2, mask, out, scratch):
    side, frames = size.side, size.frames
    parts = [
        activate(z[...], norm_rows(total, tab, tile, me[0]), mask).reshape(size.rows, LANES)
        for z, total, tab, tile in ((z0, totals, table, 0), (z2, totals2, table2, 0), (z1, totals, table, 1))
    ]
    value = assemble(*parts)
    scratch[0, : size.rows] = value[:, :LANES]
    scratch[1, : size.rows] = value[:, LANES:]

    def line(row, carry):
        start = row * side * frames
        lines = [strided(scratch, start + frame, side, frames) for frame in range(8)]
        for place, tile in enumerate(pack_rows(lines)):
            out[0, row, :, place * LANES : (place + 1) * LANES] = tile.astype(BF16)
        return carry

    unrolled(side, line, 0)


def spread(size, grad, scratch):
    value = grad[...].reshape(-1, LANES)
    count = value.shape[0]
    scratch[pl.ds(0, count, stride=2), :] = value
    scratch[pl.ds(1, count, stride=2), :] = value


def grad_chunk(size, grad, scratch, index):
    if scratch is None:
        return grad[pl.ds(index * size.step, size.step)]
    half = size.side // 2
    rows = half * size.frames
    value = scratch[pl.ds(index * rows, rows), :].reshape(half, 1, size.frames, LANES)
    value = jnp.broadcast_to(value, (half, 2, size.frames, LANES)).reshape(1, size.side, size.frames, LANES)
    value = jnp.broadcast_to(value, (2, size.side, size.frames, LANES))
    return value.reshape(size.step, size.frames, LANES)


def second_sums_kernel(size, grad, z2, totals, table, mask, stat, *scratch):
    scratch = scratch[0] if scratch else None
    if scratch is not None:
        spread(size, grad, scratch)
    rows = norm_rows(totals, table, 0)
    blank = jnp.zeros((size.frames, LANES), F32)

    def chunk(index, carry):
        shift_grad, gain_grad = carry
        z2.ready(index)
        value = z2[pl.ds(index * size.step, size.step)]
        inner, normed = inner_grad(grad_chunk(size, grad, scratch, index), value, rows, mask)
        return shift_grad + jnp.sum(inner, 0), gain_grad + jnp.sum(inner * normed, 0)

    shift_grad, gain_grad = rolled(size.chunks, chunk, (blank, blank))
    publish(stat, [collapse(shift_grad), collapse(gain_grad)])


def conv_back_kernel(size, me, grad, z2, totals, back, table, mask, kernel, delta, o0, o1, o2, field, result, turned, *scratch):
    side, frames, step = size.side, size.frames, size.step
    scratch = scratch[0] if scratch else None
    if scratch is not None:
        spread(size, grad, scratch)
    rows = norm_rows(totals, table, 0)
    field[...] = jnp.zeros_like(field)

    def first(index, carry):
        z2.ready(index)
        value = z2[pl.ds(index * step, step)]
        inner, _ = inner_grad(grad_chunk(size, grad, scratch, index), value, rows, mask)
        value = norm_delta(inner, value, rows, back, 0, mask).astype(BF16).astype(size.kept)
        delta[pl.ds(index * step, step)] = value
        delta.flush(index)
        field[pl.ds(1 + index * size.band, size.band), 1 : side + 1] = value.reshape(size.band, side, frames, LANES)
        return carry

    unrolled(size.chunks, first, 0)
    kernel.ready(0)

    def chunk(index, carry):
        parts = []
        for row in range(3):
            for column in range(3):
                part = field[pl.ds(index * size.band + 2 - row, size.band), 2 - column : 2 - column + side]
                parts.append(part.reshape(step * frames, LANES).astype(BF16))
        value = dot(jnp.concatenate(parts, 1), kernel[...].reshape(9 * LANES, 4 * REDUCED))
        result[pl.ds(index * step, step)] = value.reshape(step, frames, 4 * REDUCED)
        return carry

    unrolled(size.chunks, chunk, 0)

    def one(cell, cells, lanes):
        turned[:, lanes] = turn(size, result[pl.ds(cell, cells)], cells)

    span_blocks(size, size.whole, one)
    for position, (out, start) in enumerate(((o0, 0), (o1, 0), (o2, 0), (o2, REDUCED))):
        owner = me[0] ^ position
        mid = turned[pl.ds(pl.multiple_of(owner * MID, 8), MID), :]
        small = turned[pl.ds(pl.multiple_of(4 * MID + owner * SMALL, 8), SMALL), :]
        out[start : start + REDUCED] = jnp.concatenate([mid, small], 0).astype(BF16)


def kernel_grad_kernel(size, field, delta, mask, out, turned, boxed, taps, flat):
    side, frames, step = size.side, size.frames, size.step

    def chunk(index, carry):
        delta.ready(index)
        place = pl.ds(index * step, step)
        boxed[place] = time_box(delta[place].astype(F32), mask)
        return carry

    rolled(size.chunks, chunk, 0)

    def one(cell, cells, lanes):
        value = turn(size, boxed[pl.ds(cell, cells)], cells)
        upper = value.astype(BF16)
        turned[:LANES, lanes] = upper
        turned[LANES:, lanes] = (value - upper.astype(F32)).astype(BF16)

    span_blocks(size, size.whole, one, (), True)
    for row in range(side + 2):
        field.ready(row)

    def tap(index, carry):
        row = index // 3
        part = field[pl.ds(row, side), pl.ds(index - 3 * row, side)].reshape(size.rows, 2 * LANES).astype(BF16)
        value = dot(turned[:, : size.rows], part)
        value = (value[:LANES] + value[LANES:]) * (1.0 / 3.0)
        taps[index, 0] = value[:, :LANES]
        taps[index, 1] = value[:, LANES:]
        return carry

    for index in range(9):
        tap(index, 0)
    lane = lax.broadcasted_iota(jnp.int32, (WIDE // 4, LANES), 1)
    tiles = [None] * MID_TILES

    def add(place, value):
        tiles[place] = value if tiles[place] is None else tiles[place] + value

    for extra in range(4):
        for tap in range(9):
            rows = pl.ds(extra, WIDE // 4, stride=4)
            rest = jnp.where(lane < 4 * MID - LANES, taps[tap, 1, rows, :], 0.0)
            offset = (extra * 9 + tap) * 4 * MID
            value = jnp.concatenate([taps[tap, 0, rows, :], rest, jnp.zeros_like(rest)], 1)
            value = pltpu.roll(value, offset % LANES, 1)
            for index in range(-(-(offset % LANES + 4 * MID) // LANES)):
                add(offset // LANES + index, value[:, index * LANES : (index + 1) * LANES])
    for place, tile in enumerate(tiles):
        flat[pl.ds(place, WIDE // 4, stride=MID_TILES), :] = tile
    lane = lax.broadcasted_iota(jnp.int32, (NARROW // 4, LANES), 1)
    tiles = [None] * SMALL_TILES
    start = 4 * MID - LANES
    for extra in range(4):
        for tap in range(9):
            value = taps[tap, 1, pl.ds(WIDE + extra, NARROW // 4, stride=4), :]
            value = jnp.where((lane >= start) & (lane < start + 4 * SMALL), value, 0.0)
            offset = (extra * 9 + tap) * 4 * SMALL
            value = pltpu.roll(value, (offset - start) % LANES, 1)
            add(offset // LANES, value)
    for place, tile in enumerate(tiles):
        flat[pl.ds(MID_ROWS + place, NARROW // 4, stride=SMALL_TILES), :] = tile
    flat[MID_ROWS + SMALL_ROWS : KERNEL_ROWS, :] = jnp.zeros((KERNEL_ROWS - MID_ROWS - SMALL_ROWS, LANES), F32)
    out[...] = flat[:KERNEL_ROWS].astype(BF16)


def first_sums_kernel(size, adds, me, p0, p1, p2, p3, g0, g1, z0, z1, totals, table, mask, *refs):
    side, step, frames = size.side, size.step, size.frames
    count = len(size.parts)
    if adds:
        swapped, *refs = refs
    stat, outs, refs = refs[0], refs[1 : 1 + count], refs[1 + count :]
    if adds:
        shares, *refs = refs
    field, padded, pooled, *scratch = refs
    s0, s1 = scratch if scratch else (None, None)
    if scratch:
        spread(size, g0, s0)
        spread(size, g1, s1)
    padded[...] = jnp.zeros_like(padded)

    def one(cell, cells, place):
        value = p0[:, place].astype(F32) + p1[:, place].astype(F32)
        value += p2[:REDUCED, place].astype(F32) + p3[REDUCED:, place].astype(F32)
        value = jnp.concatenate([value, jnp.zeros((LANES - REDUCED, LANES), F32)], 0).T
        value = value.reshape(size.group, frames, LANES)
        field[pl.ds(cell, cells)] = value[:cells]

    span_blocks(size, size.whole, one)
    rows0 = norm_rows(totals, table, 0, me[0])
    rows1 = norm_rows(totals, table, 1, me[0])
    blank = jnp.zeros((frames, LANES), F32)

    def chunk(index, carry):
        place = pl.ds(index * step, step)
        z0.ready(index)
        z1.ready(index)
        grad = time_box(field[place], mask) * (1.0 / 3.0) + grad_chunk(size, g0, s0, index)
        inner0, normed0 = inner_grad(grad, z0[place], rows0, mask)
        inner1, normed1 = inner_grad(grad_chunk(size, g1, s1, index), z1[place], rows1, mask)
        field[place] = scales[0] * inner0
        pool = scales[1] * inner1
        padded[pl.ds(1 + index * size.band, size.band), 1 : side + 1] = pool.reshape(size.band, side, frames, LANES)
        sums = (inner0, inner0 * normed0, inner1, inner1 * normed1)
        return tuple(old + jnp.sum(new, 0) for old, new in zip(carry, sums))

    scales = [rows[2] * rows[1] for rows in (rows0, rows1)]
    sums = unrolled(size.chunks, chunk, (blank,) * 4)
    publish(stat, [collapse(item) for item in sums] + scales + [rows0[4]])
    stat.flush(0)
    if adds:
        swapped.ready(0)
        shares[...] = jnp.sum(swapped[...].astype(F32), 0).astype(BF16)
    pool_lines(size, padded, pooled, mask)
    for out, span in zip(outs, size.parts):

        def turned(cell, cells, lanes, out=out):
            out[0:DENSE, lanes] = turn(size, field[pl.ds(cell, cells)], cells)[:DENSE].astype(BF16)
            out[DENSE:ROWS, lanes] = turn(size, pooled[pl.ds(cell, cells)], cells)[:POOL].astype(BF16)

        span_blocks(size, span, turned, (out,))


def input_weights(size, me, weights, block, back, stacked):
    flat_row, pool_row = jnp.zeros((1, 2 * LANES), F32), jnp.zeros((1, 2 * LANES), F32)
    for position, weight in enumerate(weights):
        slope, offset = back_columns(back[position] if len(back) == 4 else back[0], me[0] ^ position)
        stacked[position * ROWS : (position + 1) * ROWS] = weight[block]
        value = weight[block].astype(F32)
        stacked[(position + 4) * ROWS : (position + 5) * ROWS] = (value * -slope).astype(BF16)
        value = value * offset
        flat_row -= collapse(value[:DENSE])
        pool_row -= collapse(value[DENSE:])
    index = lax.broadcasted_iota(jnp.int32, (16, 2 * LANES), 0)
    fixed = jnp.where(index == 0, flat_row, 0.0) + jnp.where(index == 8, pool_row, 0.0)
    stacked[8 * ROWS :] = fixed.astype(BF16)


def input_columns(size, span, streams, stack, stacked, scratch):
    for part, (start, width, _, _) in enumerate(size.columns_of(span)):
        for stream in streams:
            stream.ready(part)
        value = dot(stack[:, start : start + width], stacked[...], ((0,), (0,)))
        row = span[0] + start
        scratch[0, row : row + width, :] = value[:, :LANES]
        scratch[1, row : row + width, :] = value[:, LANES:]


def input_half_kernel(size, me, *refs):
    streams, weights, (back,) = refs[:9], refs[9:13], refs[13:14]
    first, second, third, scratch, stacked, stack = refs[14:]
    input_weights(size, me, weights, 1, (back,), stacked)
    input_columns(size, size.whole, streams, stack, stacked, scratch)
    value = jnp.concatenate([scratch[0, : size.rows, :], scratch[1, : size.rows, :]], 1)
    parts = separate(value * 0.125)
    for ref, part in zip((first, second, third), parts):
        ref[...] = part.reshape(ref.shape)


def input_half_sums_kernel(size, above, me, *refs):
    pieces, (z2, totals, table, mask), refs = refs[:14], refs[14:18], refs[18:]
    (first, second, third, stat), (scratch, stacked, wide), (stack,) = refs[:4], refs[4:7], refs[7:]
    input_half_kernel(size, me, *pieces, first, second, third, scratch, stacked, stack)
    second_sums_kernel(above, second, z2, totals, table, mask, stat, wide)


def input_kernel(size, me, *refs):
    side, frames = size.side, size.frames
    pairs_of = frames // 8
    count = 9 * len(size.parts)
    pieces, weights, back = refs[:count], refs[count : count + 4], refs[count + 4 : count + 8]
    out, scratch, stacked, *stacks = refs[count + 8 :]
    for table in back:
        table.ready(0)
    input_weights(size, me, weights, 0, back, stacked)
    done = 0
    for part, span in enumerate(size.parts):
        input_columns(size, span, pieces[9 * part : 9 * part + 9], stacks[part], stacked, scratch)
        until = sum(size.cells_of(span)) // side
        for row in range(done, until):
            lines = [strided(scratch, row * side * frames + frame, pairs_of * side, 8) for frame in range(8)]
            for place, tile in enumerate(pack_rows(lines)):
                lanes = slice(place * LANES, (place + 1) * LANES)
                out[row * side : (row + 1) * side, :, lanes] = tile.reshape(side, pairs_of, LANES)
            out.flush(row)
        done = until


def pairs(axis_size, shift):
    return [(index, index ^ shift) for index in range(axis_size)]


def gather_four(piece):
    other = lax.ppermute(piece, "chan", pairs(4, 2))
    core = lax.ppermute(piece, "chan", pairs(4, 1))
    both = lax.ppermute(other, "chan", pairs(4, 1))
    return piece, core, other, both


def exchange_four(pieces):
    result = [pieces[0]]
    for shift in (1, 2, 3):
        result.append(lax.ppermute(pieces[shift], "chan", pairs(4, shift)))
    return result


def share(stat):
    return lax.all_to_all(stat, "dp", 0, 0, tiled=True)


def share_all(stat, count):
    return lax.all_to_all(stat, ("dp", "chan"), 0, 0, tiled=True).reshape(count, 4, 8, LANES)


def swap_shares(rows, count):
    return lax.all_to_all(rows.reshape(count, -1, LANES), "dp", 0, 0, tiled=True)


def shares_kernel(*refs):
    *swapped, out = refs
    start = 0
    for ref in swapped:
        count = ref.shape[1]
        value = jnp.sum(ref[...].astype(F32), 0).astype(BF16)
        for device in range(out.shape[0]):
            out[device, start : start + count] = value
        start += count


def all_shares(swapped):
    rows = sum(item.shape[1] for item in swapped)
    (whole,) = call(shares_kernel, [shaped((swapped[0].shape[0], rows, LANES), BF16)], [], [], swapped)
    return lax.all_to_all(whole, "dp", 0, 0, tiled=True)


def other_of(rows, bit, count):
    return lax.ppermute(rows, "dp", pairs(count, 1 << bit))


def joined_halves(group, bit, mine, others):
    low = (group[0] >> bit) & 1
    return jnp.where(low == 0, jnp.concatenate([mine, others], 0), jnp.concatenate([others, mine], 0))


def together(*values):
    return lax.optimization_barrier(values)


def as_rows(flat):
    return flat.reshape(2, -1, LANES).transpose(1, 0, 2).reshape(-1, LANES)


def as_flat(rows):
    return rows.reshape(-1, 2, LANES).transpose(1, 0, 2).reshape(2, -1)


NORM_LANES = (
    (0, REDUCED, PLAIN, 0),
    (0, 0, MID, 64),
    (2, 0, WIDE, 104),
    (0, MID, SMALL, 184),
    (2, WIDE, NARROW, 192),
    (1, 0, POOL, 224),
)


def shifted_lanes(value, source, width, target):
    lane = lax.broadcasted_iota(jnp.int32, value.shape, 1)
    value = jnp.where((lane >= source) & (lane < source + width), value, 0.0)
    return pltpu.roll(value, (target - source) % value.shape[1], 1)


def mask_rows(length0, length1, frames, stride):
    frame = lax.broadcasted_iota(jnp.int32, (frames, LANES), 0)
    ends = (length0, length0 + length1)

    def ident(step):
        place = (frame + step) * stride
        return jnp.where(place >= ends[0], 1, 0) + jnp.where(place >= ends[1], 1, 0)

    here = ident(0)
    valid = jnp.where(frame * stride < ends[1], 1.0, 0.0)
    before = jnp.where((frame > 0) & (ident(-1) == here), 1.0, 0.0)
    after = jnp.where((frame < frames - 1) & (ident(1) == here), 1.0, 0.0)
    return valid, before, after


def prepare_kernel(me, lengths, plain, mid, small, pool, wide, narrow, gains, shifts, *refs):
    outs, (rows, dense, taps) = refs[:-3], refs[-3:]
    mask0, mask1, tables, sent, weights, kernels = outs[0], outs[1], outs[2:6], outs[6:10], outs[10:12], outs[12:14]
    turned, along = outs[14:16], outs[16:18]
    for ref, frames, stride in ((along[0], mask0.shape[1], 1), (along[1], mask1.shape[1], 2)):
        lane = lax.broadcasted_iota(jnp.int32, (8, LANES), 1)
        ref[...] = jnp.where(lax.rem(lane, frames) * stride < lengths[0] + lengths[1], 1.0, 0.0)
    for mask, stride in ((mask0, 1), (mask1, 2)):
        for index, value in enumerate(mask_rows(lengths[0], lengths[1], mask.shape[1], stride)):
            mask[index] = value
    for block in range(2):
        lines = []
        for source in (gains, shifts):
            value = source[...].astype(F32)
            line = jnp.concatenate([value[block : block + 1], value[block + 2 : block + 3]], 1)
            lines.append(jnp.broadcast_to(line, (8, 2 * LANES)))
        found = [[jnp.zeros((8, LANES), F32)] * 2 for _ in range(3)]
        for tile, lane, width, channel in NORM_LANES:
            for index, line in enumerate(lines):
                part = shifted_lanes(line, channel, width, lane)[:, :LANES]
                found[tile][index] = found[tile][index] + part
        tables[2 * block][...] = row_table([found[0][0], found[0][1], found[1][0], found[1][1]])
        tables[2 * block + 1][...] = row_table([found[2][0], found[2][1]])
    for ref, base, outputs in ((mid, 0, MID), (small, MID, SMALL), (plain, REDUCED, PLAIN), (pool, DENSE, POOL)):
        count = ref.shape[0]
        rows[:count, :] = ref[...].astype(F32)
        for block in range(2):
            tiles = [rows[pl.ds(2 * tile + block, outputs // 2, stride=2 * PAIR_TILES), :] for tile in range(PAIR_TILES)]
            line = jnp.concatenate(tiles, 1)
            for extra in range(2):
                place = pl.ds(base + extra, outputs // 2, stride=2)
                for owner in range(4):
                    part = unpack_rows(line, 4 * extra + owner)
                    dense[block, owner, 0, place, :] = part[:, :LANES]
                    dense[block, owner, 1, place, :] = part[:, LANES:]
    lane = lax.broadcasted_iota(jnp.int32, (ROWS, LANES), 1)
    blank = jnp.zeros((LANES, 2 * LANES), F32)
    for block in range(2):
        for owner in range(4):
            rest = jnp.where(lane < QUARTER - LANES, dense[block, owner, 1], 0.0)
            dense[block, owner, 1] = rest
            value = jnp.concatenate([dense[block, owner, 0], rest], 1)
            value = jnp.concatenate([value[:DENSE], blank[: LANES - DENSE], value[DENSE:], blank[: LANES - POOL]], 0)
            weights[block][owner] = value.T[:QUARTER].astype(BF16)
        for position in range(4):
            owner = me[0] ^ position
            value = jnp.concatenate([dense[block, owner, 0], dense[block, owner, 1]], 1)
            sent[position][block] = value.astype(BF16)
    wide_lane = lax.broadcasted_iota(jnp.int32, (WIDE // 4, LANES), 1)
    narrow_lane = lax.broadcasted_iota(jnp.int32, (NARROW // 4, LANES), 1)
    start = 4 * MID - LANES
    for block in range(2):
        rows[: wide.shape[0], :] = wide[...].astype(F32)
        taps[...] = jnp.zeros_like(taps)
        tiles = [rows[pl.ds(2 * tile + block, WIDE // 4, stride=2 * MID_TILES), :] for tile in range(MID_TILES)]
        tiles.append(tiles[0])
        for extra in range(4):
            for tap in range(9):
                offset = (extra * 9 + tap) * 4 * MID
                first, shift = offset // LANES, offset % LANES
                count = -(-(shift + 4 * MID) // LANES)
                value = jnp.concatenate(tiles[first : first + count], 1)
                value = pltpu.roll(value, (count * LANES - shift) % (count * LANES), 1)
                place = pl.ds(extra, WIDE // 4, stride=4)
                taps[tap, 0, place, :] = value[:, :LANES]
                taps[tap, 1, place, :] = jnp.where(wide_lane < start, value[:, LANES : 2 * LANES], 0.0)
        rows[: narrow.shape[0], :] = narrow[...].astype(F32)
        tiles = [rows[pl.ds(2 * tile + block, NARROW // 4, stride=2 * SMALL_TILES), :] for tile in range(SMALL_TILES)]
        for extra in range(4):
            for tap in range(9):
                offset = (extra * 9 + tap) * 4 * SMALL
                value = pltpu.roll(tiles[offset // LANES], (start - offset) % LANES, 1)
                value = jnp.where((narrow_lane >= start) & (narrow_lane < start + 4 * SMALL), value, 0.0)
                taps[tap, 1, pl.ds(WIDE + extra, NARROW // 4, stride=4), :] = value
        for tap in range(9):
            first, second = taps[tap, 0], taps[tap, 1]
            kernels[block][tap] = jnp.concatenate([first, second], 1)[:, : 4 * REDUCED].astype(BF16)
            turned[block][tap, :LANES] = first.T.astype(BF16)
            turned[block][tap, LANES:] = second.T.astype(BF16)


def place_rows(out, sources, count, pairs_rows):
    target = pairs_rows if out.shape[0] == 2 else out.near
    for block, (ref, start) in enumerate(sources):
        target[pl.ds(block, count, stride=2), :] = ref[start : start + count, :]
    if out.shape[0] == 2:
        for index in range(count // 4):
            value = pairs_rows[index * 8 : index * 8 + 8, :]
            for part in range(4):
                place = index * 4 + part
                out[:, place * LANES : (place + 1) * LANES] = value[2 * part : 2 * part + 2]


def finish_kernel(me, group, early, halves, late, first0, first1, second0, second1, *refs):
    outs, (rows, other, pairs_rows) = refs[:-3], refs[-3:]
    mid, small, plain, pool, wide, narrow, gains, shifts = outs
    count, share = late.shape[:2]
    bits = count.bit_length() - 1
    low = group[0] & 1
    for index in range(count // 2):
        device = sum(((index >> bit) & 1) << (bits - 1 - bit) for bit in range(bits))
        place = slice(index * share, (index + 1) * share)
        rows[pl.ds(pl.multiple_of((device + low) * share, 16), share)] = early[place].astype(F32)
        rows[pl.ds(pl.multiple_of((device + 1 - low) * share, 16), share)] = halves[place].astype(F32)
    late.ready(0)
    for device in range(late.shape[0]):
        place = slice(device * share, (device + 1) * share)
        other[place] = late[device].astype(F32)
    place_rows(wide, ((other, 0), (rows, 0)), MID_ROWS, pairs_rows)
    wide.flush(0)
    place_rows(narrow, ((other, MID_ROWS), (rows, MID_ROWS)), SMALL_ROWS, pairs_rows)
    start = KERNEL_ROWS
    for out, outputs in ((mid, MID), (small, SMALL), (plain, PLAIN), (pool, POOL)):
        count = outputs * CIN // LANES
        place_rows(out, ((other, start), (rows, start)), count, pairs_rows)
        start += count
    for block, first_ref, second_ref in ((0, first0, second0), (1, first1, second1)):
        first = jnp.sum(owner_rows(first_ref, me[0]), 0)
        second = jnp.sum(second_ref[...], 0)
        for out, row in ((gains, 1), (shifts, 0)):
            lines = (first[row : row + 1], first[row + 2 : row + 3], second[row : row + 1])
            total = jnp.zeros((8, 2 * LANES), F32)
            for tile, lane, width, channel in NORM_LANES:
                line = jnp.concatenate([lines[tile], jnp.zeros((1, LANES), F32)], 1)
                total += shifted_lanes(jnp.broadcast_to(line, (8, 2 * LANES)), lane, width, channel)
            out[block : block + 1, :] = total[0:1, :LANES]
            out[block + 2 : block + 3, :] = total[0:1, LANES:]


def project(size, me, pieces, positions, dense, mask, table, everyone, begun=()):
    side, cells, frames = size.side, size.cells, size.frames
    tile = shaped((cells, frames, LANES))
    count = len(positions)
    column_cells = (0, [(first, held) for _, _, first, held in size.columns_of(size.whole)])
    ins = {index: column_parts(size, size.whole) for index in range(count)}
    ins |= {count + 3 + index: column_cells for index in range(len(begun))}
    return call(
        functools.partial(project_kernel, size, positions),
        [tile, tile, shaped((everyone, 8, LANES)), shaped((REDUCED, size.padded), BF16)],
        [
            pltpu.VMEM((side + 2, side + 2, frames, LANES), F32),
            pltpu.VMEM((cells, frames, LANES), F32),
            pltpu.VMEM((count * QUARTER, 2 * LANES), BF16),
        ],
        [me],
        [*pieces, dense, mask, table, *begun],
        ins=ins,
        puts={0: column_cells, 1: line_parts(size)},
        stacks=[range(count)],
    )


def project_begin(size, me, pieces, dense):
    tile = shaped((size.cells, size.frames, LANES))
    column_cells = (0, [(first, held) for _, _, first, held in size.columns_of(size.whole)])
    return call(
        functools.partial(project_begin_kernel, size),
        [tile, tile],
        [pltpu.VMEM((2 * QUARTER, 2 * LANES), BF16)],
        [me],
        [*pieces, dense],
        ins={index: column_parts(size, size.whole) for index in range(2)},
        puts={0: column_cells, 1: column_cells},
        stacks=[range(2)],
    )


def normed_wires(size, me, z0, z1, totals, table, mask):
    outs, puts = [], {}
    for part, (_, lanes) in enumerate(size.parts):
        outs += [shaped((ROWS, lanes), BF16), shaped((16, lanes), BF16)]
        puts[2 * part] = span_parts(size, size.parts[part])
    wires = call(
        functools.partial(normed_kernel, size),
        outs,
        [
            pltpu.VMEM((size.side + 2, size.side + 2, size.frames, LANES), F32),
            pltpu.VMEM((size.cells, size.frames, LANES), F32),
        ],
        [me],
        [z0, z1, totals, table, mask],
        ins={0: cell_parts(size), 1: cell_parts(size)},
        puts=puts,
    )
    return wires[0::2], wires[1::2]


def moments(size, me, lefts, pieces):
    rows = sum(item.shape[0] for item in lefts[0])
    flat = [item for group in lefts for item in group]
    (result,) = call(
        functools.partial(moments_kernel, size),
        [shaped((4, rows, 2 * LANES))],
        [],
        [me],
        [*flat, *pieces],
        ins={len(flat) + index: (1, size.parts) for index in range(4)},
        stacks=[range(len(flat), len(flat) + 4)],
    )
    return result


def forward_second(size, me, group, pieces, totals, along, kernel, mask, count):
    side, frames = size.side, size.frames
    field, z2, stat = call(
        functools.partial(conv_kernel, size),
        [
            shaped((side + 2, side + 2, frames, 2 * LANES), size.kept),
            shaped((size.cells, frames, LANES)),
            shaped((count, 8, LANES)),
        ],
        [pltpu.VMEM((2 * LANES, size.padded), F32)],
        [me, group],
        [*pieces, totals, along, kernel, mask],
        flops=2 * size.rows * 9 * 256 * 256,
        ins={6: (0, [(0, 9)])},
        puts={0: (0, [(0, side + 2)]), 1: cell_parts(size)},
    )
    return field, z2, stat


def hop(piece, shift):
    return lax.ppermute(piece, "chan", pairs(4, shift))


def second_sums(size, grads, saved, count):
    z2, totals2, table2, mask = saved[4], saved[5], saved[7], saved[8]
    return call(
        functools.partial(second_sums_kernel, size),
        [shaped((count, 8, LANES))],
        spread_rows(size),
        [],
        [grads[1], z2, totals2, table2, mask],
        ins={1: cell_parts(size)},
    )


def spread_rows(size):
    return [pltpu.VMEM((size.rows // 4, LANES), F32)] if size.side % 2 == 0 else []


def weight_grad(size, me, inner, moment, back1, kernels, count):
    unit = count * 16
    total = -(-(KERNEL_ROWS + DENSE_ROWS) // unit) * unit
    return call(
        functools.partial(weight_grad_kernel, size),
        [shaped((total, LANES), BF16), shaped((16, LANES), BF16)],
        [pltpu.VMEM((4, 2, ROWS, LANES), F32), pltpu.VMEM((DENSE_ROWS, LANES), F32)],
        [me],
        [inner, moment, back1, kernels],
    )


def backward(size, me, grads, back2, saved, normed, weights_at, count, early=None, moment=None, group=None, above=None):
    z0, z1, totals, field, z2, totals2, table, table2, mask, kernel, pieces, _, shapes = saved
    g0, g2, g1 = grads
    side, frames = size.side, size.frames
    spreads = early is not None
    tile = shaped((size.cells, frames, LANES))
    wire = shaped((REDUCED, size.padded), BF16)
    delta2, o0, o1, o2 = call(
        functools.partial(conv_back_kernel, size),
        [shaped((size.cells, frames, LANES), size.kept), wire, wire, shaped((2 * REDUCED, size.padded), BF16)],
        [
            pltpu.VMEM((side + 2, side + 2, frames, LANES), size.kept),
            pltpu.VMEM((size.cells, frames, 4 * REDUCED), F32),
            pltpu.VMEM((4 * REDUCED, size.padded), F32),
        ]
        + spread_rows(size),
        [me],
        [g2, z2, totals2, back2, table2, mask, kernel],
        flops=2 * size.rows * 9 * 256 * 256,
        ins={1: cell_parts(size), 6: (0, [(0, 9)])},
        puts={0: cell_parts(size)},
    )
    if spreads:
        o2, normed = together(o2, normed)
        normed = [[*wires, hop(wires[2], 1)] for wires in normed]
    partial = [o0, hop(o1, 1), hop(o2, 2)]
    (kernel_grad,) = call(
        functools.partial(kernel_grad_kernel, size),
        [shaped((KERNEL_ROWS, LANES), BF16)],
        [
            pltpu.VMEM((2 * LANES, size.padded), BF16),
            pltpu.VMEM((size.cells, frames, LANES), F32),
            pltpu.VMEM((9, 2, LANES, LANES), F32),
            pltpu.VMEM((KERNEL_ROWS + 3 * ROOM, LANES), F32),
        ],
        [],
        [field, delta2, mask],
        flops=2 * size.rows * 9 * 256 * 256,
        ins={0: (0, even(side + 2, side + 2)), 1: cell_parts(size)},
    )
    if spreads:
        early, o1 = together(early, o1)
        swapped = swap_shares(early, count)
        partial[2], kernel_grad = together(partial[2], kernel_grad)
    else:
        partial[2], kernel_grad = together(partial[2], kernel_grad)
    if not spreads:
        partial[1], normed = together(partial[1], normed)
    partial.append(hop(partial[2], 1))
    if spreads:
        partial[3], swapped = together(partial[3], swapped)
    devices = count if spreads else 4 * count
    added = [shaped(swapped.shape[1:], BF16)] if spreads else []
    stat, *wires = call(
        functools.partial(first_sums_kernel, size, spreads),
        [shaped((devices, 8, LANES))] + [shaped((ROWS, lanes), BF16) for _, lanes in size.parts] + added,
        [
            pltpu.VMEM((size.cells, frames, LANES), F32),
            pltpu.VMEM((side + 2, side + 2, frames, LANES), F32),
            pltpu.VMEM((size.cells, frames, LANES), F32),
        ]
        + spread_rows(size) * 2,
        [me],
        [*partial, g0, g1, z0, z1, totals, table, mask] + ([swapped] if spreads else []),
        ins={6: cell_parts(size), 7: cell_parts(size)} | ({11: (0, [(0, count)])} if spreads else {}),
        puts={0: (0, [(0, devices)])} | {1 + part: span_parts(size, span) for part, span in enumerate(size.parts)},
    )
    if spreads:
        *wires, early = wires
    others, cores = [hop(wire, 2) for wire in wires[:1]] + [None] * (len(wires) - 1), [hop(wire, 1) for wire in wires[:1]] + [None] * (len(wires) - 1)
    inner = moments(size, me, [[wire] for wire in wires], pieces)
    if spreads:
        bits = count.bit_length() - 1
        back1 = share(stat)
        halves = other_of(early, bits - 1, count)
        back1, inner, others[0], halves = together(back1, inner, others[0], halves)
        dense_grad, table_own = weight_grad(size, me, inner, moment, back1, kernel_grad, count)
        room = wires[1].shape[1] - LANES
        wires[1] = jnp.concatenate([wires[1], jnp.pad(table_own, ((0, 0), (0, room)))], 0)
        others[1], cores[1] = hop(wires[1], 2), hop(wires[1], 1)
        tables = [wires[1], cores[1], others[1], hop(others[1], 1)]
        swapped = swap_shares(dense_grad, count)
    else:
        back1 = share_all(stat, count)
        back1, others[0], moment = together(back1, others[0], moment)

    def four(part):
        return [wires[part], cores[part], others[part], hop(others[part], 1)]

    scratch = [pltpu.VMEM((2, size.parts[0][1] + LANES, LANES), F32), pltpu.VMEM((8 * ROWS + 16, 2 * LANES), BF16)]
    if not spreads:
        top, top_args = above
        result = call(
            functools.partial(input_half_sums_kernel, size, top),
            [tile, tile, tile, shaped((count, 8, LANES))],
            scratch + spread_rows(top),
            [me],
            [*four(0), *normed[0], shapes[0], *weights_at, back1, *top_args],
            ins={index: column_parts(size, size.whole) for index in range(9)} | {14: cell_parts(top)},
            stacks=[range(9)],
        )
        return result, inner, kernel_grad, back1, moment
    shape = shaped((size.cells, frames // 8, 8 * QUARTER))
    for bit in range(bits - 1, 0, -1):
        early = joined_halves(group, bit, early, halves)
        halves = other_of(early, bit - 1, count)
        if bit == 2:
            swapped, halves = together(swapped, halves)
    late = all_shares([swapped])
    args, ins, stacks = [], {}, []
    for part, span in enumerate(size.parts):
        first = len(args)
        args += [*(tables if part else four(part)), *normed[part], shapes[part]]
        ins |= {first + index: column_parts(size, span) for index in range(9)}
        if part:
            ins |= {first + index: (*column_parts(size, span), (0, ROWS)) for index in range(4)}
        stacks.append(range(first, first + 9))
    args += weights_at
    ins |= {len(args) + index: (1, [(0, LANES)], (ROWS, 16)) for index in range(4)}
    args += tables
    result = call(
        functools.partial(input_kernel, size),
        [shape],
        [pltpu.VMEM((2, size.padded + ROOM, LANES), F32), pltpu.VMEM((8 * ROWS + 16, 2 * LANES), BF16)],
        [me],
        args,
        ins=ins,
        puts={0: line_parts(size)},
        stacks=stacks,
    )
    return result, (early, halves, late), back1


def on_device(count, clips, clip_len, w_plain, w_mid, k_mid, w_small, k_small, w_pool, gains, shifts, grad_out):
    big = Size(clips.shape[1], 8 * clips.shape[0])
    low = Size(grad_out.shape[1], 8 * grad_out.shape[0])
    me = lax.axis_index("chan").astype(jnp.int32).reshape(1)
    group = lax.axis_index("dp").astype(jnp.int32).reshape(1)
    everyone = 4 * count
    raw = clips.transpose(1, 2, 0, 3).reshape(big.cells, clips.shape[0], 8 * QUARTER)
    (own,) = call(
        functools.partial(unpack_kernel, big),
        [shaped((QUARTER, big.padded), BF16)],
        [pltpu.VMEM((2, big.rows + ROOM, LANES), F32)],
        [],
        [raw],
        ins={0: line_parts(big)},
        puts={0: span_parts(big, big.whole)},
    )
    other, core = hop(own, 2), hop(own, 1)
    low_tile = shaped((low.cells, low.frames, LANES))
    grads = call(
        functools.partial(grad_kernel, low),
        [low_tile, low_tile, low_tile],
        [pltpu.VMEM((2, low.rows + ROOM, LANES), F32)],
        [],
        [grad_out],
    )
    table = shaped((8, LANES))
    prepared = call(
        prepare_kernel,
        [shaped((3, big.frames, LANES)), shaped((3, low.frames, LANES))]
        + [table] * 4
        + [shaped((2, ROWS, 2 * LANES), BF16)] * 4
        + [shaped((4, QUARTER, 2 * LANES), BF16)] * 2
        + [shaped((9, LANES, 4 * REDUCED), BF16)] * 2
        + [shaped((9, 2 * LANES, LANES), BF16)] * 2
        + [table] * 2,
        [
            pltpu.VMEM((2 * MID_ROWS + 6 * ROOM, LANES), F32),
            pltpu.VMEM((2, 4, 2, ROWS, LANES), F32),
            pltpu.VMEM((9, 2, LANES, LANES), F32),
        ],
        [me, clip_len],
        [as_rows(item) for item in (w_plain, w_mid, w_small, w_pool, k_mid, k_small, gains, shifts)],
    )
    mask, mask_low, table0, second0, table1, second1 = prepared[:6]
    sent, (dense0, dense1), (kernel0, kernel1), (turned0, turned1), (along, along_low) = (
        prepared[6:10],
        prepared[10:12],
        prepared[12:14],
        prepared[14:16],
        prepared[16:18],
    )
    begun = project_begin(big, me, [own, core], dense0)
    other, begun, grads = together(other, begun, grads)
    pieces = [own, core, other, hop(other, 1)]
    z0, z1, stat, wire = project(big, me, pieces[2:], (2, 3), dense0, mask, table0, everyone, begun)
    mids = [wire, hop(wire, 1), hop(wire, 2)]
    totals = share_all(stat, count)
    totals, mids[2] = together(totals, mids[2])
    mids.append(hop(mids[2], 1))
    half = [pltpu.VMEM((big.rows // 4, LANES), F32)]
    h0, h1 = call(
        functools.partial(first_half_kernel, big),
        [low_tile, low_tile],
        half * 2,
        [me],
        [z0, z1, totals, table0, mask],
        flops=big.rows * 2 * LANES * 20,
        ins={0: cell_parts(big), 1: cell_parts(big)},
    )
    field, z2, stat = forward_second(big, me, group, mids, totals, along, turned0, mask, count)
    totals2 = share(stat)
    weights_at = exchange_four(sent)
    totals2, weights_at = together(totals2, weights_at)
    (own1,) = call(
        functools.partial(second_half_kernel, big),
        [shaped((QUARTER, low.padded), BF16)],
        half,
        [],
        [z2, totals2, second0, mask, h0, h1],
        flops=big.rows * LANES * 20,
        ins={0: cell_parts(big)},
    )
    pieces1 = gather_four(own1)
    y0, y1, stat, wire = project(low, me, pieces1, (0, 1, 2, 3), dense1, mask_low, table1, everyone)
    mids = exchange_four([wire] * 4)
    totals1 = share_all(stat, count)
    normed, shapes = normed_wires(big, me, z0, z1, totals, table0, mask)
    totals1, normed, shapes = together(totals1, normed, shapes)
    field1, y2, stat = forward_second(low, me, group, mids, totals1, along_low, turned1, mask_low, count)
    totals3 = share(stat)
    normed1, shapes1 = normed_wires(low, me, y0, y1, totals1, table1, mask_low)
    totals3, normed1 = together(totals3, normed1)
    (mixed,) = call(
        functools.partial(output_kernel, low),
        [shaped(grad_out.shape, BF16)],
        [pltpu.VMEM((2, low.rows + ROOM, LANES), F32)],
        [me],
        [y0, y1, y2, totals1, totals3, table1, second1, mask_low],
    )
    saved1 = (y0, y1, totals1, field1, y2, totals3, table1, second1, mask_low, kernel1, pieces1, normed1, shapes1)
    (back2,) = second_sums(low, grads, saved1, count)
    back2 = share(back2)
    moment1 = moments(low, me, list(zip(normed1, shapes1)), pieces1)
    normed1 = [[wire, hop(wire, 1), hop(wire, 2)] for wire in normed1]
    back2, mixed, normed1, moment1 = together(back2, mixed, normed1, moment1)
    normed1 = [[*wires, hop(wires[2], 1)] for wires in normed1]
    moment = moments(big, me, list(zip(normed, shapes)), pieces)
    grads, inputs1, kernel_grad1, first1, moment = backward(
        low, me, grads, back2, saved1, normed1, weights_at, count, None, moment, above=(big, (z2, totals2, second0, mask))
    )
    last1 = back2
    *grads, back2 = grads

    saved0 = (z0, z1, totals, field, z2, totals2, table0, second0, mask, kernel0, pieces, normed, shapes)
    back2, normed = together(back2, normed)
    back2 = share(back2)
    normed = [[wire, hop(wire, 1), hop(wire, 2)] for wire in normed]
    dense_grad1, _ = weight_grad(low, me, inputs1, moment1, first1, kernel_grad1, count)
    back2, dense_grad1, normed[0] = together(back2, dense_grad1, normed[0])
    last0 = back2
    (clips_grad,), (early, halves, late), first0 = backward(
        big, me, grads, back2, saved0, normed, weights_at, count, dense_grad1, moment, group
    )

    def sized(outputs):
        rows = outputs * CIN // 64
        return shaped((rows, LANES) if rows % 16 == 0 else (2, rows * 64))

    pairs_rows = pltpu.VMEM((2 * MID_ROWS + ROOM, LANES), F32)
    outs = [sized(outputs) for outputs in (MID, SMALL, PLAIN, POOL)]
    outs += [shaped((2, MID_ROWS * LANES)), shaped((2 * SMALL_ROWS, LANES))] + [shaped((4, LANES))] * 2
    mid, small, plain, pool, wide, narrow, gains_grad, shifts_grad = call(
        finish_kernel,
        outs,
        [pltpu.VMEM((count * late.shape[1], LANES), F32)] * 2 + [pairs_rows],
        [me, group],
        [early, halves, late, first0, first1, last0, last1],
        ins={2: (0, [(0, count)])},
        puts={4: (0, [(0, 2)])},
    )
    flats = [plain, mid, wide, small, narrow, pool, gains_grad, shifts_grad]
    flats = [item if item.shape[0] == 2 else as_flat(item) for item in flats]
    shape = (big.side, big.side, big.frames // 8, 8 * QUARTER)
    return mixed, clips_grad.reshape(shape).transpose(2, 0, 1, 3), *flats


def solution(mesh):
    frames = P("dp", None, None, "chan")
    flat = P(None, "chan")
    return jax.shard_map(
        functools.partial(on_device, mesh.shape["dp"]),
        mesh=mesh,
        in_specs=(frames, P("dp")) + (flat,) * 8 + (frames,),
        out_specs=(frames, frames) + (flat,) * 8,
        check_vma=False,
    )
```

```python
import functools

import jax
import jax.numpy as jnp
from jax import lax
from jax.experimental import pallas as pl
from jax.experimental.pallas import tpu as pltpu
from jax.sharding import PartitionSpec as P

CIN = 832
QUARTER = 208
WIDE, NARROW = 80, 32
MID, SMALL, PLAIN, POOL = 40, 8, 64, 32
REDUCED = MID + SMALL
DENSE = REDUCED + PLAIN
ROWS = DENSE + POOL
CLIPS = 2
EPSILON = 1e-05
F32 = jnp.float32
BF16 = jnp.bfloat16
LANES = 128
LIMIT = 64
ROOM = 64
COST = 1
MID_TILES = 4 * 9 * 160 // LANES
MID_ROWS = WIDE // 4 * MID_TILES
SMALL_TILES = 4 * 9 * 32 // LANES
SMALL_ROWS = NARROW // 4 * SMALL_TILES
KERNEL_ROWS = 976
PAIR_TILES = 2 * CIN // LANES
DENSE_ROWS = 944


class Size:
    def __init__(self, side, frames):
        self.side = side
        self.frames = frames
        self.cells = side * side
        self.rows = self.cells * frames
        self.padded = -(-self.rows // LANES) * LANES
        self.band = 2 if side % 2 == 0 else side
        self.chunks = side // self.band
        self.step = self.band * side
        self.group = LANES // frames
        self.full = self.cells // self.group
        self.rest = self.cells - self.full * self.group
        self.kept = BF16 if frames % 16 == 0 else F32
        self.whole = (0, self.padded)
        first = 13 * LANES
        self.parts = [(0, first), (first, self.padded - first)] if self.padded > 2 * first - LANES - 1 else [self.whole]

    def cells_of(self, span):
        first = span[0] // self.frames
        return first, min(span[1] // self.frames, self.cells - first)

    def columns_of(self, span, width=640):
        first, count = self.cells_of(span)
        result = []
        for start in range(0, span[1], width):
            skipped, held = start // self.frames, min(width, span[1] - start)
            result.append((start, held, first + skipped, min(held // self.frames, count - skipped)))
        return result


class Stream:
    def __init__(self, far, near, sems, axis, parts, window=None):
        self.far, self.near, self.sems, self.axis, self.parts = far, near, sems, axis, parts
        self.window = window
        self.shape, self.dtype = near.shape, near.dtype

    def copy(self, part, inward):
        if isinstance(part, int):
            start, count = self.parts[part]
        else:
            first, count = self.parts[0]
            start = first + part * count
        index = (slice(None),) * self.axis + (pl.ds(start, count),)
        away = (pl.ds(*self.window),) + index[1:] if self.window else index
        pair = (self.far.at[away], self.near.at[index])
        return pltpu.make_async_copy(*(pair if inward else pair[::-1]), self.sems.at[part])

    def ready(self, part):
        self.copy(part, True).wait()

    def flush(self, part):
        self.copy(part, False).start()

    def __getitem__(self, index):
        return self.near[index]

    def __setitem__(self, index, value):
        self.near[index] = value

    @property
    def at(self):
        return self.near.at


def even(total, count):
    return [(start * (total // count), total // count) for start in range(count)]


def cell_parts(size):
    return 0, even(size.cells, size.chunks)


def line_parts(size, first=0, count=None):
    return 0, [(row * size.side, size.side) for row in range(first, first + (count or size.side))]


def column_parts(size, span, width=640):
    return 1, [(start, held) for start, held, _, _ in size.columns_of(span, width)]


def call(body, outs, scratch, scalars, args, flops=0, ins=None, puts=None, aliases=None, stacks=()):
    ins, puts = ins or {}, puts or {}
    places = {}

    def height(index):
        plan = ins.get(index)
        return plan[2][1] if plan and len(plan) > 2 else args[index].shape[0]

    for stack, members in enumerate(stacks):
        start = 0
        for index in members:
            places[index] = (stack, start)
            start += height(index)
    aliases = {len(scalars) + index: out for index, out in (aliases or {}).items()}
    plans = [ins.get(index) for index in range(len(args))] + [puts.get(index) for index in range(len(outs))]
    arrays = list(args) + list(outs)
    buffers = []
    for index, (array, plan) in enumerate(zip(arrays, plans)):
        if index not in places:
            rows = height(index) if index < len(args) else array.shape[0]
            buffers.append(pltpu.VMEM((rows,) + array.shape[1:], array.dtype))
        buffers.append(pltpu.SemaphoreType.DMA((max(len(plan[1]), 1) if plan else 1,)))
    for members in stacks:
        rows = sum(height(index) for index in members)
        buffers.append(pltpu.VMEM((rows,) + args[members[0]].shape[1:], args[members[0]].dtype))

    def wrapped(*refs):
        numbers, refs = refs[: len(scalars)], refs[len(scalars) :]
        far, refs = refs[: len(arrays)], refs[len(arrays) :]
        own, refs = refs[: len(scratch)], list(refs[len(scratch) :])
        whole = refs[len(refs) - len(stacks) :]
        streams = []
        for index, plan in enumerate(plans):
            axis, parts, *window = plan or (0, [(0, arrays[index].shape[0])])
            if index in places:
                stack, start = places[index]
                near = whole[stack].at[pl.ds(start, height(index))]
            else:
                near = refs.pop(0)
            streams.append(Stream(far[index], near, refs.pop(0), axis, parts, *window))
        entering, leaving = streams[: len(args)], streams[len(args) :]
        for part in range(max([len(stream.parts) for stream in entering])):
            for stream in entering:
                if part < len(stream.parts):
                    stream.copy(part, True).start()
        for index, stream in enumerate(entering):
            if index not in ins:
                stream.ready(0)
        body(*numbers, *entering, *leaving, *own, *whole)
        for index, stream in enumerate(leaving):
            if index not in puts:
                stream.flush(0)
        for stream in leaving:
            for part in range(len(stream.parts)):
                stream.copy(part, False).wait()

    moved = sum(array.size * array.dtype.itemsize for array in arrays)
    return pl.pallas_call(
        wrapped,
        out_shape=outs,
        in_specs=[pl.BlockSpec(memory_space=pltpu.SMEM)] * len(scalars) + [pl.BlockSpec(memory_space=pl.ANY)] * len(args),
        out_specs=[pl.BlockSpec(memory_space=pl.ANY)] * len(outs),
        scratch_shapes=list(scratch) + buffers,
        compiler_params=pltpu.CompilerParams(vmem_limit_bytes=LIMIT * 1024 * 1024),
        cost_estimate=pl.CostEstimate(flops=COST, bytes_accessed=COST, transcendentals=0),
        input_output_aliases=aliases,
    )(*scalars, *args)


def unrolled(count, body, carry):
    for index in range(count):
        carry = body(index, carry)
    return carry


def rolled(count, body, carry):
    if count == 1:
        return body(0, carry)
    return lax.fori_loop(0, count, body, carry)


def shaped(shape, dtype=F32):
    return jax.ShapeDtypeStruct(shape, dtype)


def sigmoid(value):
    return 0.5 * jnp.tanh(0.5 * value) + 0.5


def row_table(rows):
    index = lax.broadcasted_iota(jnp.int32, (8, LANES), 0)
    table = jnp.zeros((8, LANES), F32)
    for position, row in enumerate(rows):
        table = jnp.where(index == position, row, table)
    return table


def time_box(value, mask_ref):
    cells, frames, width = value.shape
    flat = value.reshape(cells * frames, width)
    before = pltpu.roll(flat, 1, 0).reshape(value.shape)
    after = pltpu.roll(flat, cells * frames - 1, 0).reshape(value.shape)
    return value + before * mask_ref[1] + after * mask_ref[2]


def owner_rows(all_ref, owner):
    if len(all_ref.shape) == 3:
        return all_ref[...]
    return all_ref[:, pl.ds(owner, 1)].reshape(all_ref.shape[0], 8, LANES)


def norm_rows(all_ref, table_ref, tile, owner=0):
    total = jnp.sum(owner_rows(all_ref, owner), 0)
    count = total[4:5]
    mean = total[2 * tile : 2 * tile + 1] / count
    variance = total[2 * tile + 1 : 2 * tile + 2] / count - mean * mean
    inverse = lax.rsqrt(variance + EPSILON)
    gain = table_ref[2 * tile : 2 * tile + 1]
    shift = table_ref[2 * tile + 1 : 2 * tile + 2]
    return mean, inverse, gain, shift, count


def activate(value, rows, mask_ref):
    mean, inverse, gain, shift, _ = rows
    shifted = gain * ((value - mean) * inverse) + shift
    return shifted * sigmoid(shifted) * mask_ref[0]


def inner_grad(grad, value, rows, mask_ref):
    mean, inverse, gain, shift, _ = rows
    normed = (value - mean) * inverse
    shifted = gain * normed + shift
    sigma = sigmoid(shifted)
    return grad * mask_ref[0] * sigma * (1.0 + shifted * (1.0 - sigma)), normed


def norm_delta(inner, value, rows, back_ref, tile, mask_ref):
    mean, inverse, gain, _, count = rows
    total = jnp.sum(back_ref[...], 0)
    shift_grad = total[2 * tile : 2 * tile + 1] / count
    gain_grad = total[2 * tile + 1 : 2 * tile + 2] / count
    normed = (value - mean) * inverse
    return (gain * inverse) * (inner - mask_ref[0] * (shift_grad + normed * gain_grad))


def publish(stat_ref, rows):
    stat_ref[...] = jnp.broadcast_to(row_table(rows)[None], stat_ref.shape)


def collapse(value):
    return jnp.sum(value, 0, keepdims=True)


def windows():
    result = []
    for frame in range(8):
        start = frame * QUARTER
        first, offset = start // LANES, start % LANES
        result.append((first, -(-(offset + QUARTER) // LANES), offset))
    return result


def unpack_rows(line, frame):
    first, tiles, offset = windows()[frame]
    value = line[:, first * LANES : (first + tiles) * LANES]
    if offset:
        value = pltpu.roll(value, tiles * LANES - offset, 1)
    return value[:, : 2 * LANES]


def pack_rows(parts):
    tiles = [None] * 13
    for frame, value in enumerate(parts):
        first, count, offset = windows()[frame]
        if count == 3:
            value = jnp.concatenate([value, jnp.zeros((value.shape[0], LANES), value.dtype)], 1)
        if offset:
            value = pltpu.roll(value, offset, 1)
        for index in range(count):
            piece = value[:, index * LANES : (index + 1) * LANES]
            place = first + index
            tiles[place] = piece if tiles[place] is None else tiles[place] + piece
    return tiles


def assemble(first, second, third):
    blank = jnp.zeros_like(first)
    lane = lax.broadcasted_iota(jnp.int32, (first.shape[0], 2 * LANES), 1)
    plain = pltpu.roll(jnp.concatenate([first, blank], 1), 2 * LANES - REDUCED, 1)
    middle = pltpu.roll(jnp.concatenate([second, blank], 1), PLAIN, 1)
    pool = pltpu.roll(jnp.concatenate([third, blank], 1), PLAIN + WIDE + NARROW, 1)
    return jnp.where(lane < PLAIN, plain, 0.0) + middle + pool


def separate(value):
    lane = lax.broadcasted_iota(jnp.int32, (value.shape[0], LANES), 1)
    plain = pltpu.roll(value, REDUCED, 1)[:, :LANES]
    middle = pltpu.roll(value, 2 * LANES - PLAIN, 1)[:, :LANES]
    pool = pltpu.roll(value, 2 * LANES - PLAIN - WIDE - NARROW, 1)[:, :LANES]
    first = jnp.where((lane >= REDUCED) & (lane < DENSE), plain, 0.0)
    second = jnp.where(lane < WIDE + NARROW, middle, 0.0)
    third = jnp.where(lane < POOL, pool, 0.0)
    return first, second, third


def span_blocks(size, span, one, leaving=(), rolled=False):
    first, count = size.cells_of(span)
    total, whole = span[1] // LANES, count // size.group

    def block(index, cells):
        start = index * LANES
        start = start if isinstance(start, int) else pl.multiple_of(start, LANES)
        one(first + index * size.group, cells, pl.ds(start, LANES))

    def four(index, carry):
        for extra in range(4):
            block(index * 4 + extra, size.group)
        for stream in leaving:
            stream.flush(index)
        return carry

    groups = whole // 4 if rolled else 0
    if rolled:
        lax.fori_loop(0, groups, four, 0)
    for index in range(groups * 4, total):
        block(index, min(size.group, count - index * size.group))
        if index % 4 == 3 or index == total - 1:
            for stream in leaving:
                stream.flush(index // 4)


def span_parts(size, span):
    return column_parts(size, span, 4 * LANES)


def unpack_kernel(size, raw, out, scratch):
    side, frames = size.side, size.frames
    pairs_of = frames // 8
    def line(row, carry):
        raw.ready(row)
        value = raw[pl.ds(row * side, side)].astype(F32).reshape(pairs_of * side, 8 * QUARTER)
        for frame in range(8):
            place = pl.ds(row * side * frames + frame, pairs_of * side, stride=8)
            piece = unpack_rows(value, frame)
            scratch[0, place, :] = piece[:, :LANES]
            scratch[1, place, :] = piece[:, LANES:]
        return carry

    lax.fori_loop(0, side, line, 0)

    def one(cell, cells, lanes):
        start = cell * frames
        for tile, (low, high) in enumerate(((0, LANES), (LANES, QUARTER))):
            value = scratch[tile, pl.ds(start, cells * frames), :].reshape(cells, frames, LANES)
            out[low:high, lanes] = turn(size, value, cells)[: high - low].astype(BF16)

    span_blocks(size, size.whole, one, (out,))


def grad_kernel(size, raw, first, second, third, scratch):
    side, frames = size.side, size.frames

    def line(row, carry):
        value = raw[0, row].astype(F32)
        for frame in range(8):
            place = pl.ds(row * side * frames + frame, side, stride=frames)
            part = unpack_rows(value, frame)
            scratch[0, place, :] = part[:, :LANES]
            scratch[1, place, :] = part[:, LANES:]
        return carry

    unrolled(side, line, 0)
    parts = separate(jnp.concatenate([scratch[0, : size.rows], scratch[1, : size.rows]], 1))
    for ref, part in zip((first, second, third), parts):
        ref[...] = part.reshape(ref.shape)


def dot(left, right, dims=((1,), (0,))):
    return lax.dot_general(left, right, (dims, ((), ())), preferred_element_type=F32)


def into_padded(size, flat, field):
    side = size.side
    field[...] = jnp.zeros_like(field)

    def line(row, carry):
        field[row + 1, 1 : side + 1] = flat[pl.ds(row * side, side)]
        return carry

    unrolled(side, line, 0)


def stacked_weights(me, positions, w_ref, stacked):
    for index, position in enumerate(positions):
        stacked[index * QUARTER : (index + 1) * QUARTER] = w_ref[me[0] ^ position]


def each_column(size, body, carry):
    plan = size.columns_of(size.whole)
    _, width, _, cells = plan[0]

    def step(index, carry):
        return body(index, pl.multiple_of(index * width, LANES), width, index * cells, cells, carry)

    if len(plan) > 1:
        carry = lax.fori_loop(0, len(plan) - 1, step, carry)
    return body(len(plan) - 1, *plan[-1], carry)


def project_begin_kernel(size, me, x0, x1, w_ref, dense, pool, stacked, stack):
    frames = size.frames
    stacked_weights(me, (0, 1), w_ref, stacked)

    def column(index, start, width, first, cells, carry):
        for x in (x0, x1):
            x.ready(index)
        value = dot(stack[:, pl.ds(start, width)], stacked[...], ((0,), (0,)))
        value = value.reshape(width // frames, frames, 2 * LANES)[:cells]
        dense[pl.ds(first, cells)] = value[:, :, :LANES]
        pool[pl.ds(first, cells)] = value[:, :, LANES:]
        dense.flush(index)
        pool.flush(index)
        return carry

    each_column(size, column, 0)


def project_kernel(size, positions, me, *refs):
    side, frames = size.side, size.frames
    pieces, (w_ref, mask, table), refs = refs[: len(positions)], refs[len(positions) : len(positions) + 3], refs[len(positions) + 3 :]
    begun = refs[:2] if len(positions) < 4 else None
    z0, z1, stat, wire, field, flat, stacked, stack = refs[-8:]
    stacked_weights(me, positions, w_ref, stacked)
    blank = jnp.zeros((frames, LANES), F32)
    total, squares = blank, blank

    def column(index, start, width, first, cells, carry):
        total, squares = carry
        for x in pieces:
            x.ready(index)
        value = dot(stack[:, pl.ds(start, width)], stacked[...], ((0,), (0,)))
        value = value.reshape(width // frames, frames, 2 * LANES)[:cells]
        dense, pool = value[:, :, :LANES], value[:, :, LANES:]
        place = pl.ds(first, cells)
        if begun:
            for stream in begun:
                stream.ready(index)
            dense += begun[0][place]
            pool += begun[1][place]
        z0[place] = dense
        z0.flush(index)
        flat[place] = pool
        return total + jnp.sum(dense, 0), squares + jnp.sum(dense * dense, 0)

    total, squares = each_column(size, column, (total, squares))
    valid = mask[0]
    total, squares = collapse(total * valid), collapse(squares * valid)
    count = collapse(valid) * size.cells
    mean = total / count

    def one(cell, cells, lanes):
        wire[:, lanes] = turn(size, z0[pl.ds(cell, cells)] - mean, cells)[:REDUCED].astype(BF16)

    span_blocks(size, size.whole, one, (), True)
    into_padded(size, flat, field)

    def line(row, carry):
        pool_total, pool_squares = carry
        pool = pool_line(size, field, row, mask)
        z1[pl.ds(row * side, side)] = pool
        z1.flush(row)
        return pool_total + jnp.sum(pool, 0), pool_squares + jnp.sum(pool * pool, 0)

    pool_total, pool_squares = lax.fori_loop(0, side, line, (blank, blank))
    rows = [total, squares, collapse(pool_total * valid), collapse(pool_squares * valid), count]
    publish(stat, rows + [table[0:1], table[1:2]])


def normed_kernel(size, me, z0, z1, totals, table, mask, *refs):
    outs, (field, pooled) = refs[:-2], refs[-2:]
    side, frames, step = size.side, size.frames, size.step
    lane = lax.broadcasted_iota(jnp.int32, (frames, LANES), 1)
    field[...] = jnp.zeros_like(field)
    rows = [norm_rows(totals, table, tile, me[0]) for tile in range(2)]
    scales = [(gain * inverse * inverse, mean) for mean, inverse, gain, _, _ in rows]

    def chunk(index, carry):
        z1.ready(index)
        scale, mean = scales[1]
        value = (z1[pl.ds(index * step, step)] - mean) * scale
        value = jnp.where(lane == POOL, 1.0, value) * mask[0]
        field[pl.ds(1 + index * size.band, size.band), 1 : side + 1] = value.reshape(size.band, side, frames, LANES)
        return carry

    rolled(size.chunks, chunk, 0)
    pool_lines(size, field, pooled, mask)
    for index in range(size.chunks):
        z0.ready(index)
    for part, span in enumerate(size.parts):
        normed, shapes = outs[2 * part : 2 * part + 2]

        def one(cell, cells, lanes, normed=normed, shapes=shapes):
            scale, mean = scales[0]
            value = (z0[pl.ds(cell, cells)] - mean) * scale
            dense = turn(size, jnp.where(lane == DENSE, 1.0, value) * mask[0], cells)
            pool = turn(size, pooled[pl.ds(cell, cells)], cells)
            normed[0:DENSE, lanes] = dense[:DENSE].astype(BF16)
            normed[DENSE:ROWS, lanes] = pool[:POOL].astype(BF16)
            both = jnp.concatenate([dense[DENSE : DENSE + 8], pool[POOL : POOL + 8]], 0)
            shapes[:, lanes] = both.astype(BF16)

        span_blocks(size, span, one, (normed,), True)


def pool_lines(size, field, pooled, mask):
    def line(row, carry):
        pooled[pl.ds(row * size.side, size.side)] = pool_line(size, field, row, mask)
        return carry

    lax.fori_loop(0, size.side, line, 0)


def moments_kernel(size, me, *refs):
    (out, stack), pieces = refs[-2:], refs[-6:-2]
    lefts = refs[:-6]
    each = len(lefts) // len(size.parts)
    lefts = [lefts[part * each : (part + 1) * each] for part in range(len(size.parts))]
    lefts = [group[0][...] if each == 1 else jnp.concatenate([item[...] for item in group], 0) for group in lefts]
    value = jnp.zeros((4 * QUARTER, lefts[0].shape[0]), F32)
    for part, (left, (start, count)) in enumerate(zip(lefts, size.parts)):
        for x in pieces:
            x.ready(part)
        value += dot(stack[:, start : start + count], left, ((1,), (1,)))
    for position in range(4):
        piece = value[position * QUARTER : (position + 1) * QUARTER]
        piece = jnp.concatenate([piece, jnp.zeros((2 * LANES - QUARTER, piece.shape[1]), F32)], 0)
        out[me[0] ^ position] = piece.T


def back_columns(back, owner):
    if len(back.shape) == 2:
        parts = back[:, :LANES].astype(F32)
        return columns_of_table(parts[:8] + parts[8:])
    return columns_of_table(back_table(back, owner))


def back_table(back, owner):
    every = owner_rows(back, owner)
    total, own = jnp.sum(every, 0), every[0]
    count = own[6:7]
    rows = [total[1:2] / count, total[3:4] / count, own[4:5] * total[0:1] / count, own[5:6] * total[2:3] / count]
    return row_table(rows)


def columns_of_table(table):
    turned = table.T
    slope = jnp.concatenate([turned[:DENSE, 0:1], turned[:POOL, 1:2]], 0)
    offset = jnp.concatenate([turned[:DENSE, 2:3], turned[:POOL, 3:4]], 0)
    return slope, offset


def weight_grad_kernel(size, me, inner, moments, back, kernels, out, table, grads, flat):
    value = back_table(back, me[0])
    slope, offset = columns_of_table(value)
    upper = value.astype(BF16).astype(F32)
    table[...] = jnp.concatenate([upper, value - upper], 0).astype(BF16)
    for owner in range(4):
        shape = moments[owner, ROWS : ROWS + 16]
        value = inner[owner] - slope * moments[owner, 0:ROWS]
        first = value[:DENSE] - offset[:DENSE] * shape[0:1]
        last = value[DENSE:] - offset[DENSE:] * shape[8:9]
        value = jnp.concatenate([first, last], 0)
        grads[owner, 0] = value[:, :LANES]
        grads[owner, 1] = value[:, LANES:]
    parts = []
    for extra in range(2):
        rows = pl.ds(extra, ROWS // 2, stride=2)
        for owner in range(4):
            parts.append(jnp.concatenate([grads[owner, 0, rows, :], grads[owner, 1, rows, :]], 1))
    for place, tile in enumerate(pack_rows(parts)):
        flat[pl.ds(place, ROWS // 2, stride=PAIR_TILES), :] = tile
    used = ROWS // 2 * PAIR_TILES
    flat[used:, :] = jnp.zeros((DENSE_ROWS - used, LANES), F32)
    out[:KERNEL_ROWS, :] = kernels[...]
    out[KERNEL_ROWS : KERNEL_ROWS + DENSE_ROWS, :] = flat[...].astype(BF16)
    rest = out.shape[0] - KERNEL_ROWS - DENSE_ROWS
    if rest:
        out[KERNEL_ROWS + DENSE_ROWS :, :] = jnp.zeros((rest, LANES), BF16)


def pool_line(size, field, row, mask):
    side = size.side
    lines = field[pl.ds(row, 3)]
    column = lines[0] + lines[1] + lines[2]
    value = column[0:side] + column[1 : side + 1] + column[2 : side + 2]
    return time_box(value, mask) * (1.0 / 27.0)


def turn(size, value, cells):
    flat = value.reshape(cells * size.frames, value.shape[-1])
    if cells < size.group:
        blank = jnp.zeros((LANES - cells * size.frames, value.shape[-1]), value.dtype)
        flat = jnp.concatenate([flat, blank], 0)
    return flat.T


def conv_kernel(size, me, group, p0, p1, p2, p3, totals, lanes_valid, kernel, mask, field, z2, stat, joined):
    side, frames, step = size.side, size.frames, size.step
    for position, piece in enumerate((p0, p1, p2, p3)):
        owner = me[0] ^ position
        every = owner_rows(totals, owner)
        total = jnp.sum(every, 0)
        sent = totals[pl.ds(group[0], 1), pl.ds(owner, 1)].reshape(8, LANES)
        mean = total[0:1] / total[4:5]
        variance = total[1:2] / total[4:5] - mean * mean
        scale = sent[5:6] * lax.rsqrt(variance + EPSILON)
        offset = (sent[0:1] / sent[4:5] - mean) * scale + sent[6:7]
        turned = row_table([scale, offset]).T
        scale, offset = turned[:REDUCED, 0:1], turned[:REDUCED, 1:2]
        shifted = piece[...].astype(F32) * scale + offset
        value = shifted * sigmoid(shifted)
        joined[pl.ds(pl.multiple_of(owner * MID, 8), MID), :] = value[:MID]
        joined[pl.ds(pl.multiple_of(4 * MID + owner * SMALL, 8), SMALL), :] = value[MID:]
    field[...] = jnp.zeros_like(field)
    joined[4 * REDUCED :, :] = jnp.zeros((2 * LANES - 4 * REDUCED, size.padded), F32)

    def one(first, cells, lanes):
        value = (joined[:, lanes] * lanes_valid[0:1]).T
        value = value.reshape(size.group, frames, 2 * LANES).astype(size.kept)
        for index in range(cells):
            cell = first + index
            row = cell // side if isinstance(cell, int) else lax.div(cell, side)
            field[row + 1, cell - row * side + 1] = value[index]

    span_blocks(size, size.whole, one)
    field.flush(0)
    kernel.ready(0)
    blank = jnp.zeros((frames, LANES), F32)

    def chunk(index, carry):
        total, squares = carry
        parts = []
        for row in range(3):
            for column in range(3):
                part = field[pl.ds(index * size.band + row, size.band), column : column + side]
                parts.append(part.reshape(step * frames, 2 * LANES).astype(BF16))
        value = dot(jnp.concatenate(parts, 1), kernel[...].reshape(18 * LANES, LANES))
        value = time_box(value.reshape(step, frames, LANES), mask) * (1.0 / 3.0)
        z2[pl.ds(index * step, step)] = value
        z2.flush(index)
        return total + jnp.sum(value, 0), squares + jnp.sum(value * value, 0)

    total, squares = unrolled(size.chunks, chunk, (blank, blank))
    valid = mask[0]
    one_row = jnp.zeros((1, LANES), F32)
    rows = [collapse(total * valid), collapse(squares * valid), one_row, one_row, collapse(valid) * size.cells]
    publish(stat, rows)


def halve_into(size, value, scratch, index):
    half = size.side // 2
    value = value.reshape(2, half, 2, size.frames, LANES)
    value = value[0] + value[1]
    value = value[:, 0] + value[:, 1]
    rows = half * size.frames
    scratch[pl.ds(index * rows, rows), :] = value.reshape(rows, LANES)


def halved_rows(scratch):
    count = scratch.shape[0] // 2
    return (scratch[pl.ds(0, count, stride=2), :] + scratch[pl.ds(1, count, stride=2), :]) * 0.125


def first_half_kernel(size, me, z0, z1, totals, table, mask, h0, h1, s0, s1):
    for tile, (z, out, scratch) in enumerate(((z0, h0, s0), (z1, h1, s1))):
        rows = norm_rows(totals, table, tile, me[0])

        def chunk(index, carry, z=z, scratch=scratch, rows=rows):
            z.ready(index)
            value = activate(z[pl.ds(index * size.step, size.step)], rows, mask)
            halve_into(size, value, scratch, index)
            return carry

        rolled(size.chunks, chunk, 0)
        out[...] = halved_rows(scratch).reshape(out.shape)


def second_half_kernel(size, z2, totals, table, mask, h0, h1, out, scratch):
    rows = norm_rows(totals, table, 0)

    def chunk(index, carry):
        z2.ready(index)
        value = activate(z2[pl.ds(index * size.step, size.step)], rows, mask)
        halve_into(size, value, scratch, index)
        return carry

    unrolled(size.chunks, chunk, 0)
    value = halved_rows(scratch)
    count = value.shape[0]
    value = assemble(h0[...].reshape(count, LANES), value, h1[...].reshape(count, LANES))
    value = jnp.concatenate([value, jnp.zeros((out.shape[1] - count, 2 * LANES), F32)], 0)
    out[...] = value.T[:QUARTER].astype(BF16)


def strided(scratch, start, count, stride):
    place = pl.ds(start, count, stride=stride)
    return jnp.concatenate([scratch[0, place, :], scratch[1, place, :]], 1)


def output_kernel(size, me, z0, z1, z2, totals, totals2, table, table2, mask, out, scratch):
    side, frames = size.side, size.frames
    parts = [
        activate(z[...], norm_rows(total, tab, tile, me[0]), mask).reshape(size.rows, LANES)
        for z, total, tab, tile in ((z0, totals, table, 0), (z2, totals2, table2, 0), (z1, totals, table, 1))
    ]
    value = assemble(*parts)
    scratch[0, : size.rows] = value[:, :LANES]
    scratch[1, : size.rows] = value[:, LANES:]

    def line(row, carry):
        start = row * side * frames
        lines = [strided(scratch, start + frame, side, frames) for frame in range(8)]
        for place, tile in enumerate(pack_rows(lines)):
            out[0, row, :, place * LANES : (place + 1) * LANES] = tile.astype(BF16)
        return carry

    unrolled(side, line, 0)


def spread(size, grad, scratch):
    value = grad[...].reshape(-1, LANES)
    count = value.shape[0]
    scratch[pl.ds(0, count, stride=2), :] = value
    scratch[pl.ds(1, count, stride=2), :] = value


def grad_chunk(size, grad, scratch, index):
    if scratch is None:
        return grad[pl.ds(index * size.step, size.step)]
    half = size.side // 2
    rows = half * size.frames
    value = scratch[pl.ds(index * rows, rows), :].reshape(half, 1, size.frames, LANES)
    value = jnp.broadcast_to(value, (half, 2, size.frames, LANES)).reshape(1, size.side, size.frames, LANES)
    value = jnp.broadcast_to(value, (2, size.side, size.frames, LANES))
    return value.reshape(size.step, size.frames, LANES)


def second_sums_kernel(size, grad, z2, totals, table, mask, stat, *scratch):
    scratch = scratch[0] if scratch else None
    if scratch is not None:
        spread(size, grad, scratch)
    rows = norm_rows(totals, table, 0)
    blank = jnp.zeros((size.frames, LANES), F32)

    def chunk(index, carry):
        shift_grad, gain_grad = carry
        z2.ready(index)
        value = z2[pl.ds(index * size.step, size.step)]
        inner, normed = inner_grad(grad_chunk(size, grad, scratch, index), value, rows, mask)
        return shift_grad + jnp.sum(inner, 0), gain_grad + jnp.sum(inner * normed, 0)

    shift_grad, gain_grad = unrolled(size.chunks, chunk, (blank, blank))
    publish(stat, [collapse(shift_grad), collapse(gain_grad)])


def conv_back_kernel(size, me, grad, z2, totals, back, table, mask, kernel, delta, o0, o1, o2, field, result, turned, *scratch):
    side, frames, step = size.side, size.frames, size.step
    scratch = scratch[0] if scratch else None
    if scratch is not None:
        spread(size, grad, scratch)
    rows = norm_rows(totals, table, 0)
    field[...] = jnp.zeros_like(field)

    def first(index, carry):
        z2.ready(index)
        value = z2[pl.ds(index * step, step)]
        inner, _ = inner_grad(grad_chunk(size, grad, scratch, index), value, rows, mask)
        value = norm_delta(inner, value, rows, back, 0, mask).astype(BF16).astype(size.kept)
        delta[pl.ds(index * step, step)] = value
        delta.flush(index)
        field[pl.ds(1 + index * size.band, size.band), 1 : side + 1] = value.reshape(size.band, side, frames, LANES)
        return carry

    unrolled(size.chunks, first, 0)
    kernel.ready(0)

    def chunk(index, carry):
        parts = []
        for row in range(3):
            for column in range(3):
                part = field[pl.ds(index * size.band + 2 - row, size.band), 2 - column : 2 - column + side]
                parts.append(part.reshape(step * frames, LANES).astype(BF16))
        value = dot(jnp.concatenate(parts, 1), kernel[...].reshape(9 * LANES, 4 * REDUCED))
        result[pl.ds(index * step, step)] = value.reshape(step, frames, 4 * REDUCED)
        return carry

    unrolled(size.chunks, chunk, 0)

    def one(cell, cells, lanes):
        turned[:, lanes] = turn(size, result[pl.ds(cell, cells)], cells)

    span_blocks(size, size.whole, one)
    for position, (out, start) in enumerate(((o0, 0), (o1, 0), (o2, 0), (o2, REDUCED))):
        owner = me[0] ^ position
        mid = turned[pl.ds(pl.multiple_of(owner * MID, 8), MID), :]
        small = turned[pl.ds(pl.multiple_of(4 * MID + owner * SMALL, 8), SMALL), :]
        out[start : start + REDUCED] = jnp.concatenate([mid, small], 0).astype(BF16)


def kernel_grad_kernel(size, field, delta, mask, out, turned, boxed, taps, flat):
    side, frames, step = size.side, size.frames, size.step

    def chunk(index, carry):
        delta.ready(index)
        place = pl.ds(index * step, step)
        boxed[place] = time_box(delta[place].astype(F32), mask)
        return carry

    rolled(size.chunks, chunk, 0)

    def one(cell, cells, lanes):
        value = turn(size, boxed[pl.ds(cell, cells)], cells)
        upper = value.astype(BF16)
        turned[:LANES, lanes] = upper
        turned[LANES:, lanes] = (value - upper.astype(F32)).astype(BF16)

    span_blocks(size, size.whole, one, (), True)
    for row in range(side + 2):
        field.ready(row)

    def tap(index, carry):
        row = index // 3
        part = field[pl.ds(row, side), pl.ds(index - 3 * row, side)].reshape(size.rows, 2 * LANES).astype(BF16)
        value = dot(turned[:, : size.rows], part)
        value = (value[:LANES] + value[LANES:]) * (1.0 / 3.0)
        taps[index, 0] = value[:, :LANES]
        taps[index, 1] = value[:, LANES:]
        return carry

    for index in range(9):
        tap(index, 0)
    lane = lax.broadcasted_iota(jnp.int32, (WIDE // 4, LANES), 1)
    tiles = [None] * MID_TILES

    def add(place, value):
        tiles[place] = value if tiles[place] is None else tiles[place] + value

    for extra in range(4):
        for tap in range(9):
            rows = pl.ds(extra, WIDE // 4, stride=4)
            rest = jnp.where(lane < 4 * MID - LANES, taps[tap, 1, rows, :], 0.0)
            offset = (extra * 9 + tap) * 4 * MID
            value = jnp.concatenate([taps[tap, 0, rows, :], rest, jnp.zeros_like(rest)], 1)
            value = pltpu.roll(value, offset % LANES, 1)
            for index in range(-(-(offset % LANES + 4 * MID) // LANES)):
                add(offset // LANES + index, value[:, index * LANES : (index + 1) * LANES])
    for place, tile in enumerate(tiles):
        flat[pl.ds(place, WIDE // 4, stride=MID_TILES), :] = tile
    lane = lax.broadcasted_iota(jnp.int32, (NARROW // 4, LANES), 1)
    tiles = [None] * SMALL_TILES
    start = 4 * MID - LANES
    for extra in range(4):
        for tap in range(9):
            value = taps[tap, 1, pl.ds(WIDE + extra, NARROW // 4, stride=4), :]
            value = jnp.where((lane >= start) & (lane < start + 4 * SMALL), value, 0.0)
            offset = (extra * 9 + tap) * 4 * SMALL
            value = pltpu.roll(value, (offset - start) % LANES, 1)
            add(offset // LANES, value)
    for place, tile in enumerate(tiles):
        flat[pl.ds(MID_ROWS + place, NARROW // 4, stride=SMALL_TILES), :] = tile
    flat[MID_ROWS + SMALL_ROWS : KERNEL_ROWS, :] = jnp.zeros((KERNEL_ROWS - MID_ROWS - SMALL_ROWS, LANES), F32)
    out[...] = flat[:KERNEL_ROWS].astype(BF16)


def first_sums_kernel(size, adds, me, p0, p1, p2, p3, g0, g1, z0, z1, totals, table, mask, *refs):
    side, step, frames = size.side, size.step, size.frames
    count = len(size.parts)
    if adds:
        swapped, *refs = refs
    stat, outs, refs = refs[0], refs[1 : 1 + count], refs[1 + count :]
    if adds:
        shares, *refs = refs
    field, padded, pooled, *scratch = refs
    s0, s1 = scratch if scratch else (None, None)
    if scratch:
        spread(size, g0, s0)
        spread(size, g1, s1)
    padded[...] = jnp.zeros_like(padded)

    def one(cell, cells, place):
        value = p0[:, place].astype(F32) + p1[:, place].astype(F32)
        value += p2[:REDUCED, place].astype(F32) + p3[REDUCED:, place].astype(F32)
        value = jnp.concatenate([value, jnp.zeros((LANES - REDUCED, LANES), F32)], 0).T
        value = value.reshape(size.group, frames, LANES)
        field[pl.ds(cell, cells)] = value[:cells]

    span_blocks(size, size.whole, one)
    rows0 = norm_rows(totals, table, 0, me[0])
    rows1 = norm_rows(totals, table, 1, me[0])
    blank = jnp.zeros((frames, LANES), F32)

    def chunk(index, carry):
        place = pl.ds(index * step, step)
        z0.ready(index)
        z1.ready(index)
        grad = time_box(field[place], mask) * (1.0 / 3.0) + grad_chunk(size, g0, s0, index)
        inner0, normed0 = inner_grad(grad, z0[place], rows0, mask)
        inner1, normed1 = inner_grad(grad_chunk(size, g1, s1, index), z1[place], rows1, mask)
        field[place] = scales[0] * inner0
        pool = scales[1] * inner1
        padded[pl.ds(1 + index * size.band, size.band), 1 : side + 1] = pool.reshape(size.band, side, frames, LANES)
        sums = (inner0, inner0 * normed0, inner1, inner1 * normed1)
        return tuple(old + jnp.sum(new, 0) for old, new in zip(carry, sums))

    scales = [rows[2] * rows[1] for rows in (rows0, rows1)]
    sums = unrolled(size.chunks, chunk, (blank,) * 4)
    publish(stat, [collapse(item) for item in sums] + scales + [rows0[4]])
    stat.flush(0)
    if adds:
        swapped.ready(0)
        shares[...] = jnp.sum(swapped[...].astype(F32), 0).astype(BF16)
    pool_lines(size, padded, pooled, mask)
    for out, span in zip(outs, size.parts):

        def turned(cell, cells, lanes, out=out):
            out[0:DENSE, lanes] = turn(size, field[pl.ds(cell, cells)], cells)[:DENSE].astype(BF16)
            out[DENSE:ROWS, lanes] = turn(size, pooled[pl.ds(cell, cells)], cells)[:POOL].astype(BF16)

        span_blocks(size, span, turned, (out,))


def input_weights(size, me, weights, block, back, stacked):
    flat_row, pool_row = jnp.zeros((1, 2 * LANES), F32), jnp.zeros((1, 2 * LANES), F32)
    for position, weight in enumerate(weights):
        slope, offset = back_columns(back[position] if len(back) == 4 else back[0], me[0] ^ position)
        stacked[position * ROWS : (position + 1) * ROWS] = weight[block]
        value = weight[block].astype(F32)
        stacked[(position + 4) * ROWS : (position + 5) * ROWS] = (value * -slope).astype(BF16)
        value = value * offset
        flat_row -= collapse(value[:DENSE])
        pool_row -= collapse(value[DENSE:])
    index = lax.broadcasted_iota(jnp.int32, (16, 2 * LANES), 0)
    fixed = jnp.where(index == 0, flat_row, 0.0) + jnp.where(index == 8, pool_row, 0.0)
    stacked[8 * ROWS :] = fixed.astype(BF16)


def input_columns(size, span, streams, stack, stacked, scratch):
    for part, (start, width, _, _) in enumerate(size.columns_of(span)):
        for stream in streams:
            stream.ready(part)
        value = dot(stack[:, start : start + width], stacked[...], ((0,), (0,)))
        row = span[0] + start
        scratch[0, row : row + width, :] = value[:, :LANES]
        scratch[1, row : row + width, :] = value[:, LANES:]


def input_half_kernel(size, me, *refs):
    streams, weights, (back,) = refs[:9], refs[9:13], refs[13:14]
    first, second, third, scratch, stacked, stack = refs[14:]
    input_weights(size, me, weights, 1, (back,), stacked)
    input_columns(size, size.whole, streams, stack, stacked, scratch)
    value = jnp.concatenate([scratch[0, : size.rows, :], scratch[1, : size.rows, :]], 1)
    parts = separate(value * 0.125)
    for ref, part in zip((first, second, third), parts):
        ref[...] = part.reshape(ref.shape)


def input_half_sums_kernel(size, above, me, *refs):
    pieces, (z2, totals, table, mask), refs = refs[:14], refs[14:18], refs[18:]
    (first, second, third, stat), (scratch, stacked, wide), (stack,) = refs[:4], refs[4:7], refs[7:]
    input_half_kernel(size, me, *pieces, first, second, third, scratch, stacked, stack)
    second_sums_kernel(above, second, z2, totals, table, mask, stat, wide)


def input_kernel(size, me, *refs):
    side, frames = size.side, size.frames
    pairs_of = frames // 8
    count = 9 * len(size.parts)
    pieces, weights, back = refs[:count], refs[count : count + 4], refs[count + 4 : count + 8]
    out, scratch, stacked, *stacks = refs[count + 8 :]
    for table in back:
        table.ready(0)
    input_weights(size, me, weights, 0, back, stacked)
    done = 0
    for part, span in enumerate(size.parts):
        input_columns(size, span, pieces[9 * part : 9 * part + 9], stacks[part], stacked, scratch)
        until = sum(size.cells_of(span)) // side
        for row in range(done, until):
            lines = [strided(scratch, row * side * frames + frame, pairs_of * side, 8) for frame in range(8)]
            for place, tile in enumerate(pack_rows(lines)):
                lanes = slice(place * LANES, (place + 1) * LANES)
                out[row * side : (row + 1) * side, :, lanes] = tile.reshape(side, pairs_of, LANES)
            out.flush(row)
        done = until


def pairs(axis_size, shift):
    return [(index, index ^ shift) for index in range(axis_size)]


def gather_four(piece):
    other = lax.ppermute(piece, "chan", pairs(4, 2))
    core = lax.ppermute(piece, "chan", pairs(4, 1))
    both = lax.ppermute(other, "chan", pairs(4, 1))
    return piece, core, other, both


def exchange_four(pieces):
    result = [pieces[0]]
    for shift in (1, 2, 3):
        result.append(lax.ppermute(pieces[shift], "chan", pairs(4, shift)))
    return result


def share(stat):
    return lax.all_to_all(stat, "dp", 0, 0, tiled=True)


def share_all(stat, count):
    return lax.all_to_all(stat, ("dp", "chan"), 0, 0, tiled=True).reshape(count, 4, 8, LANES)


def swap_shares(rows, count):
    return lax.all_to_all(rows.reshape(count, -1, LANES), "dp", 0, 0, tiled=True)


def shares_kernel(*refs):
    *swapped, out = refs
    start = 0
    for ref in swapped:
        count = ref.shape[1]
        value = jnp.sum(ref[...].astype(F32), 0).astype(BF16)
        for device in range(out.shape[0]):
            out[device, start : start + count] = value
        start += count


def all_shares(swapped):
    rows = sum(item.shape[1] for item in swapped)
    (whole,) = call(shares_kernel, [shaped((swapped[0].shape[0], rows, LANES), BF16)], [], [], swapped)
    return lax.all_to_all(whole, "dp", 0, 0, tiled=True)


def other_of(rows, bit, count):
    return lax.ppermute(rows, "dp", pairs(count, 1 << bit))


def joined_halves(group, bit, mine, others):
    low = (group[0] >> bit) & 1
    return jnp.where(low == 0, jnp.concatenate([mine, others], 0), jnp.concatenate([others, mine], 0))


def together(*values):
    return lax.optimization_barrier(values)


def as_rows(flat):
    return flat.reshape(2, -1, LANES).transpose(1, 0, 2).reshape(-1, LANES)


def as_flat(rows):
    return rows.reshape(-1, 2, LANES).transpose(1, 0, 2).reshape(2, -1)


NORM_LANES = (
    (0, REDUCED, PLAIN, 0),
    (0, 0, MID, 64),
    (2, 0, WIDE, 104),
    (0, MID, SMALL, 184),
    (2, WIDE, NARROW, 192),
    (1, 0, POOL, 224),
)


def shifted_lanes(value, source, width, target):
    lane = lax.broadcasted_iota(jnp.int32, value.shape, 1)
    value = jnp.where((lane >= source) & (lane < source + width), value, 0.0)
    return pltpu.roll(value, (target - source) % value.shape[1], 1)


def mask_rows(length0, length1, frames, stride):
    frame = lax.broadcasted_iota(jnp.int32, (frames, LANES), 0)
    ends = (length0, length0 + length1)

    def ident(step):
        place = (frame + step) * stride
        return jnp.where(place >= ends[0], 1, 0) + jnp.where(place >= ends[1], 1, 0)

    here = ident(0)
    valid = jnp.where(frame * stride < ends[1], 1.0, 0.0)
    before = jnp.where((frame > 0) & (ident(-1) == here), 1.0, 0.0)
    after = jnp.where((frame < frames - 1) & (ident(1) == here), 1.0, 0.0)
    return valid, before, after


def prepare_kernel(me, lengths, plain, mid, small, pool, wide, narrow, gains, shifts, *refs):
    outs, (rows, dense, taps) = refs[:-3], refs[-3:]
    mask0, mask1, tables, sent, weights, kernels = outs[0], outs[1], outs[2:6], outs[6:10], outs[10:12], outs[12:14]
    turned, along = outs[14:16], outs[16:18]
    for ref, frames, stride in ((along[0], mask0.shape[1], 1), (along[1], mask1.shape[1], 2)):
        lane = lax.broadcasted_iota(jnp.int32, (8, LANES), 1)
        ref[...] = jnp.where(lax.rem(lane, frames) * stride < lengths[0] + lengths[1], 1.0, 0.0)
    for mask, stride in ((mask0, 1), (mask1, 2)):
        for index, value in enumerate(mask_rows(lengths[0], lengths[1], mask.shape[1], stride)):
            mask[index] = value
    for block in range(2):
        lines = []
        for source in (gains, shifts):
            value = source[...].astype(F32)
            line = jnp.concatenate([value[block : block + 1], value[block + 2 : block + 3]], 1)
            lines.append(jnp.broadcast_to(line, (8, 2 * LANES)))
        found = [[jnp.zeros((8, LANES), F32)] * 2 for _ in range(3)]
        for tile, lane, width, channel in NORM_LANES:
            for index, line in enumerate(lines):
                part = shifted_lanes(line, channel, width, lane)[:, :LANES]
                found[tile][index] = found[tile][index] + part
        tables[2 * block][...] = row_table([found[0][0], found[0][1], found[1][0], found[1][1]])
        tables[2 * block + 1][...] = row_table([found[2][0], found[2][1]])
    for ref, base, outputs in ((mid, 0, MID), (small, MID, SMALL), (plain, REDUCED, PLAIN), (pool, DENSE, POOL)):
        count = ref.shape[0]
        rows[:count, :] = ref[...].astype(F32)
        for block in range(2):
            tiles = [rows[pl.ds(2 * tile + block, outputs // 2, stride=2 * PAIR_TILES), :] for tile in range(PAIR_TILES)]
            line = jnp.concatenate(tiles, 1)
            for extra in range(2):
                place = pl.ds(base + extra, outputs // 2, stride=2)
                for owner in range(4):
                    part = unpack_rows(line, 4 * extra + owner)
                    dense[block, owner, 0, place, :] = part[:, :LANES]
                    dense[block, owner, 1, place, :] = part[:, LANES:]
    lane = lax.broadcasted_iota(jnp.int32, (ROWS, LANES), 1)
    blank = jnp.zeros((LANES, 2 * LANES), F32)
    for block in range(2):
        for owner in range(4):
            rest = jnp.where(lane < QUARTER - LANES, dense[block, owner, 1], 0.0)
            dense[block, owner, 1] = rest
            value = jnp.concatenate([dense[block, owner, 0], rest], 1)
            value = jnp.concatenate([value[:DENSE], blank[: LANES - DENSE], value[DENSE:], blank[: LANES - POOL]], 0)
            weights[block][owner] = value.T[:QUARTER].astype(BF16)
        for position in range(4):
            owner = me[0] ^ position
            value = jnp.concatenate([dense[block, owner, 0], dense[block, owner, 1]], 1)
            sent[position][block] = value.astype(BF16)
    wide_lane = lax.broadcasted_iota(jnp.int32, (WIDE // 4, LANES), 1)
    narrow_lane = lax.broadcasted_iota(jnp.int32, (NARROW // 4, LANES), 1)
    start = 4 * MID - LANES
    for block in range(2):
        rows[: wide.shape[0], :] = wide[...].astype(F32)
        taps[...] = jnp.zeros_like(taps)
        tiles = [rows[pl.ds(2 * tile + block, WIDE // 4, stride=2 * MID_TILES), :] for tile in range(MID_TILES)]
        tiles.append(tiles[0])
        for extra in range(4):
            for tap in range(9):
                offset = (extra * 9 + tap) * 4 * MID
                first, shift = offset // LANES, offset % LANES
                count = -(-(shift + 4 * MID) // LANES)
                value = jnp.concatenate(tiles[first : first + count], 1)
                value = pltpu.roll(value, (count * LANES - shift) % (count * LANES), 1)
                place = pl.ds(extra, WIDE // 4, stride=4)
                taps[tap, 0, place, :] = value[:, :LANES]
                taps[tap, 1, place, :] = jnp.where(wide_lane < start, value[:, LANES : 2 * LANES], 0.0)
        rows[: narrow.shape[0], :] = narrow[...].astype(F32)
        tiles = [rows[pl.ds(2 * tile + block, NARROW // 4, stride=2 * SMALL_TILES), :] for tile in range(SMALL_TILES)]
        for extra in range(4):
            for tap in range(9):
                offset = (extra * 9 + tap) * 4 * SMALL
                value = pltpu.roll(tiles[offset // LANES], (start - offset) % LANES, 1)
                value = jnp.where((narrow_lane >= start) & (narrow_lane < start + 4 * SMALL), value, 0.0)
                taps[tap, 1, pl.ds(WIDE + extra, NARROW // 4, stride=4), :] = value
        for tap in range(9):
            first, second = taps[tap, 0], taps[tap, 1]
            kernels[block][tap] = jnp.concatenate([first, second], 1)[:, : 4 * REDUCED].astype(BF16)
            turned[block][tap, :LANES] = first.T.astype(BF16)
            turned[block][tap, LANES:] = second.T.astype(BF16)


def place_rows(out, sources, count, pairs_rows):
    target = pairs_rows if out.shape[0] == 2 else out.near
    for block, (ref, start) in enumerate(sources):
        target[pl.ds(block, count, stride=2), :] = ref[start : start + count, :]
    if out.shape[0] == 2:
        for index in range(count // 4):
            value = pairs_rows[index * 8 : index * 8 + 8, :]
            for part in range(4):
                place = index * 4 + part
                out[:, place * LANES : (place + 1) * LANES] = value[2 * part : 2 * part + 2]


def finish_kernel(me, group, early, halves, late, first0, first1, second0, second1, *refs):
    outs, (rows, other, pairs_rows) = refs[:-3], refs[-3:]
    mid, small, plain, pool, wide, narrow, gains, shifts = outs
    count, share = late.shape[:2]
    bits = count.bit_length() - 1
    low = group[0] & 1
    for index in range(count // 2):
        device = sum(((index >> bit) & 1) << (bits - 1 - bit) for bit in range(bits))
        place = slice(index * share, (index + 1) * share)
        rows[pl.ds(pl.multiple_of((device + low) * share, 16), share)] = early[place].astype(F32)
        rows[pl.ds(pl.multiple_of((device + 1 - low) * share, 16), share)] = halves[place].astype(F32)
    late.ready(0)
    for device in range(late.shape[0]):
        place = slice(device * share, (device + 1) * share)
        other[place] = late[device].astype(F32)
    place_rows(wide, ((other, 0), (rows, 0)), MID_ROWS, pairs_rows)
    wide.flush(0)
    place_rows(narrow, ((other, MID_ROWS), (rows, MID_ROWS)), SMALL_ROWS, pairs_rows)
    start = KERNEL_ROWS
    for out, outputs in ((mid, MID), (small, SMALL), (plain, PLAIN), (pool, POOL)):
        count = outputs * CIN // LANES
        place_rows(out, ((other, start), (rows, start)), count, pairs_rows)
        start += count
    for block, first_ref, second_ref in ((0, first0, second0), (1, first1, second1)):
        first = jnp.sum(owner_rows(first_ref, me[0]), 0)
        second = jnp.sum(second_ref[...], 0)
        for out, row in ((gains, 1), (shifts, 0)):
            lines = (first[row : row + 1], first[row + 2 : row + 3], second[row : row + 1])
            total = jnp.zeros((8, 2 * LANES), F32)
            for tile, lane, width, channel in NORM_LANES:
                line = jnp.concatenate([lines[tile], jnp.zeros((1, LANES), F32)], 1)
                total += shifted_lanes(jnp.broadcast_to(line, (8, 2 * LANES)), lane, width, channel)
            out[block : block + 1, :] = total[0:1, :LANES]
            out[block + 2 : block + 3, :] = total[0:1, LANES:]


def project(size, me, pieces, positions, dense, mask, table, everyone, begun=()):
    side, cells, frames = size.side, size.cells, size.frames
    tile = shaped((cells, frames, LANES))
    count = len(positions)
    column_cells = (0, [(first, held) for _, _, first, held in size.columns_of(size.whole)])
    ins = {index: column_parts(size, size.whole) for index in range(count)}
    ins |= {count + 3 + index: column_cells for index in range(len(begun))}
    return call(
        functools.partial(project_kernel, size, positions),
        [tile, tile, shaped((everyone, 8, LANES)), shaped((REDUCED, size.padded), BF16)],
        [
            pltpu.VMEM((side + 2, side + 2, frames, LANES), F32),
            pltpu.VMEM((cells, frames, LANES), F32),
            pltpu.VMEM((count * QUARTER, 2 * LANES), BF16),
        ],
        [me],
        [*pieces, dense, mask, table, *begun],
        ins=ins,
        puts={0: column_cells, 1: line_parts(size)},
        stacks=[range(count)],
    )


def project_begin(size, me, pieces, dense):
    tile = shaped((size.cells, size.frames, LANES))
    column_cells = (0, [(first, held) for _, _, first, held in size.columns_of(size.whole)])
    return call(
        functools.partial(project_begin_kernel, size),
        [tile, tile],
        [pltpu.VMEM((2 * QUARTER, 2 * LANES), BF16)],
        [me],
        [*pieces, dense],
        ins={index: column_parts(size, size.whole) for index in range(2)},
        puts={0: column_cells, 1: column_cells},
        stacks=[range(2)],
    )


def normed_wires(size, me, z0, z1, totals, table, mask):
    outs, puts = [], {}
    for part, (_, lanes) in enumerate(size.parts):
        outs += [shaped((ROWS, lanes), BF16), shaped((16, lanes), BF16)]
        puts[2 * part] = span_parts(size, size.parts[part])
    wires = call(
        functools.partial(normed_kernel, size),
        outs,
        [
            pltpu.VMEM((size.side + 2, size.side + 2, size.frames, LANES), F32),
            pltpu.VMEM((size.cells, size.frames, LANES), F32),
        ],
        [me],
        [z0, z1, totals, table, mask],
        ins={0: cell_parts(size), 1: cell_parts(size)},
        puts=puts,
    )
    return wires[0::2], wires[1::2]


def moments(size, me, lefts, pieces):
    rows = sum(item.shape[0] for item in lefts[0])
    flat = [item for group in lefts for item in group]
    (result,) = call(
        functools.partial(moments_kernel, size),
        [shaped((4, rows, 2 * LANES))],
        [],
        [me],
        [*flat, *pieces],
        ins={len(flat) + index: (1, size.parts) for index in range(4)},
        stacks=[range(len(flat), len(flat) + 4)],
    )
    return result


def forward_second(size, me, group, pieces, totals, along, kernel, mask, count):
    side, frames = size.side, size.frames
    field, z2, stat = call(
        functools.partial(conv_kernel, size),
        [
            shaped((side + 2, side + 2, frames, 2 * LANES), size.kept),
            shaped((size.cells, frames, LANES)),
            shaped((count, 8, LANES)),
        ],
        [pltpu.VMEM((2 * LANES, size.padded), F32)],
        [me, group],
        [*pieces, totals, along, kernel, mask],
        flops=2 * size.rows * 9 * 256 * 256,
        ins={6: (0, [(0, 9)])},
        puts={0: (0, [(0, side + 2)]), 1: cell_parts(size)},
    )
    return field, z2, stat


def hop(piece, shift):
    return lax.ppermute(piece, "chan", pairs(4, shift))


def second_sums(size, grads, saved, count):
    z2, totals2, table2, mask = saved[4], saved[5], saved[7], saved[8]
    return call(
        functools.partial(second_sums_kernel, size),
        [shaped((count, 8, LANES))],
        spread_rows(size),
        [],
        [grads[1], z2, totals2, table2, mask],
        ins={1: cell_parts(size)},
    )


def spread_rows(size):
    return [pltpu.VMEM((size.rows // 4, LANES), F32)] if size.side % 2 == 0 else []


def weight_grad(size, me, inner, moment, back1, kernels, count):
    unit = count * 16
    total = -(-(KERNEL_ROWS + DENSE_ROWS) // unit) * unit
    return call(
        functools.partial(weight_grad_kernel, size),
        [shaped((total, LANES), BF16), shaped((16, LANES), BF16)],
        [pltpu.VMEM((4, 2, ROWS, LANES), F32), pltpu.VMEM((DENSE_ROWS, LANES), F32)],
        [me],
        [inner, moment, back1, kernels],
    )


def backward(size, me, grads, back2, saved, normed, weights_at, count, early=None, moment=None, group=None, above=None):
    z0, z1, totals, field, z2, totals2, table, table2, mask, kernel, pieces, _, shapes = saved
    g0, g2, g1 = grads
    side, frames = size.side, size.frames
    spreads = early is not None
    tile = shaped((size.cells, frames, LANES))
    wire = shaped((REDUCED, size.padded), BF16)
    delta2, o0, o1, o2 = call(
        functools.partial(conv_back_kernel, size),
        [shaped((size.cells, frames, LANES), size.kept), wire, wire, shaped((2 * REDUCED, size.padded), BF16)],
        [
            pltpu.VMEM((side + 2, side + 2, frames, LANES), size.kept),
            pltpu.VMEM((size.cells, frames, 4 * REDUCED), F32),
            pltpu.VMEM((4 * REDUCED, size.padded), F32),
        ]
        + spread_rows(size),
        [me],
        [g2, z2, totals2, back2, table2, mask, kernel],
        flops=2 * size.rows * 9 * 256 * 256,
        ins={1: cell_parts(size), 6: (0, [(0, 9)])},
        puts={0: cell_parts(size)},
    )
    if spreads:
        o2, normed = together(o2, normed)
        normed = [[*wires, hop(wires[2], 1)] for wires in normed]
    partial = [o0, hop(o1, 1), hop(o2, 2)]
    (kernel_grad,) = call(
        functools.partial(kernel_grad_kernel, size),
        [shaped((KERNEL_ROWS, LANES), BF16)],
        [
            pltpu.VMEM((2 * LANES, size.padded), BF16),
            pltpu.VMEM((size.cells, frames, LANES), F32),
            pltpu.VMEM((9, 2, LANES, LANES), F32),
            pltpu.VMEM((KERNEL_ROWS + 3 * ROOM, LANES), F32),
        ],
        [],
        [field, delta2, mask],
        flops=2 * size.rows * 9 * 256 * 256,
        ins={0: (0, even(side + 2, side + 2)), 1: cell_parts(size)},
    )
    if spreads:
        early, o1 = together(early, o1)
        swapped = swap_shares(early, count)
        partial[2], kernel_grad = together(partial[2], kernel_grad)
    else:
        partial[2], kernel_grad = together(partial[2], kernel_grad)
    if not spreads:
        partial[1], normed = together(partial[1], normed)
    partial.append(hop(partial[2], 1))
    if spreads:
        partial[3], swapped = together(partial[3], swapped)
    devices = count if spreads else 4 * count
    added = [shaped(swapped.shape[1:], BF16)] if spreads else []
    stat, *wires = call(
        functools.partial(first_sums_kernel, size, spreads),
        [shaped((devices, 8, LANES))] + [shaped((ROWS, lanes), BF16) for _, lanes in size.parts] + added,
        [
            pltpu.VMEM((size.cells, frames, LANES), F32),
            pltpu.VMEM((side + 2, side + 2, frames, LANES), F32),
            pltpu.VMEM((size.cells, frames, LANES), F32),
        ]
        + spread_rows(size) * 2,
        [me],
        [*partial, g0, g1, z0, z1, totals, table, mask] + ([swapped] if spreads else []),
        ins={6: cell_parts(size), 7: cell_parts(size)} | ({11: (0, [(0, count)])} if spreads else {}),
        puts={0: (0, [(0, devices)])} | {1 + part: span_parts(size, span) for part, span in enumerate(size.parts)},
    )
    if spreads:
        *wires, early = wires
    others, cores = [hop(wire, 2) for wire in wires[:1]] + [None] * (len(wires) - 1), [hop(wire, 1) for wire in wires[:1]] + [None] * (len(wires) - 1)
    inner = moments(size, me, [[wire] for wire in wires], pieces)
    if spreads:
        bits = count.bit_length() - 1
        back1 = share(stat)
        halves = other_of(early, bits - 1, count)
        back1, inner, others[0], halves = together(back1, inner, others[0], halves)
        dense_grad, table_own = weight_grad(size, me, inner, moment, back1, kernel_grad, count)
        room = wires[1].shape[1] - LANES
        wires[1] = jnp.concatenate([wires[1], jnp.pad(table_own, ((0, 0), (0, room)))], 0)
        others[1], cores[1] = hop(wires[1], 2), hop(wires[1], 1)
        tables = [wires[1], cores[1], others[1], hop(others[1], 1)]
        swapped = swap_shares(dense_grad, count)
    else:
        back1 = share_all(stat, count)
        back1, others[0], moment = together(back1, others[0], moment)

    def four(part):
        return [wires[part], cores[part], others[part], hop(others[part], 1)]

    scratch = [pltpu.VMEM((2, size.parts[0][1] + LANES, LANES), F32), pltpu.VMEM((8 * ROWS + 16, 2 * LANES), BF16)]
    if not spreads:
        top, top_args = above
        result = call(
            functools.partial(input_half_sums_kernel, size, top),
            [tile, tile, tile, shaped((count, 8, LANES))],
            scratch + spread_rows(top),
            [me],
            [*four(0), *normed[0], shapes[0], *weights_at, back1, *top_args],
            ins={index: column_parts(size, size.whole) for index in range(9)} | {14: cell_parts(top)},
            stacks=[range(9)],
        )
        return result, inner, kernel_grad, back1, moment
    shape = shaped((size.cells, frames // 8, 8 * QUARTER))
    for bit in range(bits - 1, 0, -1):
        early = joined_halves(group, bit, early, halves)
        halves = other_of(early, bit - 1, count)
        if bit == 2:
            swapped, halves = together(swapped, halves)
    late = all_shares([swapped])
    args, ins, stacks = [], {}, []
    for part, span in enumerate(size.parts):
        first = len(args)
        args += [*(tables if part else four(part)), *normed[part], shapes[part]]
        ins |= {first + index: column_parts(size, span) for index in range(9)}
        if part:
            ins |= {first + index: (*column_parts(size, span), (0, ROWS)) for index in range(4)}
        stacks.append(range(first, first + 9))
    args += weights_at
    ins |= {len(args) + index: (1, [(0, LANES)], (ROWS, 16)) for index in range(4)}
    args += tables
    result = call(
        functools.partial(input_kernel, size),
        [shape],
        [pltpu.VMEM((2, size.padded + ROOM, LANES), F32), pltpu.VMEM((8 * ROWS + 16, 2 * LANES), BF16)],
        [me],
        args,
        ins=ins,
        puts={0: line_parts(size)},
        stacks=stacks,
    )
    return result, (early, halves, late), back1


def on_device(count, clips, clip_len, w_plain, w_mid, k_mid, w_small, k_small, w_pool, gains, shifts, grad_out):
    big = Size(clips.shape[1], 8 * clips.shape[0])
    low = Size(grad_out.shape[1], 8 * grad_out.shape[0])
    me = lax.axis_index("chan").astype(jnp.int32).reshape(1)
    group = lax.axis_index("dp").astype(jnp.int32).reshape(1)
    everyone = 4 * count
    raw = clips.transpose(1, 2, 0, 3).reshape(big.cells, clips.shape[0], 8 * QUARTER)
    (own,) = call(
        functools.partial(unpack_kernel, big),
        [shaped((QUARTER, big.padded), BF16)],
        [pltpu.VMEM((2, big.rows + ROOM, LANES), F32)],
        [],
        [raw],
        ins={0: line_parts(big)},
        puts={0: span_parts(big, big.whole)},
    )
    other, core = hop(own, 2), hop(own, 1)
    low_tile = shaped((low.cells, low.frames, LANES))
    grads = call(
        functools.partial(grad_kernel, low),
        [low_tile, low_tile, low_tile],
        [pltpu.VMEM((2, low.rows + ROOM, LANES), F32)],
        [],
        [grad_out],
    )
    table = shaped((8, LANES))
    prepared = call(
        prepare_kernel,
        [shaped((3, big.frames, LANES)), shaped((3, low.frames, LANES))]
        + [table] * 4
        + [shaped((2, ROWS, 2 * LANES), BF16)] * 4
        + [shaped((4, QUARTER, 2 * LANES), BF16)] * 2
        + [shaped((9, LANES, 4 * REDUCED), BF16)] * 2
        + [shaped((9, 2 * LANES, LANES), BF16)] * 2
        + [table] * 2,
        [
            pltpu.VMEM((2 * MID_ROWS + 6 * ROOM, LANES), F32),
            pltpu.VMEM((2, 4, 2, ROWS, LANES), F32),
            pltpu.VMEM((9, 2, LANES, LANES), F32),
        ],
        [me, clip_len],
        [as_rows(item) for item in (w_plain, w_mid, w_small, w_pool, k_mid, k_small, gains, shifts)],
    )
    mask, mask_low, table0, second0, table1, second1 = prepared[:6]
    sent, (dense0, dense1), (kernel0, kernel1), (turned0, turned1), (along, along_low) = (
        prepared[6:10],
        prepared[10:12],
        prepared[12:14],
        prepared[14:16],
        prepared[16:18],
    )
    begun = project_begin(big, me, [own, core], dense0)
    other, begun, grads = together(other, begun, grads)
    pieces = [own, core, other, hop(other, 1)]
    z0, z1, stat, wire = project(big, me, pieces[2:], (2, 3), dense0, mask, table0, everyone, begun)
    mids = [wire, hop(wire, 1), hop(wire, 2)]
    totals = share_all(stat, count)
    totals, mids[2] = together(totals, mids[2])
    mids.append(hop(mids[2], 1))
    half = [pltpu.VMEM((big.rows // 4, LANES), F32)]
    h0, h1 = call(
        functools.partial(first_half_kernel, big),
        [low_tile, low_tile],
        half * 2,
        [me],
        [z0, z1, totals, table0, mask],
        flops=big.rows * 2 * LANES * 20,
        ins={0: cell_parts(big), 1: cell_parts(big)},
    )
    field, z2, stat = forward_second(big, me, group, mids, totals, along, turned0, mask, count)
    totals2 = share(stat)
    weights_at = exchange_four(sent)
    totals2, weights_at = together(totals2, weights_at)
    (own1,) = call(
        functools.partial(second_half_kernel, big),
        [shaped((QUARTER, low.padded), BF16)],
        half,
        [],
        [z2, totals2, second0, mask, h0, h1],
        flops=big.rows * LANES * 20,
        ins={0: cell_parts(big)},
    )
    pieces1 = gather_four(own1)
    y0, y1, stat, wire = project(low, me, pieces1, (0, 1, 2, 3), dense1, mask_low, table1, everyone)
    mids = exchange_four([wire] * 4)
    totals1 = share_all(stat, count)
    normed, shapes = normed_wires(big, me, z0, z1, totals, table0, mask)
    totals1, normed, shapes = together(totals1, normed, shapes)
    field1, y2, stat = forward_second(low, me, group, mids, totals1, along_low, turned1, mask_low, count)
    totals3 = share(stat)
    normed1, shapes1 = normed_wires(low, me, y0, y1, totals1, table1, mask_low)
    totals3, normed1 = together(totals3, normed1)
    (mixed,) = call(
        functools.partial(output_kernel, low),
        [shaped(grad_out.shape, BF16)],
        [pltpu.VMEM((2, low.rows + ROOM, LANES), F32)],
        [me],
        [y0, y1, y2, totals1, totals3, table1, second1, mask_low],
    )
    saved1 = (y0, y1, totals1, field1, y2, totals3, table1, second1, mask_low, kernel1, pieces1, normed1, shapes1)
    (back2,) = second_sums(low, grads, saved1, count)
    back2 = share(back2)
    moment1 = moments(low, me, list(zip(normed1, shapes1)), pieces1)
    normed1 = [[wire, hop(wire, 1), hop(wire, 2)] for wire in normed1]
    back2, mixed, normed1, moment1 = together(back2, mixed, normed1, moment1)
    normed1 = [[*wires, hop(wires[2], 1)] for wires in normed1]
    moment = moments(big, me, list(zip(normed, shapes)), pieces)
    grads, inputs1, kernel_grad1, first1, moment = backward(
        low, me, grads, back2, saved1, normed1, weights_at, count, None, moment, above=(big, (z2, totals2, second0, mask))
    )
    last1 = back2
    *grads, back2 = grads

    saved0 = (z0, z1, totals, field, z2, totals2, table0, second0, mask, kernel0, pieces, normed, shapes)
    back2, normed = together(back2, normed)
    back2 = share(back2)
    normed = [[wire, hop(wire, 1), hop(wire, 2)] for wire in normed]
    dense_grad1, _ = weight_grad(low, me, inputs1, moment1, first1, kernel_grad1, count)
    back2, dense_grad1, normed[0] = together(back2, dense_grad1, normed[0])
    last0 = back2
    (clips_grad,), (early, halves, late), first0 = backward(
        big, me, grads, back2, saved0, normed, weights_at, count, dense_grad1, moment, group
    )

    def sized(outputs):
        rows = outputs * CIN // 64
        return shaped((rows, LANES) if rows % 16 == 0 else (2, rows * 64))

    pairs_rows = pltpu.VMEM((2 * MID_ROWS + ROOM, LANES), F32)
    outs = [sized(outputs) for outputs in (MID, SMALL, PLAIN, POOL)]
    outs += [shaped((2, MID_ROWS * LANES)), shaped((2 * SMALL_ROWS, LANES))] + [shaped((4, LANES))] * 2
    mid, small, plain, pool, wide, narrow, gains_grad, shifts_grad = call(
        finish_kernel,
        outs,
        [pltpu.VMEM((count * late.shape[1], LANES), F32)] * 2 + [pairs_rows],
        [me, group],
        [early, halves, late, first0, first1, last0, last1],
        ins={2: (0, [(0, count)])},
        puts={4: (0, [(0, 2)])},
    )
    flats = [plain, mid, wide, small, narrow, pool, gains_grad, shifts_grad]
    flats = [item if item.shape[0] == 2 else as_flat(item) for item in flats]
    shape = (big.side, big.side, big.frames // 8, 8 * QUARTER)
    return mixed, clips_grad.reshape(shape).transpose(2, 0, 1, 3), *flats


def solution(mesh):
    frames = P("dp", None, None, "chan")
    flat = P(None, "chan")
    return jax.shard_map(
        functools.partial(on_device, mesh.shape["dp"]),
        mesh=mesh,
        in_specs=(frames, P("dp")) + (flat,) * 8 + (frames,),
        out_specs=(frames, frames) + (flat,) * 8,
        check_vma=False,
    )
```
